32 devices in a mesh: row: 4 (over y, core), col: 8 (over z, x).
Axes of the slice: x: 2, y: 2, z: 4, core: 2. Of those that a mesh axis runs over, the one named last changes fastest.
Arguments:
- block_in: bfloat16 [32768, 1024], P('col', 'row'), may hold values from -6 to 6
- norm_gain: float32 [1024], P('row'), may hold values from 0.25 to 1.75
- proj_inner: bfloat16 [1024, 32, 128], P('row', 'col'), may hold values from -0.1875 to 0.1875
- proj_state: bfloat16 [1024, 288], P('row'), may hold values from -0.1875 to 0.1875
- conv_inner: float32 [4, 2048], P(None, 'col'), may hold values from -3 to 3
- conv_inner_bias: float32 [2048], P('col'), may hold values from -3 to 3
- conv_state: float32 [4, 256], replicated, may hold values from -3 to 3
- conv_state_bias: float32 [256], replicated, may hold values from -3 to 3
- step_bias: float32 [32], P('col'), may hold values from -6.9 to -2.3
- decay_log: float32 [32], P('col'), may hold values from 0 to 2.77
- skip_gain: float32 [32], P('col'), may hold values from 0.5 to 1.5
- gate_gain: float32 [2048], P('col'), may hold values from 0.25 to 1.75
- proj_out: bfloat16 [2048, 1024], P('col', 'row'), may hold values from -0.125 to 0.125
- adapt_in_down: bfloat16 [1024, 128], P('row'), may hold values from -0.1875 to 0.1875
- adapt_in_up: bfloat16 [128, 32, 128], P(None, 'col'), may hold values from -1.5 to 1.5
- adapt_out_down: bfloat16 [128, 2048], P(None, 'col'), may hold values from -0.125 to 0.125
- adapt_out_up: bfloat16 [1024, 128], P('row'), may hold values from -1.5 to 1.5
- adapter_id: int32 [8], replicated, may hold values from 0 to 7, as said below
- cotangent: bfloat16 [32768, 1024], P('col', 'row'), may hold values from -6 to 6
Outputs:
- block_out: bfloat16 [32768, 1024], P('col', 'row')
- input_grad: float32 [32768, 1024], P('col', 'row')
- grad_in_down: float32 [1024, 128], P('row', 'col')
- grad_in_up: float32 [128, 32, 128], P(None, 'col')
- grad_out_down: float32 [128, 2048], P(None, 'col')
- grad_out_up: float32 [1024, 128], P('row', 'col')
The draws below stay inside these ranges and needn't reach their ends.
Inputs may be any that keep to these rules, and one draw needn't show every extreme that they name: `adapter_id`: each adapter is chosen by exactly 1 sequence.
All inputs are finite; a program needn't handle non-finite values.
Results may differ from the reference program's by a relative error of at most 0.025.
Values may be sent and summed in bfloat16 or wider, within the bound.
A program may use at most 640 MiB of HBM per device.

```python
import jax
import jax.numpy as jnp
from jax import lax

D = 1024
H = 32
P_SIZE = 64
N = 128
K = 4
BLOCK = 256
R = 16
NA = 8
SEQ = 4096
DI = 2048
TOKENS = 32768
SEQS = 8


def draw_adapter_id(key, part):
    key = jax.random.fold_in(key, 11)
    order = jax.random.permutation(key, SEQS)
    return (order % NA).astype(jnp.int32)


def block_levels(own_key, dims, split, low, largest):
    def one(axis_at, shards_of):
        steps = jax.random.uniform(jax.random.fold_in(jax.random.fold_in(own_key, 6), axis_at), (shards_of,), jnp.float32, low / len(split), largest / len(split))
        return jnp.repeat(jnp.exp(steps), dims[axis_at] // shards_of).reshape((-1,) + (1,) * (len(dims) - axis_at - 1))

    level = one(*split[0])
    for cut in split[1:]:
        level = level * one(*cut)
    return level


def scatter_about(key, extent, scale, reach, pieces=(), dtype=jnp.bfloat16):
    values = jax.random.normal(key, extent, jnp.float32) * scale
    if len(pieces) > 0:
        values = block_levels(key, extent, pieces, -0.22, 0.18) * values
    return jnp.clip(values, min=-reach, max=reach).astype(dtype)


def setup_inputs(seed: int = 0) -> dict:
    key_list = jax.random.split(jax.random.key(seed), 20)
    return {
        "block_in": scatter_about(key_list[0], (TOKENS, D), 1.0, 6.0, ((0, 8), (1, 4))),
        "norm_gain": jnp.clip(1.0 + 0.15 * jax.random.normal(key_list[1], (D,), jnp.float32), 0.25, 1.75),
        "proj_inner": scatter_about(key_list[2], (D, H, 2 * P_SIZE), D ** -0.5, 0.1875, ((0, 4), (1, 8))),
        "proj_state": scatter_about(key_list[3], (D, 2 * N + H), D ** -0.5, 0.1875, ((0, 4),)),
        "conv_inner": scatter_about(key_list[4], (K, DI), K ** -0.5, 3.0, ((1, 8),), jnp.float32),
        "conv_inner_bias": scatter_about(key_list[5], (DI,), 0.5, 3.0, ((0, 8),), jnp.float32),
        "conv_state": scatter_about(key_list[6], (K, 2 * N), K ** -0.5, 3.0, (), jnp.float32),
        "conv_state_bias": scatter_about(key_list[7], (2 * N,), 0.5, 3.0, (), jnp.float32),
        "step_bias": jnp.clip(-6.9 + 4.6000001430511475 * jax.random.uniform(key_list[8], (H,), jnp.float32) ** block_levels(key_list[8], (H,), ((0, 8),), -0.2, 0.2), -6.9, -2.3),
        "decay_log": jnp.clip(2.77 * jax.random.uniform(key_list[9], (H,), jnp.float32) ** block_levels(key_list[9], (H,), ((0, 8),), -0.2, 0.2), 0.0, 2.77),
        "skip_gain": jnp.clip(0.5 + 1.0 * jax.random.uniform(key_list[10], (H,), jnp.float32) ** block_levels(key_list[10], (H,), ((0, 8),), -0.2, 0.2), 0.5, 1.5),
        "gate_gain": jnp.clip(1.0 + 0.15 * jax.random.normal(key_list[11], (DI,), jnp.float32), 0.25, 1.75),
        "proj_out": scatter_about(key_list[12], (DI, D), DI ** -0.5, 0.125, ((0, 8), (1, 4))),
        "adapt_in_down": scatter_about(key_list[13], (D, NA * R), D ** -0.5, 0.1875, ((0, 4),)),
        "adapt_in_up": scatter_about(key_list[14], (NA * R, H, 2 * P_SIZE), R ** -0.5, 1.5, ((1, 8),)),
        "adapt_out_down": scatter_about(key_list[15], (NA * R, DI), DI ** -0.5, 0.125, ((1, 8),)),
        "adapt_out_up": scatter_about(key_list[16], (D, NA * R), R ** -0.5, 1.5, ((0, 4),)),
        "adapter_id": draw_adapter_id(jax.random.fold_in(key_list[19], 71), 0),
        "cotangent": scatter_about(key_list[18], (TOKENS, D), 1.0, 6.0, ((0, 8), (1, 4))),
    }


EPS = 1e-05
HIGHEST = lax.Precision.HIGHEST

@jax.custom_vjp
def low(v):
    return lax.optimization_barrier(v.astype(jnp.bfloat16)).astype(jnp.float32)

@jax.custom_vjp
def low_back(v):
    return v

def low_keep(v):
    return (low(v), None)

def low_pass(kept, grad):
    return (grad,)

def back_keep(v):
    return (v, None)

def back_low(kept, grad):
    return (low(grad),)
low.defvjp(low_keep, low_pass)
low_back.defvjp(back_keep, back_low)

def to_float(array):
    return array.astype(jnp.float32)

def matmul(left, right):
    return jnp.dot(left, right, precision=HIGHEST, preferred_element_type=jnp.float32)

def causal_conv(values, kernel, bias_row, seq_len):
    length = values.shape[0]
    position = jnp.arange(length) % seq_len
    summed = values * kernel[0] + bias_row
    for offset in range(1, kernel.shape[0]):
        shifted = jnp.concatenate([jnp.zeros((offset, values.shape[1]), jnp.float32), values[:-offset]], axis=0)
        summed = summed + jnp.where((position >= offset)[:, None], shifted, 0.0) * kernel[offset]
    return summed

def scan_blocks(value_heads, b_rows, c_rows, step_size, log_decay, seq_len, block):
    length, head_count, head_dim = value_heads.shape
    states = b_rows.shape[1]
    blocks = length // block
    per_seq = seq_len // block
    seq_count = blocks // per_seq
    value_block = value_heads.reshape(blocks, block, head_count, head_dim)
    b_block = b_rows.reshape(blocks, block, states)
    c_block = c_rows.reshape(blocks, block, states)
    step_block = jnp.swapaxes(step_size.reshape(blocks, block, head_count), 1, 2)
    cumul = jnp.cumsum(jnp.swapaxes(log_decay.reshape(blocks, block, head_count), 1, 2), axis=2)
    scores = jnp.einsum('ctn,csn->cts', c_block, b_block, precision=HIGHEST)
    causal = (jnp.arange(block)[:, None] >= jnp.arange(block)[None, :])[None, None]
    spread = cumul[:, :, :, None] - cumul[:, :, None, :]
    damping = jnp.where(causal, jnp.exp(jnp.where(causal, spread, 0.0)), 0.0)
    weights = low(scores[:, None] * damping * step_block[:, :, None, :])
    within = jnp.einsum('chts,cshp->cthp', weights, value_block, precision=HIGHEST)
    to_end = jnp.exp(cumul[:, :, -1:] - cumul) * step_block
    b_weighted = low(b_block[:, None, :, :] * to_end[..., None])
    added = jnp.einsum('chsn,cshp->chnp', b_weighted, value_block, precision=HIGHEST)
    falloff = jnp.exp(cumul[:, :, -1])

    def advance(carried, inputs):
        factor, addend = inputs
        return (factor[:, :, None, None] * carried + addend, carried)
    initial = jnp.zeros((seq_count, head_count, states, head_dim), jnp.float32)
    fall_steps = jnp.swapaxes(falloff.reshape(seq_count, per_seq, head_count), 0, 1)
    add_steps = jnp.swapaxes(added.reshape(seq_count, per_seq, head_count, states, head_dim), 0, 1)
    _, entering = lax.scan(jax.checkpoint(advance), initial, (fall_steps, add_steps))
    entering = low(jnp.swapaxes(entering, 0, 1).reshape(blocks, head_count, states, head_dim))
    carried_out = jnp.exp(cumul)[..., None] * jnp.einsum('ctn,chnp->chtp', c_block, entering, precision=HIGHEST)
    return (within + jnp.swapaxes(carried_out, 1, 2)).reshape(length, head_count, head_dim)

def mix_heads(inner_value, state_cols, head_first, conv_inner, conv_inner_bias, conv_state, conv_state_bias, step_bias, decay_log, skip_gain, seq_len, block):
    length, head_count, double = inner_value.shape
    head_dim = double // 2
    states = conv_state.shape[1] // 2
    gate_part = inner_value[:, :, :head_dim]
    value_part = inner_value[:, :, head_dim:].reshape(length, head_count * head_dim)
    value_conv = jax.nn.silu(causal_conv(value_part, conv_inner, conv_inner_bias, seq_len))
    state_conv = jax.nn.silu(causal_conv(state_cols[:, :2 * states], conv_state, conv_state_bias, seq_len))
    step_raw = lax.dynamic_slice_in_dim(state_cols, 2 * states + head_first, head_count, 1)
    step_size = jax.nn.softplus(step_raw + step_bias)
    log_decay = -jnp.exp(decay_log) * step_size
    value_low = low(value_conv).reshape(length, head_count, head_dim)
    scanned = scan_blocks(value_low, low(state_conv[:, :states]), low(state_conv[:, states:]), step_size, log_decay, seq_len, block)
    output = scanned + skip_gain[:, None] * value_conv.reshape(length, head_count, head_dim)
    return (output * jax.nn.silu(gate_part)).reshape(length, head_count * head_dim)

def reference(block_in, norm_gain, proj_inner, proj_state, conv_inner, conv_inner_bias, conv_state, conv_state_bias, step_bias, decay_log, skip_gain, gate_gain, proj_out, adapt_in_down, adapt_in_up, adapt_out_down, adapt_out_up, adapter_id, cotangent):
    inner_weight = to_float(proj_inner).reshape(D, H * 2 * P_SIZE)
    state_weight = to_float(proj_state)
    out_weight = to_float(proj_out)
    taps_inner = to_float(conv_inner)
    taps_inner_bias = to_float(conv_inner_bias)
    taps_state = to_float(conv_state)
    taps_state_bias = to_float(conv_state_bias)
    step_offset = to_float(step_bias)
    decay_rates = to_float(decay_log)
    skip_rates = to_float(skip_gain)
    gain_norm = to_float(norm_gain)
    gain_gate = to_float(gate_gain)
    groups = jnp.arange(NA * R) // R
    adapters = (to_float(adapt_in_down), to_float(adapt_in_up), to_float(adapt_out_down), to_float(adapt_out_up))

    def one_sequence(totals, inputs):
        seq_in, seq_cot, chosen = inputs
        picked = (groups == chosen).astype(jnp.float32)[None, :]

        def forward(x_val, in_down, in_up, out_down, out_up):
            inv_rms = lax.rsqrt(lax.optimization_barrier(jnp.mean(x_val * x_val, axis=1, keepdims=True)) + EPS)
            normed = low(x_val * inv_rms * gain_norm)
            state_val = low_back(matmul(normed, state_weight))
            adapt_val = low(low_back(picked * matmul(normed, in_down)))
            inner_val = low_back(matmul(normed, inner_weight) + matmul(adapt_val, in_up.reshape(NA * R, H * 2 * P_SIZE)))
            gated = mix_heads(inner_val.reshape(SEQ, H, 2 * P_SIZE), state_val, 0, taps_inner, taps_inner_bias, taps_state, taps_state_bias, step_offset, decay_rates, skip_rates, SEQ, BLOCK)
            gate_rms = lax.rsqrt(lax.optimization_barrier(jnp.mean(gated * gated, axis=1, keepdims=True)) + EPS)
            mixed = low(gated * gate_rms * gain_gate)
            side_val = low(low_back(picked * matmul(mixed, out_down.T)))
            return x_val + matmul(mixed, out_weight) + matmul(side_val, out_up.T)
        result, pullback = jax.vjp(forward, to_float(seq_in), adapters[0], adapters[1], adapters[2], adapters[3])
        gradients = pullback(to_float(seq_cot))
        totals = tuple((before + addend for before, addend in zip(totals, gradients[1:])))
        return (totals, (result.astype(jnp.bfloat16), gradients[0]))
    initial = tuple((jnp.zeros(adapter.shape, jnp.float32) for adapter in adapters))
    totals, (outputs, input_grads) = lax.scan(one_sequence, initial, (block_in.reshape(SEQS, SEQ, D), cotangent.reshape(SEQS, SEQ, D), adapter_id))
    return (outputs.reshape(TOKENS, D), input_grads.reshape(TOKENS, D), totals[0], totals[1], totals[2], totals[3])
```

```python
import functools

import jax
import jax.numpy as jnp
from jax import lax
from jax.experimental import pallas as pl
from jax.experimental.pallas import tpu as pltpu
from jax.sharding import PartitionSpec as P

D = 1024
HEADS = 32
P_SIZE = 64
STATES = 128
BLOCK = 256
RANK = 16
SEQ = 4096
DI = 2048
EPS = 1e-05
LOG2E = 1.4426950408889634

HALO = 16
QUAD = 4
WIDTH = QUAD * P_SIZE
GROUPS = HEADS // QUAD
LANES = 128
VMEM_BYTES = 60 * 1024 * 1024
F32 = jnp.float32
BF16 = jnp.bfloat16


def mm(left, right):
    return jnp.dot(left, right, preferred_element_type=F32)


def mm_nt(left, right):
    return lax.dot_general(left, right, (((1,), (1,)), ((), ())), preferred_element_type=F32)


def mm_tn(left, right):
    return lax.dot_general(left, right, (((0,), (0,)), ((), ())), preferred_element_type=F32)


def split_left(ones, value):
    high = value.astype(BF16)
    rest = value - high.astype(F32)
    middle = rest.astype(BF16)
    low = (rest - middle.astype(F32)).astype(BF16)
    return mm(ones, high) + mm(ones, middle) + mm(ones, low)


def split_right(value, ones):
    high = value.astype(BF16)
    low = (value - high.astype(F32)).astype(BF16)
    return mm(high, ones) + mm(low, ones)


def sigmoid(value):
    return 0.5 * jnp.tanh(0.5 * value) + 0.5


def iota(shape, axis):
    return lax.broadcasted_iota(jnp.int32, shape, axis)


def widen(cols):
    lane = iota((cols.shape[0], LANES), 1) < P_SIZE
    left = jnp.where(lane, cols[:, 0:1], cols[:, 1:2])
    right = jnp.where(lane, cols[:, 2:3], cols[:, 3:4])
    return jnp.concatenate([left, right], axis=1)


def to_front(cols, group):
    return pltpu.roll(cols, lax.rem(LANES - QUAD * group, LANES), 1)


def head_only(values, head):
    lane = iota(values.shape, 1) // P_SIZE
    return jnp.where(lane == head, values, jnp.zeros_like(values))


def delays(window, taps, bias):
    total = window[8:] * taps[0:1] + bias
    for k in range(1, 4):
        total = total + pltpu.roll(window, k, 0)[8:] * taps[k : k + 1]
    return total


def advances(window, taps, count):
    length = window.shape[0]
    total = window[:count] * taps[0:1]
    for k in range(1, 4):
        total = total + pltpu.roll(window, length - k, 0)[:count] * taps[k : k + 1]
    return total


def at_block(k):
    return pl.ds(pl.multiple_of(k * BLOCK, BLOCK), BLOCK)


def at_rows(k):
    return pl.ds(pl.multiple_of(HALO + k * BLOCK, HALO), BLOCK)


def front_kernel(
    x_ref, gain_ref, wst_ref, sp_ref, hp_ref, w_ref, up_ref, vp_ref,
    normed_ref, scpre_ref, raw_ref, step_ref, cum_ref, cum_t_ref, bs_ref, cs_ref, cs_t_ref, adv_ref,
    gate_ref, u_ref, eloc_ref, fin_ref, dec_ref,
    st_scr, bs_t_scr, val_scr,
):
    group = pl.program_id(0)
    row_count, _, part = x_ref.shape
    blocks = eloc_ref.shape[0]

    @pl.when(group == 0)
    def _():
        def project(rows):
            pieces = [x_ref[r, rows, :].astype(F32) for r in range(row_count)]
            square = sum(jnp.sum(piece * piece, axis=1, keepdims=True) for piece in pieces)
            inv = lax.rsqrt(square / D + EPS)
            total = None
            for r in range(row_count):
                normed = (pieces[r] * inv * gain_ref[r]).astype(BF16)
                normed_ref[rows, r * part : (r + 1) * part] = normed
                term = mm(normed, wst_ref[r])
                total = term if total is None else total + term
            st_scr[rows, :] = total
            adv_ref[rows, :] = total[:, 384:512].astype(BF16)

        project(pl.ds(0, HALO))

        @pl.loop(0, blocks)
        def _(k):
            project(at_rows(k))

        lower = (iota((BLOCK, BLOCK), 0) >= iota((BLOCK, BLOCK), 1)).astype(BF16)
        rate = -jnp.exp(hp_ref[1:2]) * LOG2E

        @pl.loop(0, blocks)
        def _(k):
            window = st_scr[pl.ds(pl.multiple_of(8 + k * BLOCK, 8), BLOCK + 8), :256]
            pre = delays(window, sp_ref[0:4], sp_ref[4:5])
            conv = pre * sigmoid(pre)
            b_rows = conv[:, :STATES].astype(BF16)
            c_rows = conv[:, STATES:].astype(BF16)
            scpre_ref[at_block(k), :] = pre
            bs_ref[at_block(k), :] = b_rows
            cs_ref[at_block(k), :] = c_rows
            bs_t_scr[k] = conv[:, :STATES].T.astype(BF16)
            cs_t_ref[k] = conv[:, STATES:].T.astype(BF16)
            raw = st_scr[at_rows(k), 256:384] + hp_ref[0:1]
            small = jnp.exp(-jnp.abs(raw))
            tail = jnp.where(
                small < 0.01, small * (1.0 - small * (0.5 - small * (1.0 / 3.0))), jnp.log(1.0 + small)
            )
            step = jnp.maximum(raw, 0.0) + tail
            cum = split_left(lower, step * rate)
            raw_ref[at_block(k), :] = raw
            step_ref[at_block(k), :] = step
            cum_ref[at_block(k), :] = cum
            flipped = cum.T
            for g in range(GROUPS):
                cum_t_ref[g, :, at_block(k)] = flipped[g * QUAD : (g + 1) * QUAD]

    def inner(rows):
        total = mm(adv_ref[rows, :], up_ref[0])
        for r in range(row_count):
            total = total + mm(normed_ref[rows, r * part : (r + 1) * part], w_ref[0, r, :part, :])
        return total

    val_scr[0:HALO, :] = inner(pl.ds(0, HALO))[:, WIDTH:]
    taps = vp_ref[0]

    def one_block(k, carry):
        state, decay = carry
        product = inner(at_rows(k))
        gate_ref[at_block(k), :] = product[:, :WIDTH].astype(BF16)
        val_scr[at_rows(k), :] = product[:, WIDTH:]
        window = val_scr[pl.ds(pl.multiple_of(8 + k * BLOCK, 8), BLOCK + 8), :]
        pre = delays(window, taps[0:4], taps[4:5])
        u_ref[at_block(k), :] = pre.astype(BF16)
        xs = (pre * sigmoid(pre)).astype(BF16).astype(F32)
        cum = cum_ref[at_block(k), :]
        last = cum[BLOCK - 1 : BLOCK]
        weight = to_front(step_ref[at_block(k), :] * jnp.exp2(last - cum), group)
        weighted = (xs * widen(weight)).astype(BF16)
        eloc_ref[k] = state
        last8 = to_front(jnp.broadcast_to(last, (8, LANES)), group)
        fall = widen(jnp.exp2(last8))[0:1]
        return fall * state + mm(bs_t_scr[k], weighted), decay * fall

    start = (jnp.zeros((STATES, WIDTH), F32), jnp.ones((1, WIDTH), F32))
    state, decay = lax.fori_loop(0, blocks, one_block, start)
    fin_ref[...] = state.astype(BF16)
    dec_ref[...] = jnp.broadcast_to(decay, (8, WIDTH))


def scan_kernel(
    x_ref, g_ref, oup_ref, w_ref, down_ref, vp_ref, gate_ref, u_ref, eloc_ref, ein_ref,
    step_ref, cum_ref, cum_t_ref, bs_ref, cs_ref,
    out_ref, o_ref, ent_ref, aux_ref, sg_ref, gup_ref,
    score_scr, acc_scr, side_scr, square_scr,
):
    group = pl.program_id(0)
    row_count, _, part = x_ref.shape
    blocks = eloc_ref.shape[0]

    @pl.when(group == 0)
    def _():
        acc_scr[...] = jnp.zeros_like(acc_scr)
        side_scr[...] = jnp.zeros_like(side_scr)
        square_scr[...] = jnp.zeros_like(square_scr)
        keep = iota((BLOCK, BLOCK), 0) >= iota((BLOCK, BLOCK), 1)

        @pl.loop(0, blocks)
        def _(k):
            score = mm_nt(cs_ref[at_block(k), :], bs_ref[at_block(k), :])
            score_scr[k] = jnp.where(keep, score, 0.0)

    taps = vp_ref[0]

    def one_block(k, before):
        rows = at_block(k)
        pre = u_ref[rows, :].astype(F32)
        conv = pre * sigmoid(pre)
        cum = to_front(cum_ref[rows, :], group)
        step = to_front(step_ref[rows, :], group)
        scaled = (conv.astype(BF16).astype(F32) * widen(step)).astype(BF16)
        score = score_scr[k]
        entering = (eloc_ref[k] + before * ein_ref[...]).astype(BF16)
        ent_ref[k] = entering
        total = widen(jnp.exp2(cum)) * mm(cs_ref[rows, :], entering)
        for h in range(QUAD):
            spread = cum[:, h : h + 1] - cum_t_ref[0, h : h + 1, rows]
            weights = (score * jnp.exp2(jnp.minimum(spread, 0.0))).astype(BF16)
            total = total + mm(weights, head_only(scaled, h))
        output = total + taps[6:7] * conv
        o_ref[rows, :] = output.astype(BF16)
        gate = gate_ref[rows, :].astype(F32)
        gated = output * gate * sigmoid(gate)
        square = gated * gated
        square_scr[rows, :] += square[:, :LANES] + square[:, LANES:]
        gained = (gated * taps[5:6]).astype(BF16)
        for r in range(row_count):
            cols = slice(r * part, (r + 1) * part)
            acc_scr[rows, cols] += mm(gained, w_ref[0, r, :, :part])
        side_scr[rows, :] += mm(gained, down_ref[0])
        return before * widen(jnp.exp2(cum[BLOCK - 8 :]))[7:8]

    lax.fori_loop(0, blocks, one_block, jnp.ones((1, WIDTH), F32))

    @pl.when(group == pl.num_programs(0) - 1)
    def _():
        gup_ref[...] = jnp.zeros_like(gup_ref)

        @pl.loop(0, blocks)
        def _(k):
            rows = at_block(k)
            mean = jnp.sum(square_scr[rows, :], axis=1, keepdims=True) / DI
            rms = lax.rsqrt(mean + EPS)
            side_raw = side_scr[rows, :]
            side = (side_raw * rms).astype(BF16)
            side_grad = None
            for r in range(row_count):
                term = mm(g_ref[r, rows, :], oup_ref[r])
                side_grad = term if side_grad is None else side_grad + term
            side_grad = side_grad.astype(BF16)
            product = jnp.sum(side_grad.astype(F32) * side_raw, axis=1, keepdims=True)
            for r in range(row_count):
                cols = slice(r * part, (r + 1) * part)
                raw = acc_scr[rows, cols]
                cot = g_ref[r, rows, :]
                product = product + jnp.sum(raw * cot.astype(F32), axis=1, keepdims=True)
                total = x_ref[r, at_rows(k), :].astype(F32) + raw * rms + mm_nt(side, oup_ref[r])
                out_ref[r, rows, :] = total.astype(BF16)
                gup_ref[:, cols] += mm_tn(side, cot)[:RANK]
            coefficient = rms * rms * rms * product / DI
            lane = iota((BLOCK, LANES), 1)
            aux_ref[rows, :] = jnp.where(lane == 0, rms, coefficient)
            sg_ref[rows, :] = side_grad


def gate_kernel(
    g_ref, w_ref, sg_ref, down_ref, vp_ref, gate_ref, o_ref, aux_ref, cum_ref, cs_t_ref,
    dgate_ref, dy_ref, gloc_ref, gfin_ref, gdown_ref,
    sg_t_scr,
):
    group = pl.program_id(0)
    row_count, _, part = g_ref.shape
    blocks = gloc_ref.shape[0]

    @pl.when(group == 0)
    def _():
        @pl.loop(0, blocks)
        def _(k):
            sg_t_scr[k] = sg_ref[at_block(k), :].astype(F32).T[:RANK].astype(BF16)

    taps = vp_ref[0]
    gdown_ref[...] = jnp.zeros_like(gdown_ref)

    def one_block(i, state):
        k = blocks - 1 - i
        rows = at_block(k)
        dmix = mm_nt(sg_ref[rows, :], down_ref[0])
        for r in range(row_count):
            dmix = dmix + mm_nt(g_ref[r, rows, :], w_ref[0, r, :, :part])
        gate = gate_ref[rows, :].astype(F32)
        output = o_ref[rows, :].astype(F32)
        sig = sigmoid(gate)
        act = gate * sig
        gated = output * act
        rms = aux_ref[rows, 0:1]
        coefficient = aux_ref[rows, 1:2]
        scale = rms * taps[5:6]
        mixed = (gated * scale).astype(BF16)
        gdown_ref[...] += mm(sg_t_scr[k], mixed)
        gated_grad = scale * dmix - gated * coefficient
        dy = gated_grad * act
        dgate = gated_grad * output * (sig + act * (1.0 - sig))
        dgate_ref[rows, :] = dgate.astype(BF16)
        dy_ref[rows, :] = dy.astype(BF16)
        cum = to_front(cum_ref[rows, :], group)
        factor = widen(jnp.exp2(cum))
        gloc_ref[k] = state
        return factor[BLOCK - 1 : BLOCK] * state + mm(cs_t_ref[k], (factor * dy).astype(BF16))

    state = lax.fori_loop(0, blocks, one_block, jnp.zeros((STATES, WIDTH), F32))
    gfin_ref[...] = state.astype(BF16)


def back_kernel(
    x_ref, gain_ref, normed_ref, wst_ref, w_ref, up_ref, adv_ref, vp_ref, sp_ref, hp_ref,
    u_ref, o_ref, dy_ref, dgate_ref, ent_ref, gloc_ref, gin_ref,
    step_ref, cum_ref, cum_t_ref, raw_ref, scpre_ref, bs_ref, cs_ref,
    corr_ref, gup_ref, gdown_ref,
    score_scr, dscore_scr, db_scr, dc_scr, dcum_scr, dstep_scr, dlast_scr, du_scr, ig_scr, ng_scr, adg_scr, adv_t_scr,
):
    group = pl.program_id(0)
    row_count, _, part = x_ref.shape
    blocks = gloc_ref.shape[0]
    total_rows = normed_ref.shape[0]

    @pl.when(group == 0)
    def _():
        for ref in (dscore_scr, db_scr, dc_scr, dcum_scr, dstep_scr, dlast_scr, ng_scr, adg_scr):
            ref[...] = jnp.zeros_like(ref)
        du_scr[0:HALO, :] = jnp.zeros((HALO, WIDTH), F32)
        du_scr[total_rows : total_rows + HALO, :] = jnp.zeros((HALO, WIDTH), F32)

        @pl.loop(0, blocks)
        def _(k):
            score_scr[k] = mm_nt(bs_ref[at_block(k), :], cs_ref[at_block(k), :])
            adv_t_scr[k] = adv_ref[at_rows(k), :].astype(F32).T[:RANK].astype(BF16)

    keep = iota((BLOCK, BLOCK), 0) <= iota((BLOCK, BLOCK), 1)
    taps = vp_ref[0]
    pick = (iota((WIDTH, LANES), 1) == QUAD * group + iota((WIDTH, LANES), 0) // P_SIZE).astype(BF16)

    def one_block(i, after):
        k = blocks - 1 - i
        rows = at_block(k)
        pre = u_ref[rows, :].astype(F32)
        sig = sigmoid(pre)
        conv = pre * sig
        xs = conv.astype(BF16).astype(F32)
        cum = to_front(cum_ref[rows, :], group)
        step_w = widen(to_front(step_ref[rows, :], group))
        scaled_low = (xs * step_w).astype(BF16)
        scaled = scaled_low.astype(F32)
        dy_low = dy_ref[rows, :]
        dy = dy_low.astype(F32)
        b_rows = bs_ref[rows, :]
        c_rows = cs_ref[rows, :]
        score = jnp.where(keep, score_scr[k], 0.0)
        dscore = dscore_scr[k]
        ending = gloc_ref[k] + after * gin_ref[...]
        ending_low = ending.astype(BF16)
        last = cum[BLOCK - 1 : BLOCK]
        to_end = widen(jnp.exp2(last - cum))
        dscaled_state = to_end * mm(b_rows, ending_low)
        dscaled = dscaled_state
        for h in range(QUAD):
            spread = cum_t_ref[0, h : h + 1, rows] - cum[:, h : h + 1]
            damp = jnp.exp2(jnp.minimum(spread, 0.0))
            weights = (score * damp).astype(BF16)
            dy_head = head_only(dy_low, h)
            dscaled = dscaled + mm(weights, dy_head)
            dscore = dscore + mm_nt(scaled_low, dy_head) * damp
        dscore_scr[k] = dscore
        from_start = widen(jnp.exp2(cum))
        fall = from_start[BLOCK - 1 : BLOCK]
        entering_low = ent_ref[k]
        entering = entering_low.astype(F32)
        dc_scr[rows, :] += mm_nt((from_start * dy).astype(BF16), entering_low)
        db_scr[rows, :] += mm_nt((to_end * scaled).astype(BF16), ending_low)
        scan_out = o_ref[rows, :].astype(F32) - taps[6:7] * conv
        dcum_scr[rows, :] += split_right(dy * scan_out - scaled * dscaled, pick)
        dstep_scr[rows, :] += split_right(xs * dscaled, pick)
        ends = jnp.sum(scaled * dscaled_state, axis=0, keepdims=True)
        ends = ends + fall * jnp.sum(entering * ending, axis=0, keepdims=True)
        dlast_scr[k] += split_right(jnp.broadcast_to(ends, (8, WIDTH)), pick)
        dconv = taps[6:7] * dy + step_w * dscaled
        du_scr[at_rows(k), :] = dconv * (sig + conv * (1.0 - sig))
        return after * fall

    lax.fori_loop(0, blocks, one_block, jnp.ones((1, WIDTH), F32))

    def spread_back(rows, window, count):
        dval = advances(window, taps[0:4], count)
        ig_scr[rows, WIDTH:] = dval.astype(BF16)
        grad = ig_scr[rows, :]
        adg_scr[rows, :] += mm_nt(grad, up_ref[0])
        for r in range(row_count):
            ng_scr[rows, r * part : (r + 1) * part] += mm_nt(grad, w_ref[0, r, :part, :])
        return grad

    ig_scr[0:HALO, :WIDTH] = jnp.zeros((HALO, WIDTH), BF16)
    first = spread_back(pl.ds(0, HALO), du_scr[0 : HALO + 8, :], HALO)
    gup_ref[0] = mm_tn(adv_ref[0:HALO, :], first)[:RANK]

    @pl.loop(0, blocks)
    def _(k):
        ig_scr[at_rows(k), :WIDTH] = dgate_ref[at_block(k), :]
        window = du_scr[pl.ds(pl.multiple_of(HALO + k * BLOCK, 8), BLOCK + 8), :]
        grad = spread_back(at_rows(k), window, BLOCK)
        gup_ref[0] += mm(adv_t_scr[k], grad)

    @pl.when(group == pl.num_programs(0) - 1)
    def _():
        upper = (iota((BLOCK, BLOCK), 0) <= iota((BLOCK, BLOCK), 1)).astype(BF16)
        rate = -jnp.exp(hp_ref[1:2])

        @pl.loop(0, blocks)
        def _(k):
            rows = at_block(k)
            dscore = jnp.where(keep, dscore_scr[k], 0.0).astype(BF16)
            db = db_scr[rows, :] + mm(dscore, cs_ref[rows, :])
            dc = dc_scr[rows, :] + mm_tn(dscore, bs_ref[rows, :])
            pre = scpre_ref[rows, :]
            sig = sigmoid(pre)
            slope = sig + pre * sig * (1.0 - sig)
            du_scr[at_rows(k), :] = jnp.concatenate([db, dc], axis=1) * slope
            is_last = iota((BLOCK, LANES), 0) == BLOCK - 1
            dcum = dcum_scr[rows, :] + jnp.where(is_last, dlast_scr[k, 0:1, :], 0.0)
            dstep = dstep_scr[rows, :] + split_left(upper, dcum) * rate
            dstep_scr[rows, :] = dstep * sigmoid(raw_ref[rows, :])

        def finish(rows, window, count, draw):
            dstate = advances(window, sp_ref[0:4], count).astype(BF16)
            adapt = adg_scr[rows, :].astype(BF16)
            total = jnp.zeros((count, 1), F32)
            square = jnp.zeros((count, 1), F32)
            grads = []
            for r in range(row_count):
                cols = slice(r * part, (r + 1) * part)
                grad = ng_scr[rows, cols] + mm_nt(dstate, wst_ref[r, :, 0:256])
                grad = grad + mm_nt(adapt, wst_ref[r, :, 384:512])
                if draw is not None:
                    grad = grad + mm_nt(draw, wst_ref[r, :, 256:384])
                grad = grad * gain_ref[r]
                piece = x_ref[r, rows, :].astype(F32)
                total = total + jnp.sum(piece * grad, axis=1, keepdims=True)
                square = square + jnp.sum(piece * piece, axis=1, keepdims=True)
                grads.append(grad)
                gdown_ref[:, cols] += mm_tn(adapt, normed_ref[rows, cols])[:RANK]
            inv = lax.rsqrt(square / D + EPS)
            factor = inv * inv * inv * total / D
            for r in range(row_count):
                piece = x_ref[r, rows, :].astype(F32)
                corr_ref[r, rows, :] = (inv * grads[r] - factor * piece).astype(BF16)

        gdown_ref[...] = jnp.zeros_like(gdown_ref)
        finish(pl.ds(0, HALO), du_scr[0 : HALO + 8, :], HALO, None)

        @pl.loop(0, blocks)
        def _(k):
            window = du_scr[pl.ds(pl.multiple_of(HALO + k * BLOCK, 8), BLOCK + 8), :]
            finish(at_rows(k), window, BLOCK, dstep_scr[at_block(k), :].astype(BF16))


def whole_spec(shape):
    return pl.BlockSpec(shape, lambda c: (0,) * len(shape))


def lead_spec(shape):
    return pl.BlockSpec((1,) + tuple(shape[1:]), lambda c: (c,) + (0,) * (len(shape) - 1))


def lane_spec(shape):
    block = tuple(shape[:-1]) + (WIDTH,)
    return pl.BlockSpec(block, lambda c: (0,) * (len(shape) - 1) + (c,))


KINDS = {"a": whole_spec, "c": lead_spec, "l": lane_spec}


def grouped_call(kernel, inputs, kinds, outputs, out_kinds, scratch):
    return pl.pallas_call(
        kernel,
        grid=(GROUPS,),
        in_specs=[KINDS[kind](value.shape) for kind, value in zip(kinds, inputs)],
        out_specs=[KINDS[kind](shape) for kind, (shape, _) in zip(out_kinds, outputs)],
        out_shape=[jax.ShapeDtypeStruct(shape, dtype) for shape, dtype in outputs],
        scratch_shapes=[pltpu.VMEM(shape, dtype) for shape, dtype in scratch],
        compiler_params=pltpu.CompilerParams(vmem_limit_bytes=VMEM_BYTES),
    )(*inputs)


def to_groups(value, heads_here):
    cols = value.shape[0]
    middle = value.shape[1:-1]
    if heads_here == QUAD:
        return value
    if heads_here > QUAD:
        parts = heads_here // QUAD
        value = value.reshape((cols,) + middle + (parts, WIDTH))
        value = jnp.moveaxis(value, -2, 1)
        return value.reshape((GROUPS,) + middle + (WIDTH,))
    parts = QUAD // heads_here
    value = value.reshape((GROUPS, parts) + middle + (heads_here * P_SIZE,))
    value = jnp.moveaxis(value, 1, -2)
    return value.reshape((GROUPS,) + middle + (WIDTH,))


def to_cols(value, heads_here, col_count):
    middle = value.shape[1:-1]
    if heads_here == QUAD:
        return value
    if heads_here > QUAD:
        parts = heads_here // QUAD
        value = value.reshape((col_count, parts) + middle + (WIDTH,))
        value = jnp.moveaxis(value, 1, -2)
        return value.reshape((col_count,) + middle + (heads_here * P_SIZE,))
    parts = QUAD // heads_here
    value = value.reshape((GROUPS,) + middle + (parts, heads_here * P_SIZE))
    value = jnp.moveaxis(value, -2, 1)
    return value.reshape((col_count,) + middle + (heads_here * P_SIZE,))


def pad_lanes(value, width):
    return jnp.pad(value, [(0, 0)] * (value.ndim - 1) + [(0, width - value.shape[-1])])


def carry_in(state, decay, row_count, col_count, seq_cols, forward):
    row = lax.axis_index("row")
    col = lax.axis_index("col")
    total = state
    factor = decay
    before = jnp.zeros(state.shape, F32)
    reach = jnp.ones_like(decay)
    span = 1
    while span < row_count:
        pairs = [(i, i ^ span) for i in range(row_count)]
        other = lax.ppermute(total, "row", pairs).astype(F32)
        other_factor = lax.ppermute(factor, "row", pairs)
        behind = ((row & span) != 0) == forward
        mine = total.astype(F32)
        before = jnp.where(behind, before + reach * other, before)
        reach = jnp.where(behind, reach * other_factor, reach)
        joined = jnp.where(behind, other * factor + mine, mine * other_factor + other)
        total = joined.astype(BF16)
        factor = factor * other_factor
        span *= 2
    place = lax.rem(col, seq_cols)
    for hop in range(1, seq_cols):
        shift = hop if forward else -hop
        pairs = [(i, (i + shift) % col_count) for i in range(col_count)]
        other = lax.ppermute(total, "col", pairs).astype(F32)
        other_factor = lax.ppermute(factor, "col", pairs)
        inside = place >= hop if forward else place < seq_cols - hop
        before = jnp.where(inside, before + reach * other, before)
        reach = jnp.where(inside, reach * other_factor, reach)
    return before


def per_device(
    block_in, norm_gain, proj_inner, proj_state, conv_inner, conv_inner_bias, conv_state, conv_state_bias,
    step_bias, decay_log, skip_gain, gate_gain, proj_out, adapt_in_down, adapt_in_up, adapt_out_down,
    adapt_out_up, adapter_id, cotangent,
):
    row_count = lax.axis_size("row")
    col_count = lax.axis_size("col")
    row = lax.axis_index("row")
    col = lax.axis_index("col")
    col_tokens, part = block_in.shape
    chunk = col_tokens // row_count
    total_rows = chunk + HALO
    blocks = chunk // BLOCK
    seq_cols = SEQ // col_tokens
    heads_here = proj_inner.shape[1]
    local = heads_here * P_SIZE
    rank_total = adapt_in_down.shape[1]
    rank_part = rank_total // row_count
    rank_share = rank_total // col_count
    adapter = lax.dynamic_index_in_dim(adapter_id, col // seq_cols, keepdims=False)

    head = jnp.zeros((HALO, part), BF16)
    if seq_cols > 1:
        pairs = [(i, (i + 1) % col_count) for i in range(col_count)]
        head = lax.ppermute(block_in[-HALO:], "col", pairs)
        head = jnp.where(lax.rem(col, seq_cols) > 0, head, jnp.zeros_like(head))
    padded = jnp.concatenate([head, block_in], axis=0)
    windows = jnp.stack([padded[r * chunk : r * chunk + total_rows] for r in range(row_count)])
    x_rows = lax.all_to_all(windows, "row", 0, 0, tiled=True)
    g_rows = lax.all_to_all(cotangent.reshape(row_count, chunk, part), "row", 0, 0, tiled=True)

    def split_pairs(value):
        value = value.reshape(value.shape[0], heads_here, 2, P_SIZE)
        return jnp.swapaxes(value, 1, 2).reshape(value.shape[0], 2, local)

    up_part = lax.dynamic_slice_in_dim(adapt_in_up, row * rank_part, rank_part, 0)
    w_block = jnp.concatenate([split_pairs(proj_inner), split_pairs(up_part)], axis=0)
    w_all = lax.all_gather(w_block.reshape(part + rank_part, 2 * local), ("col", "row"))
    w_all = w_all.reshape(col_count, row_count, part + rank_part, 2, local)
    w_all = to_groups(w_all, heads_here).reshape(GROUPS, row_count, part + rank_part, 2 * WIDTH)
    up_all = w_all[:, :, part:, :].reshape(GROUPS, rank_total, 2 * WIDTH)
    up_all = lax.dynamic_slice_in_dim(up_all, adapter * RANK, RANK, 1)
    up_all = jnp.pad(up_all, ((0, 0), (0, LANES - RANK), (0, 0)))

    down_part = lax.dynamic_slice_in_dim(adapt_out_down, row * rank_part, rank_part, 0)
    p_block = jnp.concatenate([proj_out, down_part.T], axis=1)
    p_all = lax.all_gather(p_block, ("col", "row")).reshape(col_count, row_count, local, part + rank_part)
    if heads_here != QUAD:
        p_all = jnp.moveaxis(p_all, 1, 0).reshape(row_count, GROUPS, WIDTH, part + rank_part)
        p_all = jnp.moveaxis(p_all, 0, 1)
    down_all = jnp.swapaxes(p_all[..., part:], 1, 2).reshape(GROUPS, WIDTH, rank_total)
    down_all = pad_lanes(lax.dynamic_slice_in_dim(down_all, adapter * RANK, RANK, 2), LANES)

    in_down = lax.dynamic_slice_in_dim(adapt_in_down, adapter * RANK, RANK, 1)
    out_up = lax.dynamic_slice_in_dim(adapt_out_up, adapter * RANK, RANK, 1)
    state_width = proj_state.shape[1]
    shared = lax.all_gather(jnp.concatenate([proj_state, in_down, out_up], axis=1), "row")
    w_state = jnp.concatenate(
        [
            pad_lanes(shared[..., :state_width], 384),
            pad_lanes(shared[..., state_width : state_width + RANK], LANES),
        ],
        axis=2,
    )
    out_up_all = pad_lanes(shared[..., state_width + RANK :], LANES)
    gain_all = lax.all_gather(norm_gain, "row").reshape(row_count, 1, part)

    scalars = jnp.concatenate([step_bias, decay_log, skip_gain])
    vectors = jnp.concatenate(
        [conv_inner, conv_inner_bias[None], gate_gain[None], pad_lanes(scalars, local)[None]], axis=0
    )
    vectors = lax.all_gather(vectors, "col")
    scalars = vectors[:, 6, : 3 * heads_here].reshape(col_count, 3, heads_here)
    scalars = jnp.swapaxes(scalars, 0, 1).reshape(3, HEADS)
    head_rows = jnp.pad(scalars[:2], ((0, 6), (0, LANES - HEADS)))
    skip_wide = jnp.repeat(scalars[2], P_SIZE).reshape(GROUPS, 1, WIDTH)
    vectors = jnp.concatenate(
        [to_groups(vectors[:, :6], heads_here), skip_wide, jnp.zeros_like(skip_wide)], axis=1
    )
    state_taps = jnp.concatenate([conv_state, conv_state_bias[None], jnp.zeros((3, 256), F32)], axis=0)

    token_f32 = ((chunk, LANES), F32)
    token_low = ((chunk, LANES), BF16)
    inner_low = ((chunk, DI), BF16)
    states = ((blocks, STATES, DI), F32)
    score_box = ((blocks, BLOCK, BLOCK), F32)
    turned = ((blocks, STATES, BLOCK), BF16)
    (
        normed, scpre, raw, step, cum, cum_t, bs, cs, cs_t, adv, gate, u, eloc, fin, dec,
    ) = grouped_call(
        front_kernel,
        (x_rows, gain_all, w_state, state_taps, head_rows, w_all, up_all, vectors),
        "aaaaaccc",
        [
            ((total_rows, D), BF16), ((chunk, 256), F32), token_f32, token_f32, token_f32,
            ((GROUPS, QUAD, chunk), F32), token_low, token_low, turned, ((total_rows, LANES), BF16),
            inner_low, inner_low, states, ((STATES, DI), BF16), ((8, DI), F32),
        ],
        "aaaaaaaaaalllll",
        [((total_rows, 512), F32), turned, ((total_rows, WIDTH), F32)],
    )
    decay = dec[0:1]
    entry = carry_in(fin, decay, row_count, col_count, seq_cols, True)
    out_rows, o, ent, aux, side_grad, out_up_grad = grouped_call(
        scan_kernel,
        (x_rows, g_rows, out_up_all, p_all, down_all, vectors, gate, u, eloc, entry, step, cum, cum_t, bs, cs),
        "aaacccllllaacaa",
        [
            ((row_count, chunk, part), BF16), inner_low, ((blocks, STATES, DI), BF16), token_f32, token_low,
            ((RANK, D), F32),
        ],
        "allaaa",
        [score_box, ((chunk, D), F32), token_f32, token_f32],
    )
    dgate, dy, gloc, gfin, out_down_grad = grouped_call(
        gate_kernel,
        (g_rows, p_all, side_grad, down_all, vectors, gate, o, aux, cum, cs_t),
        "acaccllaaa",
        [inner_low, inner_low, states, ((STATES, DI), BF16), ((RANK, DI), F32)],
        "lllll",
        [((blocks, RANK, BLOCK), BF16)],
    )
    exit_grad = carry_in(gfin, decay, row_count, col_count, seq_cols, False)
    corr, in_up_grad, in_down_grad = grouped_call(
        back_kernel,
        (
            x_rows, gain_all, normed, w_state, w_all, up_all, adv, vectors, state_taps, head_rows,
            u, o, dy, dgate, ent, gloc, exit_grad, step, cum, cum_t, raw, scpre, bs, cs,
        ),
        "aaaaccacaalllllllaacaaaa",
        [((row_count, total_rows, part), BF16), ((GROUPS, RANK, 2 * WIDTH), F32), ((RANK, D), F32)],
        "aca",
        [
            score_box, score_box, token_f32, token_f32, token_f32, token_f32, ((blocks, 8, LANES), F32),
            ((total_rows + HALO, WIDTH), F32), ((total_rows, 2 * WIDTH), BF16), ((total_rows, D), F32),
            ((total_rows, LANES), F32), ((blocks, RANK, BLOCK), BF16),
        ],
    )

    block_out = lax.all_to_all(out_rows, "row", 0, 0, tiled=True).reshape(col_tokens, part)
    corr = lax.all_to_all(corr, "row", 0, 0, tiled=True).astype(F32)
    early = corr[:, :HALO]
    input_grad = cotangent.astype(F32) + corr[:, HALO:].reshape(col_tokens, part)
    for r in range(1, row_count):
        input_grad = input_grad.at[r * chunk - HALO : r * chunk].add(early[r])
    if seq_cols > 1:
        pairs = [(i, (i - 1) % col_count) for i in range(col_count)]
        late = lax.ppermute(early[0].astype(BF16), "col", pairs).astype(F32)
        late = jnp.where(lax.rem(col, seq_cols) < seq_cols - 1, late, jnp.zeros_like(late))
        input_grad = input_grad.at[-HALO:].add(late)

    thin = jnp.concatenate([in_down_grad, out_up_grad], axis=0).astype(BF16)
    thin = lax.psum_scatter(thin, "row", scatter_dimension=1, tiled=True)
    thin = lax.all_gather(thin, "col").astype(F32)
    wide = in_up_grad.reshape(GROUPS, RANK, 2, WIDTH)
    wide = to_cols(wide, heads_here, col_count)
    tall = jnp.swapaxes(out_down_grad.reshape(RANK, GROUPS, WIDTH), 0, 1)
    tall = to_cols(tall, heads_here, col_count)
    wide = jnp.concatenate([wide.reshape(col_count, RANK, 2 * local), tall], axis=2).astype(BF16)
    wide = lax.all_to_all(wide, "col", 0, 0, tiled=True)
    wide = lax.psum(wide, "row").astype(F32)
    owner = jnp.repeat(adapter_id, seq_cols)
    adapters = rank_total // RANK
    chosen = owner[:, None] == jnp.arange(adapters, dtype=jnp.int32)[None, :]
    wide = jnp.sum(jnp.where(chosen[:, :, None, None], wide[:, None], 0.0), axis=0)
    wide = wide.reshape(rank_total, 3 * local)
    in_up = wide[:, : 2 * local].reshape(rank_total, 2, heads_here, P_SIZE)
    in_up = jnp.swapaxes(in_up, 1, 2).reshape(rank_total, heads_here, 2 * P_SIZE)
    out_down = wide[:, 2 * local :]
    thin = jnp.sum(jnp.where(chosen[:, :, None, None], thin[:, None], 0.0), axis=0)
    thin = thin.reshape(adapters, 2, RANK, part)
    thin = jnp.transpose(thin, (1, 3, 0, 2)).reshape(2, part, rank_total)
    thin = lax.dynamic_slice_in_dim(thin, col * rank_share, rank_share, 2)
    return block_out, input_grad, thin[0], in_up, out_down, thin[1]


def solution(mesh):
    placed = (
        P("col", "row"), P("row"), P("row", "col", None), P("row", None), P(None, "col"), P("col"), P(), P(),
        P("col"), P("col"), P("col"), P("col"), P("col", "row"), P("row", None), P(None, "col", None),
        P(None, "col"), P("row", None), P(), P("col", "row"),
    )
    return jax.shard_map(
        per_device,
        mesh=mesh,
        in_specs=placed,
        out_specs=(
            P("col", "row"), P("col", "row"), P("row", "col"), P(None, "col", None), P(None, "col"),
            P("row", "col"),
        ),
        check_vma=False,
    )
```

```python
import functools

import jax
import jax.numpy as jnp
from jax import lax
from jax.experimental import pallas as pl
from jax.experimental.pallas import tpu as pltpu
from jax.sharding import PartitionSpec as P

D = 1024
HEADS = 32
P_SIZE = 64
STATES = 128
BLOCK = 256
RANK = 16
SEQ = 4096
DI = 2048
EPS = 1e-05
LOG2E = 1.4426950408889634

HALO = 16
QUAD = 4
WIDTH = QUAD * P_SIZE
GROUPS = HEADS // QUAD
LANES = 128
VMEM_BYTES = 60 * 1024 * 1024
F32 = jnp.float32
BF16 = jnp.bfloat16
MESH = pl.DeviceIdType.MESH


def mm(left, right):
    return jnp.dot(left, right, preferred_element_type=F32)


def mm_nt(left, right):
    return lax.dot_general(left, right, (((1,), (1,)), ((), ())), preferred_element_type=F32)


def mm_tn(left, right):
    return lax.dot_general(left, right, (((0,), (0,)), ((), ())), preferred_element_type=F32)


def split_left(ones, value):
    high = value.astype(BF16)
    rest = value - high.astype(F32)
    middle = rest.astype(BF16)
    low = (rest - middle.astype(F32)).astype(BF16)
    return mm(ones, high) + mm(ones, middle) + mm(ones, low)


def split_right(value, ones):
    high = value.astype(BF16)
    low = (value - high.astype(F32)).astype(BF16)
    return mm(high, ones) + mm(low, ones)


def sigmoid(value):
    return 0.5 * jnp.tanh(0.5 * value) + 0.5


def iota(shape, axis):
    return lax.broadcasted_iota(jnp.int32, shape, axis)


def widen(cols):
    lane = iota((cols.shape[0], LANES), 1) < P_SIZE
    left = jnp.where(lane, cols[:, 0:1], cols[:, 1:2])
    right = jnp.where(lane, cols[:, 2:3], cols[:, 3:4])
    return jnp.concatenate([left, right], axis=1)


def to_front(cols, group):
    return pltpu.roll(cols, lax.rem(LANES - QUAD * group, LANES), 1)


def head_only(values, head):
    lane = iota(values.shape, 1) // P_SIZE
    return jnp.where(lane == head, values, jnp.zeros_like(values))


def delays(window, taps, bias):
    total = window[8:] * taps[0:1] + bias
    for k in range(1, 4):
        total = total + pltpu.roll(window, k, 0)[8:] * taps[k : k + 1]
    return total


def advances(window, taps, count):
    length = window.shape[0]
    total = window[:count] * taps[0:1]
    for k in range(1, 4):
        total = total + pltpu.roll(window, length - k, 0)[:count] * taps[k : k + 1]
    return total


def at_block(k):
    return pl.ds(pl.multiple_of(k * BLOCK, BLOCK), BLOCK)


def at_rows(k):
    return pl.ds(pl.multiple_of(HALO + k * BLOCK, HALO), BLOCK)


def front_kernel(
    x_ref, gain_ref, wst_ref, sp_ref, hp_ref, w_ref, up_ref, vp_ref,
    normed_ref, scpre_ref, raw_ref, step_ref, cum_ref, cum_t_ref, bs_ref, cs_ref, cs_t_ref, adv_ref,
    gate_ref, u_ref, eloc_ref, fin_ref, dec_ref,
    st_scr, bs_t_scr, val_scr,
):
    group = pl.program_id(0)
    row_count, _, part = x_ref.shape
    blocks = eloc_ref.shape[0]

    @pl.when(group == 0)
    def _():
        def project(rows):
            pieces = [x_ref[r, rows, :].astype(F32) for r in range(row_count)]
            square = sum(jnp.sum(piece * piece, axis=1, keepdims=True) for piece in pieces)
            inv = lax.rsqrt(square / D + EPS)
            total = None
            for r in range(row_count):
                normed = (pieces[r] * inv * gain_ref[r]).astype(BF16)
                normed_ref[rows, r * part : (r + 1) * part] = normed
                term = mm(normed, wst_ref[r])
                total = term if total is None else total + term
            st_scr[rows, :] = total
            adv_ref[rows, :] = total[:, 384:512].astype(BF16)

        project(pl.ds(0, HALO))

        @pl.loop(0, blocks)
        def _(k):
            project(at_rows(k))

        lower = (iota((BLOCK, BLOCK), 0) >= iota((BLOCK, BLOCK), 1)).astype(BF16)
        rate = -jnp.exp(hp_ref[1:2]) * LOG2E

        @pl.loop(0, blocks)
        def _(k):
            window = st_scr[pl.ds(pl.multiple_of(8 + k * BLOCK, 8), BLOCK + 8), :256]
            pre = delays(window, sp_ref[0:4], sp_ref[4:5])
            conv = pre * sigmoid(pre)
            b_rows = conv[:, :STATES].astype(BF16)
            c_rows = conv[:, STATES:].astype(BF16)
            scpre_ref[at_block(k), :] = pre
            bs_ref[at_block(k), :] = b_rows
            cs_ref[at_block(k), :] = c_rows
            bs_t_scr[k] = conv[:, :STATES].T.astype(BF16)
            cs_t_ref[k] = conv[:, STATES:].T.astype(BF16)
            raw = st_scr[at_rows(k), 256:384] + hp_ref[0:1]
            small = jnp.exp(-jnp.abs(raw))
            tail = jnp.where(
                small < 0.01, small * (1.0 - small * (0.5 - small * (1.0 / 3.0))), jnp.log(1.0 + small)
            )
            step = jnp.maximum(raw, 0.0) + tail
            cum = split_left(lower, step * rate)
            raw_ref[at_block(k), :] = raw
            step_ref[at_block(k), :] = step
            cum_ref[at_block(k), :] = cum
            flipped = cum.T
            for g in range(GROUPS):
                cum_t_ref[g, :, at_block(k)] = flipped[g * QUAD : (g + 1) * QUAD]

    def inner(rows):
        total = mm(adv_ref[rows, :], up_ref[0])
        for r in range(row_count):
            total = total + mm(normed_ref[rows, r * part : (r + 1) * part], w_ref[0, r, :part, :])
        return total

    val_scr[0:HALO, :] = inner(pl.ds(0, HALO))[:, WIDTH:]
    taps = vp_ref[0]

    def one_block(k, carry):
        state, decay = carry
        product = inner(at_rows(k))
        gate_ref[at_block(k), :] = product[:, :WIDTH].astype(BF16)
        val_scr[at_rows(k), :] = product[:, WIDTH:]
        window = val_scr[pl.ds(pl.multiple_of(8 + k * BLOCK, 8), BLOCK + 8), :]
        pre = delays(window, taps[0:4], taps[4:5])
        u_ref[at_block(k), :] = pre.astype(BF16)
        xs = (pre * sigmoid(pre)).astype(BF16).astype(F32)
        cum = cum_ref[at_block(k), :]
        last = cum[BLOCK - 1 : BLOCK]
        weight = to_front(step_ref[at_block(k), :] * jnp.exp2(last - cum), group)
        weighted = (xs * widen(weight)).astype(BF16)
        eloc_ref[k] = state
        last8 = to_front(jnp.broadcast_to(last, (8, LANES)), group)
        fall = widen(jnp.exp2(last8))[0:1]
        return fall * state + mm(bs_t_scr[k], weighted), decay * fall

    start = (jnp.zeros((STATES, WIDTH), F32), jnp.ones((1, WIDTH), F32))
    state, decay = lax.fori_loop(0, blocks, one_block, start)
    fin_ref[...] = state.astype(BF16)
    dec_ref[...] = jnp.broadcast_to(decay, (8, WIDTH))


def scan_kernel(
    x_ref, g_ref, oup_ref, w_ref, down_ref, vp_ref, gate_ref, u_ref, eloc_ref, ein_ref,
    step_ref, cum_ref, cum_t_ref, bs_ref, cs_ref,
    out_ref, o_ref, ent_ref, aux_ref, sg_ref, gup_ref,
    score_scr, acc_scr, side_scr, square_scr,
):
    group = pl.program_id(0)
    row_count, _, part = x_ref.shape
    blocks = eloc_ref.shape[0]

    @pl.when(group == 0)
    def _():
        acc_scr[...] = jnp.zeros_like(acc_scr)
        side_scr[...] = jnp.zeros_like(side_scr)
        square_scr[...] = jnp.zeros_like(square_scr)
        keep = iota((BLOCK, BLOCK), 0) >= iota((BLOCK, BLOCK), 1)

        @pl.loop(0, blocks)
        def _(k):
            score = mm_nt(cs_ref[at_block(k), :], bs_ref[at_block(k), :])
            score_scr[k] = jnp.where(keep, score, 0.0)

    taps = vp_ref[0]

    def one_block(k, before):
        rows = at_block(k)
        pre = u_ref[rows, :].astype(F32)
        conv = pre * sigmoid(pre)
        cum = to_front(cum_ref[rows, :], group)
        step = to_front(step_ref[rows, :], group)
        scaled = (conv.astype(BF16).astype(F32) * widen(step)).astype(BF16)
        score = score_scr[k]
        entering = (eloc_ref[k] + before * ein_ref[...]).astype(BF16)
        ent_ref[k] = entering
        total = widen(jnp.exp2(cum)) * mm(cs_ref[rows, :], entering)
        for h in range(QUAD):
            spread = cum[:, h : h + 1] - cum_t_ref[0, h : h + 1, rows]
            weights = (score * jnp.exp2(jnp.minimum(spread, 0.0))).astype(BF16)
            total = total + mm(weights, head_only(scaled, h))
        output = total + taps[6:7] * conv
        o_ref[rows, :] = output.astype(BF16)
        gate = gate_ref[rows, :].astype(F32)
        gated = output * gate * sigmoid(gate)
        square = gated * gated
        square_scr[rows, :] += square[:, :LANES] + square[:, LANES:]
        gained = (gated * taps[5:6]).astype(BF16)
        for r in range(row_count):
            cols = slice(r * part, (r + 1) * part)
            acc_scr[rows, cols] += mm(gained, w_ref[0, r, :, :part])
        side_scr[rows, :] += mm(gained, down_ref[0])
        return before * widen(jnp.exp2(cum[BLOCK - 8 :]))[7:8]

    lax.fori_loop(0, blocks, one_block, jnp.ones((1, WIDTH), F32))

    @pl.when(group == pl.num_programs(0) - 1)
    def _():
        gup_ref[...] = jnp.zeros_like(gup_ref)

        @pl.loop(0, blocks)
        def _(k):
            rows = at_block(k)
            mean = jnp.sum(square_scr[rows, :], axis=1, keepdims=True) / DI
            rms = lax.rsqrt(mean + EPS)
            side_raw = side_scr[rows, :]
            side = (side_raw * rms).astype(BF16)
            side_grad = None
            for r in range(row_count):
                term = mm(g_ref[r, rows, :], oup_ref[r])
                side_grad = term if side_grad is None else side_grad + term
            side_grad = side_grad.astype(BF16)
            product = jnp.sum(side_grad.astype(F32) * side_raw, axis=1, keepdims=True)
            for r in range(row_count):
                cols = slice(r * part, (r + 1) * part)
                raw = acc_scr[rows, cols]
                cot = g_ref[r, rows, :]
                product = product + jnp.sum(raw * cot.astype(F32), axis=1, keepdims=True)
                total = x_ref[r, at_rows(k), :].astype(F32) + raw * rms + mm_nt(side, oup_ref[r])
                out_ref[r, rows, :] = total.astype(BF16)
                gup_ref[:, cols] += mm_tn(side, cot)[:RANK]
            coefficient = rms * rms * rms * product / DI
            lane = iota((BLOCK, LANES), 1)
            aux_ref[rows, :] = jnp.where(lane == 0, rms, coefficient)
            sg_ref[rows, :] = side_grad


def gate_kernel(
    g_ref, w_ref, sg_ref, down_ref, vp_ref, gate_ref, o_ref, aux_ref, cum_ref, cs_t_ref,
    dgate_ref, dy_ref, gloc_ref, gfin_ref, gdown_ref,
    sg_t_scr,
):
    group = pl.program_id(0)
    row_count, _, part = g_ref.shape
    blocks = gloc_ref.shape[0]

    @pl.when(group == 0)
    def _():
        @pl.loop(0, blocks)
        def _(k):
            sg_t_scr[k] = sg_ref[at_block(k), :].astype(F32).T[:RANK].astype(BF16)

    taps = vp_ref[0]
    gdown_ref[0] = jnp.zeros((RANK, WIDTH), F32)

    def one_block(i, state):
        k = blocks - 1 - i
        rows = at_block(k)
        dmix = mm_nt(sg_ref[rows, :], down_ref[0])
        for r in range(row_count):
            dmix = dmix + mm_nt(g_ref[r, rows, :], w_ref[0, r, :, :part])
        gate = gate_ref[rows, :].astype(F32)
        output = o_ref[rows, :].astype(F32)
        sig = sigmoid(gate)
        act = gate * sig
        gated = output * act
        rms = aux_ref[rows, 0:1]
        coefficient = aux_ref[rows, 1:2]
        scale = rms * taps[5:6]
        mixed = (gated * scale).astype(BF16)
        gdown_ref[0] += mm(sg_t_scr[k], mixed)
        gated_grad = scale * dmix - gated * coefficient
        dy = gated_grad * act
        dgate = gated_grad * output * (sig + act * (1.0 - sig))
        dgate_ref[rows, :] = dgate.astype(BF16)
        dy_ref[rows, :] = dy.astype(BF16)
        cum = to_front(cum_ref[rows, :], group)
        factor = widen(jnp.exp2(cum))
        gloc_ref[k] = state
        return factor[BLOCK - 1 : BLOCK] * state + mm(cs_t_ref[k], (factor * dy).astype(BF16))

    state = lax.fori_loop(0, blocks, one_block, jnp.zeros((STATES, WIDTH), F32))
    gfin_ref[...] = state.astype(BF16)


def back_kernel(
    x_ref, gain_ref, normed_ref, wst_ref, w_ref, up_ref, adv_ref, vp_ref, sp_ref, hp_ref,
    u_ref, o_ref, dy_ref, dgate_ref, ent_ref, gloc_ref, gin_ref,
    step_ref, cum_ref, cum_t_ref, raw_ref, scpre_ref, bs_ref, cs_ref, out_down_ref, out_up_ref,
    corr_ref, wide_ref, thin_ref,
    score_scr, dscore_scr, db_scr, dc_scr, dcum_scr, dstep_scr, dlast_scr, du_scr, ig_scr, ng_scr, adg_scr, adv_t_scr, up_scr, in_scr,
):
    group = pl.program_id(0)
    row_count, _, part = x_ref.shape
    blocks = gloc_ref.shape[0]
    total_rows = normed_ref.shape[0]

    @pl.when(group == 0)
    def _():
        for ref in (dscore_scr, db_scr, dc_scr, dcum_scr, dstep_scr, dlast_scr, ng_scr, adg_scr):
            ref[...] = jnp.zeros_like(ref)
        du_scr[0:HALO, :] = jnp.zeros((HALO, WIDTH), F32)
        du_scr[total_rows : total_rows + HALO, :] = jnp.zeros((HALO, WIDTH), F32)

        @pl.loop(0, blocks)
        def _(k):
            score_scr[k] = mm_nt(bs_ref[at_block(k), :], cs_ref[at_block(k), :])
            adv_t_scr[k] = adv_ref[at_rows(k), :].astype(F32).T[:RANK].astype(BF16)

    keep = iota((BLOCK, BLOCK), 0) <= iota((BLOCK, BLOCK), 1)
    taps = vp_ref[0]
    pick = (iota((WIDTH, LANES), 1) == QUAD * group + iota((WIDTH, LANES), 0) // P_SIZE).astype(BF16)

    def one_block(i, after):
        k = blocks - 1 - i
        rows = at_block(k)
        pre = u_ref[rows, :].astype(F32)
        sig = sigmoid(pre)
        conv = pre * sig
        xs = conv.astype(BF16).astype(F32)
        cum = to_front(cum_ref[rows, :], group)
        step_w = widen(to_front(step_ref[rows, :], group))
        scaled_low = (xs * step_w).astype(BF16)
        scaled = scaled_low.astype(F32)
        dy_low = dy_ref[rows, :]
        dy = dy_low.astype(F32)
        b_rows = bs_ref[rows, :]
        c_rows = cs_ref[rows, :]
        score = jnp.where(keep, score_scr[k], 0.0)
        dscore = dscore_scr[k]
        ending = gloc_ref[k] + after * gin_ref[...]
        ending_low = ending.astype(BF16)
        last = cum[BLOCK - 1 : BLOCK]
        to_end = widen(jnp.exp2(last - cum))
        dscaled_state = to_end * mm(b_rows, ending_low)
        dscaled = dscaled_state
        for h in range(QUAD):
            spread = cum_t_ref[0, h : h + 1, rows] - cum[:, h : h + 1]
            damp = jnp.exp2(jnp.minimum(spread, 0.0))
            weights = (score * damp).astype(BF16)
            dy_head = head_only(dy_low, h)
            dscaled = dscaled + mm(weights, dy_head)
            dscore = dscore + mm_nt(scaled_low, dy_head) * damp
        dscore_scr[k] = dscore
        from_start = widen(jnp.exp2(cum))
        fall = from_start[BLOCK - 1 : BLOCK]
        entering_low = ent_ref[k]
        entering = entering_low.astype(F32)
        dc_scr[rows, :] += mm_nt((from_start * dy).astype(BF16), entering_low)
        db_scr[rows, :] += mm_nt((to_end * scaled).astype(BF16), ending_low)
        scan_out = o_ref[rows, :].astype(F32) - taps[6:7] * conv
        dcum_scr[rows, :] += split_right(dy * scan_out - scaled * dscaled, pick)
        dstep_scr[rows, :] += split_right(xs * dscaled, pick)
        ends = jnp.sum(scaled * dscaled_state, axis=0, keepdims=True)
        ends = ends + fall * jnp.sum(entering * ending, axis=0, keepdims=True)
        dlast_scr[k] += split_right(jnp.broadcast_to(ends, (8, WIDTH)), pick)
        dconv = taps[6:7] * dy + step_w * dscaled
        du_scr[at_rows(k), :] = dconv * (sig + conv * (1.0 - sig))
        return after * fall

    lax.fori_loop(0, blocks, one_block, jnp.ones((1, WIDTH), F32))

    def spread_back(rows, window, count):
        dval = advances(window, taps[0:4], count)
        ig_scr[rows, WIDTH:] = dval.astype(BF16)
        grad = ig_scr[rows, :]
        adg_scr[rows, :] += mm_nt(grad, up_ref[0])
        for r in range(row_count):
            ng_scr[rows, r * part : (r + 1) * part] += mm_nt(grad, w_ref[0, r, :part, :])
        return grad

    ig_scr[0:HALO, :WIDTH] = jnp.zeros((HALO, WIDTH), BF16)
    first = spread_back(pl.ds(0, HALO), du_scr[0 : HALO + 8, :], HALO)
    up_scr[...] = mm_tn(adv_ref[0:HALO, :], first)[:RANK]

    @pl.loop(0, blocks)
    def _(k):
        ig_scr[at_rows(k), :WIDTH] = dgate_ref[at_block(k), :]
        window = du_scr[pl.ds(pl.multiple_of(HALO + k * BLOCK, 8), BLOCK + 8), :]
        grad = spread_back(at_rows(k), window, BLOCK)
        up_scr[...] += mm(adv_t_scr[k], grad)

    share = RANK // row_count
    for r in range(row_count):
        wide_ref[r, 0, :, : 2 * WIDTH] = up_scr[r * share : (r + 1) * share, :]
        wide_ref[r, 0, :, 2 * WIDTH :] = out_down_ref[0, r * share : (r + 1) * share, :]

    @pl.when(group == pl.num_programs(0) - 1)
    def _():
        upper = (iota((BLOCK, BLOCK), 0) <= iota((BLOCK, BLOCK), 1)).astype(BF16)
        rate = -jnp.exp(hp_ref[1:2])

        @pl.loop(0, blocks)
        def _(k):
            rows = at_block(k)
            dscore = jnp.where(keep, dscore_scr[k], 0.0).astype(BF16)
            db = db_scr[rows, :] + mm(dscore, cs_ref[rows, :])
            dc = dc_scr[rows, :] + mm_tn(dscore, bs_ref[rows, :])
            pre = scpre_ref[rows, :]
            sig = sigmoid(pre)
            slope = sig + pre * sig * (1.0 - sig)
            du_scr[at_rows(k), :] = jnp.concatenate([db, dc], axis=1) * slope
            is_last = iota((BLOCK, LANES), 0) == BLOCK - 1
            dcum = dcum_scr[rows, :] + jnp.where(is_last, dlast_scr[k, 0:1, :], 0.0)
            dstep = dstep_scr[rows, :] + split_left(upper, dcum) * rate
            dstep_scr[rows, :] = dstep * sigmoid(raw_ref[rows, :])

        def finish(rows, window, count, draw):
            dstate = advances(window, sp_ref[0:4], count).astype(BF16)
            adapt = adg_scr[rows, :].astype(BF16)
            total = jnp.zeros((count, 1), F32)
            square = jnp.zeros((count, 1), F32)
            grads = []
            for r in range(row_count):
                cols = slice(r * part, (r + 1) * part)
                grad = ng_scr[rows, cols] + mm_nt(dstate, wst_ref[r, :, 0:256])
                grad = grad + mm_nt(adapt, wst_ref[r, :, 384:512])
                if draw is not None:
                    grad = grad + mm_nt(draw, wst_ref[r, :, 256:384])
                grad = grad * gain_ref[r]
                piece = x_ref[r, rows, :].astype(F32)
                total = total + jnp.sum(piece * grad, axis=1, keepdims=True)
                square = square + jnp.sum(piece * piece, axis=1, keepdims=True)
                grads.append(grad)
                in_scr[:, cols] += mm_tn(adapt, normed_ref[rows, cols])[:RANK]
            inv = lax.rsqrt(square / D + EPS)
            factor = inv * inv * inv * total / D
            for r in range(row_count):
                piece = x_ref[r, rows, :].astype(F32)
                corr_ref[r, rows, :] = (inv * grads[r] - factor * piece).astype(BF16)

        in_scr[...] = jnp.zeros_like(in_scr)
        finish(pl.ds(0, HALO), du_scr[0 : HALO + 8, :], HALO, None)

        @pl.loop(0, blocks)
        def _(k):
            window = du_scr[pl.ds(pl.multiple_of(HALO + k * BLOCK, 8), BLOCK + 8), :]
            finish(at_rows(k), window, BLOCK, dstep_scr[at_block(k), :].astype(BF16))

        for r in range(row_count):
            thin_ref[r, 0:RANK, :] = in_scr[:, r * part : (r + 1) * part]
            thin_ref[r, RANK:, :] = out_up_ref[:, r * part : (r + 1) * part]


def on_row(row):
    return {"row": row}


def on_col(col):
    return {"col": col}


def tail_kernel(
    corr_ref, wide_ref, thin_ref,
    corr_out, wide_out, thin_out,
    wide_scr, thin_scr, wide_sum, thin_sum, wide_col,
    own_sem, corr_send, corr_recv, row_send, row_recv, col_send, col_recv, last_send, last_recv,
):
    row_count = corr_ref.shape[0]
    col_count = thin_out.shape[0]
    row = lax.axis_index("row")
    col = lax.axis_index("col")
    barrier = pltpu.get_barrier_semaphore()
    for d in range(1, row_count):
        pl.semaphore_signal(barrier, inc=1, device_id=on_row(lax.rem(row + d, row_count)), device_id_type=MESH)
    for d in range(1, col_count):
        pl.semaphore_signal(barrier, inc=1, device_id=on_col(lax.rem(col + d, col_count)), device_id_type=MESH)
    pl.semaphore_wait(barrier, row_count + col_count - 2)

    def send(source, target, sends, recvs, index, device):
        copy = pltpu.make_async_remote_copy(
            src_ref=source, dst_ref=target, send_sem=sends.at[index], recv_sem=recvs.at[index],
            device_id=device, device_id_type=MESH,
        )
        copy.start()
        return copy

    first = []
    for d in range(1, row_count):
        peer = lax.rem(row + d, row_count)
        first.append(send(wide_ref.at[peer], wide_scr.at[row], row_send, row_recv, d, on_row(peer)))
        first.append(send(thin_ref.at[peer], thin_scr.at[row], row_send, row_recv, row_count + d, on_row(peer)))
    moved = []
    for d in range(1, row_count):
        peer = lax.rem(row + d, row_count)
        moved.append(send(corr_ref.at[peer], corr_out.at[row], corr_send, corr_recv, d, on_row(peer)))
    own = pltpu.make_async_copy(corr_ref.at[row], corr_out.at[row], own_sem.at[0])
    own.start()
    for copy in first:
        copy.wait()
    wide = wide_ref[row]
    thin = thin_ref[row]
    for d in range(1, row_count):
        peer = lax.rem(row + d, row_count)
        wide = wide + wide_scr[peer]
        thin = thin + thin_scr[peer]
    wide_sum[...] = wide
    thin_sum[...] = thin
    second = []
    for d in range(1, col_count):
        peer = lax.rem(col + d, col_count)
        second.append(send(wide_sum.at[peer], wide_col.at[col], col_send, col_recv, d, on_col(peer)))
        second.append(send(thin_sum, thin_out.at[col], col_send, col_recv, col_count + d, on_col(peer)))
    wide_col[col] = wide_sum[col]
    thin_out[col] = thin
    for copy in second:
        copy.wait()
    third = []
    for d in range(1, row_count):
        peer = lax.rem(row + d, row_count)
        third.append(send(wide_col, wide_out.at[row], last_send, last_recv, d, on_row(peer)))
    wide_out[row] = wide_col[...]
    for copy in third:
        copy.wait()
    for copy in moved:
        copy.wait()
    own.wait()


def finish_exchange(corr, wide, thin):
    row_count = corr.shape[0]
    col_count = wide.shape[1]
    share, width = wide.shape[2:]
    vmem = pl.BlockSpec(memory_space=pltpu.VMEM)
    anywhere = pl.BlockSpec(memory_space=pl.ANY)
    dma = pltpu.SemaphoreType.DMA
    return pl.pallas_call(
        tail_kernel,
        in_specs=[anywhere, vmem, vmem],
        out_specs=[anywhere, vmem, vmem],
        out_shape=[
            jax.ShapeDtypeStruct(corr.shape, corr.dtype),
            jax.ShapeDtypeStruct((row_count, col_count, share, width), F32),
            jax.ShapeDtypeStruct((col_count,) + thin.shape[1:], F32),
        ],
        scratch_shapes=[
            pltpu.VMEM(wide.shape, F32), pltpu.VMEM(thin.shape, F32), pltpu.VMEM(wide.shape[1:], F32),
            pltpu.VMEM(thin.shape[1:], F32), pltpu.VMEM(wide.shape[1:], F32),
            dma((1,)), dma((row_count,)), dma((row_count,)), dma((2 * row_count,)), dma((2 * row_count,)),
            dma((2 * col_count,)), dma((2 * col_count,)), dma((row_count,)), dma((row_count,)),
        ],
        compiler_params=pltpu.CompilerParams(
            collective_id=0, has_side_effects=True, vmem_limit_bytes=VMEM_BYTES // 2
        ),
    )(corr, wide, thin)


def whole_spec(shape):
    return pl.BlockSpec(shape, lambda c: (0,) * len(shape))


def lead_spec(shape):
    return pl.BlockSpec((1,) + tuple(shape[1:]), lambda c: (c,) + (0,) * (len(shape) - 1))


def lane_spec(shape):
    block = tuple(shape[:-1]) + (WIDTH,)
    return pl.BlockSpec(block, lambda c: (0,) * (len(shape) - 1) + (c,))


def second_spec(shape):
    block = (shape[0], 1) + tuple(shape[2:])
    return pl.BlockSpec(block, lambda c: (0, c) + (0,) * (len(shape) - 2))


KINDS = {"s": second_spec, "a": whole_spec, "c": lead_spec, "l": lane_spec}


def grouped_call(kernel, inputs, kinds, outputs, out_kinds, scratch, flops=0):
    return pl.pallas_call(
        kernel,
        grid=(GROUPS,),
        in_specs=[KINDS[kind](value.shape) for kind, value in zip(kinds, inputs)],
        out_specs=[KINDS[kind](shape) for kind, (shape, _) in zip(out_kinds, outputs)],
        out_shape=[jax.ShapeDtypeStruct(shape, dtype) for shape, dtype in outputs],
        scratch_shapes=[pltpu.VMEM(shape, dtype) for shape, dtype in scratch],
        compiler_params=pltpu.CompilerParams(vmem_limit_bytes=VMEM_BYTES),
        cost_estimate=pl.CostEstimate(flops=flops, bytes_accessed=40_000_000, transcendentals=0),
    )(*inputs)


def to_groups(value, heads_here):
    cols = value.shape[0]
    middle = value.shape[1:-1]
    if heads_here == QUAD:
        return value
    if heads_here > QUAD:
        parts = heads_here // QUAD
        value = value.reshape((cols,) + middle + (parts, WIDTH))
        value = jnp.moveaxis(value, -2, 1)
        return value.reshape((GROUPS,) + middle + (WIDTH,))
    parts = QUAD // heads_here
    value = value.reshape((GROUPS, parts) + middle + (heads_here * P_SIZE,))
    value = jnp.moveaxis(value, 1, -2)
    return value.reshape((GROUPS,) + middle + (WIDTH,))


def to_cols(value, heads_here, col_count):
    middle = value.shape[1:-1]
    if heads_here == QUAD:
        return value
    if heads_here > QUAD:
        parts = heads_here // QUAD
        value = value.reshape((col_count, parts) + middle + (WIDTH,))
        value = jnp.moveaxis(value, 1, -2)
        return value.reshape((col_count,) + middle + (heads_here * P_SIZE,))
    parts = QUAD // heads_here
    value = value.reshape((GROUPS,) + middle + (parts, heads_here * P_SIZE))
    value = jnp.moveaxis(value, -2, 1)
    return value.reshape((col_count,) + middle + (heads_here * P_SIZE,))


def pad_lanes(value, width):
    return jnp.pad(value, [(0, 0)] * (value.ndim - 1) + [(0, width - value.shape[-1])])


def carry_in(state, decay, row_count, col_count, seq_cols, forward):
    row = lax.axis_index("row")
    col = lax.axis_index("col")
    total = state
    factor = decay
    before = jnp.zeros(state.shape, F32)
    reach = jnp.ones_like(decay)
    span = 1
    while span < row_count:
        pairs = [(i, i ^ span) for i in range(row_count)]
        other = lax.ppermute(total, "row", pairs).astype(F32)
        other_factor = lax.ppermute(factor, "row", pairs)
        behind = ((row & span) != 0) == forward
        mine = total.astype(F32)
        before = jnp.where(behind, before + reach * other, before)
        reach = jnp.where(behind, reach * other_factor, reach)
        joined = jnp.where(behind, other * factor + mine, mine * other_factor + other)
        total = joined.astype(BF16)
        factor = factor * other_factor
        span *= 2
    place = lax.rem(col, seq_cols)
    for hop in range(1, seq_cols):
        shift = hop if forward else -hop
        pairs = [(i, (i + shift) % col_count) for i in range(col_count)]
        other = lax.ppermute(total, "col", pairs).astype(F32)
        other_factor = lax.ppermute(factor, "col", pairs)
        inside = place >= hop if forward else place < seq_cols - hop
        before = jnp.where(inside, before + reach * other, before)
        reach = jnp.where(inside, reach * other_factor, reach)
    return before


def rows_to_parts(value):
    row_count = value.shape[0]
    row = lax.axis_index("row")
    result = value
    for d in range(1, row_count):
        peer = lax.rem(row + d, row_count)
        pairs = [(i, (i + d) % row_count) for i in range(row_count)]
        piece = lax.ppermute(lax.dynamic_index_in_dim(value, peer), "row", pairs)
        source = lax.rem(row + row_count - d, row_count)
        result = lax.dynamic_update_slice_in_dim(result, piece, source, 0)
    return result


def per_device(
    block_in, norm_gain, proj_inner, proj_state, conv_inner, conv_inner_bias, conv_state, conv_state_bias,
    step_bias, decay_log, skip_gain, gate_gain, proj_out, adapt_in_down, adapt_in_up, adapt_out_down,
    adapt_out_up, adapter_id, cotangent,
):
    row_count = lax.axis_size("row")
    col_count = lax.axis_size("col")
    row = lax.axis_index("row")
    col = lax.axis_index("col")
    col_tokens, part = block_in.shape
    chunk = col_tokens // row_count
    total_rows = chunk + HALO
    blocks = chunk // BLOCK
    seq_cols = SEQ // col_tokens
    heads_here = proj_inner.shape[1]
    local = heads_here * P_SIZE
    rank_total = adapt_in_down.shape[1]
    rank_part = rank_total // row_count
    rank_share = rank_total // col_count
    adapter = lax.dynamic_index_in_dim(adapter_id, col // seq_cols, keepdims=False)

    head = jnp.zeros((HALO, part), BF16)
    if seq_cols > 1:
        pairs = [(i, (i + 1) % col_count) for i in range(col_count)]
        head = lax.ppermute(block_in[-HALO:], "col", pairs)
        head = jnp.where(lax.rem(col, seq_cols) > 0, head, jnp.zeros_like(head))
    padded = jnp.concatenate([head, block_in], axis=0)
    windows = jnp.stack([padded[r * chunk : r * chunk + total_rows] for r in range(row_count)])
    x_rows = lax.all_to_all(windows, "row", 0, 0, tiled=True)
    g_rows = lax.all_to_all(cotangent.reshape(row_count, chunk, part), "row", 0, 0, tiled=True)

    def split_pairs(value):
        value = value.reshape(value.shape[0], heads_here, 2, P_SIZE)
        return jnp.swapaxes(value, 1, 2).reshape(value.shape[0], 2, local)

    up_part = lax.dynamic_slice_in_dim(adapt_in_up, row * rank_part, rank_part, 0)
    w_block = jnp.concatenate([split_pairs(proj_inner), split_pairs(up_part)], axis=0)
    w_all = lax.all_gather(w_block.reshape(part + rank_part, 2 * local), ("col", "row"))
    w_all = w_all.reshape(col_count, row_count, part + rank_part, 2, local)
    w_all = to_groups(w_all, heads_here).reshape(GROUPS, row_count, part + rank_part, 2 * WIDTH)
    up_all = w_all[:, :, part:, :].reshape(GROUPS, rank_total, 2 * WIDTH)
    up_all = lax.dynamic_slice_in_dim(up_all, adapter * RANK, RANK, 1)
    up_all = jnp.pad(up_all, ((0, 0), (0, LANES - RANK), (0, 0)))

    down_part = lax.dynamic_slice_in_dim(adapt_out_down, row * rank_part, rank_part, 0)
    p_block = jnp.concatenate([proj_out, down_part.T], axis=1)
    p_all = lax.all_gather(p_block, ("col", "row")).reshape(col_count, row_count, local, part + rank_part)
    if heads_here != QUAD:
        p_all = jnp.moveaxis(p_all, 1, 0).reshape(row_count, GROUPS, WIDTH, part + rank_part)
        p_all = jnp.moveaxis(p_all, 0, 1)
    down_all = jnp.swapaxes(p_all[..., part:], 1, 2).reshape(GROUPS, WIDTH, rank_total)
    down_all = pad_lanes(lax.dynamic_slice_in_dim(down_all, adapter * RANK, RANK, 2), LANES)

    in_down = lax.dynamic_slice_in_dim(adapt_in_down, adapter * RANK, RANK, 1)
    out_up = lax.dynamic_slice_in_dim(adapt_out_up, adapter * RANK, RANK, 1)
    state_width = proj_state.shape[1]
    shared = lax.all_gather(jnp.concatenate([proj_state, in_down, out_up], axis=1), "row")
    w_state = jnp.concatenate(
        [
            pad_lanes(shared[..., :state_width], 384),
            pad_lanes(shared[..., state_width : state_width + RANK], LANES),
        ],
        axis=2,
    )
    out_up_all = pad_lanes(shared[..., state_width + RANK :], LANES)
    gain_all = lax.all_gather(norm_gain, "row").reshape(row_count, 1, part)

    scalars = jnp.concatenate([step_bias, decay_log, skip_gain])
    vectors = jnp.concatenate(
        [conv_inner, conv_inner_bias[None], gate_gain[None], pad_lanes(scalars, local)[None]], axis=0
    )
    vectors = lax.all_gather(vectors, "col")
    scalars = vectors[:, 6, : 3 * heads_here].reshape(col_count, 3, heads_here)
    scalars = jnp.swapaxes(scalars, 0, 1).reshape(3, HEADS)
    head_rows = jnp.pad(scalars[:2], ((0, 6), (0, LANES - HEADS)))
    skip_wide = jnp.repeat(scalars[2], P_SIZE).reshape(GROUPS, 1, WIDTH)
    vectors = jnp.concatenate(
        [to_groups(vectors[:, :6], heads_here), skip_wide, jnp.zeros_like(skip_wide)], axis=1
    )
    state_taps = jnp.concatenate([conv_state, conv_state_bias[None], jnp.zeros((3, 256), F32)], axis=0)

    token_f32 = ((chunk, LANES), F32)
    token_low = ((chunk, LANES), BF16)
    inner_low = ((chunk, DI), BF16)
    states = ((blocks, STATES, DI), F32)
    score_box = ((blocks, BLOCK, BLOCK), F32)
    turned = ((blocks, STATES, BLOCK), BF16)
    (
        normed, scpre, raw, step, cum, cum_t, bs, cs, cs_t, adv, gate, u, eloc, fin, dec,
    ) = grouped_call(
        front_kernel,
        (x_rows, gain_all, w_state, state_taps, head_rows, w_all, up_all, vectors),
        "aaaaaccc",
        [
            ((total_rows, D), BF16), ((chunk, 256), F32), token_f32, token_f32, token_f32,
            ((GROUPS, QUAD, chunk), F32), token_low, token_low, turned, ((total_rows, LANES), BF16),
            inner_low, inner_low, states, ((STATES, DI), BF16), ((8, DI), F32),
        ],
        "aaaaaaaaaalllll",
        [((total_rows, 512), F32), turned, ((total_rows, WIDTH), F32)],
        flops=int(45e9),
    )
    decay = dec[0:1]
    entry = carry_in(fin, decay, row_count, col_count, seq_cols, True)
    out_rows, o, ent, aux, side_grad, out_up_grad = grouped_call(
        scan_kernel,
        (x_rows, g_rows, out_up_all, p_all, down_all, vectors, gate, u, eloc, entry, step, cum, cum_t, bs, cs),
        "aaacccllllaacaa",
        [
            ((row_count, chunk, part), BF16), inner_low, ((blocks, STATES, DI), BF16), token_f32, token_low,
            ((RANK, D), F32),
        ],
        "allaaa",
        [score_box, ((chunk, D), F32), token_f32, token_f32],
        flops=int(45e9),
    )
    block_out = rows_to_parts(out_rows).reshape(col_tokens, part)
    dgate, dy, gloc, gfin, out_down_grad = grouped_call(
        gate_kernel,
        (g_rows, p_all, side_grad, down_all, vectors, gate, o, aux, cum, cs_t),
        "acaccllaaa",
        [inner_low, inner_low, states, ((STATES, DI), BF16), ((GROUPS, RANK, WIDTH), F32)],
        "llllc",
        [((blocks, RANK, BLOCK), BF16)],
        flops=int(25e9),
    )
    exit_grad = carry_in(gfin, decay, row_count, col_count, seq_cols, False)
    corr, wide, thin = grouped_call(
        back_kernel,
        (
            x_rows, gain_all, normed, w_state, w_all, up_all, adv, vectors, state_taps, head_rows,
            u, o, dy, dgate, ent, gloc, exit_grad, step, cum, cum_t, raw, scpre, bs, cs,
            out_down_grad, out_up_grad,
        ),
        "aaaaccacaalllllllaacaaaaca",
        [
            ((row_count, total_rows, part), BF16), ((row_count, GROUPS, RANK // row_count, 3 * WIDTH), F32),
            ((row_count, 2 * RANK, part), F32),
        ],
        "asa",
        [
            score_box, score_box, token_f32, token_f32, token_f32, token_f32, ((blocks, 8, LANES), F32),
            ((total_rows + HALO, WIDTH), F32), ((total_rows, 2 * WIDTH), BF16), ((total_rows, D), F32),
            ((total_rows, LANES), F32), ((blocks, RANK, BLOCK), BF16),
            ((RANK, 2 * WIDTH), F32), ((RANK, D), F32),
        ],
        flops=int(75e9),
    )

    if heads_here != QUAD:
        share = RANK // row_count
        wide = jnp.swapaxes(wide.reshape(row_count, GROUPS, share, 3, WIDTH), 0, 1)
        wide = to_cols(wide, heads_here, col_count)
        wide = jnp.swapaxes(wide, 0, 1).reshape(row_count, col_count, share, 3 * local)
    corr, wide, thin = finish_exchange(corr, wide, thin)
    input_grad = cotangent.astype(F32) + corr[:, HALO:].reshape(col_tokens, part).astype(F32)
    early = corr[:, :HALO].astype(F32)
    for r in range(1, row_count):
        input_grad = input_grad.at[r * chunk - HALO : r * chunk].add(early[r])
    if seq_cols > 1:
        pairs = [(i, (i - 1) % col_count) for i in range(col_count)]
        late = lax.ppermute(corr[0, :HALO], "col", pairs).astype(F32)
        late = jnp.where(lax.rem(col, seq_cols) < seq_cols - 1, late, jnp.zeros_like(late))
        input_grad = input_grad.at[-HALO:].add(late)
    wide = jnp.swapaxes(wide, 0, 1).reshape(col_count, RANK, 3 * local)
    owner = jnp.repeat(adapter_id, seq_cols)
    adapters = rank_total // RANK
    chosen = owner[:, None] == jnp.arange(adapters, dtype=jnp.int32)[None, :]
    wide = jnp.sum(jnp.where(chosen[:, :, None, None], wide[:, None], 0.0), axis=0)
    wide = wide.reshape(rank_total, 3 * local)
    in_up = wide[:, : 2 * local].reshape(rank_total, 2, heads_here, P_SIZE)
    in_up = jnp.swapaxes(in_up, 1, 2).reshape(rank_total, heads_here, 2 * P_SIZE)
    out_down = wide[:, 2 * local :]
    thin = jnp.sum(jnp.where(chosen[:, :, None, None], thin[:, None], 0.0), axis=0)
    thin = thin.reshape(adapters, 2, RANK, part)
    thin = jnp.transpose(thin, (1, 3, 0, 2)).reshape(2, part, rank_total)
    thin = lax.dynamic_slice_in_dim(thin, col * rank_share, rank_share, 2)
    return block_out, input_grad, thin[0], in_up, out_down, thin[1]


def solution(mesh):
    placed = (
        P("col", "row"), P("row"), P("row", "col", None), P("row", None), P(None, "col"), P("col"), P(), P(),
        P("col"), P("col"), P("col"), P("col"), P("col", "row"), P("row", None), P(None, "col", None),
        P(None, "col"), P("row", None), P(), P("col", "row"),
    )
    return jax.shard_map(
        per_device,
        mesh=mesh,
        in_specs=placed,
        out_specs=(
            P("col", "row"), P("col", "row"), P("row", "col"), P(None, "col", None), P(None, "col"),
            P("row", "col"),
        ),
        check_vma=False,
    )
```

```python
import functools

import jax
import jax.numpy as jnp
from jax import lax
from jax.experimental import pallas as pl
from jax.experimental.pallas import tpu as pltpu
from jax.sharding import PartitionSpec as P

D = 1024
HEADS = 32
P_SIZE = 64
STATES = 128
BLOCK = 256
RANK = 16
SEQ = 4096
DI = 2048
EPS = 1e-05
LOG2E = 1.4426950408889634

HALO = 16
IN_LANE = 32
OUT_LANE = 48
QUAD = 4
WIDTH = QUAD * P_SIZE
GROUPS = HEADS // QUAD
LANES = 128
VMEM_BYTES = 60 * 1024 * 1024
F32 = jnp.float32
BF16 = jnp.bfloat16
MESH = pl.DeviceIdType.MESH


def mm(left, right):
    return jnp.dot(left, right, preferred_element_type=F32)


def mm_nt(left, right):
    return lax.dot_general(left, right, (((1,), (1,)), ((), ())), preferred_element_type=F32)


def mm_tn(left, right):
    return lax.dot_general(left, right, (((0,), (0,)), ((), ())), preferred_element_type=F32)


def split_left(ones, value):
    high = value.astype(BF16)
    rest = value - high.astype(F32)
    middle = rest.astype(BF16)
    low = (rest - middle.astype(F32)).astype(BF16)
    return mm(ones, high) + mm(ones, middle) + mm(ones, low)


def split_right(value, ones):
    high = value.astype(BF16)
    low = (value - high.astype(F32)).astype(BF16)
    return mm(high, ones) + mm(low, ones)


def sigmoid(value):
    return 0.5 * jnp.tanh(0.5 * value) + 0.5


def iota(shape, axis):
    return lax.broadcasted_iota(jnp.int32, shape, axis)


def widen(cols):
    lane = iota((cols.shape[0], LANES), 1) < P_SIZE
    left = jnp.where(lane, cols[:, 0:1], cols[:, 1:2])
    right = jnp.where(lane, cols[:, 2:3], cols[:, 3:4])
    return jnp.concatenate([left, right], axis=1)


def to_front(cols, group):
    return pltpu.roll(cols, lax.rem(LANES - QUAD * group, LANES), 1)


def lane_range(values, first):
    lane = iota(values.shape, 1)
    return jnp.where((lane >= first) & (lane < first + RANK), values, 0.0)


def out_block(w_ref, row, part):
    if w_ref.shape[2] == WIDTH:
        return w_ref[0, row, :, :part]
    rows = WIDTH // 2
    return jnp.concatenate([w_ref[0, row, :rows, :part], w_ref[0, row, :rows, part:]], axis=0)


def head_only(values, head):
    lane = iota(values.shape, 1) // P_SIZE
    return jnp.where(lane == head, values, jnp.zeros_like(values))


def delays(window, taps, bias):
    total = window[8:] * taps[0:1] + bias
    for k in range(1, 4):
        total = total + pltpu.roll(window, k, 0)[8:] * taps[k : k + 1]
    return total


def advances(window, taps, count):
    length = window.shape[0]
    total = window[:count] * taps[0:1]
    for k in range(1, 4):
        total = total + pltpu.roll(window, length - k, 0)[:count] * taps[k : k + 1]
    return total


def at_block(k):
    return pl.ds(pl.multiple_of(k * BLOCK, BLOCK), BLOCK)


def at_rows(k):
    return pl.ds(pl.multiple_of(HALO + k * BLOCK, HALO), BLOCK)


def front_kernel(
    x_ref, gain_ref, wst_ref, sp_ref, hp_ref, w_ref, up_ref, vp_ref,
    normed_ref, scpre_ref, raw_ref, step_ref, cum_ref, cum_t_ref, bs_ref, cs_ref, cs_t_ref, adv_ref,
    gate_ref, u_ref, eloc_ref, fin_ref, dec_ref,
    st_scr, bs_t_scr, val_scr,
):
    group = pl.program_id(0)
    row_count, _, part = x_ref.shape
    blocks = eloc_ref.shape[0]

    @pl.when(group == 0)
    def _():
        def project(rows):
            pieces = [x_ref[r, rows, :].astype(F32) for r in range(row_count)]
            square = sum(jnp.sum(piece * piece, axis=1, keepdims=True) for piece in pieces)
            inv = lax.rsqrt(square / D + EPS)
            total = None
            for r in range(row_count):
                normed = (pieces[r] * inv * gain_ref[r]).astype(BF16)
                normed_ref[rows, r * part : (r + 1) * part] = normed
                term = mm(normed, wst_ref[r])
                total = term if total is None else total + term
            st_scr[rows, :] = total
            adv_ref[rows, :] = lane_range(total[:, 256:384], IN_LANE).astype(BF16)

        project(pl.ds(0, HALO))

        @pl.loop(0, blocks)
        def _(k):
            project(at_rows(k))

        lower = (iota((BLOCK, BLOCK), 0) >= iota((BLOCK, BLOCK), 1)).astype(BF16)
        rate = -jnp.exp(hp_ref[1:2]) * LOG2E

        @pl.loop(0, blocks)
        def _(k):
            window = st_scr[pl.ds(pl.multiple_of(8 + k * BLOCK, 8), BLOCK + 8), :256]
            pre = delays(window, sp_ref[0:4], sp_ref[4:5])
            conv = pre * sigmoid(pre)
            b_rows = conv[:, :STATES].astype(BF16)
            c_rows = conv[:, STATES:].astype(BF16)
            scpre_ref[at_block(k), :] = pre
            bs_ref[at_block(k), :] = b_rows
            cs_ref[at_block(k), :] = c_rows
            bs_t_scr[k] = conv[:, :STATES].T.astype(BF16)
            cs_t_ref[k] = conv[:, STATES:].T.astype(BF16)
            raw = st_scr[at_rows(k), 256:384] + hp_ref[0:1]
            small = jnp.exp(-jnp.abs(raw))
            tail = jnp.where(
                small < 0.01, small * (1.0 - small * (0.5 - small * (1.0 / 3.0))), jnp.log(1.0 + small)
            )
            step = jnp.maximum(raw, 0.0) + tail
            cum = split_left(lower, step * rate)
            raw_ref[at_block(k), :] = raw
            step_ref[at_block(k), :] = step
            cum_ref[at_block(k), :] = cum
            flipped = cum.T
            for g in range(GROUPS):
                cum_t_ref[g, :, at_block(k)] = flipped[g * QUAD : (g + 1) * QUAD]

    def inner(rows):
        total = mm(adv_ref[rows, :], up_ref[0])
        for r in range(row_count):
            total = total + mm(normed_ref[rows, r * part : (r + 1) * part], w_ref[0, r, :part, :])
        return total

    val_scr[0:HALO, :] = inner(pl.ds(0, HALO))[:, WIDTH:]
    taps = vp_ref[0]

    def one_block(k, carry):
        state, decay = carry
        product = inner(at_rows(k))
        gate_ref[at_block(k), :] = product[:, :WIDTH].astype(BF16)
        val_scr[at_rows(k), :] = product[:, WIDTH:]
        window = val_scr[pl.ds(pl.multiple_of(8 + k * BLOCK, 8), BLOCK + 8), :]
        pre = delays(window, taps[0:4], taps[4:5])
        u_ref[at_block(k), :] = pre.astype(BF16)
        xs = (pre * sigmoid(pre)).astype(BF16).astype(F32)
        cum = cum_ref[at_block(k), :]
        last = cum[BLOCK - 1 : BLOCK]
        weight = to_front(step_ref[at_block(k), :] * jnp.exp2(last - cum), group)
        weighted = (xs * widen(weight)).astype(BF16)
        eloc_ref[k] = state
        last8 = to_front(jnp.broadcast_to(last, (8, LANES)), group)
        fall = widen(jnp.exp2(last8))[0:1]
        return fall * state + mm(bs_t_scr[k], weighted), decay * fall

    start = (jnp.zeros((STATES, WIDTH), F32), jnp.ones((1, WIDTH), F32))
    state, decay = lax.fori_loop(0, blocks, one_block, start)
    fin_ref[...] = state.astype(BF16)
    dec_ref[...] = jnp.broadcast_to(decay, (8, WIDTH))


def scan_kernel(
    x_ref, g_ref, wst_ref, w_ref, down_ref, vp_ref, gate_ref, u_ref, eloc_ref, ein_ref,
    step_ref, cum_ref, cum_t_ref, bs_ref, cs_ref,
    out_ref, o_ref, ent_ref, aux_ref, sg_ref, gup_ref,
    score_scr, acc_scr, side_scr, square_scr,
):
    group = pl.program_id(0)
    row_count, _, part = x_ref.shape
    blocks = eloc_ref.shape[0]

    @pl.when(group == 0)
    def _():
        acc_scr[...] = jnp.zeros_like(acc_scr)
        side_scr[...] = jnp.zeros_like(side_scr)
        square_scr[...] = jnp.zeros_like(square_scr)
        keep = iota((BLOCK, BLOCK), 0) >= iota((BLOCK, BLOCK), 1)

        @pl.loop(0, blocks)
        def _(k):
            score = mm_nt(cs_ref[at_block(k), :], bs_ref[at_block(k), :])
            score_scr[k] = jnp.where(keep, score, 0.0)

    taps = vp_ref[0]

    def one_block(k, before):
        rows = at_block(k)
        pre = u_ref[rows, :].astype(F32)
        conv = pre * sigmoid(pre)
        cum = to_front(cum_ref[rows, :], group)
        step = to_front(step_ref[rows, :], group)
        scaled = (conv.astype(BF16).astype(F32) * widen(step)).astype(BF16)
        score = score_scr[k]
        entering = (eloc_ref[k] + before * ein_ref[...]).astype(BF16)
        ent_ref[k] = entering
        total = widen(jnp.exp2(cum)) * mm(cs_ref[rows, :], entering)
        for h in range(QUAD):
            spread = cum[:, h : h + 1] - cum_t_ref[0, h : h + 1, rows]
            weights = (score * jnp.exp2(jnp.minimum(spread, 0.0))).astype(BF16)
            total = total + mm(weights, head_only(scaled, h))
        output = total + taps[6:7] * conv
        o_ref[rows, :] = output.astype(BF16)
        gate = gate_ref[rows, :].astype(F32)
        gated = output * gate * sigmoid(gate)
        square = gated * gated
        square_scr[rows, :] += square[:, :LANES] + square[:, LANES:]
        gained = (gated * taps[5:6]).astype(BF16)
        for r in range(row_count):
            cols = slice(r * part, (r + 1) * part)
            acc_scr[rows, cols] += mm(gained, out_block(w_ref, r, part))
        side_scr[rows, :] += mm_nt(gained, down_ref[0])
        return before * widen(jnp.exp2(cum[BLOCK - 8 :]))[7:8]

    lax.fori_loop(0, blocks, one_block, jnp.ones((1, WIDTH), F32))

    @pl.when(group == pl.num_programs(0) - 1)
    def _():
        gup_ref[...] = jnp.zeros_like(gup_ref)

        @pl.loop(0, blocks)
        def _(k):
            rows = at_block(k)
            mean = jnp.sum(square_scr[rows, :], axis=1, keepdims=True) / DI
            rms = lax.rsqrt(mean + EPS)
            side_raw = side_scr[rows, :]
            side = (side_raw * rms).astype(BF16)
            side_grad = None
            for r in range(row_count):
                term = mm(g_ref[r, rows, :], wst_ref[r, :, 256:384])
                side_grad = term if side_grad is None else side_grad + term
            side_grad = lane_range(side_grad, OUT_LANE).astype(BF16)
            product = jnp.sum(side_grad.astype(F32) * side_raw, axis=1, keepdims=True)
            for r in range(row_count):
                cols = slice(r * part, (r + 1) * part)
                raw = acc_scr[rows, cols]
                cot = g_ref[r, rows, :]
                product = product + jnp.sum(raw * cot.astype(F32), axis=1, keepdims=True)
                total = x_ref[r, at_rows(k), :].astype(F32) + raw * rms + mm_nt(side, wst_ref[r, :, 256:384])
                out_ref[r, rows, :] = total.astype(BF16)
                gup_ref[:, cols] += mm_tn(side, cot)[OUT_LANE : OUT_LANE + RANK]
            coefficient = rms * rms * rms * product / DI
            lane = iota((BLOCK, LANES), 1)
            aux_ref[rows, :] = jnp.where(lane == 0, rms, coefficient)
            sg_ref[rows, :] = side_grad


def gate_kernel(
    g_ref, w_ref, sg_ref, down_ref, vp_ref, gate_ref, o_ref, aux_ref, cum_ref, cs_t_ref,
    dgate_ref, dy_ref, gloc_ref, gfin_ref, gdown_ref,
    sg_t_scr,
):
    group = pl.program_id(0)
    row_count, _, part = g_ref.shape
    blocks = gloc_ref.shape[0]

    @pl.when(group == 0)
    def _():
        @pl.loop(0, blocks)
        def _(k):
            sg_t_scr[k] = sg_ref[at_block(k), :].astype(F32).T[OUT_LANE : OUT_LANE + RANK].astype(BF16)

    taps = vp_ref[0]
    gdown_ref[0] = jnp.zeros((RANK, WIDTH), F32)

    def one_block(i, state):
        k = blocks - 1 - i
        rows = at_block(k)
        dmix = mm(sg_ref[rows, :], down_ref[0])
        for r in range(row_count):
            dmix = dmix + mm_nt(g_ref[r, rows, :], out_block(w_ref, r, part))
        gate = gate_ref[rows, :].astype(F32)
        output = o_ref[rows, :].astype(F32)
        sig = sigmoid(gate)
        act = gate * sig
        gated = output * act
        rms = aux_ref[rows, 0:1]
        coefficient = aux_ref[rows, 1:2]
        scale = rms * taps[5:6]
        mixed = (gated * scale).astype(BF16)
        gdown_ref[0] += mm(sg_t_scr[k], mixed)
        gated_grad = scale * dmix - gated * coefficient
        dy = gated_grad * act
        dgate = gated_grad * output * (sig + act * (1.0 - sig))
        dgate_ref[rows, :] = dgate.astype(BF16)
        dy_ref[rows, :] = dy.astype(BF16)
        cum = to_front(cum_ref[rows, :], group)
        factor = widen(jnp.exp2(cum))
        gloc_ref[k] = state
        return factor[BLOCK - 1 : BLOCK] * state + mm(cs_t_ref[k], (factor * dy).astype(BF16))

    state = lax.fori_loop(0, blocks, one_block, jnp.zeros((STATES, WIDTH), F32))
    gfin_ref[...] = state.astype(BF16)


def back_kernel(
    x_ref, gain_ref, normed_ref, wst_ref, w_ref, up_ref, adv_ref, vp_ref, sp_ref, hp_ref,
    u_ref, o_ref, dy_ref, dgate_ref, ent_ref, gloc_ref, gin_ref,
    step_ref, cum_ref, cum_t_ref, raw_ref, scpre_ref, bs_ref, cs_ref, out_down_ref, out_up_ref,
    corr_ref, wide_ref, thin_ref,
    score_scr, dscore_scr, db_scr, dc_scr, dcum_scr, dstep_scr, dlast_scr, du_scr, ig_scr, ng_scr, adg_scr, adv_t_scr, up_scr, in_scr,
):
    group = pl.program_id(0)
    row_count, _, part = x_ref.shape
    blocks = gloc_ref.shape[0]
    total_rows = normed_ref.shape[0]

    @pl.when(group == 0)
    def _():
        for ref in (dscore_scr, db_scr, dc_scr, dcum_scr, dstep_scr, dlast_scr, ng_scr, adg_scr):
            ref[...] = jnp.zeros_like(ref)
        du_scr[0:HALO, :] = jnp.zeros((HALO, WIDTH), F32)
        du_scr[total_rows : total_rows + HALO, :] = jnp.zeros((HALO, WIDTH), F32)

        @pl.loop(0, blocks)
        def _(k):
            score_scr[k] = mm_nt(bs_ref[at_block(k), :], cs_ref[at_block(k), :])
            adv_t_scr[k] = adv_ref[at_rows(k), :].astype(F32).T[IN_LANE : IN_LANE + RANK].astype(BF16)

    keep = iota((BLOCK, BLOCK), 0) <= iota((BLOCK, BLOCK), 1)
    taps = vp_ref[0]
    pick = (iota((WIDTH, LANES), 1) == QUAD * group + iota((WIDTH, LANES), 0) // P_SIZE).astype(BF16)

    def one_block(i, after):
        k = blocks - 1 - i
        rows = at_block(k)
        pre = u_ref[rows, :].astype(F32)
        sig = sigmoid(pre)
        conv = pre * sig
        xs = conv.astype(BF16).astype(F32)
        cum = to_front(cum_ref[rows, :], group)
        step_w = widen(to_front(step_ref[rows, :], group))
        scaled_low = (xs * step_w).astype(BF16)
        scaled = scaled_low.astype(F32)
        dy_low = dy_ref[rows, :]
        dy = dy_low.astype(F32)
        b_rows = bs_ref[rows, :]
        c_rows = cs_ref[rows, :]
        score = jnp.where(keep, score_scr[k], 0.0)
        dscore = dscore_scr[k]
        ending = gloc_ref[k] + after * gin_ref[...]
        ending_low = ending.astype(BF16)
        last = cum[BLOCK - 1 : BLOCK]
        to_end = widen(jnp.exp2(last - cum))
        dscaled_state = to_end * mm(b_rows, ending_low)
        dscaled = dscaled_state
        for h in range(QUAD):
            spread = cum_t_ref[0, h : h + 1, rows] - cum[:, h : h + 1]
            damp = jnp.exp2(jnp.minimum(spread, 0.0))
            weights = (score * damp).astype(BF16)
            dy_head = head_only(dy_low, h)
            dscaled = dscaled + mm(weights, dy_head)
            dscore = dscore + mm_nt(scaled_low, dy_head) * damp
        dscore_scr[k] = dscore
        from_start = widen(jnp.exp2(cum))
        fall = from_start[BLOCK - 1 : BLOCK]
        entering_low = ent_ref[k]
        entering = entering_low.astype(F32)
        dc_scr[rows, :] += mm_nt((from_start * dy).astype(BF16), entering_low)
        db_scr[rows, :] += mm_nt((to_end * scaled).astype(BF16), ending_low)
        scan_out = o_ref[rows, :].astype(F32) - taps[6:7] * conv
        dcum_scr[rows, :] += split_right(dy * scan_out - scaled * dscaled, pick)
        dstep_scr[rows, :] += split_right(xs * dscaled, pick)
        ends = jnp.sum(scaled * dscaled_state, axis=0, keepdims=True)
        ends = ends + fall * jnp.sum(entering * ending, axis=0, keepdims=True)
        dlast_scr[k] += split_right(jnp.broadcast_to(ends, (8, WIDTH)), pick)
        dconv = taps[6:7] * dy + step_w * dscaled
        du_scr[at_rows(k), :] = dconv * (sig + conv * (1.0 - sig))
        return after * fall

    lax.fori_loop(0, blocks, one_block, jnp.ones((1, WIDTH), F32))

    def spread_back(rows, window, count):
        dval = advances(window, taps[0:4], count)
        ig_scr[rows, WIDTH:] = dval.astype(BF16)
        grad = ig_scr[rows, :]
        adg_scr[rows, :] += mm_nt(grad, up_ref[0])
        for r in range(row_count):
            ng_scr[rows, r * part : (r + 1) * part] += mm_nt(grad, w_ref[0, r, :part, :])
        return grad

    ig_scr[0:HALO, :WIDTH] = jnp.zeros((HALO, WIDTH), BF16)
    first = spread_back(pl.ds(0, HALO), du_scr[0 : HALO + 8, :], HALO)
    up_scr[...] = mm_tn(adv_ref[0:HALO, :], first)[IN_LANE : IN_LANE + RANK]

    @pl.loop(0, blocks)
    def _(k):
        ig_scr[at_rows(k), :WIDTH] = dgate_ref[at_block(k), :]
        window = du_scr[pl.ds(pl.multiple_of(HALO + k * BLOCK, 8), BLOCK + 8), :]
        grad = spread_back(at_rows(k), window, BLOCK)
        up_scr[...] += mm(adv_t_scr[k], grad)

    share = RANK // row_count
    for r in range(row_count):
        wide_ref[r, 0, :, : 2 * WIDTH] = up_scr[r * share : (r + 1) * share, :]
        wide_ref[r, 0, :, 2 * WIDTH :] = out_down_ref[0, r * share : (r + 1) * share, :]

    @pl.when(group == pl.num_programs(0) - 1)
    def _():
        upper = (iota((BLOCK, BLOCK), 0) <= iota((BLOCK, BLOCK), 1)).astype(BF16)
        rate = -jnp.exp(hp_ref[1:2])

        @pl.loop(0, blocks)
        def _(k):
            rows = at_block(k)
            dscore = jnp.where(keep, dscore_scr[k], 0.0).astype(BF16)
            db = db_scr[rows, :] + mm(dscore, cs_ref[rows, :])
            dc = dc_scr[rows, :] + mm_tn(dscore, bs_ref[rows, :])
            pre = scpre_ref[rows, :]
            sig = sigmoid(pre)
            slope = sig + pre * sig * (1.0 - sig)
            du_scr[at_rows(k), :] = jnp.concatenate([db, dc], axis=1) * slope
            is_last = iota((BLOCK, LANES), 0) == BLOCK - 1
            dcum = dcum_scr[rows, :] + jnp.where(is_last, dlast_scr[k, 0:1, :], 0.0)
            dstep = dstep_scr[rows, :] + split_left(upper, dcum) * rate
            dstep_scr[rows, :] = dstep * sigmoid(raw_ref[rows, :])

        def finish(rows, window, count, draw):
            dstate = advances(window, sp_ref[0:4], count).astype(BF16)
            adapt = adg_scr[rows, :].astype(BF16)
            mixed = adapt if draw is None else adapt + draw
            total = jnp.zeros((count, 1), F32)
            square = jnp.zeros((count, 1), F32)
            grads = []
            for r in range(row_count):
                cols = slice(r * part, (r + 1) * part)
                grad = ng_scr[rows, cols] + mm_nt(dstate, wst_ref[r, :, 0:256])
                grad = grad + mm_nt(mixed, wst_ref[r, :, 256:384])
                grad = grad * gain_ref[r]
                piece = x_ref[r, rows, :].astype(F32)
                total = total + jnp.sum(piece * grad, axis=1, keepdims=True)
                square = square + jnp.sum(piece * piece, axis=1, keepdims=True)
                grads.append(grad)
                in_scr[:, cols] += mm_tn(adapt, normed_ref[rows, cols])[IN_LANE : IN_LANE + RANK]
            inv = lax.rsqrt(square / D + EPS)
            factor = inv * inv * inv * total / D
            for r in range(row_count):
                piece = x_ref[r, rows, :].astype(F32)
                corr_ref[r, rows, :] = (inv * grads[r] - factor * piece).astype(BF16)

        in_scr[...] = jnp.zeros_like(in_scr)
        finish(pl.ds(0, HALO), du_scr[0 : HALO + 8, :], HALO, None)

        @pl.loop(0, blocks)
        def _(k):
            window = du_scr[pl.ds(pl.multiple_of(HALO + k * BLOCK, 8), BLOCK + 8), :]
            finish(at_rows(k), window, BLOCK, dstep_scr[at_block(k), :].astype(BF16))

        for r in range(row_count):
            thin_ref[r, 0:RANK, :] = in_scr[:, r * part : (r + 1) * part]
            thin_ref[r, RANK:, :] = out_up_ref[:, r * part : (r + 1) * part]


def on_row(row):
    return {"row": row}


def on_col(col):
    return {"col": col}


def tail_kernel(
    corr_ref, wide_ref, thin_ref,
    corr_out, wide_out, thin_out,
    wide_scr, thin_scr, wide_sum, thin_sum, wide_col,
    own_sem, corr_send, corr_recv, row_send, row_recv, col_send, col_recv, last_send, last_recv,
):
    row_count = corr_ref.shape[0]
    col_count = thin_out.shape[0]
    row = lax.axis_index("row")
    col = lax.axis_index("col")
    barrier = pltpu.get_barrier_semaphore()
    for d in range(1, row_count):
        pl.semaphore_signal(barrier, inc=1, device_id=on_row(lax.rem(row + d, row_count)), device_id_type=MESH)
    for d in range(1, col_count):
        pl.semaphore_signal(barrier, inc=1, device_id=on_col(lax.rem(col + d, col_count)), device_id_type=MESH)
    pl.semaphore_wait(barrier, row_count + col_count - 2)

    def send(source, target, sends, recvs, index, device):
        copy = pltpu.make_async_remote_copy(
            src_ref=source, dst_ref=target, send_sem=sends.at[index], recv_sem=recvs.at[index],
            device_id=device, device_id_type=MESH,
        )
        copy.start()
        return copy

    first = []
    for d in range(1, row_count):
        peer = lax.rem(row + d, row_count)
        first.append(send(wide_ref.at[peer], wide_scr.at[row], row_send, row_recv, d, on_row(peer)))
        first.append(send(thin_ref.at[peer], thin_scr.at[row], row_send, row_recv, row_count + d, on_row(peer)))
    moved = []
    for d in range(1, row_count):
        peer = lax.rem(row + d, row_count)
        moved.append(send(corr_ref.at[peer], corr_out.at[row], corr_send, corr_recv, d, on_row(peer)))
    own = pltpu.make_async_copy(corr_ref.at[row], corr_out.at[row], own_sem.at[0])
    own.start()
    for copy in first:
        copy.wait()
    wide = wide_ref[row]
    thin = thin_ref[row]
    for d in range(1, row_count):
        peer = lax.rem(row + d, row_count)
        wide = wide + wide_scr[peer]
        thin = thin + thin_scr[peer]
    wide_sum[...] = wide
    thin_sum[...] = thin
    second = []
    for d in range(1, col_count):
        peer = lax.rem(col + d, col_count)
        second.append(send(wide_sum.at[peer], wide_col.at[col], col_send, col_recv, d, on_col(peer)))
        second.append(send(thin_sum, thin_out.at[col], col_send, col_recv, col_count + d, on_col(peer)))
    wide_col[col] = wide_sum[col]
    thin_out[col] = thin
    for copy in second:
        copy.wait()
    third = []
    for d in range(1, row_count):
        peer = lax.rem(row + d, row_count)
        third.append(send(wide_col, wide_out.at[row], last_send, last_recv, d, on_row(peer)))
    wide_out[row] = wide_col[...]
    for copy in third:
        copy.wait()
    for copy in moved:
        copy.wait()
    own.wait()


def start_kernel(
    x_ref, w_ref, up_ref, p_ref, down_ref, shared_ref, gain_ref, conv_ref, bias_ref, gate_ref, step_ref, rate_ref,
    skip_ref,
    x_out, w_out, shared_out, gain_out, vec_out, head_out,
    block_scr, zero_scr,
    own_sem, send_sem, recv_sem, row_send, row_recv, col_send, col_recv,
):
    col_count, row_count = w_out.shape[:2]
    high_count = col_count // 2
    part = x_ref.shape[1]
    chunk = x_ref.shape[0] // row_count
    rank_part = up_ref.shape[0] // row_count
    row = lax.axis_index("row")
    col = lax.axis_index("col")
    low = lax.rem(col, 2)
    high = col // 2
    core = row + 1 - 2 * lax.rem(row, 2)
    across = lax.rem(row + 2, row_count)
    side = col + 1 - 2 * low
    barrier = pltpu.get_barrier_semaphore()
    for d in range(1, row_count):
        pl.semaphore_signal(barrier, inc=1, device_id=on_row(lax.rem(row + d, row_count)), device_id_type=MESH)
    for d in range(1, col_count):
        pl.semaphore_signal(barrier, inc=1, device_id=on_col(lax.rem(col + d, col_count)), device_id_type=MESH)

    def paired(value):
        lane = iota((value.shape[0], LANES), 1) < P_SIZE
        tiles = [value[:, h * LANES : (h + 1) * LANES].astype(F32) for h in range(QUAD)]
        turned = [pltpu.roll(tile, P_SIZE, 1) for tile in tiles]
        gates = [jnp.where(lane, tiles[h], turned[h + 1]) for h in (0, 2)]
        values = [jnp.where(lane, turned[h], tiles[h + 1]) for h in (0, 2)]
        return jnp.concatenate(gates + values, axis=1).astype(BF16)

    block_scr[0:part, :] = paired(w_ref[...])
    ranks = pl.ds(pl.multiple_of(row * rank_part, rank_part), rank_part)
    block_scr[part : part + rank_part, :] = paired(up_ref[ranks, :])
    first = part + rank_part
    half = WIDTH // 2
    block_scr[first : first + half, :WIDTH] = p_ref[:half, :]
    block_scr[first : first + half, WIDTH:] = p_ref[half:, :]
    first = first + half
    downs = down_ref[ranks, :]
    block_scr[first : first + rank_part // 2, :WIDTH] = downs[: rank_part // 2]
    block_scr[first : first + rank_part // 2, WIDTH:] = downs[rank_part // 2 :]
    zero_scr[...] = jnp.zeros_like(zero_scr)
    vec_out[col, 0:4, :] = conv_ref[...]
    vec_out[col, 4:5, :] = bias_ref[...]
    vec_out[col, 5:6, :] = gate_ref[...]
    vec_out[col, 6:7, :] = widen(skip_ref[...])
    lane = iota((1, WIDTH), 1)
    scalars = jnp.zeros((1, WIDTH), F32)
    for h in range(QUAD):
        scalars = jnp.where(lane == h, step_ref[:, h : h + 1], scalars)
        scalars = jnp.where(lane == QUAD + h, rate_ref[:, h : h + 1], scalars)
    vec_out[col, 7:8, :] = scalars
    gain_out[row] = gain_ref[...]
    pl.semaphore_wait(barrier, row_count + col_count - 2)

    def remote(source, target, sends, recvs, index, device):
        return pltpu.make_async_remote_copy(
            src_ref=source, dst_ref=target, send_sem=sends.at[index], recv_sem=recvs.at[index],
            device_id=device, device_id_type=MESH,
        )

    own_block = pltpu.make_async_copy(block_scr, w_out.at[col, row], own_sem.at[0])
    own_block.start()

    def whole_window(target, slot, index, peer):
        source = x_ref.at[pl.ds(pl.multiple_of(target * chunk - HALO, HALO), chunk + HALO)]
        return remote(source, x_out.at[slot], row_send, row_recv, index, on_row(peer))

    def first_window(slot, index, peer):
        source = x_ref.at[pl.ds(0, chunk)]
        return remote(source, x_out.at[slot, pl.ds(HALO, chunk)], row_send, row_recv, index, on_row(peer))

    def each_window(sending, act):
        for d in range(1, row_count):
            peer = lax.rem(row + d, row_count)
            chosen = peer if sending else row
            slot = row if sending else lax.rem(row + row_count - d, row_count)

            @pl.when(chosen > 0)
            def _():
                act(whole_window(jnp.maximum(chosen, 1), slot, d, peer))

            @pl.when(chosen == 0)
            def _():
                act(first_window(slot, d, peer))

    @pl.when(row > 0)
    def _():
        source = x_ref.at[pl.ds(pl.multiple_of(jnp.maximum(row, 1) * chunk - HALO, HALO), chunk + HALO)]
        pltpu.make_async_copy(source, x_out.at[row], own_sem.at[1]).start()

    @pl.when(row == 0)
    def _():
        pltpu.make_async_copy(x_ref.at[pl.ds(0, chunk)], x_out.at[row, pl.ds(HALO, chunk)], own_sem.at[1]).start()
        for r in range(row_count):
            pltpu.make_async_copy(zero_scr, x_out.at[r, pl.ds(0, HALO)], own_sem.at[3 + r]).start()

    own_shared = pltpu.make_async_copy(shared_ref, shared_out.at[row], own_sem.at[2])
    own_shared.start()
    small = []
    for d in range(1, col_count):
        peer = lax.rem(col + d, col_count)
        small.append(remote(vec_out.at[col], vec_out.at[col], col_send, col_recv, d, on_col(peer)))
    for d in range(1, row_count):
        peer = lax.rem(row + d, row_count)
        small.append(remote(shared_ref, shared_out.at[row], row_send, row_recv, row_count + d, on_row(peer)))
        small.append(
            remote(gain_out.at[row], gain_out.at[row], row_send, row_recv, 2 * row_count + d, on_row(peer))
        )
    for copy in small:
        copy.start()

    cut = (w_out.shape[2] * 60 // 100 + 8) // 16 * 16
    spans = (pl.ds(0, cut), pl.ds(cut, w_out.shape[2] - cut))
    has_up = high < high_count - 1
    has_down = high > 0
    routes = {
        "up": (0, has_up, on_col(lax.rem(col + 2, col_count))),
        "down": (1, has_down, on_col(lax.rem(col + col_count - 2, col_count))),
        "x": (2, None, on_col(side)),
        "y": (3, None, on_row(across)),
        "core": (4, None, on_row(core)),
    }

    def piece(section, c, r, kind, device):
        ref = w_out.at[c, r, spans[section]]
        return pltpu.make_async_remote_copy(
            src_ref=ref, dst_ref=ref, send_sem=send_sem.at[section, c, r, kind],
            recv_sem=recv_sem.at[section, c, r], device_id=device, device_id_type=MESH,
        )

    def event(starting, section, c, r, names, arrives=True, valid=None):
        def act():
            if starting and arrives:
                piece(section, c, r, 4, on_row(core)).wait_recv()
            for name in names:
                kind, allowed, device = routes[name]
                copy = piece(section, c, r, kind, device)
                if allowed is None:
                    copy.start() if starting else copy.wait_send()
                else:

                    @pl.when(allowed)
                    def _():
                        copy.start() if starting else copy.wait_send()

        if valid is None:
            act()
        else:
            pl.when(valid)(act)

    def far(column, step, distance):
        return lax.rem(column + step * distance + 4 * col_count, col_count)

    def within(step, distance):
        return high >= distance if step < 0 else high + distance < high_count

    onward = {-2: "up", 2: "down"}

    def along(starting, section, distance):
        for step in (-2, 2):
            valid = within(step, distance)
            if section == 0:
                names = (onward[step], "y", "x", "core")
                event(starting, 0, far(col, step, distance), row, names, valid=valid)
            else:
                for column, r in ((col, row), (side, row), (col, across), (side, across)):
                    event(starting, 1, far(column, step, distance), r, (onward[step], "core"), valid=valid)

    def over(starting, distance):
        for step in (-2, 2):
            valid = within(step, distance)
            event(starting, 0, far(side, step, distance), row, ("core",), valid=valid)
            event(starting, 0, far(col, step, distance), across, ("x", "core"), valid=valid)

    def last(starting, distance):
        for step in (-2, 2):
            event(starting, 0, far(side, step, distance), across, ("core",), valid=within(step, distance))

    def relay(starting):
        event(starting, 1, col, row, ("x", "y"), arrives=False)
        event(starting, 0, col, row, ("up", "down", "y", "x"), arrives=False)
        event(starting, 1, col, row, ("up", "down", "core"), arrives=False)
        event(starting, 0, col, row, ("core",), arrives=False)
        event(starting, 1, side, row, ("y", "up", "down", "core"))
        event(starting, 1, col, across, ("up", "down", "core"))
        along(starting, 0, 1)
        event(starting, 1, side, across, ("up", "down", "core"))
        if starting:
            each_window(True, lambda copy: copy.start())
        event(starting, 0, col, across, ("x", "core"))
        for d in range(2, high_count):
            along(starting, 0, d)
            along(starting, 1, d - 1)
            if d == 2:
                event(starting, 0, side, row, ("core",))
                over(starting, 1)
                event(starting, 0, side, across, ("core",))
            else:
                over(starting, d - 1)
                last(starting, d - 2)
        along(starting, 1, high_count - 1)
        over(starting, high_count - 1)
        if high_count > 2:
            last(starting, high_count - 2)
        last(starting, high_count - 1)

    own_block.wait()
    relay(True)
    for copy in small:
        copy.wait()
    lane = iota((1, LANES), 1) < QUAD
    steps = jnp.zeros((1, LANES), F32)
    rates = jnp.zeros((1, LANES), F32)
    for c in range(col_count):
        values = vec_out[c, 7:8, :LANES]
        steps = steps + pltpu.roll(jnp.where(lane, values, 0.0), (QUAD * c) % LANES, 1)
        values = pltpu.roll(values, LANES - QUAD, 1)
        rates = rates + pltpu.roll(jnp.where(lane, values, 0.0), (QUAD * c) % LANES, 1)
    head_out[...] = jnp.concatenate([steps, rates, jnp.zeros((6, LANES), F32)], axis=0)
    own_shared.wait()
    each_window(True, lambda copy: copy.wait_send())
    each_window(False, lambda copy: copy.wait_recv())

    @pl.when(row > 0)
    def _():
        source = x_ref.at[pl.ds(0, chunk + HALO)]
        pltpu.make_async_copy(source, x_out.at[row], own_sem.at[1]).wait()

    @pl.when(row == 0)
    def _():
        pltpu.make_async_copy(x_ref.at[pl.ds(0, chunk)], x_out.at[row, pl.ds(HALO, chunk)], own_sem.at[1]).wait()
        for r in range(row_count):
            pltpu.make_async_copy(zero_scr, x_out.at[r, pl.ds(0, HALO)], own_sem.at[3 + r]).wait()

    core_across = lax.rem(core + 2, row_count)
    for c in range(col_count):
        for r in (core, core_across):
            for section in range(2):
                piece(section, c, r, 4, on_row(core)).wait_recv()
    relay(False)


def start_exchange(x, w, up, p, down, shared, vectors, row_count, col_count):
    part = x.shape[1]
    rank_part = up.shape[0] // row_count
    block_rows = part + rank_part + WIDTH // 2 + rank_part // 2
    chunk = x.shape[0] // row_count
    vmem = pl.BlockSpec(memory_space=pltpu.VMEM)
    anywhere = pl.BlockSpec(memory_space=pl.ANY)
    dma = pltpu.SemaphoreType.DMA
    return pl.pallas_call(
        start_kernel,
        in_specs=[anywhere] + [vmem] * (5 + len(vectors)),
        out_specs=[anywhere] * 3 + [vmem] * 3,
        out_shape=[
            jax.ShapeDtypeStruct((row_count, chunk + HALO, part), BF16),
            jax.ShapeDtypeStruct((col_count, row_count, block_rows, 2 * WIDTH), BF16),
            jax.ShapeDtypeStruct((row_count,) + shared.shape, BF16),
            jax.ShapeDtypeStruct((row_count, 1, part), F32),
            jax.ShapeDtypeStruct((col_count, 8, WIDTH), F32),
            jax.ShapeDtypeStruct((8, LANES), F32),
        ],
        scratch_shapes=[
            pltpu.VMEM((block_rows, 2 * WIDTH), BF16), pltpu.VMEM((HALO, part), BF16),
            dma((3 + row_count,)), dma((2, col_count, row_count, 5)), dma((2, col_count, row_count)),
            dma((3 * row_count,)), dma((3 * row_count,)), dma((col_count,)), dma((col_count,)),
        ],
        compiler_params=pltpu.CompilerParams(
            collective_id=1, has_side_effects=True, vmem_limit_bytes=VMEM_BYTES
        ),
    )(x, w, up, p, down, shared, *vectors)


def finish_exchange(corr, wide, thin):
    row_count = corr.shape[0]
    col_count = wide.shape[1]
    share, width = wide.shape[2:]
    vmem = pl.BlockSpec(memory_space=pltpu.VMEM)
    anywhere = pl.BlockSpec(memory_space=pl.ANY)
    dma = pltpu.SemaphoreType.DMA
    return pl.pallas_call(
        tail_kernel,
        in_specs=[anywhere, vmem, vmem],
        out_specs=[anywhere, vmem, vmem],
        out_shape=[
            jax.ShapeDtypeStruct(corr.shape, corr.dtype),
            jax.ShapeDtypeStruct((row_count, col_count, share, width), F32),
            jax.ShapeDtypeStruct((col_count,) + thin.shape[1:], F32),
        ],
        scratch_shapes=[
            pltpu.VMEM(wide.shape, F32), pltpu.VMEM(thin.shape, F32), pltpu.VMEM(wide.shape[1:], F32),
            pltpu.VMEM(thin.shape[1:], F32), pltpu.VMEM(wide.shape[1:], F32),
            dma((1,)), dma((row_count,)), dma((row_count,)), dma((2 * row_count,)), dma((2 * row_count,)),
            dma((2 * col_count,)), dma((2 * col_count,)), dma((row_count,)), dma((row_count,)),
        ],
        compiler_params=pltpu.CompilerParams(
            collective_id=0, has_side_effects=True, vmem_limit_bytes=VMEM_BYTES
        ),
    )(corr, wide, thin)


def whole_spec(shape):
    return pl.BlockSpec(shape, lambda c: (0,) * len(shape))


def lead_spec(shape):
    return pl.BlockSpec((1,) + tuple(shape[1:]), lambda c: (c,) + (0,) * (len(shape) - 1))


def lane_spec(shape):
    block = tuple(shape[:-1]) + (WIDTH,)
    return pl.BlockSpec(block, lambda c: (0,) * (len(shape) - 1) + (c,))


def second_spec(shape):
    block = (shape[0], 1) + tuple(shape[2:])
    return pl.BlockSpec(block, lambda c: (0, c) + (0,) * (len(shape) - 2))


def front_spec(shape):
    if shape[2] % 3 == 0 and shape[2] // 3 * 2 >= WIDTH and shape[3] == 2 * WIDTH and shape[1] == 4:
        return pl.BlockSpec((1, shape[1], shape[2] // 3 * 2, shape[3]), lambda c: (c, 0, 0, 0))
    return lead_spec(shape)


def back_spec(shape):
    if shape[2] > WIDTH:
        return pl.BlockSpec((1, shape[1], shape[2] // 3, shape[3]), lambda c: (c, 0, 2, 0))
    return lead_spec(shape)


KINDS = {"w": front_spec, "p": back_spec, "s": second_spec, "a": whole_spec, "c": lead_spec, "l": lane_spec}


def grouped_call(kernel, inputs, kinds, outputs, out_kinds, scratch, flops=0):
    return pl.pallas_call(
        kernel,
        grid=(GROUPS,),
        in_specs=[KINDS[kind](value.shape) for kind, value in zip(kinds, inputs)],
        out_specs=[KINDS[kind](shape) for kind, (shape, _) in zip(out_kinds, outputs)],
        out_shape=[jax.ShapeDtypeStruct(shape, dtype) for shape, dtype in outputs],
        scratch_shapes=[pltpu.VMEM(shape, dtype) for shape, dtype in scratch],
        compiler_params=pltpu.CompilerParams(vmem_limit_bytes=VMEM_BYTES),
        cost_estimate=pl.CostEstimate(flops=flops, bytes_accessed=40_000_000, transcendentals=0),
    )(*inputs)


def to_groups(value, heads_here):
    cols = value.shape[0]
    middle = value.shape[1:-1]
    if heads_here == QUAD:
        return value
    if heads_here > QUAD:
        parts = heads_here // QUAD
        value = value.reshape((cols,) + middle + (parts, WIDTH))
        value = jnp.moveaxis(value, -2, 1)
        return value.reshape((GROUPS,) + middle + (WIDTH,))
    parts = QUAD // heads_here
    value = value.reshape((GROUPS, parts) + middle + (heads_here * P_SIZE,))
    value = jnp.moveaxis(value, 1, -2)
    return value.reshape((GROUPS,) + middle + (WIDTH,))


def to_cols(value, heads_here, col_count):
    middle = value.shape[1:-1]
    if heads_here == QUAD:
        return value
    if heads_here > QUAD:
        parts = heads_here // QUAD
        value = value.reshape((col_count, parts) + middle + (WIDTH,))
        value = jnp.moveaxis(value, 1, -2)
        return value.reshape((col_count,) + middle + (heads_here * P_SIZE,))
    parts = QUAD // heads_here
    value = value.reshape((GROUPS,) + middle + (parts, heads_here * P_SIZE))
    value = jnp.moveaxis(value, -2, 1)
    return value.reshape((col_count,) + middle + (heads_here * P_SIZE,))


def pad_lanes(value, width):
    return jnp.pad(value, [(0, 0)] * (value.ndim - 1) + [(0, width - value.shape[-1])])


def carry_in(state, decay, row_count, col_count, seq_cols, forward):
    row = lax.axis_index("row")
    col = lax.axis_index("col")
    total = state
    factor = decay
    before = jnp.zeros(state.shape, F32)
    reach = jnp.ones_like(decay)
    span = 1
    while span < row_count:
        pairs = [(i, i ^ span) for i in range(row_count)]
        other = lax.ppermute(total, "row", pairs).astype(F32)
        other_factor = lax.ppermute(factor, "row", pairs)
        behind = ((row & span) != 0) == forward
        mine = total.astype(F32)
        before = jnp.where(behind, before + reach * other, before)
        reach = jnp.where(behind, reach * other_factor, reach)
        joined = jnp.where(behind, other * factor + mine, mine * other_factor + other)
        total = joined.astype(BF16)
        factor = factor * other_factor
        span *= 2
    place = lax.rem(col, seq_cols)
    for hop in range(1, seq_cols):
        shift = hop if forward else -hop
        pairs = [(i, (i + shift) % col_count) for i in range(col_count)]
        other = lax.ppermute(total, "col", pairs).astype(F32)
        other_factor = lax.ppermute(factor, "col", pairs)
        inside = place >= hop if forward else place < seq_cols - hop
        before = jnp.where(inside, before + reach * other, before)
        reach = jnp.where(inside, reach * other_factor, reach)
    return before


def rows_to_parts(value):
    row_count = value.shape[0]
    row = lax.axis_index("row")
    result = value
    for d in range(1, row_count):
        peer = lax.rem(row + d, row_count)
        pairs = [(i, (i + d) % row_count) for i in range(row_count)]
        piece = lax.ppermute(lax.dynamic_index_in_dim(value, peer), "row", pairs)
        source = lax.rem(row + row_count - d, row_count)
        result = lax.dynamic_update_slice_in_dim(result, piece, source, 0)
    return result


def per_device(
    block_in, norm_gain, proj_inner, proj_state, conv_inner, conv_inner_bias, conv_state, conv_state_bias,
    step_bias, decay_log, skip_gain, gate_gain, proj_out, adapt_in_down, adapt_in_up, adapt_out_down,
    adapt_out_up, adapter_id, cotangent,
):
    row_count = lax.axis_size("row")
    col_count = lax.axis_size("col")
    row = lax.axis_index("row")
    col = lax.axis_index("col")
    col_tokens, part = block_in.shape
    chunk = col_tokens // row_count
    total_rows = chunk + HALO
    blocks = chunk // BLOCK
    seq_cols = SEQ // col_tokens
    heads_here = proj_inner.shape[1]
    local = heads_here * P_SIZE
    rank_total = adapt_in_down.shape[1]
    rank_part = rank_total // row_count
    rank_share = rank_total // col_count
    adapter = lax.dynamic_index_in_dim(adapter_id, col // seq_cols, keepdims=False)

    in_down = lax.dynamic_slice_in_dim(adapt_in_down, adapter * RANK, RANK, 1)
    out_up = lax.dynamic_slice_in_dim(adapt_out_up, adapter * RANK, RANK, 1)
    shared = pad_lanes(jnp.concatenate([proj_state, in_down, out_up], axis=1), 384)
    relayed = row_count == 4 and heads_here == QUAD and seq_cols == 1 and part == WIDTH
    if relayed:
        x_rows, w_all, w_state, gain_all, vectors, head_rows = start_exchange(
            block_in, proj_inner.reshape(part, 2 * local), adapt_in_up.reshape(rank_total, 2 * local), proj_out,
            adapt_out_down, shared,
            (
                norm_gain[None], conv_inner, conv_inner_bias[None], gate_gain[None], step_bias[None],
                decay_log[None], skip_gain[None],
            ),
            row_count, col_count,
        )
        per_part = rank_part // RANK
        source = adapter // per_part
        place = lax.rem(adapter, per_part)
        zero = jnp.int32(0)
        up_all = lax.dynamic_slice(
            w_all, (zero, source, part + place * RANK, zero), (GROUPS, 1, RANK, 2 * WIDTH)
        )[:, 0]
        down_all = lax.dynamic_slice(
            w_all, (zero, source, jnp.int32(part + rank_part + WIDTH // 2), place * WIDTH), (GROUPS, 1, RANK, WIDTH)
        )[:, 0]
        p_all = w_all
        g_rows = lax.all_to_all(cotangent.reshape(row_count, chunk, part), "row", 0, 0, tiled=True)
    else:
        head = jnp.zeros((HALO, part), BF16)
        if seq_cols > 1:
            pairs = [(i, (i + 1) % col_count) for i in range(col_count)]
            head = lax.ppermute(block_in[-HALO:], "col", pairs)
            head = jnp.where(lax.rem(col, seq_cols) > 0, head, jnp.zeros_like(head))
        padded = jnp.concatenate([head, block_in], axis=0)
        windows = jnp.stack([padded[r * chunk : r * chunk + total_rows] for r in range(row_count)])
        x_rows = lax.all_to_all(windows, "row", 0, 0, tiled=True)
        g_rows = lax.all_to_all(cotangent.reshape(row_count, chunk, part), "row", 0, 0, tiled=True)

        def split_pairs(value):
            value = value.reshape(value.shape[0], heads_here, 2, P_SIZE)
            return jnp.swapaxes(value, 1, 2).reshape(value.shape[0], 2, local)

        up_part = lax.dynamic_slice_in_dim(adapt_in_up, row * rank_part, rank_part, 0)
        w_block = jnp.concatenate([split_pairs(proj_inner), split_pairs(up_part)], axis=0)
        w_all = lax.all_gather(w_block.reshape(part + rank_part, 2 * local), ("col", "row"))
        w_all = w_all.reshape(col_count, row_count, part + rank_part, 2, local)
        w_all = to_groups(w_all, heads_here).reshape(GROUPS, row_count, part + rank_part, 2 * WIDTH)
        up_all = w_all[:, :, part:, :].reshape(GROUPS, rank_total, 2 * WIDTH)
        up_all = lax.dynamic_slice_in_dim(up_all, adapter * RANK, RANK, 1)

        down_part = lax.dynamic_slice_in_dim(adapt_out_down, row * rank_part, rank_part, 0)
        p_block = jnp.concatenate([proj_out, down_part.T], axis=1)
        p_all = lax.all_gather(p_block, ("col", "row")).reshape(col_count, row_count, local, part + rank_part)
        if heads_here != QUAD:
            p_all = jnp.moveaxis(p_all, 1, 0).reshape(row_count, GROUPS, WIDTH, part + rank_part)
            p_all = jnp.moveaxis(p_all, 0, 1)
        down_all = jnp.swapaxes(p_all[..., part:], 1, 2).reshape(GROUPS, WIDTH, rank_total)
        down_all = jnp.swapaxes(lax.dynamic_slice_in_dim(down_all, adapter * RANK, RANK, 2), 1, 2)

        w_state = lax.all_gather(shared, "row")
        gain_all = lax.all_gather(norm_gain, "row").reshape(row_count, 1, part)

        scalars = jnp.concatenate([step_bias, decay_log, skip_gain])
        vectors = jnp.concatenate(
            [conv_inner, conv_inner_bias[None], gate_gain[None], pad_lanes(scalars, local)[None]], axis=0
        )
        vectors = lax.all_gather(vectors, "col")
        scalars = vectors[:, 6, : 3 * heads_here].reshape(col_count, 3, heads_here)
        scalars = jnp.swapaxes(scalars, 0, 1).reshape(3, HEADS)
        head_rows = jnp.pad(scalars[:2], ((0, 6), (0, LANES - HEADS)))
        skip_wide = jnp.repeat(scalars[2], P_SIZE).reshape(GROUPS, 1, WIDTH)
        vectors = jnp.concatenate(
            [to_groups(vectors[:, :6], heads_here), skip_wide, jnp.zeros_like(skip_wide)], axis=1
        )
    up_all = jnp.pad(up_all, ((0, 0), (IN_LANE, LANES - IN_LANE - RANK), (0, 0)))
    down_all = jnp.pad(down_all, ((0, 0), (OUT_LANE, LANES - OUT_LANE - RANK), (0, 0)))
    state_taps = jnp.concatenate([conv_state, conv_state_bias[None], jnp.zeros((3, 256), F32)], axis=0)

    token_f32 = ((chunk, LANES), F32)
    token_low = ((chunk, LANES), BF16)
    inner_low = ((chunk, DI), BF16)
    states = ((blocks, STATES, DI), F32)
    score_box = ((blocks, BLOCK, BLOCK), F32)
    turned = ((blocks, STATES, BLOCK), BF16)
    (
        normed, scpre, raw, step, cum, cum_t, bs, cs, cs_t, adv, gate, u, eloc, fin, dec,
    ) = grouped_call(
        front_kernel,
        (x_rows, gain_all, w_state, state_taps, head_rows, w_all, up_all, vectors),
        "aaaaawcc",
        [
            ((total_rows, D), BF16), ((chunk, 256), F32), token_f32, token_f32, token_f32,
            ((GROUPS, QUAD, chunk), F32), token_low, token_low, turned, ((total_rows, LANES), BF16),
            inner_low, inner_low, states, ((STATES, DI), BF16), ((8, DI), F32),
        ],
        "aaaaaaaaaalllll",
        [((total_rows, 384), F32), turned, ((total_rows, WIDTH), F32)],
        flops=int(45e9),
    )
    decay = dec[0:1]
    entry = carry_in(fin, decay, row_count, col_count, seq_cols, True)
    out_rows, o, ent, aux, side_grad, out_up_grad = grouped_call(
        scan_kernel,
        (x_rows, g_rows, w_state, p_all, down_all, vectors, gate, u, eloc, entry, step, cum, cum_t, bs, cs),
        "aaapccllllaacaa",
        [
            ((row_count, chunk, part), BF16), inner_low, ((blocks, STATES, DI), BF16), token_f32, token_low,
            ((RANK, D), F32),
        ],
        "allaaa",
        [score_box, ((chunk, D), F32), token_f32, token_f32],
        flops=int(45e9),
    )
    block_out = rows_to_parts(out_rows).reshape(col_tokens, part)
    dgate, dy, gloc, gfin, out_down_grad = grouped_call(
        gate_kernel,
        (g_rows, p_all, side_grad, down_all, vectors, gate, o, aux, cum, cs_t),
        "apaccllaaa",
        [inner_low, inner_low, states, ((STATES, DI), BF16), ((GROUPS, RANK, WIDTH), F32)],
        "llllc",
        [((blocks, RANK, BLOCK), BF16)],
        flops=int(25e9),
    )
    exit_grad = carry_in(gfin, decay, row_count, col_count, seq_cols, False)
    corr, wide, thin = grouped_call(
        back_kernel,
        (
            x_rows, gain_all, normed, w_state, w_all, up_all, adv, vectors, state_taps, head_rows,
            u, o, dy, dgate, ent, gloc, exit_grad, step, cum, cum_t, raw, scpre, bs, cs,
            out_down_grad, out_up_grad,
        ),
        "aaaawcacaalllllllaacaaaaca",
        [
            ((row_count, total_rows, part), BF16), ((row_count, GROUPS, RANK // row_count, 3 * WIDTH), F32),
            ((row_count, 2 * RANK, part), F32),
        ],
        "asa",
        [
            score_box, score_box, token_f32, token_f32, token_f32, token_f32, ((blocks, 8, LANES), F32),
            ((total_rows + HALO, WIDTH), F32), ((total_rows, 2 * WIDTH), BF16), ((total_rows, D), F32),
            ((total_rows, LANES), F32), ((blocks, RANK, BLOCK), BF16),
            ((RANK, 2 * WIDTH), F32), ((RANK, D), F32),
        ],
        flops=int(75e9),
    )

    if heads_here != QUAD:
        share = RANK // row_count
        wide = jnp.swapaxes(wide.reshape(row_count, GROUPS, share, 3, WIDTH), 0, 1)
        wide = to_cols(wide, heads_here, col_count)
        wide = jnp.swapaxes(wide, 0, 1).reshape(row_count, col_count, share, 3 * local)
    corr, wide, thin = finish_exchange(corr, wide, thin)
    input_grad = cotangent.astype(F32) + corr[:, HALO:].reshape(col_tokens, part).astype(F32)
    early = corr[:, :HALO].astype(F32)
    for r in range(1, row_count):
        input_grad = input_grad.at[r * chunk - HALO : r * chunk].add(early[r])
    if seq_cols > 1:
        pairs = [(i, (i - 1) % col_count) for i in range(col_count)]
        late = lax.ppermute(corr[0, :HALO], "col", pairs).astype(F32)
        late = jnp.where(lax.rem(col, seq_cols) < seq_cols - 1, late, jnp.zeros_like(late))
        input_grad = input_grad.at[-HALO:].add(late)
    wide = jnp.swapaxes(wide, 0, 1).reshape(col_count, RANK, 3 * local)
    owner = jnp.repeat(adapter_id, seq_cols)
    adapters = rank_total // RANK
    chosen = owner[:, None] == jnp.arange(adapters, dtype=jnp.int32)[None, :]
    wide = jnp.sum(jnp.where(chosen[:, :, None, None], wide[:, None], 0.0), axis=0)
    wide = wide.reshape(rank_total, 3 * local)
    in_up = wide[:, : 2 * local].reshape(rank_total, 2, heads_here, P_SIZE)
    in_up = jnp.swapaxes(in_up, 1, 2).reshape(rank_total, heads_here, 2 * P_SIZE)
    out_down = wide[:, 2 * local :]
    thin = jnp.sum(jnp.where(chosen[:, :, None, None], thin[:, None], 0.0), axis=0)
    thin = thin.reshape(adapters, 2, RANK, part)
    thin = jnp.transpose(thin, (1, 3, 0, 2)).reshape(2, part, rank_total)
    thin = lax.dynamic_slice_in_dim(thin, col * rank_share, rank_share, 2)
    return block_out, input_grad, thin[0], in_up, out_down, thin[1]


def solution(mesh):
    placed = (
        P("col", "row"), P("row"), P("row", "col", None), P("row", None), P(None, "col"), P("col"), P(), P(),
        P("col"), P("col"), P("col"), P("col"), P("col", "row"), P("row", None), P(None, "col", None),
        P(None, "col"), P("row", None), P(), P("col", "row"),
    )
    return jax.shard_map(
        per_device,
        mesh=mesh,
        in_specs=placed,
        out_specs=(
            P("col", "row"), P("col", "row"), P("row", "col"), P(None, "col", None), P(None, "col"),
            P("row", "col"),
        ),
        check_vma=False,
    )
```

```python
import functools

import jax
import jax.numpy as jnp
from jax import lax
from jax.experimental import pallas as pl
from jax.experimental.pallas import tpu as pltpu
from jax.sharding import PartitionSpec as P

D = 1024
HEADS = 32
P_SIZE = 64
STATES = 128
BLOCK = 256
RANK = 16
SEQ = 4096
DI = 2048
EPS = 1e-05
LOG2E = 1.4426950408889634

HALO = 16
IN_LANE = 32
OUT_LANE = 48
CAP = 80.0
QUAD = 4
WIDTH = QUAD * P_SIZE
GROUPS = HEADS // QUAD
LANES = 128
VMEM_BYTES = 60 * 1024 * 1024
F32 = jnp.float32
BF16 = jnp.bfloat16
MESH = pl.DeviceIdType.MESH


def mm(left, right):
    return jnp.dot(left, right, preferred_element_type=F32)


def mm_nt(left, right):
    return lax.dot_general(left, right, (((1,), (1,)), ((), ())), preferred_element_type=F32)


def mm_tn(left, right):
    return lax.dot_general(left, right, (((0,), (0,)), ((), ())), preferred_element_type=F32)


def split_left(ones, value):
    high = value.astype(BF16)
    rest = value - high.astype(F32)
    middle = rest.astype(BF16)
    low = (rest - middle.astype(F32)).astype(BF16)
    return mm(ones, high) + mm(ones, middle) + mm(ones, low)


def split_right(value, ones):
    high = value.astype(BF16)
    low = (value - high.astype(F32)).astype(BF16)
    return mm(high, ones) + mm(low, ones)


def sigmoid(value):
    return 0.5 * jnp.tanh(0.5 * value) + 0.5


def iota(shape, axis):
    return lax.broadcasted_iota(jnp.int32, shape, axis)


def widen(cols):
    lane = iota((cols.shape[0], LANES), 1) < P_SIZE
    left = jnp.where(lane, cols[:, 0:1], cols[:, 1:2])
    right = jnp.where(lane, cols[:, 2:3], cols[:, 3:4])
    return jnp.concatenate([left, right], axis=1)


def to_front(cols, group):
    return pltpu.roll(cols, lax.rem(LANES - QUAD * group, LANES), 1)


def lane_range(values, first):
    lane = iota(values.shape, 1)
    return jnp.where((lane >= first) & (lane < first + RANK), values, 0.0)


def out_block(w_ref, group, row, part):
    if w_ref.shape[2] == WIDTH:
        return w_ref[group, row, :, :part]
    rows = WIDTH // 2
    return jnp.concatenate([w_ref[group, row, :rows, :part], w_ref[group, row, :rows, part:]], axis=0)


def head_only(values, head):
    lane = iota(values.shape, 1) // P_SIZE
    return jnp.where(lane == head, values, jnp.zeros_like(values))


def delays(window, taps, bias):
    total = window[8:] * taps[0:1] + bias
    for k in range(1, 4):
        total = total + pltpu.roll(window, k, 0)[8:] * taps[k : k + 1]
    return total


def advances(window, taps, count):
    length = window.shape[0]
    total = window[:count] * taps[0:1]
    for k in range(1, 4):
        total = total + pltpu.roll(window, length - k, 0)[:count] * taps[k : k + 1]
    return total


def at_block(k):
    if isinstance(k, int):
        return pl.ds(k * BLOCK, BLOCK)
    return pl.ds(pl.multiple_of(k * BLOCK, BLOCK), BLOCK)


def at_rows(k):
    if isinstance(k, int):
        return pl.ds(HALO + k * BLOCK, BLOCK)
    return pl.ds(pl.multiple_of(HALO + k * BLOCK, HALO), BLOCK)


def with_halo(k):
    if k == 0:
        return pl.ds(0, HALO + BLOCK)
    return pl.ds(HALO + k * BLOCK, BLOCK)


def padded_rows(value, first):
    before = jnp.zeros((first, value.shape[1]), value.dtype)
    after = jnp.zeros((LANES - first - value.shape[0], value.shape[1]), value.dtype)
    return jnp.concatenate([before, value, after], axis=0)


def front_kernel(
    place_ref, x_ref, gain_ref, wst_ref, sp_ref, hp_ref, w_ref, up_ref, vp_ref,
    normed_ref, scpre_ref, ratio_ref, sig_ref, cum_ref, lead_ref, turned_ref, bs_ref, cs_ref, cs_t_ref, adv_ref,
    gate_ref, u_ref, eloc_ref, fin_ref, dec_ref,
    st_scr, bs_t_scr, val_scr,
):
    group = pl.program_id(0)
    row_count, _, part = x_ref.shape
    blocks = eloc_ref.shape[0]

    @pl.when(group == 0)
    def _():
        def project(rows):
            pieces = [x_ref[r, rows, :].astype(F32) for r in range(row_count)]
            square = sum(jnp.sum(piece * piece, axis=1, keepdims=True) for piece in pieces)
            inv = lax.rsqrt(square / D + EPS)
            total = None
            for r in range(row_count):
                normed = (pieces[r] * inv * gain_ref[r]).astype(BF16)
                normed_ref[rows, r * part : (r + 1) * part] = normed
                term = mm(normed, wst_ref[r])
                total = term if total is None else total + term
            st_scr[rows, :] = total
            adv_ref[rows, :] = lane_range(total[:, 256:384], IN_LANE).astype(BF16)

        project(pl.ds(0, HALO))

        @pl.loop(0, blocks)
        def _(k):
            project(at_rows(k))

        lower = (iota((BLOCK, BLOCK), 0) >= iota((BLOCK, BLOCK), 1)).astype(BF16)
        rate = -jnp.exp(hp_ref[1:2]) * LOG2E

        @pl.loop(0, blocks)
        def _(k):
            window = st_scr[pl.ds(pl.multiple_of(8 + k * BLOCK, 8), BLOCK + 8), :256]
            pre = delays(window, sp_ref[0:4], sp_ref[4:5])
            conv = pre * sigmoid(pre)
            b_rows = conv[:, :STATES].astype(BF16)
            c_rows = conv[:, STATES:].astype(BF16)
            scpre_ref[at_block(k), :] = pre
            bs_ref[at_block(k), :] = b_rows
            cs_ref[at_block(k), :] = c_rows
            bs_t_scr[k] = conv[:, :STATES].T.astype(BF16)
            cs_t_ref[k] = conv[:, STATES:].T.astype(BF16)
            raw = st_scr[at_rows(k), 256:384] + hp_ref[0:1]
            small = jnp.exp(-jnp.abs(raw))
            tail = jnp.where(
                small < 0.01, small * (1.0 - small * (0.5 - small * (1.0 / 3.0))), jnp.log(1.0 + small)
            )
            step = jnp.maximum(raw, 0.0) + tail
            cum = split_left(lower, step * rate)
            sig = sigmoid(raw)
            ratio_ref[at_block(k), :] = jnp.where(raw < -20.0, 1.0, sig / jnp.maximum(step, 1e-30))
            sig_ref[at_block(k), :] = sig
            lead = jnp.log(jnp.maximum(step, 1e-37)) * LOG2E - cum
            cum_ref[at_block(k), :] = cum
            lead_ref[at_block(k), :] = lead
            flipped = cum.T
            flipped_lead = lead.T
            for g in range(GROUPS):
                turned_ref[g, :QUAD, at_block(k)] = flipped[g * QUAD : (g + 1) * QUAD]
                turned_ref[g, QUAD:, at_block(k)] = flipped_lead[g * QUAD : (g + 1) * QUAD]

    up_rows = padded_rows(up_ref[0, 0], IN_LANE)

    def inner(rows):
        total = mm(adv_ref[rows, :], up_rows)
        for r in range(row_count):
            total = total + mm(normed_ref[rows, r * part : (r + 1) * part], w_ref[0, r, :part, :])
        return total

    taps = vp_ref[0]

    def one_block(k, carry):
        state, decay = carry
        product = inner(with_halo(k))
        skip = HALO if k == 0 else 0
        gate_ref[at_block(k), :] = product[skip:, :WIDTH].astype(BF16)
        val_scr[with_halo(k), :] = product[:, WIDTH:]
        window = val_scr[pl.ds(8 + k * BLOCK, BLOCK + 8), :]
        pre = delays(window, taps[0:4], taps[4:5])
        u_ref[at_block(k), :] = pre.astype(BF16)
        xs = (pre * sigmoid(pre)).astype(BF16).astype(F32)
        cum = cum_ref[at_block(k), :]
        last = cum[BLOCK - 1 : BLOCK]
        weight = to_front(jnp.exp2(last + lead_ref[at_block(k), :]), group)
        weighted = (xs * widen(weight)).astype(BF16)
        eloc_ref[k] = state.astype(BF16)
        last8 = to_front(jnp.broadcast_to(last, (8, LANES)), group)
        fall = widen(jnp.exp2(last8))[0:1]
        return fall * state + mm(bs_t_scr[k], weighted), decay * fall

    carry = (jnp.zeros((STATES, WIDTH), F32), jnp.ones((1, WIDTH), F32))
    for k in range(blocks):
        carry = one_block(k, carry)
    state, decay = carry
    fin_ref[...] = state.astype(BF16)
    dec_ref[...] = jnp.broadcast_to(decay, (8, WIDTH))


def scan_kernel(
    place_ref, x_ref, g_ref, wst_ref, w_ref, down_ref, vp_ref, gate_ref, u_ref, eloc_ref, ein_ref,
    cum_ref, turned_ref, bs_ref, cs_ref,
    out_ref, o_ref, ent_ref, aux_ref, sg_ref, gup_ref,
    score_scr, gained_scr, side_scr, square_scr,
):
    group = pl.program_id(0)
    row_count, _, part = x_ref.shape
    blocks = eloc_ref.shape[0]

    @pl.when(group == 0)
    def _():
        side_scr[...] = jnp.zeros_like(side_scr)
        square_scr[...] = jnp.zeros_like(square_scr)
        keep = iota((BLOCK, BLOCK), 0) >= iota((BLOCK, BLOCK), 1)

        @pl.loop(0, blocks)
        def _(k):
            score = mm_nt(cs_ref[at_block(k), :], bs_ref[at_block(k), :])
            score_scr[k] = jnp.where(keep, score, 0.0)

    taps = vp_ref[0]

    down_rows = padded_rows(down_ref[0, 0], OUT_LANE)

    def one_block(k, before):
        rows = at_block(k)
        pre = u_ref[rows, :].astype(F32)
        conv = pre * sigmoid(pre)
        cum = to_front(cum_ref[rows, :], group)
        xs = conv.astype(BF16)
        score = score_scr[k]
        entering = (eloc_ref[k].astype(F32) + before * ein_ref[...]).astype(BF16)
        ent_ref[k] = entering
        total = widen(jnp.exp2(cum)) * mm(cs_ref[rows, :], entering)
        for h in range(QUAD):
            spread = cum[:, h : h + 1] + turned_ref[0, QUAD + h : QUAD + h + 1, rows]
            weights = (score * jnp.exp2(jnp.minimum(spread, CAP))).astype(BF16)
            total = total + mm(weights, head_only(xs, h))
        output = total + taps[6:7] * conv
        o_ref[rows, :] = output.astype(BF16)
        gate = gate_ref[rows, :].astype(F32)
        gated = output * gate * sigmoid(gate)
        square = gated * gated
        square_scr[rows, :] += square[:, :LANES] + square[:, LANES:]
        gained = (gated * taps[5:6]).astype(BF16)
        gained_scr[group, rows, :] = gained
        side_scr[rows, :] += mm_nt(gained, down_rows)
        return before * widen(jnp.exp2(cum[BLOCK - 8 :]))[7:8]

    before = jnp.ones((1, WIDTH), F32)
    for k in range(blocks):
        before = one_block(k, before)

    @pl.when(group == pl.num_programs(0) - 1)
    def _():
        gup_ref[...] = jnp.zeros_like(gup_ref)

        @pl.loop(0, blocks)
        def _(k):
            rows = at_block(k)
            mean = jnp.sum(square_scr[rows, :], axis=1, keepdims=True) / DI
            rms = lax.rsqrt(mean + EPS)
            side_raw = side_scr[rows, :]
            side = (side_raw * rms).astype(BF16)
            side_grad = None
            for r in range(row_count):
                term = mm(g_ref[r, rows, :], wst_ref[r, :, 256:384])
                side_grad = term if side_grad is None else side_grad + term
            side_grad = lane_range(side_grad, OUT_LANE).astype(BF16)
            product = jnp.sum(side_grad.astype(F32) * side_raw, axis=1, keepdims=True)
            for r in range(row_count):
                cols = slice(r * part, (r + 1) * part)
                raw = mm(gained_scr[0, rows, :], out_block(w_ref, 0, r, part))
                for c in range(1, GROUPS):
                    raw = raw + mm(gained_scr[c, rows, :], out_block(w_ref, c, r, part))
                cot = g_ref[r, rows, :]
                product = product + jnp.sum(raw * cot.astype(F32), axis=1, keepdims=True)
                total = x_ref[r, at_rows(k), :].astype(F32) + raw * rms + mm_nt(side, wst_ref[r, :, 256:384])
                out_ref[r, rows, :] = total.astype(BF16)
                gup_ref[:, cols] += mm_tn(side, cot)[OUT_LANE : OUT_LANE + RANK]
            coefficient = rms * rms * rms * product / DI
            lane = iota((BLOCK, LANES), 1)
            aux_ref[rows, :] = jnp.where(lane == 0, rms, coefficient)
            sg_ref[rows, :] = side_grad


def gate_kernel(
    place_ref, g_ref, w_ref, sg_ref, down_ref, vp_ref, gate_ref, o_ref, aux_ref, cum_ref, cs_t_ref,
    dgate_ref, dy_ref, gloc_ref, gfin_ref, gdown_ref,
    sg_t_scr,
):
    group = pl.program_id(0)
    row_count, _, part = g_ref.shape
    blocks = gloc_ref.shape[0]

    @pl.when(group == 0)
    def _():
        @pl.loop(0, blocks)
        def _(k):
            sg_t_scr[k] = sg_ref[at_block(k), :].astype(F32).T[OUT_LANE : OUT_LANE + RANK].astype(BF16)

    taps = vp_ref[0]
    gdown_ref[0] = jnp.zeros((RANK, WIDTH), F32)

    down_rows = padded_rows(down_ref[0, 0], OUT_LANE)

    def one_block(i, state):
        k = blocks - 1 - i
        rows = at_block(k)
        dmix = mm(sg_ref[rows, :], down_rows)
        for r in range(row_count):
            dmix = dmix + mm_nt(g_ref[r, rows, :], out_block(w_ref, 0, r, part))
        gate = gate_ref[rows, :].astype(F32)
        output = o_ref[rows, :].astype(F32)
        sig = sigmoid(gate)
        act = gate * sig
        gated = output * act
        rms = aux_ref[rows, 0:1]
        coefficient = aux_ref[rows, 1:2]
        scale = rms * taps[5:6]
        mixed = (gated * scale).astype(BF16)
        gdown_ref[0] += mm(sg_t_scr[k], mixed)
        gated_grad = scale * dmix - gated * coefficient
        dy = gated_grad * act
        dgate = gated_grad * output * (sig + act * (1.0 - sig))
        dgate_ref[rows, :] = dgate.astype(BF16)
        dy_ref[rows, :] = dy.astype(BF16)
        cum = to_front(cum_ref[rows, :], group)
        factor = widen(jnp.exp2(cum))
        gloc_ref[k] = state.astype(BF16)
        return factor[BLOCK - 1 : BLOCK] * state + mm(cs_t_ref[k], (factor * dy).astype(BF16))

    state = jnp.zeros((STATES, WIDTH), F32)
    for i in range(blocks):
        state = one_block(i, state)
    gfin_ref[...] = state.astype(BF16)


def back_kernel(
    place_ref, x_ref, gain_ref, normed_ref, wst_ref, w_ref, up_ref, adv_ref, vp_ref, sp_ref, hp_ref,
    u_ref, o_ref, dy_ref, dgate_ref, ent_ref, gloc_ref, gin_ref,
    cum_ref, lead_ref, turned_ref, ratio_ref, sig_ref, scpre_ref, bs_ref, cs_ref, out_down_ref, out_up_ref,
    corr_ref, wide_ref, thin_ref,
    score_scr, dscore_scr, db_scr, dc_scr, dcum_scr, dstep_scr, dlast_scr, du_scr, ig_scr, ng_scr, adg_scr, adv_t_scr, up_scr, in_scr,
):
    group = pl.program_id(0)
    row_count, _, part = x_ref.shape
    blocks = gloc_ref.shape[0]
    total_rows = normed_ref.shape[0]

    @pl.when(group == 0)
    def _():
        for ref in (dscore_scr, db_scr, dc_scr, dcum_scr, dstep_scr, dlast_scr, ng_scr, adg_scr):
            ref[...] = jnp.zeros_like(ref)
        du_scr[0:HALO, :] = jnp.zeros((HALO, WIDTH), F32)
        du_scr[total_rows : total_rows + HALO, :] = jnp.zeros((HALO, WIDTH), F32)

        @pl.loop(0, blocks)
        def _(k):
            score_scr[k] = mm_nt(bs_ref[at_block(k), :], cs_ref[at_block(k), :])
            adv_t_scr[k] = adv_ref[at_rows(k), :].astype(F32).T[IN_LANE : IN_LANE + RANK].astype(BF16)

    keep = iota((BLOCK, BLOCK), 0) <= iota((BLOCK, BLOCK), 1)
    taps = vp_ref[0]
    pick = (iota((WIDTH, LANES), 1) == QUAD * group + iota((WIDTH, LANES), 0) // P_SIZE).astype(BF16)

    def one_block(i, after):
        k = blocks - 1 - i
        rows = at_block(k)
        pre = u_ref[rows, :].astype(F32)
        sig = sigmoid(pre)
        conv = pre * sig
        xs_low = conv.astype(BF16)
        xs = xs_low.astype(F32)
        cum = to_front(cum_ref[rows, :], group)
        lead = to_front(lead_ref[rows, :], group)
        dy_low = dy_ref[rows, :]
        dy = dy_low.astype(F32)
        b_rows = bs_ref[rows, :]
        c_rows = cs_ref[rows, :]
        score = jnp.where(keep, score_scr[k], 0.0)
        dscore = dscore_scr[k]
        ending = gloc_ref[k].astype(F32) + after * gin_ref[...]
        ending_low = ending.astype(BF16)
        last = cum[BLOCK - 1 : BLOCK]
        to_end = widen(jnp.exp2(last + lead))
        dxs_state = to_end * mm(b_rows, ending_low)
        dxs = dxs_state
        for h in range(QUAD):
            spread = turned_ref[0, h : h + 1, rows] + lead[:, h : h + 1]
            damp = jnp.exp2(jnp.minimum(spread, CAP))
            weights = (score * damp).astype(BF16)
            dy_head = head_only(dy_low, h)
            dxs = dxs + mm(weights, dy_head)
            dscore = dscore + mm_nt(xs_low, dy_head) * damp
        dscore_scr[k] = dscore
        from_start = widen(jnp.exp2(cum))
        fall = from_start[BLOCK - 1 : BLOCK]
        entering_low = ent_ref[k]
        entering = entering_low.astype(F32)
        dc_scr[rows, :] += mm_nt((from_start * dy).astype(BF16), entering_low)
        db_scr[rows, :] += mm_nt((to_end * xs).astype(BF16), ending_low)
        scan_out = o_ref[rows, :].astype(F32) - taps[6:7] * conv
        inward = mm((xs * dxs).astype(BF16), pick)
        dcum_scr[rows, :] += mm((dy * scan_out).astype(BF16), pick) - inward
        dstep_scr[rows, :] += inward
        ends = jnp.sum(xs * dxs_state, axis=0, keepdims=True)
        ends = ends + fall * jnp.sum(entering * ending, axis=0, keepdims=True)
        dlast_scr[k] += split_right(jnp.broadcast_to(ends, (8, WIDTH)), pick)
        dconv = taps[6:7] * dy + dxs
        du_scr[at_rows(k), :] = dconv * (sig + conv * (1.0 - sig))
        return after * fall

    after = jnp.ones((1, WIDTH), F32)
    for i in range(blocks):
        after = one_block(i, after)
    up_rows = padded_rows(up_ref[0, 0], IN_LANE)

    ig_scr[0:HALO, :WIDTH] = jnp.zeros((HALO, WIDTH), BF16)
    for k in range(blocks):
        rows = with_halo(k)
        extra = HALO if k == 0 else 0
        ig_scr[at_rows(k), :WIDTH] = dgate_ref[at_block(k), :]
        window = du_scr[pl.ds(HALO + k * BLOCK - extra, BLOCK + extra + 8), :]
        ig_scr[rows, WIDTH:] = advances(window, taps[0:4], BLOCK + extra).astype(BF16)
        grad = ig_scr[rows, :]
        adg_scr[rows, :] += mm_nt(grad, up_rows)
        for r in range(row_count):
            ng_scr[rows, r * part : (r + 1) * part] += mm_nt(grad, w_ref[0, r, :part, :])
        if k == 0:
            up_scr[...] = mm_tn(adv_ref[0:HALO, :], grad[:HALO])[IN_LANE : IN_LANE + RANK]
        up_scr[...] += mm(adv_t_scr[k], grad[extra:])

    share = RANK // row_count
    for r in range(row_count):
        wide_ref[r, 0, :, : 2 * WIDTH] = up_scr[r * share : (r + 1) * share, :]
        wide_ref[r, 0, :, 2 * WIDTH :] = out_down_ref[0, r * share : (r + 1) * share, :]

    @pl.when(group == pl.num_programs(0) - 1)
    def _():
        upper = (iota((BLOCK, BLOCK), 0) <= iota((BLOCK, BLOCK), 1)).astype(BF16)
        rate = -jnp.exp(hp_ref[1:2])

        @pl.loop(0, blocks)
        def _(k):
            rows = at_block(k)
            dscore = jnp.where(keep, dscore_scr[k], 0.0).astype(BF16)
            db = db_scr[rows, :] + mm(dscore, cs_ref[rows, :])
            dc = dc_scr[rows, :] + mm_tn(dscore, bs_ref[rows, :])
            pre = scpre_ref[rows, :]
            sig = sigmoid(pre)
            slope = sig + pre * sig * (1.0 - sig)
            du_scr[at_rows(k), :] = jnp.concatenate([db, dc], axis=1) * slope
            is_last = iota((BLOCK, LANES), 0) == BLOCK - 1
            dcum = dcum_scr[rows, :] + jnp.where(is_last, dlast_scr[k, 0:1, :], 0.0)
            slower = split_left(upper, dcum) * (rate * sig_ref[rows, :])
            dstep_scr[rows, :] = dstep_scr[rows, :] * ratio_ref[rows, :] + slower

        def finish(rows, window, count, draw):
            dstate = advances(window, sp_ref[0:4], count).astype(BF16)
            adapt = adg_scr[rows, :].astype(BF16)
            mixed = adapt + draw
            total = jnp.zeros((count, 1), F32)
            square = jnp.zeros((count, 1), F32)
            grads = []
            for r in range(row_count):
                cols = slice(r * part, (r + 1) * part)
                grad = ng_scr[rows, cols] + mm_nt(dstate, wst_ref[r, :, 0:256])
                grad = grad + mm_nt(mixed, wst_ref[r, :, 256:384])
                grad = grad * gain_ref[r]
                piece = x_ref[r, rows, :].astype(F32)
                total = total + jnp.sum(piece * grad, axis=1, keepdims=True)
                square = square + jnp.sum(piece * piece, axis=1, keepdims=True)
                grads.append(grad)
                in_scr[:, cols] += mm_tn(adapt, normed_ref[rows, cols])[IN_LANE : IN_LANE + RANK]
            inv = lax.rsqrt(square / D + EPS)
            factor = inv * inv * inv * total / D
            for r in range(row_count):
                piece = x_ref[r, rows, :].astype(F32)
                corr_ref[r, rows, :] = (inv * grads[r] - factor * piece).astype(BF16)

        in_scr[...] = jnp.zeros_like(in_scr)
        for k in range(blocks):
            extra = HALO if k == 0 else 0
            window = du_scr[pl.ds(HALO + k * BLOCK - extra, BLOCK + extra + 8), :]
            draw = dstep_scr[at_block(k), :].astype(BF16)
            if k == 0:
                draw = jnp.concatenate([jnp.zeros((HALO, LANES), BF16), draw], axis=0)
            finish(with_halo(k), window, BLOCK + extra, draw)

        for r in range(row_count):
            thin_ref[r, 0:RANK, :] = in_scr[:, r * part : (r + 1) * part]
            thin_ref[r, RANK:, :] = out_up_ref[:, r * part : (r + 1) * part]


def on_row(row):
    return {"row": row}


def on_col(col):
    return {"col": col}


def tail_kernel(
    corr_ref, wide_ref, thin_ref,
    corr_out, wide_out, thin_out,
    wide_scr, thin_scr, wide_sum, thin_sum, wide_col,
    own_sem, corr_send, corr_recv, row_send, row_recv, col_send, col_recv, last_send, last_recv,
):
    row_count = corr_ref.shape[0]
    col_count = thin_out.shape[0]
    row = lax.axis_index("row")
    col = lax.axis_index("col")
    barrier = pltpu.get_barrier_semaphore()
    for d in range(1, row_count):
        pl.semaphore_signal(barrier, inc=1, device_id=on_row(lax.rem(row + d, row_count)), device_id_type=MESH)
    for d in range(1, col_count):
        pl.semaphore_signal(barrier, inc=1, device_id=on_col(lax.rem(col + d, col_count)), device_id_type=MESH)
    pl.semaphore_wait(barrier, row_count + col_count - 2)

    def send(source, target, sends, recvs, index, device):
        copy = pltpu.make_async_remote_copy(
            src_ref=source, dst_ref=target, send_sem=sends.at[index], recv_sem=recvs.at[index],
            device_id=device, device_id_type=MESH,
        )
        copy.start()
        return copy

    first = []
    for d in range(1, row_count):
        peer = lax.rem(row + d, row_count)
        first.append(send(wide_ref.at[peer], wide_scr.at[row], row_send, row_recv, d, on_row(peer)))
        first.append(send(thin_ref.at[peer], thin_scr.at[row], row_send, row_recv, row_count + d, on_row(peer)))
    moved = []
    for d in range(1, row_count):
        peer = lax.rem(row + d, row_count)
        moved.append(send(corr_ref.at[peer], corr_out.at[row], corr_send, corr_recv, d, on_row(peer)))
    own = pltpu.make_async_copy(corr_ref.at[row], corr_out.at[row], own_sem.at[0])
    own.start()
    for copy in first:
        copy.wait()
    wide = wide_ref[row]
    thin = thin_ref[row]
    for d in range(1, row_count):
        peer = lax.rem(row + d, row_count)
        wide = wide + wide_scr[peer]
        thin = thin + thin_scr[peer]
    wide_sum[...] = wide
    thin_sum[...] = thin
    second = []
    for d in range(1, col_count):
        peer = lax.rem(col + d, col_count)
        second.append(send(wide_sum.at[peer], wide_col.at[col], col_send, col_recv, d, on_col(peer)))
        second.append(send(thin_sum, thin_out.at[col], col_send, col_recv, col_count + d, on_col(peer)))
    wide_col[col] = wide_sum[col]
    thin_out[col] = thin
    for copy in second:
        copy.wait()
    third = []
    for d in range(1, row_count):
        peer = lax.rem(row + d, row_count)
        third.append(send(wide_col, wide_out.at[row], last_send, last_recv, d, on_row(peer)))
    wide_out[row] = wide_col[...]
    for copy in third:
        copy.wait()
    for copy in moved:
        copy.wait()
    own.wait()


def start_kernel(
    x_ref, w_ref, up_ref, p_ref, down_ref, state_ref, in_ref, out_ref, gain_ref, conv_ref, bias_ref, gate_ref, step_ref, rate_ref,
    skip_ref, adapter_ref,
    x_out, w_out, shared_out, gain_out, vec_out, head_out,
    block_scr, zero_scr, shared_ref,
    own_sem, send_sem, recv_sem, row_send, row_recv, col_send, col_recv,
):
    col_count, row_count = w_out.shape[:2]
    high_count = col_count // 2
    part = x_ref.shape[1]
    chunk = x_ref.shape[0] // row_count
    rank_part = up_ref.shape[0] // row_count
    row = lax.axis_index("row")
    col = lax.axis_index("col")
    low = lax.rem(col, 2)
    high = col // 2
    core = row + 1 - 2 * lax.rem(row, 2)
    across = lax.rem(row + 2, row_count)
    side = col + 1 - 2 * low
    barrier = pltpu.get_barrier_semaphore()
    for d in range(1, row_count):
        pl.semaphore_signal(barrier, inc=1, device_id=on_row(lax.rem(row + d, row_count)), device_id_type=MESH)
    for d in range(1, col_count):
        pl.semaphore_signal(barrier, inc=1, device_id=on_col(lax.rem(col + d, col_count)), device_id_type=MESH)

    def paired(value):
        lane = iota((value.shape[0], LANES), 1) < P_SIZE
        tiles = [value[:, h * LANES : (h + 1) * LANES].astype(F32) for h in range(QUAD)]
        turned = [pltpu.roll(tile, P_SIZE, 1) for tile in tiles]
        gates = [jnp.where(lane, tiles[h], turned[h + 1]) for h in (0, 2)]
        values = [jnp.where(lane, turned[h], tiles[h + 1]) for h in (0, 2)]
        return jnp.concatenate(gates + values, axis=1).astype(BF16)

    block_scr[0:part, :] = paired(w_ref[...])
    ranks = pl.ds(pl.multiple_of(row * rank_part, rank_part), rank_part)
    block_scr[part : part + rank_part, :] = paired(up_ref[ranks, :])
    first = part + rank_part
    half = WIDTH // 2
    block_scr[first : first + half, :WIDTH] = p_ref[:half, :]
    block_scr[first : first + half, WIDTH:] = p_ref[half:, :]
    first = first + half
    downs = down_ref[ranks, :]
    block_scr[first : first + rank_part // 2, :WIDTH] = downs[: rank_part // 2]
    block_scr[first : first + rank_part // 2, WIDTH:] = downs[rank_part // 2 :]
    zero_scr[...] = jnp.zeros_like(zero_scr)
    shift = adapter_ref[col] * RANK
    source = iota((LANES, LANES), 0) - shift
    target = iota((LANES, LANES), 1)
    chosen = (source >= 0) & (source < RANK)
    ins = (chosen & (source == target - IN_LANE)).astype(F32).astype(BF16)
    outs = (chosen & (source == target - OUT_LANE)).astype(F32).astype(BF16)
    states = 2 * STATES
    shared_ref[:, :states] = state_ref[:states, :].astype(F32).T.astype(BF16)
    steps = jnp.concatenate(
        [state_ref[states:, :].astype(F32), jnp.zeros((LANES - HEADS, part), F32)], axis=0
    ).T
    shared_ref[:, states:] = (steps + mm(in_ref[...], ins) + mm(out_ref[...], outs)).astype(BF16)
    vec_out[col, 0:4, :] = conv_ref[...]
    vec_out[col, 4:5, :] = bias_ref[...]
    vec_out[col, 5:6, :] = gate_ref[...]
    vec_out[col, 6:7, :] = widen(skip_ref[...])
    lane = iota((1, WIDTH), 1)
    scalars = jnp.zeros((1, WIDTH), F32)
    for h in range(QUAD):
        scalars = jnp.where(lane == h, step_ref[:, h : h + 1], scalars)
        scalars = jnp.where(lane == QUAD + h, rate_ref[:, h : h + 1], scalars)
    vec_out[col, 7:8, :] = scalars
    gain_out[row] = gain_ref[...]
    pl.semaphore_wait(barrier, row_count + col_count - 2)

    def remote(source, target, sends, recvs, index, device):
        return pltpu.make_async_remote_copy(
            src_ref=source, dst_ref=target, send_sem=sends.at[index], recv_sem=recvs.at[index],
            device_id=device, device_id_type=MESH,
        )

    own_block = pltpu.make_async_copy(block_scr, w_out.at[col, row], own_sem.at[0])
    own_block.start()

    def whole_window(target, slot, index, peer):
        source = x_ref.at[pl.ds(pl.multiple_of(target * chunk - HALO, HALO), chunk + HALO)]
        return remote(source, x_out.at[slot], row_send, row_recv, index, on_row(peer))

    def first_window(slot, index, peer):
        source = x_ref.at[pl.ds(0, chunk)]
        return remote(source, x_out.at[slot, pl.ds(HALO, chunk)], row_send, row_recv, index, on_row(peer))

    def each_window(sending, act):
        for d in range(1, row_count):
            peer = lax.rem(row + d, row_count)
            chosen = peer if sending else row
            slot = row if sending else lax.rem(row + row_count - d, row_count)

            @pl.when(chosen > 0)
            def _():
                act(whole_window(jnp.maximum(chosen, 1), slot, d, peer))

            @pl.when(chosen == 0)
            def _():
                act(first_window(slot, d, peer))

    @pl.when(row > 0)
    def _():
        source = x_ref.at[pl.ds(pl.multiple_of(jnp.maximum(row, 1) * chunk - HALO, HALO), chunk + HALO)]
        pltpu.make_async_copy(source, x_out.at[row], own_sem.at[1]).start()

    @pl.when(row == 0)
    def _():
        pltpu.make_async_copy(x_ref.at[pl.ds(0, chunk)], x_out.at[row, pl.ds(HALO, chunk)], own_sem.at[1]).start()
        for r in range(row_count):
            pltpu.make_async_copy(zero_scr, x_out.at[r, pl.ds(0, HALO)], own_sem.at[3 + r]).start()

    own_shared = pltpu.make_async_copy(shared_ref, shared_out.at[row], own_sem.at[2])
    own_shared.start()
    small = []
    for d in range(1, col_count):
        peer = lax.rem(col + d, col_count)
        small.append(remote(vec_out.at[col], vec_out.at[col], col_send, col_recv, d, on_col(peer)))
    for d in range(1, row_count):
        peer = lax.rem(row + d, row_count)
        small.append(remote(shared_ref, shared_out.at[row], row_send, row_recv, row_count + d, on_row(peer)))
        small.append(
            remote(gain_out.at[row], gain_out.at[row], row_send, row_recv, 2 * row_count + d, on_row(peer))
        )
    for copy in small:
        copy.start()

    cut = (w_out.shape[2] * 65 // 100 + 8) // 16 * 16
    spans = (pl.ds(0, cut), pl.ds(cut, w_out.shape[2] - cut))
    has_up = high < high_count - 1
    has_down = high > 0
    routes = {
        "up": (0, has_up, on_col(lax.rem(col + 2, col_count))),
        "down": (1, has_down, on_col(lax.rem(col + col_count - 2, col_count))),
        "x": (2, None, on_col(side)),
        "y": (3, None, on_row(across)),
        "core": (4, None, on_row(core)),
    }

    def piece(section, c, r, kind, device):
        ref = w_out.at[c, r, spans[section]]
        return pltpu.make_async_remote_copy(
            src_ref=ref, dst_ref=ref, send_sem=send_sem.at[section, c, r, kind],
            recv_sem=recv_sem.at[section, c, r], device_id=device, device_id_type=MESH,
        )

    def event(starting, section, c, r, names, arrives=True, valid=None):
        def act():
            if starting and arrives:
                piece(section, c, r, 4, on_row(core)).wait_recv()
            for name in names:
                kind, allowed, device = routes[name]
                copy = piece(section, c, r, kind, device)
                if allowed is None:
                    copy.start() if starting else copy.wait_send()
                else:

                    @pl.when(allowed)
                    def _():
                        copy.start() if starting else copy.wait_send()

        if valid is None:
            act()
        else:
            pl.when(valid)(act)

    def far(column, step, distance):
        return lax.rem(column + step * distance + 4 * col_count, col_count)

    def within(step, distance):
        return high >= distance if step < 0 else high + distance < high_count

    onward = {-2: "up", 2: "down"}

    def along(starting, section, distance):
        for step in (-2, 2):
            valid = within(step, distance)
            if section == 0:
                names = (onward[step], "y", "x", "core")
                event(starting, 0, far(col, step, distance), row, names, valid=valid)
            else:
                for column, r in ((col, row), (side, row), (col, across), (side, across)):
                    event(starting, 1, far(column, step, distance), r, (onward[step], "core"), valid=valid)

    def over(starting, distance):
        for step in (-2, 2):
            valid = within(step, distance)
            event(starting, 0, far(side, step, distance), row, ("core",), valid=valid)
            event(starting, 0, far(col, step, distance), across, ("x", "core"), valid=valid)

    def last(starting, distance):
        for step in (-2, 2):
            event(starting, 0, far(side, step, distance), across, ("core",), valid=within(step, distance))

    def relay(starting):
        def windows():
            if starting:
                each_window(True, lambda copy: copy.start())

        event(starting, 0, col, row, ("up", "down"), arrives=False)
        event(starting, 1, col, row, ("x", "y"), arrives=False)
        event(starting, 0, col, row, ("y", "x", "core"), arrives=False)
        event(starting, 1, col, row, ("core",), arrives=False)
        event(starting, 1, side, row, ("y", "core"))
        along(starting, 0, 1)
        event(starting, 1, col, row, ("up", "down"), arrives=False)
        event(starting, 0, col, across, ("x", "core"))
        event(starting, 1, side, row, ("up", "down"), arrives=False)
        event(starting, 1, col, across, ("up", "down", "core"))
        for d in range(2, high_count - 1):
            along(starting, 0, d)
        event(starting, 1, side, across, ("up", "down", "core"))
        over(starting, 1)
        along(starting, 0, high_count - 1)
        windows()
        along(starting, 1, 1)
        over(starting, 2)
        event(starting, 0, side, row, ("core",))
        event(starting, 0, side, across, ("core",))
        last(starting, 1)
        for d in range(2, high_count):
            if d > 2:
                over(starting, d)
            along(starting, 1, d)
            if d > 2:
                last(starting, d - 1)
        last(starting, high_count - 1)

    own_block.wait()
    relay(True)
    for copy in small:
        copy.wait()
    lane = iota((1, LANES), 1) < QUAD
    steps = jnp.zeros((1, LANES), F32)
    rates = jnp.zeros((1, LANES), F32)
    for c in range(col_count):
        values = vec_out[c, 7:8, :LANES]
        steps = steps + pltpu.roll(jnp.where(lane, values, 0.0), (QUAD * c) % LANES, 1)
        values = pltpu.roll(values, LANES - QUAD, 1)
        rates = rates + pltpu.roll(jnp.where(lane, values, 0.0), (QUAD * c) % LANES, 1)
    head_out[...] = jnp.concatenate([steps, rates, jnp.zeros((6, LANES), F32)], axis=0)
    own_shared.wait()
    each_window(True, lambda copy: copy.wait_send())
    each_window(False, lambda copy: copy.wait_recv())

    @pl.when(row > 0)
    def _():
        source = x_ref.at[pl.ds(0, chunk + HALO)]
        pltpu.make_async_copy(source, x_out.at[row], own_sem.at[1]).wait()

    @pl.when(row == 0)
    def _():
        pltpu.make_async_copy(x_ref.at[pl.ds(0, chunk)], x_out.at[row, pl.ds(HALO, chunk)], own_sem.at[1]).wait()
        for r in range(row_count):
            pltpu.make_async_copy(zero_scr, x_out.at[r, pl.ds(0, HALO)], own_sem.at[3 + r]).wait()

    core_across = lax.rem(core + 2, row_count)
    for c in range(col_count):
        for r in (core, core_across):
            for section in range(2):
                piece(section, c, r, 4, on_row(core)).wait_recv()
    relay(False)


def start_exchange(x, w, up, p, down, shared, vectors, adapter_id, row_count, col_count):
    part = x.shape[1]
    rank_part = up.shape[0] // row_count
    block_rows = part + rank_part + WIDTH // 2 + rank_part // 2
    chunk = x.shape[0] // row_count
    vmem = pl.BlockSpec(memory_space=pltpu.VMEM)
    anywhere = pl.BlockSpec(memory_space=pl.ANY)
    dma = pltpu.SemaphoreType.DMA
    return pl.pallas_call(
        start_kernel,
        in_specs=[anywhere] + [vmem] * (7 + len(vectors)) + [pl.BlockSpec(memory_space=pltpu.SMEM)],
        out_specs=[anywhere] * 3 + [vmem] * 3,
        out_shape=[
            jax.ShapeDtypeStruct((row_count, chunk + HALO, part), BF16),
            jax.ShapeDtypeStruct((col_count, row_count, block_rows, 2 * WIDTH), BF16),
            jax.ShapeDtypeStruct((row_count, part, 384), BF16),
            jax.ShapeDtypeStruct((row_count, 1, part), F32),
            jax.ShapeDtypeStruct((col_count, 8, WIDTH), F32),
            jax.ShapeDtypeStruct((8, LANES), F32),
        ],
        scratch_shapes=[
            pltpu.VMEM((block_rows, 2 * WIDTH), BF16), pltpu.VMEM((HALO, part), BF16),
            pltpu.VMEM((part, 384), BF16), dma((3 + row_count,)), dma((2, col_count, row_count, 5)), dma((2, col_count, row_count)),
            dma((3 * row_count,)), dma((3 * row_count,)), dma((col_count,)), dma((col_count,)),
        ],
        compiler_params=pltpu.CompilerParams(
            collective_id=1, has_side_effects=True, vmem_limit_bytes=VMEM_BYTES
        ),
    )(x, w, up, p, down, *shared, *vectors, adapter_id)


def finish_exchange(corr, wide, thin):
    row_count = corr.shape[0]
    col_count = wide.shape[1]
    share, width = wide.shape[2:]
    vmem = pl.BlockSpec(memory_space=pltpu.VMEM)
    anywhere = pl.BlockSpec(memory_space=pl.ANY)
    dma = pltpu.SemaphoreType.DMA
    return pl.pallas_call(
        tail_kernel,
        in_specs=[anywhere, vmem, vmem],
        out_specs=[anywhere, vmem, vmem],
        out_shape=[
            jax.ShapeDtypeStruct(corr.shape, corr.dtype),
            jax.ShapeDtypeStruct((row_count, col_count, share, width), F32),
            jax.ShapeDtypeStruct((col_count,) + thin.shape[1:], F32),
        ],
        scratch_shapes=[
            pltpu.VMEM(wide.shape, F32), pltpu.VMEM(thin.shape, F32), pltpu.VMEM(wide.shape[1:], F32),
            pltpu.VMEM(thin.shape[1:], F32), pltpu.VMEM(wide.shape[1:], F32),
            dma((1,)), dma((row_count,)), dma((row_count,)), dma((2 * row_count,)), dma((2 * row_count,)),
            dma((2 * col_count,)), dma((2 * col_count,)), dma((row_count,)), dma((row_count,)),
        ],
        compiler_params=pltpu.CompilerParams(
            collective_id=0, has_side_effects=True, vmem_limit_bytes=VMEM_BYTES
        ),
    )(corr, wide, thin)


def whole_spec(shape):
    return pl.BlockSpec(shape, lambda c, s: (0,) * len(shape))


def lead_spec(shape):
    return pl.BlockSpec((1,) + tuple(shape[1:]), lambda c, s: (c,) + (0,) * (len(shape) - 1))


def lane_spec(shape):
    block = tuple(shape[:-1]) + (WIDTH,)
    return pl.BlockSpec(block, lambda c, s: (0,) * (len(shape) - 1) + (c,))


def second_spec(shape):
    block = (shape[0], 1) + tuple(shape[2:])
    return pl.BlockSpec(block, lambda c, s: (0, c) + (0,) * (len(shape) - 2))


def front_spec(shape):
    if shape[2] % 3 == 0 and shape[2] // 3 * 2 >= WIDTH and shape[3] == 2 * WIDTH and shape[1] == 4:
        return pl.BlockSpec((1, shape[1], shape[2] // 3 * 2, shape[3]), lambda c, s: (c, 0, 0, 0))
    return lead_spec(shape)


def full_back_spec(shape):
    if shape[2] > WIDTH:
        return pl.BlockSpec((shape[0], shape[1], shape[2] // 3, shape[3]), lambda c, s: (0, 0, 2, 0))
    return whole_spec(shape)


def back_spec(shape):
    if shape[2] > WIDTH:
        return pl.BlockSpec((1, shape[1], shape[2] // 3, shape[3]), lambda c, s: (c, 0, 2, 0))
    return lead_spec(shape)


def up_spec(shape):
    first = WIDTH // RANK if shape[2] > RANK else 0
    return pl.BlockSpec((1, 1, RANK, 2 * WIDTH), lambda c, s: (c, s[0], first + s[1], 0))


def down_spec(shape):
    first = shape[2] // RANK - 1
    return pl.BlockSpec((1, 1, RANK, WIDTH), lambda c, s: (c, s[0], first, s[1]))


KINDS = {
    "a": whole_spec, "c": lead_spec, "l": lane_spec, "s": second_spec, "w": front_spec, "f": full_back_spec,
    "p": back_spec, "u": up_spec, "d": down_spec,
}


def grouped_call(kernel, place, inputs, kinds, outputs, out_kinds, scratch, flops=0):
    return pl.pallas_call(
        kernel,
        grid_spec=pltpu.PrefetchScalarGridSpec(
            num_scalar_prefetch=1,
            grid=(GROUPS,),
            in_specs=[KINDS[kind](value.shape) for kind, value in zip(kinds, inputs)],
            out_specs=[KINDS[kind](shape) for kind, (shape, _) in zip(out_kinds, outputs)],
            scratch_shapes=[pltpu.VMEM(shape, dtype) for shape, dtype in scratch],
        ),
        out_shape=[jax.ShapeDtypeStruct(shape, dtype) for shape, dtype in outputs],
        compiler_params=pltpu.CompilerParams(vmem_limit_bytes=VMEM_BYTES),
        cost_estimate=pl.CostEstimate(flops=flops, bytes_accessed=40_000_000, transcendentals=0),
    )(place, *inputs)


def to_groups(value, heads_here):
    cols = value.shape[0]
    middle = value.shape[1:-1]
    if heads_here == QUAD:
        return value
    if heads_here > QUAD:
        parts = heads_here // QUAD
        value = value.reshape((cols,) + middle + (parts, WIDTH))
        value = jnp.moveaxis(value, -2, 1)
        return value.reshape((GROUPS,) + middle + (WIDTH,))
    parts = QUAD // heads_here
    value = value.reshape((GROUPS, parts) + middle + (heads_here * P_SIZE,))
    value = jnp.moveaxis(value, 1, -2)
    return value.reshape((GROUPS,) + middle + (WIDTH,))


def to_cols(value, heads_here, col_count):
    middle = value.shape[1:-1]
    if heads_here == QUAD:
        return value
    if heads_here > QUAD:
        parts = heads_here // QUAD
        value = value.reshape((col_count, parts) + middle + (WIDTH,))
        value = jnp.moveaxis(value, 1, -2)
        return value.reshape((col_count,) + middle + (heads_here * P_SIZE,))
    parts = QUAD // heads_here
    value = value.reshape((GROUPS,) + middle + (parts, heads_here * P_SIZE))
    value = jnp.moveaxis(value, -2, 1)
    return value.reshape((col_count,) + middle + (heads_here * P_SIZE,))


def pad_lanes(value, width):
    return jnp.pad(value, [(0, 0)] * (value.ndim - 1) + [(0, width - value.shape[-1])])


def carry_in(state, decay, row_count, col_count, seq_cols, forward):
    row = lax.axis_index("row")
    col = lax.axis_index("col")
    total = state
    factor = decay
    before = jnp.zeros(state.shape, F32)
    reach = jnp.ones_like(decay)
    span = 1
    while span < row_count:
        pairs = [(i, i ^ span) for i in range(row_count)]
        other = lax.ppermute(total, "row", pairs).astype(F32)
        other_factor = lax.ppermute(factor, "row", pairs)
        behind = ((row & span) != 0) == forward
        mine = total.astype(F32)
        before = jnp.where(behind, before + reach * other, before)
        reach = jnp.where(behind, reach * other_factor, reach)
        joined = jnp.where(behind, other * factor + mine, mine * other_factor + other)
        total = joined.astype(BF16)
        factor = factor * other_factor
        span *= 2
    place = lax.rem(col, seq_cols)
    for hop in range(1, seq_cols):
        shift = hop if forward else -hop
        pairs = [(i, (i + shift) % col_count) for i in range(col_count)]
        other = lax.ppermute(total, "col", pairs).astype(F32)
        other_factor = lax.ppermute(factor, "col", pairs)
        inside = place >= hop if forward else place < seq_cols - hop
        before = jnp.where(inside, before + reach * other, before)
        reach = jnp.where(inside, reach * other_factor, reach)
    return before


def per_device(
    block_in, norm_gain, proj_inner, proj_state, conv_inner, conv_inner_bias, conv_state, conv_state_bias,
    step_bias, decay_log, skip_gain, gate_gain, proj_out, adapt_in_down, adapt_in_up, adapt_out_down,
    adapt_out_up, adapter_id, cotangent,
):
    row_count = lax.axis_size("row")
    col_count = lax.axis_size("col")
    row = lax.axis_index("row")
    col = lax.axis_index("col")
    col_tokens, part = block_in.shape
    chunk = col_tokens // row_count
    total_rows = chunk + HALO
    blocks = chunk // BLOCK
    seq_cols = SEQ // col_tokens
    heads_here = proj_inner.shape[1]
    local = heads_here * P_SIZE
    rank_total = adapt_in_down.shape[1]
    rank_part = rank_total // row_count
    rank_share = rank_total // col_count
    adapter = lax.dynamic_index_in_dim(adapter_id, col // seq_cols, keepdims=False)

    relayed = row_count == 4 and heads_here == QUAD and seq_cols == 1 and part == WIDTH
    place = jnp.zeros((2,), jnp.int32)
    if relayed:
        x_rows, w_all, w_state, gain_all, vectors, head_rows = start_exchange(
            block_in, proj_inner.reshape(part, 2 * local), adapt_in_up.reshape(rank_total, 2 * local), proj_out,
            adapt_out_down, (proj_state.T, adapt_in_down, adapt_out_up),
            (
                norm_gain[None], conv_inner, conv_inner_bias[None], gate_gain[None], step_bias[None],
                decay_log[None], skip_gain[None],
            ),
            adapter_id, row_count, col_count,
        )
        per_part = rank_part // RANK
        place = jnp.stack([adapter // per_part, lax.rem(adapter, per_part)])
        up_all = down_all = p_all = w_all
        x_rows, cot = lax.optimization_barrier((x_rows, cotangent))
        g_rows = lax.all_to_all(cot.reshape(row_count, chunk, part), "row", 0, 0, tiled=True)
    else:
        head = jnp.zeros((HALO, part), BF16)
        if seq_cols > 1:
            pairs = [(i, (i + 1) % col_count) for i in range(col_count)]
            head = lax.ppermute(block_in[-HALO:], "col", pairs)
            head = jnp.where(lax.rem(col, seq_cols) > 0, head, jnp.zeros_like(head))
        padded = jnp.concatenate([head, block_in], axis=0)
        windows = jnp.stack([padded[r * chunk : r * chunk + total_rows] for r in range(row_count)])
        x_rows = lax.all_to_all(windows, "row", 0, 0, tiled=True)
        g_rows = lax.all_to_all(cotangent.reshape(row_count, chunk, part), "row", 0, 0, tiled=True)

        def split_pairs(value):
            value = value.reshape(value.shape[0], heads_here, 2, P_SIZE)
            return jnp.swapaxes(value, 1, 2).reshape(value.shape[0], 2, local)

        up_part = lax.dynamic_slice_in_dim(adapt_in_up, row * rank_part, rank_part, 0)
        w_block = jnp.concatenate([split_pairs(proj_inner), split_pairs(up_part)], axis=0)
        w_all = lax.all_gather(w_block.reshape(part + rank_part, 2 * local), ("col", "row"))
        w_all = w_all.reshape(col_count, row_count, part + rank_part, 2, local)
        w_all = to_groups(w_all, heads_here).reshape(GROUPS, row_count, part + rank_part, 2 * WIDTH)
        up_all = w_all[:, :, part:, :].reshape(GROUPS, rank_total, 2 * WIDTH)
        up_all = lax.dynamic_slice_in_dim(up_all, adapter * RANK, RANK, 1)[:, None]

        down_part = lax.dynamic_slice_in_dim(adapt_out_down, row * rank_part, rank_part, 0)
        p_block = jnp.concatenate([proj_out, down_part.T], axis=1)
        p_all = lax.all_gather(p_block, ("col", "row")).reshape(col_count, row_count, local, part + rank_part)
        if heads_here != QUAD:
            p_all = jnp.moveaxis(p_all, 1, 0).reshape(row_count, GROUPS, WIDTH, part + rank_part)
            p_all = jnp.moveaxis(p_all, 0, 1)
        down_all = jnp.swapaxes(p_all[..., part:], 1, 2).reshape(GROUPS, WIDTH, rank_total)
        down_all = jnp.swapaxes(lax.dynamic_slice_in_dim(down_all, adapter * RANK, RANK, 2), 1, 2)[:, None]

        in_down = lax.dynamic_slice_in_dim(adapt_in_down, adapter * RANK, RANK, 1)
        out_up = lax.dynamic_slice_in_dim(adapt_out_up, adapter * RANK, RANK, 1)
        shared = pad_lanes(jnp.concatenate([proj_state, in_down, out_up], axis=1), 384)
        w_state = lax.all_gather(shared, "row")
        gain_all = lax.all_gather(norm_gain, "row").reshape(row_count, 1, part)

        scalars = jnp.concatenate([step_bias, decay_log, skip_gain])
        vectors = jnp.concatenate(
            [conv_inner, conv_inner_bias[None], gate_gain[None], pad_lanes(scalars, local)[None]], axis=0
        )
        vectors = lax.all_gather(vectors, "col")
        scalars = vectors[:, 6, : 3 * heads_here].reshape(col_count, 3, heads_here)
        scalars = jnp.swapaxes(scalars, 0, 1).reshape(3, HEADS)
        head_rows = jnp.pad(scalars[:2], ((0, 6), (0, LANES - HEADS)))
        skip_wide = jnp.repeat(scalars[2], P_SIZE).reshape(GROUPS, 1, WIDTH)
        vectors = jnp.concatenate(
            [to_groups(vectors[:, :6], heads_here), skip_wide, jnp.zeros_like(skip_wide)], axis=1
        )
    state_taps = jnp.concatenate([conv_state, conv_state_bias[None], jnp.zeros((3, 256), F32)], axis=0)

    token_f32 = ((chunk, LANES), F32)
    token_low = ((chunk, LANES), BF16)
    inner_low = ((chunk, DI), BF16)
    states = ((blocks, STATES, DI), BF16)
    score_box = ((blocks, BLOCK, BLOCK), F32)
    flipped = ((blocks, STATES, BLOCK), BF16)
    (
        normed, scpre, ratio, sig, cum, lead, turned, bs, cs, cs_t, adv, gate, u, eloc, fin, dec,
    ) = grouped_call(
        front_kernel,
        place,
        (x_rows, gain_all, w_state, state_taps, head_rows, w_all, up_all, vectors),
        "aaaaawuc",
        [
            ((total_rows, D), BF16), ((chunk, 256), F32), token_f32, token_f32, token_f32, token_f32,
            ((GROUPS, 2 * QUAD, chunk), F32), token_low, token_low, flipped, ((total_rows, LANES), BF16),
            inner_low, inner_low, states, ((STATES, DI), BF16), ((8, DI), F32),
        ],
        "aaaaaaaaaaalllll",
        [((total_rows, 384), F32), flipped, ((total_rows, WIDTH), F32)],
        flops=int(45e9),
    )
    decay = dec[0:1]
    fin, g_rows = lax.optimization_barrier((fin, g_rows))
    entry = carry_in(fin, decay, row_count, col_count, seq_cols, True)
    out_rows, o, ent, aux, side_grad, out_up_grad = grouped_call(
        scan_kernel,
        place,
        (x_rows, g_rows, w_state, p_all, down_all, vectors, gate, u, eloc, entry, cum, turned, bs, cs),
        "aaafdcllllacaa",
        [
            ((row_count, chunk, part), BF16), inner_low, ((blocks, STATES, DI), BF16), token_f32, token_low,
            ((RANK, D), F32),
        ],
        "allaaa",
        [score_box, ((GROUPS, chunk, WIDTH), BF16), token_f32, token_f32],
        flops=int(45e9),
    )
    block_out = lax.all_to_all(out_rows, "row", 0, 0, tiled=True).reshape(col_tokens, part)
    dgate, dy, gloc, gfin, out_down_grad = grouped_call(
        gate_kernel,
        place,
        (g_rows, p_all, side_grad, down_all, vectors, gate, o, aux, cum, cs_t),
        "apadcllaaa",
        [inner_low, inner_low, states, ((STATES, DI), BF16), ((GROUPS, RANK, WIDTH), F32)],
        "llllc",
        [((blocks, RANK, BLOCK), BF16)],
        flops=int(25e9),
    )
    gfin, block_out = lax.optimization_barrier((gfin, block_out))
    exit_grad = carry_in(gfin, decay, row_count, col_count, seq_cols, False)
    corr, wide, thin = grouped_call(
        back_kernel,
        place,
        (
            x_rows, gain_all, normed, w_state, w_all, up_all, adv, vectors, state_taps, head_rows,
            u, o, dy, dgate, ent, gloc, exit_grad, cum, lead, turned, ratio, sig, scpre, bs, cs,
            out_down_grad, out_up_grad,
        ),
        "aaaawuacaalllllllaacaaaaaca",
        [
            ((row_count, total_rows, part), BF16), ((row_count, GROUPS, RANK // row_count, 3 * WIDTH), F32),
            ((row_count, 2 * RANK, part), F32),
        ],
        "asa",
        [
            score_box, score_box, token_f32, token_f32, token_f32, token_f32, ((blocks, 8, LANES), F32),
            ((total_rows + HALO, WIDTH), F32), ((total_rows, 2 * WIDTH), BF16), ((total_rows, D), F32),
            ((total_rows, LANES), F32), ((blocks, RANK, BLOCK), BF16),
            ((RANK, 2 * WIDTH), F32), ((RANK, D), F32),
        ],
        flops=int(75e9),
    )

    if heads_here != QUAD:
        share = RANK // row_count
        wide = jnp.swapaxes(wide.reshape(row_count, GROUPS, share, 3, WIDTH), 0, 1)
        wide = to_cols(wide, heads_here, col_count)
        wide = jnp.swapaxes(wide, 0, 1).reshape(row_count, col_count, share, 3 * local)
    corr, wide, thin = finish_exchange(corr, wide, thin)
    late = jnp.zeros((1, HALO, part), BF16)
    if seq_cols > 1:
        pairs = [(i, (i - 1) % col_count) for i in range(col_count)]
        late = lax.ppermute(corr[0:1, :HALO], "col", pairs)
        late = jnp.where(lax.rem(col, seq_cols) < seq_cols - 1, late, jnp.zeros_like(late))
    early = jnp.concatenate([corr[1:, :HALO], late], axis=0)
    early = jnp.pad(early, ((0, 0), (chunk - HALO, 0), (0, 0))).astype(F32)
    input_grad = cotangent.reshape(row_count, chunk, part).astype(F32) + corr[:, HALO:].astype(F32) + early
    input_grad = input_grad.reshape(col_tokens, part)
    wide = jnp.swapaxes(wide, 0, 1).reshape(col_count, RANK, 3 * local)
    owner = jnp.repeat(adapter_id, seq_cols)
    adapters = rank_total // RANK
    chosen = owner[:, None] == jnp.arange(adapters, dtype=jnp.int32)[None, :]
    wide = jnp.sum(jnp.where(chosen[:, :, None, None], wide[:, None], 0.0), axis=0)
    wide = wide.reshape(rank_total, 3 * local)
    in_up = wide[:, : 2 * local].reshape(rank_total, 2, heads_here, P_SIZE)
    in_up = jnp.swapaxes(in_up, 1, 2).reshape(rank_total, heads_here, 2 * P_SIZE)
    out_down = wide[:, 2 * local :]
    if rank_share <= RANK:
        mine = owner == (col * rank_share) // RANK
        thin = jnp.sum(jnp.where(mine[:, None, None], thin, 0.0), axis=0).reshape(2, RANK, part)
        thin = lax.dynamic_slice_in_dim(thin, lax.rem(col * rank_share, RANK), rank_share, 1)
        thin = jnp.swapaxes(thin, 1, 2)
    else:
        thin = jnp.sum(jnp.where(chosen[:, :, None, None], thin[:, None], 0.0), axis=0)
        thin = thin.reshape(adapters, 2, RANK, part)
        thin = jnp.transpose(thin, (1, 3, 0, 2)).reshape(2, part, rank_total)
        thin = lax.dynamic_slice_in_dim(thin, col * rank_share, rank_share, 2)
    return block_out, input_grad, thin[0], in_up, out_down, thin[1]


def solution(mesh):
    placed = (
        P("col", "row"), P("row"), P("row", "col", None), P("row", None), P(None, "col"), P("col"), P(), P(),
        P("col"), P("col"), P("col"), P("col"), P("col", "row"), P("row", None), P(None, "col", None),
        P(None, "col"), P("row", None), P(), P("col", "row"),
    )
    return jax.shard_map(
        per_device,
        mesh=mesh,
        in_specs=placed,
        out_specs=(
            P("col", "row"), P("col", "row"), P("row", "col"), P(None, "col", None), P(None, "col"),
            P("row", "col"),
        ),
        check_vma=False,
    )
```

```python
import functools

import jax
import jax.numpy as jnp
from jax import lax
from jax.experimental import pallas as pl
from jax.experimental.pallas import tpu as pltpu
from jax.sharding import PartitionSpec as P

D = 1024
HEADS = 32
P_SIZE = 64
STATES = 128
BLOCK = 256
RANK = 16
SEQ = 4096
DI = 2048
EPS = 1e-05
LOG2E = 1.4426950408889634

HALO = 16
IN_LANE = 32
OUT_LANE = 48
CAP = 80.0
QUAD = 4
WIDTH = QUAD * P_SIZE
GROUPS = HEADS // QUAD
LANES = 128
VMEM_BYTES = 60 * 1024 * 1024
F32 = jnp.float32
BF16 = jnp.bfloat16
MESH = pl.DeviceIdType.MESH


def mm(left, right):
    return jnp.dot(left, right, preferred_element_type=F32)


def mm_nt(left, right):
    return lax.dot_general(left, right, (((1,), (1,)), ((), ())), preferred_element_type=F32)


def mm_tn(left, right):
    return lax.dot_general(left, right, (((0,), (0,)), ((), ())), preferred_element_type=F32)


def split_left(ones, value):
    high = value.astype(BF16)
    rest = value - high.astype(F32)
    middle = rest.astype(BF16)
    low = (rest - middle.astype(F32)).astype(BF16)
    return mm(ones, high) + mm(ones, middle) + mm(ones, low)


def split_right(value, ones):
    high = value.astype(BF16)
    low = (value - high.astype(F32)).astype(BF16)
    return mm(high, ones) + mm(low, ones)


def sigmoid(value):
    return 0.5 * jnp.tanh(0.5 * value) + 0.5


def iota(shape, axis):
    return lax.broadcasted_iota(jnp.int32, shape, axis)


def widen(cols):
    lane = iota((cols.shape[0], LANES), 1) < P_SIZE
    left = jnp.where(lane, cols[:, 0:1], cols[:, 1:2])
    right = jnp.where(lane, cols[:, 2:3], cols[:, 3:4])
    return jnp.concatenate([left, right], axis=1)


def to_front(cols, group):
    return pltpu.roll(cols, lax.rem(LANES - QUAD * group, LANES), 1)


def lane_range(values, first):
    lane = iota(values.shape, 1)
    return jnp.where((lane >= first) & (lane < first + RANK), values, 0.0)


def out_block(w_ref, group, row, part):
    if w_ref.shape[2] == WIDTH:
        return w_ref[group, row, :, :part]
    rows = WIDTH // 2
    return jnp.concatenate([w_ref[group, row, :rows, :part], w_ref[group, row, :rows, part:]], axis=0)


def head_only(values, head):
    lane = iota(values.shape, 1) // P_SIZE
    return jnp.where(lane == head, values, jnp.zeros_like(values))


def delays(window, taps, bias):
    total = window[8:] * taps[0:1] + bias
    for k in range(1, 4):
        total = total + pltpu.roll(window, k, 0)[8:] * taps[k : k + 1]
    return total


def advances(window, taps, count):
    length = window.shape[0]
    total = window[:count] * taps[0:1]
    for k in range(1, 4):
        total = total + pltpu.roll(window, length - k, 0)[:count] * taps[k : k + 1]
    return total


def at_block(k):
    if isinstance(k, int):
        return pl.ds(k * BLOCK, BLOCK)
    return pl.ds(pl.multiple_of(k * BLOCK, BLOCK), BLOCK)


def at_rows(k):
    if isinstance(k, int):
        return pl.ds(HALO + k * BLOCK, BLOCK)
    return pl.ds(pl.multiple_of(HALO + k * BLOCK, HALO), BLOCK)


def with_halo(k):
    if k == 0:
        return pl.ds(0, HALO + BLOCK)
    return pl.ds(HALO + k * BLOCK, BLOCK)


def padded_rows(value, first):
    before = jnp.zeros((first, value.shape[1]), value.dtype)
    after = jnp.zeros((LANES - first - value.shape[0], value.shape[1]), value.dtype)
    return jnp.concatenate([before, value, after], axis=0)


def front_kernel(
    place_ref, x_ref, gain_ref, wst_ref, sp_ref, sb_ref, hp_ref, w_ref, up_ref, vp_ref,
    normed_ref, scpre_ref, ratio_ref, sig_ref, cum_ref, lead_ref, turned_ref, bs_ref, cs_ref, cs_t_ref, adv_ref,
    gate_ref, u_ref, eloc_ref, fin_ref, dec_ref,
    st_scr, bs_t_scr, val_scr,
):
    group = pl.program_id(0)
    row_count, _, part = x_ref.shape
    blocks = eloc_ref.shape[0]

    @pl.when(group == 0)
    def _():
        def project(rows):
            pieces = [x_ref[r, rows, :].astype(F32) for r in range(row_count)]
            square = sum(jnp.sum(piece * piece, axis=1, keepdims=True) for piece in pieces)
            inv = lax.rsqrt(square / D + EPS)
            total = None
            for r in range(row_count):
                normed = (pieces[r] * inv * gain_ref[r]).astype(BF16)
                normed_ref[rows, r * part : (r + 1) * part] = normed
                term = mm(normed, wst_ref[r])
                total = term if total is None else total + term
            st_scr[rows, :] = total
            adv_ref[rows, :] = lane_range(total[:, 256:384], IN_LANE).astype(BF16)

        project(pl.ds(0, HALO))

        @pl.loop(0, blocks)
        def _(k):
            project(at_rows(k))

        lower = (iota((BLOCK, BLOCK), 0) >= iota((BLOCK, BLOCK), 1)).astype(BF16)
        rate = -jnp.exp(hp_ref[1:2]) * LOG2E

        @pl.loop(0, blocks)
        def _(k):
            window = st_scr[pl.ds(pl.multiple_of(8 + k * BLOCK, 8), BLOCK + 8), :256]
            pre = delays(window, sp_ref[...], sb_ref[...])
            conv = pre * sigmoid(pre)
            b_rows = conv[:, :STATES].astype(BF16)
            c_rows = conv[:, STATES:].astype(BF16)
            scpre_ref[at_block(k), :] = pre
            bs_ref[at_block(k), :] = b_rows
            cs_ref[at_block(k), :] = c_rows
            bs_t_scr[k] = conv[:, :STATES].T.astype(BF16)
            cs_t_ref[k] = conv[:, STATES:].T.astype(BF16)
            raw = st_scr[at_rows(k), 256:384] + hp_ref[0:1]
            small = jnp.exp(-jnp.abs(raw))
            tail = jnp.where(
                small < 0.01, small * (1.0 - small * (0.5 - small * (1.0 / 3.0))), jnp.log(1.0 + small)
            )
            step = jnp.maximum(raw, 0.0) + tail
            cum = split_left(lower, step * rate)
            sig = sigmoid(raw)
            ratio_ref[at_block(k), :] = jnp.where(raw < -20.0, 1.0, sig / jnp.maximum(step, 1e-30))
            sig_ref[at_block(k), :] = sig
            lead = jnp.log(jnp.maximum(step, 1e-37)) * LOG2E - cum
            cum_ref[at_block(k), :] = cum
            lead_ref[at_block(k), :] = lead
            flipped = cum.T
            flipped_lead = lead.T
            for g in range(GROUPS):
                turned_ref[g, :QUAD, at_block(k)] = flipped[g * QUAD : (g + 1) * QUAD]
                turned_ref[g, QUAD:, at_block(k)] = flipped_lead[g * QUAD : (g + 1) * QUAD]

    up_rows = padded_rows(up_ref[0, 0], IN_LANE)

    def inner(rows):
        total = mm(adv_ref[rows, :], up_rows)
        for r in range(row_count):
            total = total + mm(normed_ref[rows, r * part : (r + 1) * part], w_ref[0, r, :part, :])
        return total

    taps = vp_ref[0]

    def one_block(k, carry):
        state, decay = carry
        product = inner(with_halo(k))
        skip = HALO if k == 0 else 0
        gate_ref[at_block(k), :] = product[skip:, :WIDTH].astype(BF16)
        val_scr[with_halo(k), :] = product[:, WIDTH:]
        window = val_scr[pl.ds(8 + k * BLOCK, BLOCK + 8), :]
        pre = delays(window, taps[0:4], taps[4:5])
        u_ref[at_block(k), :] = pre.astype(BF16)
        xs = (pre * sigmoid(pre)).astype(BF16).astype(F32)
        cum = cum_ref[at_block(k), :]
        last = cum[BLOCK - 1 : BLOCK]
        weight = to_front(jnp.exp2(last + lead_ref[at_block(k), :]), group)
        weighted = (xs * widen(weight)).astype(BF16)
        eloc_ref[k] = state.astype(BF16)
        last8 = to_front(jnp.broadcast_to(last, (8, LANES)), group)
        fall = widen(jnp.exp2(last8))[0:1]
        return fall * state + mm(bs_t_scr[k], weighted), decay * fall

    carry = (jnp.zeros((STATES, WIDTH), F32), jnp.ones((1, WIDTH), F32))
    for k in range(blocks):
        carry = one_block(k, carry)
    state, decay = carry
    fin_ref[...] = state.astype(BF16)
    dec_ref[...] = jnp.broadcast_to(decay, (8, WIDTH))


def scan_kernel(
    place_ref, x_ref, g_ref, wst_ref, w_ref, down_ref, vp_ref, gate_ref, u_ref, eloc_ref, ein_ref,
    cum_ref, turned_ref, bs_ref, cs_ref,
    out_ref, o_ref, ent_ref, aux_ref, sg_ref, gup_ref,
    score_scr, gained_scr, side_scr, square_scr,
):
    group = pl.program_id(0)
    row_count, _, part = x_ref.shape
    blocks = eloc_ref.shape[0]

    @pl.when(group == 0)
    def _():
        side_scr[...] = jnp.zeros_like(side_scr)
        square_scr[...] = jnp.zeros_like(square_scr)
        keep = iota((BLOCK, BLOCK), 0) >= iota((BLOCK, BLOCK), 1)

        @pl.loop(0, blocks)
        def _(k):
            score = mm_nt(cs_ref[at_block(k), :], bs_ref[at_block(k), :])
            score_scr[k] = jnp.where(keep, score, 0.0)

    taps = vp_ref[0]

    down_rows = padded_rows(down_ref[0, 0], OUT_LANE)

    def one_block(k, before):
        rows = at_block(k)
        pre = u_ref[rows, :].astype(F32)
        conv = pre * sigmoid(pre)
        cum = to_front(cum_ref[rows, :], group)
        xs = conv.astype(BF16)
        score = score_scr[k]
        entering = (eloc_ref[k].astype(F32) + before * ein_ref[...]).astype(BF16)
        ent_ref[k] = entering
        total = widen(jnp.exp2(cum)) * mm(cs_ref[rows, :], entering)
        for h in range(QUAD):
            spread = cum[:, h : h + 1] + turned_ref[0, QUAD + h : QUAD + h + 1, rows]
            weights = (score * jnp.exp2(jnp.minimum(spread, CAP))).astype(BF16)
            total = total + mm(weights, head_only(xs, h))
        output = total + taps[6:7] * conv
        o_ref[rows, :] = output.astype(BF16)
        gate = gate_ref[rows, :].astype(F32)
        gated = output * gate * sigmoid(gate)
        square = gated * gated
        square_scr[rows, :] += square[:, :LANES] + square[:, LANES:]
        gained = (gated * taps[5:6]).astype(BF16)
        gained_scr[group, rows, :] = gained
        side_scr[rows, :] += mm_nt(gained, down_rows)
        return before * widen(jnp.exp2(cum[BLOCK - 8 :]))[7:8]

    before = jnp.ones((1, WIDTH), F32)
    for k in range(blocks):
        before = one_block(k, before)

    @pl.when(group == pl.num_programs(0) - 1)
    def _():
        gup_ref[...] = jnp.zeros_like(gup_ref)

        @pl.loop(0, blocks)
        def _(k):
            rows = at_block(k)
            mean = jnp.sum(square_scr[rows, :], axis=1, keepdims=True) / DI
            rms = lax.rsqrt(mean + EPS)
            side_raw = side_scr[rows, :]
            side = (side_raw * rms).astype(BF16)
            side_grad = None
            for r in range(row_count):
                term = mm(g_ref[r, rows, :], wst_ref[r, :, 256:384])
                side_grad = term if side_grad is None else side_grad + term
            side_grad = lane_range(side_grad, OUT_LANE).astype(BF16)
            product = jnp.sum(side_grad.astype(F32) * side_raw, axis=1, keepdims=True)
            for r in range(row_count):
                cols = slice(r * part, (r + 1) * part)
                raw = mm(gained_scr[0, rows, :], out_block(w_ref, 0, r, part))
                for c in range(1, GROUPS):
                    raw = raw + mm(gained_scr[c, rows, :], out_block(w_ref, c, r, part))
                cot = g_ref[r, rows, :]
                product = product + jnp.sum(raw * cot.astype(F32), axis=1, keepdims=True)
                total = x_ref[r, at_rows(k), :].astype(F32) + raw * rms + mm_nt(side, wst_ref[r, :, 256:384])
                out_ref[r, rows, :] = total.astype(BF16)
                gup_ref[:, cols] += mm_tn(side, cot)[OUT_LANE : OUT_LANE + RANK]
            coefficient = rms * rms * rms * product / DI
            lane = iota((BLOCK, LANES), 1)
            aux_ref[rows, :] = jnp.where(lane == 0, rms, coefficient)
            sg_ref[rows, :] = side_grad


def gate_kernel(
    place_ref, g_ref, w_ref, sg_ref, down_ref, vp_ref, gate_ref, o_ref, aux_ref, cum_ref, cs_t_ref,
    dgate_ref, dy_ref, gloc_ref, gfin_ref, gdown_ref,
    sg_t_scr,
):
    group = pl.program_id(0)
    row_count, _, part = g_ref.shape
    blocks = gloc_ref.shape[0]

    @pl.when(group == 0)
    def _():
        @pl.loop(0, blocks)
        def _(k):
            sg_t_scr[k] = sg_ref[at_block(k), :].astype(F32).T[OUT_LANE : OUT_LANE + RANK].astype(BF16)

    taps = vp_ref[0]
    gdown_ref[0] = jnp.zeros((RANK, WIDTH), F32)

    down_rows = padded_rows(down_ref[0, 0], OUT_LANE)

    def one_block(i, state):
        k = blocks - 1 - i
        rows = at_block(k)
        dmix = mm(sg_ref[rows, :], down_rows)
        for r in range(row_count):
            dmix = dmix + mm_nt(g_ref[r, rows, :], out_block(w_ref, 0, r, part))
        gate = gate_ref[rows, :].astype(F32)
        output = o_ref[rows, :].astype(F32)
        sig = sigmoid(gate)
        act = gate * sig
        gated = output * act
        rms = aux_ref[rows, 0:1]
        coefficient = aux_ref[rows, 1:2]
        scale = rms * taps[5:6]
        mixed = (gated * scale).astype(BF16)
        gdown_ref[0] += mm(sg_t_scr[k], mixed)
        gated_grad = scale * dmix - gated * coefficient
        dy = gated_grad * act
        dgate = gated_grad * output * (sig + act * (1.0 - sig))
        dgate_ref[rows, :] = dgate.astype(BF16)
        dy_ref[rows, :] = dy.astype(BF16)
        cum = to_front(cum_ref[rows, :], group)
        factor = widen(jnp.exp2(cum))
        gloc_ref[k] = state.astype(BF16)
        return factor[BLOCK - 1 : BLOCK] * state + mm(cs_t_ref[k], (factor * dy).astype(BF16))

    state = jnp.zeros((STATES, WIDTH), F32)
    for i in range(blocks):
        state = one_block(i, state)
    gfin_ref[...] = state.astype(BF16)


def back_kernel(
    place_ref, x_ref, gain_ref, normed_ref, wst_ref, w_ref, up_ref, adv_ref, vp_ref, sp_ref, hp_ref,
    u_ref, o_ref, dy_ref, dgate_ref, ent_ref, gloc_ref, gin_ref,
    cum_ref, lead_ref, turned_ref, ratio_ref, sig_ref, scpre_ref, bs_ref, cs_ref, out_down_ref, out_up_ref,
    corr_ref, wide_ref, thin_ref,
    score_scr, dscore_scr, db_scr, dc_scr, dcum_scr, dstep_scr, dlast_scr, du_scr, ig_scr, ng_scr, adg_scr, adv_t_scr, up_scr, in_scr,
):
    group = pl.program_id(0)
    row_count, _, part = x_ref.shape
    blocks = gloc_ref.shape[0]
    total_rows = normed_ref.shape[0]

    @pl.when(group == 0)
    def _():
        for ref in (dscore_scr, db_scr, dc_scr, dcum_scr, dstep_scr, dlast_scr, ng_scr, adg_scr):
            ref[...] = jnp.zeros_like(ref)
        du_scr[0:HALO, :] = jnp.zeros((HALO, WIDTH), F32)
        du_scr[total_rows : total_rows + HALO, :] = jnp.zeros((HALO, WIDTH), F32)

        @pl.loop(0, blocks)
        def _(k):
            score_scr[k] = mm_nt(bs_ref[at_block(k), :], cs_ref[at_block(k), :])
            adv_t_scr[k] = adv_ref[at_rows(k), :].astype(F32).T[IN_LANE : IN_LANE + RANK].astype(BF16)

    keep = iota((BLOCK, BLOCK), 0) <= iota((BLOCK, BLOCK), 1)
    taps = vp_ref[0]
    pick = (iota((WIDTH, LANES), 1) == QUAD * group + iota((WIDTH, LANES), 0) // P_SIZE).astype(BF16)

    def one_block(i, after):
        k = blocks - 1 - i
        rows = at_block(k)
        pre = u_ref[rows, :].astype(F32)
        sig = sigmoid(pre)
        conv = pre * sig
        xs_low = conv.astype(BF16)
        xs = xs_low.astype(F32)
        cum = to_front(cum_ref[rows, :], group)
        lead = to_front(lead_ref[rows, :], group)
        dy_low = dy_ref[rows, :]
        dy = dy_low.astype(F32)
        b_rows = bs_ref[rows, :]
        c_rows = cs_ref[rows, :]
        score = jnp.where(keep, score_scr[k], 0.0)
        dscore = dscore_scr[k]
        ending = gloc_ref[k].astype(F32) + after * gin_ref[...]
        ending_low = ending.astype(BF16)
        last = cum[BLOCK - 1 : BLOCK]
        to_end = widen(jnp.exp2(last + lead))
        dxs_state = to_end * mm(b_rows, ending_low)
        dxs = dxs_state
        for h in range(QUAD):
            spread = turned_ref[0, h : h + 1, rows] + lead[:, h : h + 1]
            damp = jnp.exp2(jnp.minimum(spread, CAP))
            weights = (score * damp).astype(BF16)
            dy_head = head_only(dy_low, h)
            dxs = dxs + mm(weights, dy_head)
            dscore = dscore + mm_nt(xs_low, dy_head) * damp
        dscore_scr[k] = dscore
        from_start = widen(jnp.exp2(cum))
        fall = from_start[BLOCK - 1 : BLOCK]
        entering_low = ent_ref[k]
        entering = entering_low.astype(F32)
        dc_scr[rows, :] += mm_nt((from_start * dy).astype(BF16), entering_low)
        db_scr[rows, :] += mm_nt((to_end * xs).astype(BF16), ending_low)
        scan_out = o_ref[rows, :].astype(F32) - taps[6:7] * conv
        inward = mm((xs * dxs).astype(BF16), pick)
        dcum_scr[rows, :] += mm((dy * scan_out).astype(BF16), pick) - inward
        dstep_scr[rows, :] += inward
        ends = jnp.sum(xs * dxs_state, axis=0, keepdims=True)
        ends = ends + fall * jnp.sum(entering * ending, axis=0, keepdims=True)
        dlast_scr[k] += split_right(jnp.broadcast_to(ends, (8, WIDTH)), pick)
        dconv = taps[6:7] * dy + dxs
        du_scr[at_rows(k), :] = dconv * (sig + conv * (1.0 - sig))
        return after * fall

    after = jnp.ones((1, WIDTH), F32)
    for i in range(blocks):
        after = one_block(i, after)
    up_rows = padded_rows(up_ref[0, 0], IN_LANE)

    ig_scr[0:HALO, :WIDTH] = jnp.zeros((HALO, WIDTH), BF16)
    for k in range(blocks):
        rows = with_halo(k)
        extra = HALO if k == 0 else 0
        ig_scr[at_rows(k), :WIDTH] = dgate_ref[at_block(k), :]
        window = du_scr[pl.ds(HALO + k * BLOCK - extra, BLOCK + extra + 8), :]
        ig_scr[rows, WIDTH:] = advances(window, taps[0:4], BLOCK + extra).astype(BF16)
        grad = ig_scr[rows, :]
        adg_scr[rows, :] += mm_nt(grad, up_rows)
        for r in range(row_count):
            ng_scr[rows, r * part : (r + 1) * part] += mm_nt(grad, w_ref[0, r, :part, :])
        if k == 0:
            up_scr[...] = mm_tn(adv_ref[0:HALO, :], grad[:HALO])[IN_LANE : IN_LANE + RANK]
        up_scr[...] += mm(adv_t_scr[k], grad[extra:])

    share = RANK // row_count
    for r in range(row_count):
        wide_ref[r, 0, :, : 2 * WIDTH] = up_scr[r * share : (r + 1) * share, :]
        wide_ref[r, 0, :, 2 * WIDTH :] = out_down_ref[0, r * share : (r + 1) * share, :]

    @pl.when(group == pl.num_programs(0) - 1)
    def _():
        upper = (iota((BLOCK, BLOCK), 0) <= iota((BLOCK, BLOCK), 1)).astype(BF16)
        rate = -jnp.exp(hp_ref[1:2])

        @pl.loop(0, blocks)
        def _(k):
            rows = at_block(k)
            dscore = jnp.where(keep, dscore_scr[k], 0.0).astype(BF16)
            db = db_scr[rows, :] + mm(dscore, cs_ref[rows, :])
            dc = dc_scr[rows, :] + mm_tn(dscore, bs_ref[rows, :])
            pre = scpre_ref[rows, :]
            sig = sigmoid(pre)
            slope = sig + pre * sig * (1.0 - sig)
            du_scr[at_rows(k), :] = jnp.concatenate([db, dc], axis=1) * slope
            is_last = iota((BLOCK, LANES), 0) == BLOCK - 1
            dcum = dcum_scr[rows, :] + jnp.where(is_last, dlast_scr[k, 0:1, :], 0.0)
            slower = split_left(upper, dcum) * (rate * sig_ref[rows, :])
            dstep_scr[rows, :] = dstep_scr[rows, :] * ratio_ref[rows, :] + slower

        def finish(rows, window, count, draw):
            dstate = advances(window, sp_ref[...], count).astype(BF16)
            adapt = adg_scr[rows, :].astype(BF16)
            mixed = adapt + draw
            total = jnp.zeros((count, 1), F32)
            square = jnp.zeros((count, 1), F32)
            grads = []
            for r in range(row_count):
                cols = slice(r * part, (r + 1) * part)
                grad = ng_scr[rows, cols] + mm_nt(dstate, wst_ref[r, :, 0:256])
                grad = grad + mm_nt(mixed, wst_ref[r, :, 256:384])
                grad = grad * gain_ref[r]
                piece = x_ref[r, rows, :].astype(F32)
                total = total + jnp.sum(piece * grad, axis=1, keepdims=True)
                square = square + jnp.sum(piece * piece, axis=1, keepdims=True)
                grads.append(grad)
                in_scr[:, cols] += mm_tn(adapt, normed_ref[rows, cols])[IN_LANE : IN_LANE + RANK]
            inv = lax.rsqrt(square / D + EPS)
            factor = inv * inv * inv * total / D
            for r in range(row_count):
                piece = x_ref[r, rows, :].astype(F32)
                corr_ref[r, rows, :] = (inv * grads[r] - factor * piece).astype(BF16)

        in_scr[...] = jnp.zeros_like(in_scr)
        for k in range(blocks):
            extra = HALO if k == 0 else 0
            window = du_scr[pl.ds(HALO + k * BLOCK - extra, BLOCK + extra + 8), :]
            draw = dstep_scr[at_block(k), :].astype(BF16)
            if k == 0:
                draw = jnp.concatenate([jnp.zeros((HALO, LANES), BF16), draw], axis=0)
            finish(with_halo(k), window, BLOCK + extra, draw)

        for r in range(row_count):
            thin_ref[r, 0:RANK, :] = in_scr[:, r * part : (r + 1) * part]
            thin_ref[r, RANK:, :] = out_up_ref[:, r * part : (r + 1) * part]


def on_row(row):
    return {"row": row}


def on_col(col):
    return {"col": col}


def tail_kernel(
    corr_ref, wide_ref, thin_ref,
    corr_out, wide_out, thin_out,
    wide_pair, thin_pair, wide_both, thin_both, wide_scr, thin_scr, wide_sum, thin_sum, wide_col,
    own_sem, corr_send, corr_recv, pair_send, pair_recv, row_send, row_recv, col_send, col_recv, last_send, last_recv,
    core_send, core_recv,
):
    row_count = corr_ref.shape[0]
    col_count = thin_out.shape[0]
    row = lax.axis_index("row")
    col = lax.axis_index("col")
    barrier = pltpu.get_barrier_semaphore()
    for d in range(1, row_count):
        pl.semaphore_signal(barrier, inc=1, device_id=on_row(lax.rem(row + d, row_count)), device_id_type=MESH)
    for d in range(1, col_count):
        pl.semaphore_signal(barrier, inc=1, device_id=on_col(lax.rem(col + d, col_count)), device_id_type=MESH)
    pl.semaphore_wait(barrier, row_count + col_count - 2)

    def send(source, target, sends, recvs, index, device):
        copy = pltpu.make_async_remote_copy(
            src_ref=source, dst_ref=target, send_sem=sends.at[index], recv_sem=recvs.at[index],
            device_id=device, device_id_type=MESH,
        )
        copy.start()
        return copy

    chips = row_count // 2
    parity = lax.rem(row, 2)
    chip = row // 2
    core = row + 1 - 2 * parity
    first = []
    for j in range(chips):
        theirs = 2 * j + 1 - parity
        first.append(send(wide_ref.at[theirs], wide_pair.at[j], pair_send, pair_recv, j, on_row(core)))
        first.append(send(thin_ref.at[theirs], thin_pair.at[j], pair_send, pair_recv, chips + j, on_row(core)))
    moved = []
    for d in range(1, row_count):
        peer = lax.rem(row + d, row_count)
        moved.append(send(corr_ref.at[peer], corr_out.at[row], corr_send, corr_recv, d, on_row(peer)))
    own = pltpu.make_async_copy(corr_ref.at[row], corr_out.at[row], own_sem.at[0])
    own.start()
    for copy in first:
        copy.wait()
    for j in range(chips):
        wide_both[j] = wide_ref[2 * j + parity] + wide_pair[j]
        thin_both[j] = thin_ref[2 * j + parity] + thin_pair[j]
    across = []
    for d in range(1, chips):
        there = lax.rem(chip + d, chips)
        peer = on_row(2 * there + parity)
        across.append(send(wide_both.at[there], wide_scr.at[chip], row_send, row_recv, d, peer))
        across.append(send(thin_both.at[there], thin_scr.at[chip], row_send, row_recv, chips + d, peer))
    for copy in across:
        copy.wait()
    wide = wide_both[chip]
    thin = thin_both[chip]
    for d in range(1, chips):
        there = lax.rem(chip + d, chips)
        wide = wide + wide_scr[there]
        thin = thin + thin_scr[there]
    wide_sum[...] = wide
    thin_sum[...] = thin
    second = []
    for d in range(1, col_count):
        peer = lax.rem(col + d, col_count)
        second.append(send(wide_sum.at[peer], wide_col.at[col], col_send, col_recv, d, on_col(peer)))
        second.append(send(thin_sum, thin_out.at[col], col_send, col_recv, col_count + d, on_col(peer)))
    wide_col[col] = wide_sum[col]
    thin_out[col] = thin
    for copy in second:
        copy.wait()
    third = []
    for d in range(1, chips):
        there = lax.rem(chip + d, chips)
        third.append(send(wide_col, wide_out.at[row], last_send, last_recv, d, on_row(2 * there + parity)))
    fourth = [send(wide_col, wide_out.at[row], core_send, core_recv, 0, on_row(core))]
    wide_out[row] = wide_col[...]
    for d in range(1, chips):
        third[d - 1].wait_recv()
        source = 2 * lax.rem(chip + chips - d, chips) + parity
        fourth.append(send(wide_out.at[source], wide_out.at[source], core_send, core_recv, d, on_row(core)))
    for copy in third:
        copy.wait_send()
    for copy in fourth:
        copy.wait()
    for copy in moved:
        copy.wait()
    own.wait()


def start_kernel(
    x_ref, w_ref, up_ref, p_ref, down_ref, state_ref, in_ref, out_ref, gain_ref, conv_ref, bias_ref, gate_ref, step_ref, rate_ref,
    skip_ref, adapter_ref,
    x_out, w_out, shared_out, gain_out, vec_out, head_out, place_out,
    block_scr, zero_scr, shared_ref,
    own_sem, send_sem, recv_sem, row_send, row_recv, col_send, col_recv,
):
    col_count, row_count = w_out.shape[:2]
    high_count = col_count // 2
    part = x_ref.shape[1]
    chunk = x_ref.shape[0] // row_count
    rank_part = up_ref.shape[0] // row_count
    row = lax.axis_index("row")
    col = lax.axis_index("col")
    low = lax.rem(col, 2)
    high = col // 2
    core = row + 1 - 2 * lax.rem(row, 2)
    across = lax.rem(row + 2, row_count)
    side = col + 1 - 2 * low
    barrier = pltpu.get_barrier_semaphore()
    for d in range(1, row_count):
        pl.semaphore_signal(barrier, inc=1, device_id=on_row(lax.rem(row + d, row_count)), device_id_type=MESH)
    for d in range(1, col_count):
        pl.semaphore_signal(barrier, inc=1, device_id=on_col(lax.rem(col + d, col_count)), device_id_type=MESH)

    def paired(value):
        lane = iota((value.shape[0], LANES), 1) < P_SIZE
        tiles = [value[:, h * LANES : (h + 1) * LANES].astype(F32) for h in range(QUAD)]
        turned = [pltpu.roll(tile, P_SIZE, 1) for tile in tiles]
        gates = [jnp.where(lane, tiles[h], turned[h + 1]) for h in (0, 2)]
        values = [jnp.where(lane, turned[h], tiles[h + 1]) for h in (0, 2)]
        return jnp.concatenate(gates + values, axis=1).astype(BF16)

    block_scr[0:part, :] = paired(w_ref[...])
    ranks = pl.ds(pl.multiple_of(row * rank_part, rank_part), rank_part)
    block_scr[part : part + rank_part, :] = paired(up_ref[ranks, :])
    first = part + rank_part
    half = WIDTH // 2
    block_scr[first : first + half, :WIDTH] = p_ref[:half, :]
    block_scr[first : first + half, WIDTH:] = p_ref[half:, :]
    first = first + half
    downs = down_ref[ranks, :]
    block_scr[first : first + rank_part // 2, :WIDTH] = downs[: rank_part // 2]
    block_scr[first : first + rank_part // 2, WIDTH:] = downs[rank_part // 2 :]
    zero_scr[...] = jnp.zeros_like(zero_scr)
    adapter = adapter_ref[col]
    shift = adapter * RANK
    per_part = rank_part // RANK
    place_out[0] = adapter // per_part
    place_out[1] = adapter - adapter // per_part * per_part
    source = iota((LANES, LANES), 0) - shift
    target = iota((LANES, LANES), 1)
    chosen = (source >= 0) & (source < RANK)
    ins = (chosen & (source == target - IN_LANE)).astype(F32).astype(BF16)
    outs = (chosen & (source == target - OUT_LANE)).astype(F32).astype(BF16)
    states = 2 * STATES
    shared_ref[:, :states] = state_ref[:states, :].astype(F32).T.astype(BF16)
    steps = jnp.concatenate(
        [state_ref[states:, :].astype(F32), jnp.zeros((LANES - HEADS, part), F32)], axis=0
    ).T
    shared_ref[:, states:] = (steps + mm(in_ref[...], ins) + mm(out_ref[...], outs)).astype(BF16)
    vec_out[col, 0:4, :] = conv_ref[...]
    vec_out[col, 4:5, :] = bias_ref[...]
    vec_out[col, 5:6, :] = gate_ref[...]
    vec_out[col, 6:7, :] = widen(skip_ref[...])
    lane = iota((1, WIDTH), 1)
    scalars = jnp.zeros((1, WIDTH), F32)
    for h in range(QUAD):
        scalars = jnp.where(lane == h, step_ref[:, h : h + 1], scalars)
        scalars = jnp.where(lane == QUAD + h, rate_ref[:, h : h + 1], scalars)
    vec_out[col, 7:8, :] = scalars
    gain_out[row] = gain_ref[...]
    pl.semaphore_wait(barrier, row_count + col_count - 2)

    def remote(source, target, sends, recvs, index, device):
        return pltpu.make_async_remote_copy(
            src_ref=source, dst_ref=target, send_sem=sends.at[index], recv_sem=recvs.at[index],
            device_id=device, device_id_type=MESH,
        )

    own_block = pltpu.make_async_copy(block_scr, w_out.at[col, row], own_sem.at[0])
    own_block.start()

    def whole_window(target, slot, index, peer):
        source = x_ref.at[pl.ds(pl.multiple_of(target * chunk - HALO, HALO), chunk + HALO)]
        return remote(source, x_out.at[slot], row_send, row_recv, index, on_row(peer))

    def first_window(slot, index, peer):
        source = x_ref.at[pl.ds(0, chunk)]
        return remote(source, x_out.at[slot, pl.ds(HALO, chunk)], row_send, row_recv, index, on_row(peer))

    def each_window(sending, act):
        for d in range(1, row_count):
            peer = lax.rem(row + d, row_count)
            chosen = peer if sending else row
            slot = row if sending else lax.rem(row + row_count - d, row_count)

            @pl.when(chosen > 0)
            def _():
                act(whole_window(jnp.maximum(chosen, 1), slot, d, peer))

            @pl.when(chosen == 0)
            def _():
                act(first_window(slot, d, peer))

    @pl.when(row > 0)
    def _():
        source = x_ref.at[pl.ds(pl.multiple_of(jnp.maximum(row, 1) * chunk - HALO, HALO), chunk + HALO)]
        pltpu.make_async_copy(source, x_out.at[row], own_sem.at[1]).start()

    @pl.when(row == 0)
    def _():
        pltpu.make_async_copy(x_ref.at[pl.ds(0, chunk)], x_out.at[row, pl.ds(HALO, chunk)], own_sem.at[1]).start()
        for r in range(row_count):
            pltpu.make_async_copy(zero_scr, x_out.at[r, pl.ds(0, HALO)], own_sem.at[3 + r]).start()

    own_shared = pltpu.make_async_copy(shared_ref, shared_out.at[row], own_sem.at[2])
    own_shared.start()
    small = []
    for d in range(1, col_count):
        peer = lax.rem(col + d, col_count)
        small.append(remote(vec_out.at[col], vec_out.at[col], col_send, col_recv, d, on_col(peer)))
    for d in range(1, row_count):
        peer = lax.rem(row + d, row_count)
        small.append(remote(shared_ref, shared_out.at[row], row_send, row_recv, row_count + d, on_row(peer)))
        small.append(
            remote(gain_out.at[row], gain_out.at[row], row_send, row_recv, 2 * row_count + d, on_row(peer))
        )
    for copy in small:
        copy.start()

    cut = (w_out.shape[2] * 65 // 100 + 8) // 16 * 16
    spans = (pl.ds(0, cut), pl.ds(cut, w_out.shape[2] - cut))
    has_up = high < high_count - 1
    has_down = high > 0
    routes = {
        "up": (0, has_up, on_col(lax.rem(col + 2, col_count))),
        "down": (1, has_down, on_col(lax.rem(col + col_count - 2, col_count))),
        "x": (2, None, on_col(side)),
        "y": (3, None, on_row(across)),
        "core": (4, None, on_row(core)),
    }

    def piece(section, c, r, kind, device):
        ref = w_out.at[c, r, spans[section]]
        return pltpu.make_async_remote_copy(
            src_ref=ref, dst_ref=ref, send_sem=send_sem.at[section, c, r, kind],
            recv_sem=recv_sem.at[section, c, r], device_id=device, device_id_type=MESH,
        )

    def event(starting, section, c, r, names, arrives=True, valid=None):
        def act():
            if starting and arrives:
                piece(section, c, r, 4, on_row(core)).wait_recv()
            for name in names:
                kind, allowed, device = routes[name]
                copy = piece(section, c, r, kind, device)
                if allowed is None:
                    copy.start() if starting else copy.wait_send()
                else:

                    @pl.when(allowed)
                    def _():
                        copy.start() if starting else copy.wait_send()

        if valid is None:
            act()
        else:
            pl.when(valid)(act)

    def far(column, step, distance):
        return lax.rem(column + step * distance + 4 * col_count, col_count)

    def within(step, distance):
        return high >= distance if step < 0 else high + distance < high_count

    onward = {-2: "up", 2: "down"}

    def along(starting, section, distance):
        for step in (-2, 2):
            valid = within(step, distance)
            if section == 0:
                names = (onward[step], "y", "x", "core")
                event(starting, 0, far(col, step, distance), row, names, valid=valid)
            else:
                for column, r in ((col, row), (side, row), (col, across), (side, across)):
                    event(starting, 1, far(column, step, distance), r, (onward[step], "core"), valid=valid)

    def over(starting, distance):
        for step in (-2, 2):
            valid = within(step, distance)
            event(starting, 0, far(side, step, distance), row, ("core",), valid=valid)
            event(starting, 0, far(col, step, distance), across, ("x", "core"), valid=valid)

    def last(starting, distance):
        for step in (-2, 2):
            event(starting, 0, far(side, step, distance), across, ("core",), valid=within(step, distance))

    def relay(starting):
        def windows():
            if starting:
                each_window(True, lambda copy: copy.start())

        event(starting, 0, col, row, ("up", "down"), arrives=False)
        event(starting, 1, col, row, ("x", "y"), arrives=False)
        event(starting, 0, col, row, ("y", "x", "core"), arrives=False)
        event(starting, 1, col, row, ("core",), arrives=False)
        event(starting, 1, side, row, ("y", "core"))
        along(starting, 0, 1)
        event(starting, 1, col, row, ("up", "down"), arrives=False)
        event(starting, 0, col, across, ("x", "core"))
        event(starting, 1, side, row, ("up", "down"), arrives=False)
        event(starting, 1, col, across, ("up", "down", "core"))
        for d in range(2, high_count - 1):
            along(starting, 0, d)
        event(starting, 1, side, across, ("up", "down", "core"))
        over(starting, 1)
        along(starting, 0, high_count - 1)
        windows()
        along(starting, 1, 1)
        over(starting, 2)
        event(starting, 0, side, row, ("core",))
        event(starting, 0, side, across, ("core",))
        last(starting, 1)
        for d in range(2, high_count):
            if d > 2:
                over(starting, d)
            along(starting, 1, d)
            if d > 2:
                last(starting, d - 1)
        last(starting, high_count - 1)

    own_block.wait()
    relay(True)
    for copy in small:
        copy.wait()
    lane = iota((1, LANES), 1) < QUAD
    steps = jnp.zeros((1, LANES), F32)
    rates = jnp.zeros((1, LANES), F32)
    for c in range(col_count):
        values = vec_out[c, 7:8, :LANES]
        steps = steps + pltpu.roll(jnp.where(lane, values, 0.0), (QUAD * c) % LANES, 1)
        values = pltpu.roll(values, LANES - QUAD, 1)
        rates = rates + pltpu.roll(jnp.where(lane, values, 0.0), (QUAD * c) % LANES, 1)
    head_out[...] = jnp.concatenate([steps, rates, jnp.zeros((6, LANES), F32)], axis=0)
    own_shared.wait()
    each_window(True, lambda copy: copy.wait_send())
    each_window(False, lambda copy: copy.wait_recv())

    @pl.when(row > 0)
    def _():
        source = x_ref.at[pl.ds(0, chunk + HALO)]
        pltpu.make_async_copy(source, x_out.at[row], own_sem.at[1]).wait()

    @pl.when(row == 0)
    def _():
        pltpu.make_async_copy(x_ref.at[pl.ds(0, chunk)], x_out.at[row, pl.ds(HALO, chunk)], own_sem.at[1]).wait()
        for r in range(row_count):
            pltpu.make_async_copy(zero_scr, x_out.at[r, pl.ds(0, HALO)], own_sem.at[3 + r]).wait()

    core_across = lax.rem(core + 2, row_count)
    for c in range(col_count):
        for r in (core, core_across):
            for section in range(2):
                piece(section, c, r, 4, on_row(core)).wait_recv()
    relay(False)


def start_exchange(x, w, up, p, down, shared, vectors, adapter_id, row_count, col_count):
    part = x.shape[1]
    rank_part = up.shape[0] // row_count
    block_rows = part + rank_part + WIDTH // 2 + rank_part // 2
    chunk = x.shape[0] // row_count
    vmem = pl.BlockSpec(memory_space=pltpu.VMEM)
    anywhere = pl.BlockSpec(memory_space=pl.ANY)
    dma = pltpu.SemaphoreType.DMA
    return pl.pallas_call(
        start_kernel,
        in_specs=[anywhere] + [vmem] * (7 + len(vectors)) + [pl.BlockSpec(memory_space=pltpu.SMEM)],
        out_specs=[anywhere] * 3 + [vmem] * 3 + [pl.BlockSpec(memory_space=pltpu.SMEM)],
        out_shape=[
            jax.ShapeDtypeStruct((row_count, chunk + HALO, part), BF16),
            jax.ShapeDtypeStruct((col_count, row_count, block_rows, 2 * WIDTH), BF16),
            jax.ShapeDtypeStruct((row_count, part, 384), BF16),
            jax.ShapeDtypeStruct((row_count, 1, part), F32),
            jax.ShapeDtypeStruct((col_count, 8, WIDTH), F32),
            jax.ShapeDtypeStruct((8, LANES), F32),
            jax.ShapeDtypeStruct((2,), jnp.int32),
        ],
        scratch_shapes=[
            pltpu.VMEM((block_rows, 2 * WIDTH), BF16), pltpu.VMEM((HALO, part), BF16),
            pltpu.VMEM((part, 384), BF16), dma((3 + row_count,)), dma((2, col_count, row_count, 5)), dma((2, col_count, row_count)),
            dma((3 * row_count,)), dma((3 * row_count,)), dma((col_count,)), dma((col_count,)),
        ],
        compiler_params=pltpu.CompilerParams(
            collective_id=1, has_side_effects=True, vmem_limit_bytes=VMEM_BYTES
        ),
    )(x, w, up, p, down, *shared, *vectors, adapter_id)


def carry_kernel(
    forward, state_ref, decay_ref,
    out_ref,
    other_scr, other_decay, total_scr, total_in,
    core_send, core_recv, across_send, across_recv, share_send, share_recv,
):
    row = lax.axis_index("row")
    parity = lax.rem(row, 2)
    chip = row // 2
    core = row + 1 - 2 * parity
    across = lax.rem(row + 2, 4)
    barrier = pltpu.get_barrier_semaphore()
    for peer in (core, across):
        pl.semaphore_signal(barrier, inc=1, device_id=on_row(peer), device_id_type=MESH)
    pl.semaphore_wait(barrier, 2)

    def remote(source, target, sends, recvs, index, peer):
        return pltpu.make_async_remote_copy(
            src_ref=source, dst_ref=target, send_sem=sends.at[index], recv_sem=recvs.at[index],
            device_id=on_row(peer), device_id_type=MESH,
        )

    swaps = [
        remote(state_ref, other_scr, core_send, core_recv, 0, core),
        remote(decay_ref, other_decay, core_send, core_recv, 1, core),
    ]
    for copy in swaps:
        copy.start()
    for copy in swaps:
        copy.wait()
    half = state_ref.shape[1] // 2
    rows = state_ref.shape[0] // 2
    second = parity == (1 if forward else 0)
    sends = chip == (0 if forward else 1)

    @pl.when(sends)
    def _():
        for p in range(2):

            @pl.when(parity == p)
            def _():
                cols = slice(p * half, (p + 1) * half)
                for q in range(2):
                    part = slice(q * rows, (q + 1) * rows)
                    mine = state_ref[part, cols].astype(F32)
                    other = other_scr[part, cols].astype(F32)
                    late = mine + other * decay_ref[0:1, cols]
                    early = other + mine * other_decay[0:1, cols]
                    total_scr[q] = jnp.where(second, late, early).astype(BF16)
                    remote(total_scr.at[q], total_in.at[p, q], across_send, across_recv, q, across).start()
        out_ref[...] = jnp.where(second, other_scr[...].astype(F32), 0.0)
        for q in range(2):
            remote(total_scr.at[q], total_in.at[parity, q], across_send, across_recv, q, across).wait_send()

    @pl.when(jnp.logical_not(sends))
    def _():
        for q in range(2):
            remote(total_scr.at[q], total_in.at[parity, q], across_send, across_recv, q, across).wait_recv()
            remote(
                total_in.at[parity, q], total_in.at[parity, q], share_send, share_recv, q, core
            ).start()
        for q in range(2):
            remote(
                total_in.at[parity, q], total_in.at[1 - parity, q], share_send, share_recv, q, core
            ).wait()
        for p in range(2):
            for q in range(2):
                cols = slice(p * half, (p + 1) * half)
                part = slice(q * rows, (q + 1) * rows)
                total = total_in[p, q].astype(F32)
                later = other_scr[part, cols].astype(F32) + total * other_decay[0:1, cols]
                out_ref[part, cols] = jnp.where(second, later, total)


def carry_over(state, decay, forward):
    vmem = pl.BlockSpec(memory_space=pltpu.VMEM)
    dma = pltpu.SemaphoreType.DMA
    rows, cols = state.shape
    return pl.pallas_call(
        functools.partial(carry_kernel, forward),
        in_specs=[vmem, vmem],
        out_specs=vmem,
        out_shape=jax.ShapeDtypeStruct(state.shape, F32),
        scratch_shapes=[
            pltpu.VMEM(state.shape, BF16), pltpu.VMEM(decay.shape, F32),
            pltpu.VMEM((2, rows // 2, cols // 2), BF16), pltpu.VMEM((2, 2, rows // 2, cols // 2), BF16),
            dma((2,)), dma((2,)), dma((2,)), dma((2,)), dma((2,)), dma((2,)),
        ],
        compiler_params=pltpu.CompilerParams(
            collective_id=2 if forward else 3, has_side_effects=True, vmem_limit_bytes=VMEM_BYTES
        ),
    )(state, decay)


def finish_exchange(corr, wide, thin):
    row_count = corr.shape[0]
    col_count = wide.shape[1]
    share, width = wide.shape[2:]
    vmem = pl.BlockSpec(memory_space=pltpu.VMEM)
    anywhere = pl.BlockSpec(memory_space=pl.ANY)
    dma = pltpu.SemaphoreType.DMA
    return pl.pallas_call(
        tail_kernel,
        in_specs=[anywhere, vmem, vmem],
        out_specs=[anywhere, vmem, vmem],
        out_shape=[
            jax.ShapeDtypeStruct(corr.shape, corr.dtype),
            jax.ShapeDtypeStruct((row_count, col_count, share, width), F32),
            jax.ShapeDtypeStruct((col_count,) + thin.shape[1:], F32),
        ],
        scratch_shapes=[
            *[pltpu.VMEM((row_count // 2,) + value.shape[1:], F32) for value in (wide, thin) * 3],
            pltpu.VMEM(wide.shape[1:], F32), pltpu.VMEM(thin.shape[1:], F32), pltpu.VMEM(wide.shape[1:], F32),
            dma((1,)), dma((row_count,)), dma((row_count,)), dma((row_count,)), dma((row_count,)),
            dma((row_count,)), dma((row_count,)), dma((2 * col_count,)), dma((2 * col_count,)),
            dma((row_count // 2,)), dma((row_count // 2,)), dma((row_count // 2,)), dma((row_count // 2,)),
        ],
        compiler_params=pltpu.CompilerParams(
            collective_id=0, has_side_effects=True, vmem_limit_bytes=VMEM_BYTES
        ),
    )(corr, wide, thin)


def whole_spec(shape):
    return pl.BlockSpec(shape, lambda c, s: (0,) * len(shape))


def lead_spec(shape):
    return pl.BlockSpec((1,) + tuple(shape[1:]), lambda c, s: (c,) + (0,) * (len(shape) - 1))


def lane_spec(shape):
    block = tuple(shape[:-1]) + (WIDTH,)
    return pl.BlockSpec(block, lambda c, s: (0,) * (len(shape) - 1) + (c,))


def second_spec(shape):
    block = (shape[0], 1) + tuple(shape[2:])
    return pl.BlockSpec(block, lambda c, s: (0, c) + (0,) * (len(shape) - 2))


def front_spec(shape):
    if shape[2] % 3 == 0 and shape[2] // 3 * 2 >= WIDTH and shape[3] == 2 * WIDTH and shape[1] == 4:
        return pl.BlockSpec((1, shape[1], shape[2] // 3 * 2, shape[3]), lambda c, s: (c, 0, 0, 0))
    return lead_spec(shape)


def full_back_spec(shape):
    if shape[2] > WIDTH:
        return pl.BlockSpec((shape[0], shape[1], shape[2] // 3, shape[3]), lambda c, s: (0, 0, 2, 0))
    return whole_spec(shape)


def back_spec(shape):
    if shape[2] > WIDTH:
        return pl.BlockSpec((1, shape[1], shape[2] // 3, shape[3]), lambda c, s: (c, 0, 2, 0))
    return lead_spec(shape)


def up_spec(shape):
    first = WIDTH // RANK if shape[2] > RANK else 0
    return pl.BlockSpec((1, 1, RANK, 2 * WIDTH), lambda c, s: (c, s[0], first + s[1], 0))


def down_spec(shape):
    first = shape[2] // RANK - 1
    return pl.BlockSpec((1, 1, RANK, WIDTH), lambda c, s: (c, s[0], first, s[1]))


KINDS = {
    "a": whole_spec, "c": lead_spec, "l": lane_spec, "s": second_spec, "w": front_spec, "f": full_back_spec,
    "p": back_spec, "u": up_spec, "d": down_spec,
}


def grouped_call(kernel, place, inputs, kinds, outputs, out_kinds, scratch, flops=0):
    return pl.pallas_call(
        kernel,
        grid_spec=pltpu.PrefetchScalarGridSpec(
            num_scalar_prefetch=1,
            grid=(GROUPS,),
            in_specs=[KINDS[kind](value.shape) for kind, value in zip(kinds, inputs)],
            out_specs=[KINDS[kind](shape) for kind, (shape, _) in zip(out_kinds, outputs)],
            scratch_shapes=[pltpu.VMEM(shape, dtype) for shape, dtype in scratch],
        ),
        out_shape=[jax.ShapeDtypeStruct(shape, dtype) for shape, dtype in outputs],
        compiler_params=pltpu.CompilerParams(vmem_limit_bytes=VMEM_BYTES),
        cost_estimate=pl.CostEstimate(flops=flops, bytes_accessed=40_000_000, transcendentals=0),
    )(place, *inputs)


def to_groups(value, heads_here):
    cols = value.shape[0]
    middle = value.shape[1:-1]
    if heads_here == QUAD:
        return value
    if heads_here > QUAD:
        parts = heads_here // QUAD
        value = value.reshape((cols,) + middle + (parts, WIDTH))
        value = jnp.moveaxis(value, -2, 1)
        return value.reshape((GROUPS,) + middle + (WIDTH,))
    parts = QUAD // heads_here
    value = value.reshape((GROUPS, parts) + middle + (heads_here * P_SIZE,))
    value = jnp.moveaxis(value, 1, -2)
    return value.reshape((GROUPS,) + middle + (WIDTH,))


def to_cols(value, heads_here, col_count):
    middle = value.shape[1:-1]
    if heads_here == QUAD:
        return value
    if heads_here > QUAD:
        parts = heads_here // QUAD
        value = value.reshape((col_count, parts) + middle + (WIDTH,))
        value = jnp.moveaxis(value, 1, -2)
        return value.reshape((col_count,) + middle + (heads_here * P_SIZE,))
    parts = QUAD // heads_here
    value = value.reshape((GROUPS,) + middle + (parts, heads_here * P_SIZE))
    value = jnp.moveaxis(value, -2, 1)
    return value.reshape((col_count,) + middle + (heads_here * P_SIZE,))


def pad_lanes(value, width):
    return jnp.pad(value, [(0, 0)] * (value.ndim - 1) + [(0, width - value.shape[-1])])


def carry_in(state, decay, row_count, col_count, seq_cols, forward):
    row = lax.axis_index("row")
    col = lax.axis_index("col")
    total = state
    factor = decay
    before = jnp.zeros(state.shape, F32)
    reach = jnp.ones_like(decay)
    span = 1
    while span < row_count:
        pairs = [(i, i ^ span) for i in range(row_count)]
        other = lax.ppermute(total, "row", pairs).astype(F32)
        other_factor = lax.ppermute(factor, "row", pairs)
        behind = ((row & span) != 0) == forward
        mine = total.astype(F32)
        before = jnp.where(behind, before + reach * other, before)
        reach = jnp.where(behind, reach * other_factor, reach)
        joined = jnp.where(behind, other * factor + mine, mine * other_factor + other)
        total = joined.astype(BF16)
        factor = factor * other_factor
        span *= 2
    place = lax.rem(col, seq_cols)
    for hop in range(1, seq_cols):
        shift = hop if forward else -hop
        pairs = [(i, (i + shift) % col_count) for i in range(col_count)]
        other = lax.ppermute(total, "col", pairs).astype(F32)
        other_factor = lax.ppermute(factor, "col", pairs)
        inside = place >= hop if forward else place < seq_cols - hop
        before = jnp.where(inside, before + reach * other, before)
        reach = jnp.where(inside, reach * other_factor, reach)
    return before


def per_device(
    block_in, norm_gain, proj_inner, proj_state, conv_inner, conv_inner_bias, conv_state, conv_state_bias,
    step_bias, decay_log, skip_gain, gate_gain, proj_out, adapt_in_down, adapt_in_up, adapt_out_down,
    adapt_out_up, adapter_id, cotangent,
):
    row_count = lax.axis_size("row")
    col_count = lax.axis_size("col")
    row = lax.axis_index("row")
    col = lax.axis_index("col")
    col_tokens, part = block_in.shape
    chunk = col_tokens // row_count
    total_rows = chunk + HALO
    blocks = chunk // BLOCK
    seq_cols = SEQ // col_tokens
    heads_here = proj_inner.shape[1]
    local = heads_here * P_SIZE
    rank_total = adapt_in_down.shape[1]
    rank_part = rank_total // row_count
    rank_share = rank_total // col_count
    adapter = lax.dynamic_index_in_dim(adapter_id, col // seq_cols, keepdims=False)

    relayed = row_count == 4 and heads_here == QUAD and seq_cols == 1 and part == WIDTH
    place = jnp.zeros((2,), jnp.int32)
    if relayed:
        x_rows, w_all, w_state, gain_all, vectors, head_rows, place = start_exchange(
            block_in, proj_inner.reshape(part, 2 * local), adapt_in_up.reshape(rank_total, 2 * local), proj_out,
            adapt_out_down, (proj_state.T, adapt_in_down, adapt_out_up),
            (
                norm_gain[None], conv_inner, conv_inner_bias[None], gate_gain[None], step_bias[None],
                decay_log[None], skip_gain[None],
            ),
            adapter_id, row_count, col_count,
        )
        up_all = down_all = p_all = w_all
        x_rows, cot = lax.optimization_barrier((x_rows, cotangent))
        g_rows = lax.all_to_all(cot.reshape(row_count, chunk, part), "row", 0, 0, tiled=True)
    else:
        head = jnp.zeros((HALO, part), BF16)
        if seq_cols > 1:
            pairs = [(i, (i + 1) % col_count) for i in range(col_count)]
            head = lax.ppermute(block_in[-HALO:], "col", pairs)
            head = jnp.where(lax.rem(col, seq_cols) > 0, head, jnp.zeros_like(head))
        padded = jnp.concatenate([head, block_in], axis=0)
        windows = jnp.stack([padded[r * chunk : r * chunk + total_rows] for r in range(row_count)])
        x_rows = lax.all_to_all(windows, "row", 0, 0, tiled=True)
        g_rows = lax.all_to_all(cotangent.reshape(row_count, chunk, part), "row", 0, 0, tiled=True)

        def split_pairs(value):
            value = value.reshape(value.shape[0], heads_here, 2, P_SIZE)
            return jnp.swapaxes(value, 1, 2).reshape(value.shape[0], 2, local)

        up_part = lax.dynamic_slice_in_dim(adapt_in_up, row * rank_part, rank_part, 0)
        w_block = jnp.concatenate([split_pairs(proj_inner), split_pairs(up_part)], axis=0)
        w_all = lax.all_gather(w_block.reshape(part + rank_part, 2 * local), ("col", "row"))
        w_all = w_all.reshape(col_count, row_count, part + rank_part, 2, local)
        w_all = to_groups(w_all, heads_here).reshape(GROUPS, row_count, part + rank_part, 2 * WIDTH)
        up_all = w_all[:, :, part:, :].reshape(GROUPS, rank_total, 2 * WIDTH)
        up_all = lax.dynamic_slice_in_dim(up_all, adapter * RANK, RANK, 1)[:, None]

        down_part = lax.dynamic_slice_in_dim(adapt_out_down, row * rank_part, rank_part, 0)
        p_block = jnp.concatenate([proj_out, down_part.T], axis=1)
        p_all = lax.all_gather(p_block, ("col", "row")).reshape(col_count, row_count, local, part + rank_part)
        if heads_here != QUAD:
            p_all = jnp.moveaxis(p_all, 1, 0).reshape(row_count, GROUPS, WIDTH, part + rank_part)
            p_all = jnp.moveaxis(p_all, 0, 1)
        down_all = jnp.swapaxes(p_all[..., part:], 1, 2).reshape(GROUPS, WIDTH, rank_total)
        down_all = jnp.swapaxes(lax.dynamic_slice_in_dim(down_all, adapter * RANK, RANK, 2), 1, 2)[:, None]

        in_down = lax.dynamic_slice_in_dim(adapt_in_down, adapter * RANK, RANK, 1)
        out_up = lax.dynamic_slice_in_dim(adapt_out_up, adapter * RANK, RANK, 1)
        shared = pad_lanes(jnp.concatenate([proj_state, in_down, out_up], axis=1), 384)
        w_state = lax.all_gather(shared, "row")
        gain_all = lax.all_gather(norm_gain, "row").reshape(row_count, 1, part)

        scalars = jnp.concatenate([step_bias, decay_log, skip_gain])
        vectors = jnp.concatenate(
            [conv_inner, conv_inner_bias[None], gate_gain[None], pad_lanes(scalars, local)[None]], axis=0
        )
        vectors = lax.all_gather(vectors, "col")
        scalars = vectors[:, 6, : 3 * heads_here].reshape(col_count, 3, heads_here)
        scalars = jnp.swapaxes(scalars, 0, 1).reshape(3, HEADS)
        head_rows = jnp.pad(scalars[:2], ((0, 6), (0, LANES - HEADS)))
        skip_wide = jnp.repeat(scalars[2], P_SIZE).reshape(GROUPS, 1, WIDTH)
        vectors = jnp.concatenate(
            [to_groups(vectors[:, :6], heads_here), skip_wide, jnp.zeros_like(skip_wide)], axis=1
        )
    state_taps = conv_state

    token_f32 = ((chunk, LANES), F32)
    token_low = ((chunk, LANES), BF16)
    inner_low = ((chunk, DI), BF16)
    states = ((blocks, STATES, DI), BF16)
    score_box = ((blocks, BLOCK, BLOCK), F32)
    flipped = ((blocks, STATES, BLOCK), BF16)
    (
        normed, scpre, ratio, sig, cum, lead, turned, bs, cs, cs_t, adv, gate, u, eloc, fin, dec,
    ) = grouped_call(
        front_kernel,
        place,
        (x_rows, gain_all, w_state, state_taps, conv_state_bias[None], head_rows, w_all, up_all, vectors),
        "aaaaaawuc",
        [
            ((total_rows, D), BF16), ((chunk, 256), F32), token_f32, token_f32, token_f32, token_f32,
            ((GROUPS, 2 * QUAD, chunk), F32), token_low, token_low, flipped, ((total_rows, LANES), BF16),
            inner_low, inner_low, states, ((STATES, DI), BF16), ((8, DI), F32),
        ],
        "aaaaaaaaaaalllll",
        [((total_rows, 384), F32), flipped, ((total_rows, WIDTH), F32)],
        flops=int(45e9),
    )
    decay = dec[0:1]
    fin, g_rows = lax.optimization_barrier((fin, g_rows))
    if relayed:
        entry = carry_over(fin, dec, True)
    else:
        entry = carry_in(fin, decay, row_count, col_count, seq_cols, True)
    out_rows, o, ent, aux, side_grad, out_up_grad = grouped_call(
        scan_kernel,
        place,
        (x_rows, g_rows, w_state, p_all, down_all, vectors, gate, u, eloc, entry, cum, turned, bs, cs),
        "aaafdcllllacaa",
        [
            ((row_count, chunk, part), BF16), inner_low, ((blocks, STATES, DI), BF16), token_f32, token_low,
            ((RANK, D), F32),
        ],
        "allaaa",
        [score_box, ((GROUPS, chunk, WIDTH), BF16), token_f32, token_f32],
        flops=int(45e9),
    )
    block_out = lax.all_to_all(out_rows, "row", 0, 0, tiled=True).reshape(col_tokens, part)
    dgate, dy, gloc, gfin, out_down_grad = grouped_call(
        gate_kernel,
        place,
        (g_rows, p_all, side_grad, down_all, vectors, gate, o, aux, cum, cs_t),
        "apadcllaaa",
        [inner_low, inner_low, states, ((STATES, DI), BF16), ((GROUPS, RANK, WIDTH), F32)],
        "llllc",
        [((blocks, RANK, BLOCK), BF16)],
        flops=int(25e9),
    )
    gfin, block_out = lax.optimization_barrier((gfin, block_out))
    if relayed:
        exit_grad = carry_over(gfin, dec, False)
    else:
        exit_grad = carry_in(gfin, decay, row_count, col_count, seq_cols, False)
    corr, wide, thin = grouped_call(
        back_kernel,
        place,
        (
            x_rows, gain_all, normed, w_state, w_all, up_all, adv, vectors, state_taps, head_rows,
            u, o, dy, dgate, ent, gloc, exit_grad, cum, lead, turned, ratio, sig, scpre, bs, cs,
            out_down_grad, out_up_grad,
        ),
        "aaaawuacaalllllllaacaaaaaca",
        [
            ((row_count, total_rows, part), BF16), ((row_count, GROUPS, RANK // row_count, 3 * WIDTH), F32),
            ((row_count, 2 * RANK, part), F32),
        ],
        "asa",
        [
            score_box, score_box, token_f32, token_f32, token_f32, token_f32, ((blocks, 8, LANES), F32),
            ((total_rows + HALO, WIDTH), F32), ((total_rows, 2 * WIDTH), BF16), ((total_rows, D), F32),
            ((total_rows, LANES), F32), ((blocks, RANK, BLOCK), BF16),
            ((RANK, 2 * WIDTH), F32), ((RANK, D), F32),
        ],
        flops=int(75e9),
    )

    if heads_here != QUAD:
        share = RANK // row_count
        wide = jnp.swapaxes(wide.reshape(row_count, GROUPS, share, 3, WIDTH), 0, 1)
        wide = to_cols(wide, heads_here, col_count)
        wide = jnp.swapaxes(wide, 0, 1).reshape(row_count, col_count, share, 3 * local)
    corr, wide, thin = finish_exchange(corr, wide, thin)
    late = jnp.zeros((1, HALO, part), BF16)
    if seq_cols > 1:
        pairs = [(i, (i - 1) % col_count) for i in range(col_count)]
        late = lax.ppermute(corr[0:1, :HALO], "col", pairs)
        late = jnp.where(lax.rem(col, seq_cols) < seq_cols - 1, late, jnp.zeros_like(late))
    early = jnp.concatenate([corr[1:, :HALO], late], axis=0)
    early = jnp.pad(early, ((0, 0), (chunk - HALO, 0), (0, 0))).astype(F32)
    input_grad = cotangent.reshape(row_count, chunk, part).astype(F32) + corr[:, HALO:].astype(F32) + early
    input_grad = input_grad.reshape(col_tokens, part)
    wide = jnp.swapaxes(wide, 0, 1).reshape(col_count, RANK, 3 * local)
    owner = jnp.repeat(adapter_id, seq_cols)
    adapters = rank_total // RANK
    chosen = owner[:, None] == jnp.arange(adapters, dtype=jnp.int32)[None, :]
    wide = jnp.sum(jnp.where(chosen[:, :, None, None], wide[:, None], 0.0), axis=0)
    wide = wide.reshape(rank_total, 3 * local)
    in_up = wide[:, : 2 * local].reshape(rank_total, 2, heads_here, P_SIZE)
    in_up = jnp.swapaxes(in_up, 1, 2).reshape(rank_total, heads_here, 2 * P_SIZE)
    out_down = wide[:, 2 * local :]
    if rank_share <= RANK:
        mine = owner == (col * rank_share) // RANK
        thin = jnp.sum(jnp.where(mine[:, None, None], thin, 0.0), axis=0).reshape(2, RANK, part)
        thin = lax.dynamic_slice_in_dim(thin, lax.rem(col * rank_share, RANK), rank_share, 1)
        thin = jnp.swapaxes(thin, 1, 2)
    else:
        thin = jnp.sum(jnp.where(chosen[:, :, None, None], thin[:, None], 0.0), axis=0)
        thin = thin.reshape(adapters, 2, RANK, part)
        thin = jnp.transpose(thin, (1, 3, 0, 2)).reshape(2, part, rank_total)
        thin = lax.dynamic_slice_in_dim(thin, col * rank_share, rank_share, 2)
    return block_out, input_grad, thin[0], in_up, out_down, thin[1]


def solution(mesh):
    placed = (
        P("col", "row"), P("row"), P("row", "col", None), P("row", None), P(None, "col"), P("col"), P(), P(),
        P("col"), P("col"), P("col"), P("col"), P("col", "row"), P("row", None), P(None, "col", None),
        P(None, "col"), P("row", None), P(), P("col", "row"),
    )
    return jax.shard_map(
        per_device,
        mesh=mesh,
        in_specs=placed,
        out_specs=(
            P("col", "row"), P("col", "row"), P("row", "col"), P(None, "col", None), P(None, "col"),
            P("row", "col"),
        ),
        check_vma=False,
    )
```

```python
import functools

import jax
import jax.numpy as jnp
from jax import lax
from jax.experimental import pallas as pl
from jax.experimental.pallas import tpu as pltpu
from jax.sharding import PartitionSpec as P

D = 1024
HEADS = 32
P_SIZE = 64
STATES = 128
BLOCK = 256
RANK = 16
SEQ = 4096
DI = 2048
EPS = 1e-05
LOG2E = 1.4426950408889634

HALO = 16
IN_LANE = 32
OUT_LANE = 48
CAP = 80.0
QUAD = 4
WIDTH = QUAD * P_SIZE
GROUPS = HEADS // QUAD
LANES = 128
VMEM_BYTES = 60 * 1024 * 1024
F32 = jnp.float32
BF16 = jnp.bfloat16
MESH = pl.DeviceIdType.MESH


def mm(left, right):
    return jnp.dot(left, right, preferred_element_type=F32)


def mm_nt(left, right):
    return lax.dot_general(left, right, (((1,), (1,)), ((), ())), preferred_element_type=F32)


def mm_tn(left, right):
    return lax.dot_general(left, right, (((0,), (0,)), ((), ())), preferred_element_type=F32)


def split_left(ones, value):
    high = value.astype(BF16)
    rest = value - high.astype(F32)
    middle = rest.astype(BF16)
    low = (rest - middle.astype(F32)).astype(BF16)
    return mm(ones, high) + mm(ones, middle) + mm(ones, low)


def split_right(value, ones):
    high = value.astype(BF16)
    low = (value - high.astype(F32)).astype(BF16)
    return mm(high, ones) + mm(low, ones)


def sigmoid(value):
    return 0.5 * jnp.tanh(0.5 * value) + 0.5


def iota(shape, axis):
    return lax.broadcasted_iota(jnp.int32, shape, axis)


def widen(cols):
    lane = iota((cols.shape[0], LANES), 1) < P_SIZE
    left = jnp.where(lane, cols[:, 0:1], cols[:, 1:2])
    right = jnp.where(lane, cols[:, 2:3], cols[:, 3:4])
    return jnp.concatenate([left, right], axis=1)


def to_front(cols, group):
    return pltpu.roll(cols, lax.rem(LANES - QUAD * group, LANES), 1)


def lane_range(values, first):
    lane = iota(values.shape, 1)
    return jnp.where((lane >= first) & (lane < first + RANK), values, 0.0)


def out_block(w_ref, group, row, part):
    if w_ref.shape[2] == WIDTH:
        return w_ref[group, row, :, :part]
    rows = WIDTH // 2
    return jnp.concatenate([w_ref[group, row, :rows, :part], w_ref[group, row, :rows, part:]], axis=0)


def head_only(values, head):
    lane = iota(values.shape, 1) // P_SIZE
    return jnp.where(lane == head, values, jnp.zeros_like(values))


def delays(window, taps, bias):
    total = window[8:] * taps[0:1] + bias
    for k in range(1, 4):
        total = total + pltpu.roll(window, k, 0)[8:] * taps[k : k + 1]
    return total


def advances(window, taps, count):
    length = window.shape[0]
    total = window[:count] * taps[0:1]
    for k in range(1, 4):
        total = total + pltpu.roll(window, length - k, 0)[:count] * taps[k : k + 1]
    return total


def at_block(k):
    if isinstance(k, int):
        return pl.ds(k * BLOCK, BLOCK)
    return pl.ds(pl.multiple_of(k * BLOCK, BLOCK), BLOCK)


def at_rows(k):
    if isinstance(k, int):
        return pl.ds(HALO + k * BLOCK, BLOCK)
    return pl.ds(pl.multiple_of(HALO + k * BLOCK, HALO), BLOCK)


def with_halo(k):
    if k == 0:
        return pl.ds(0, HALO + BLOCK)
    return pl.ds(HALO + k * BLOCK, BLOCK)


def padded_rows(value, first):
    before = jnp.zeros((first, value.shape[1]), value.dtype)
    after = jnp.zeros((LANES - first - value.shape[0], value.shape[1]), value.dtype)
    return jnp.concatenate([before, value, after], axis=0)


def front_kernel(
    place_ref, x_ref, gain_ref, wst_ref, sp_ref, sb_ref, hp_ref, w_ref, up_ref, vp_ref,
    normed_ref, scpre_ref, ratio_ref, sig_ref, cum_ref, lead_ref, turned_ref, bs_ref, cs_ref, cs_t_ref, adv_ref,
    gate_ref, u_ref, eloc_ref, fin_ref, dec_ref,
    st_scr, bs_t_scr, val_scr,
):
    group = pl.program_id(0)
    row_count, _, part = x_ref.shape
    blocks = eloc_ref.shape[0]

    @pl.when(group == 0)
    def _():
        def project(rows):
            pieces = [x_ref[r, rows, :].astype(F32) for r in range(row_count)]
            square = sum(jnp.sum(piece * piece, axis=1, keepdims=True) for piece in pieces)
            inv = lax.rsqrt(square / D + EPS)
            total = None
            for r in range(row_count):
                normed = (pieces[r] * inv * gain_ref[r]).astype(BF16)
                normed_ref[rows, r * part : (r + 1) * part] = normed
                term = mm(normed, wst_ref[r])
                total = term if total is None else total + term
            st_scr[rows, :] = total
            adv_ref[rows, :] = lane_range(total[:, 256:384], IN_LANE).astype(BF16)

        project(pl.ds(0, HALO))

        @pl.loop(0, blocks)
        def _(k):
            project(at_rows(k))

        lower = (iota((BLOCK, BLOCK), 0) >= iota((BLOCK, BLOCK), 1)).astype(BF16)
        rate = -jnp.exp(hp_ref[1:2]) * LOG2E

        @pl.loop(0, blocks)
        def _(k):
            window = st_scr[pl.ds(pl.multiple_of(8 + k * BLOCK, 8), BLOCK + 8), :256]
            pre = delays(window, sp_ref[...], sb_ref[...])
            conv = pre * sigmoid(pre)
            b_rows = conv[:, :STATES].astype(BF16)
            c_rows = conv[:, STATES:].astype(BF16)
            scpre_ref[at_block(k), :] = pre
            bs_ref[at_block(k), :] = b_rows
            cs_ref[at_block(k), :] = c_rows
            bs_t_scr[k] = conv[:, :STATES].T.astype(BF16)
            cs_t_ref[k] = conv[:, STATES:].T.astype(BF16)
            raw = st_scr[at_rows(k), 256:384] + hp_ref[0:1]
            small = jnp.exp(-jnp.abs(raw))
            tail = jnp.where(
                small < 0.01, small * (1.0 - small * (0.5 - small * (1.0 / 3.0))), jnp.log(1.0 + small)
            )
            step = jnp.maximum(raw, 0.0) + tail
            cum = split_left(lower, step * rate)
            sig = sigmoid(raw)
            ratio_ref[at_block(k), :] = jnp.where(raw < -20.0, 1.0, sig / jnp.maximum(step, 1e-30))
            sig_ref[at_block(k), :] = sig
            lead = jnp.log(jnp.maximum(step, 1e-37)) * LOG2E - cum
            cum_ref[at_block(k), :] = cum
            lead_ref[at_block(k), :] = lead
            flipped = cum.T
            flipped_lead = lead.T
            for g in range(GROUPS):
                turned_ref[g, :QUAD, at_block(k)] = flipped[g * QUAD : (g + 1) * QUAD]
                turned_ref[g, QUAD:, at_block(k)] = flipped_lead[g * QUAD : (g + 1) * QUAD]

    up_rows = padded_rows(up_ref[0, 0], IN_LANE)

    def inner(rows):
        total = mm(adv_ref[rows, :], up_rows)
        for r in range(row_count):
            total = total + mm(normed_ref[rows, r * part : (r + 1) * part], w_ref[0, r, :part, :])
        return total

    taps = vp_ref[0]

    def one_block(k, carry):
        state, decay = carry
        product = inner(with_halo(k))
        skip = HALO if k == 0 else 0
        gate_ref[at_block(k), :] = product[skip:, :WIDTH].astype(BF16)
        val_scr[with_halo(k), :] = product[:, WIDTH:]
        window = val_scr[pl.ds(8 + k * BLOCK, BLOCK + 8), :]
        pre = delays(window, taps[0:4], taps[4:5])
        u_ref[at_block(k), :] = pre.astype(BF16)
        xs = (pre * sigmoid(pre)).astype(BF16).astype(F32)
        cum = cum_ref[at_block(k), :]
        last = cum[BLOCK - 1 : BLOCK]
        weight = to_front(jnp.exp2(last + lead_ref[at_block(k), :]), group)
        weighted = (xs * widen(weight)).astype(BF16)
        eloc_ref[k] = state.astype(BF16)
        last8 = to_front(jnp.broadcast_to(last, (8, LANES)), group)
        fall = widen(jnp.exp2(last8))[0:1]
        return fall * state + mm(bs_t_scr[k], weighted), decay * fall

    carry = (jnp.zeros((STATES, WIDTH), F32), jnp.ones((1, WIDTH), F32))
    for k in range(blocks):
        carry = one_block(k, carry)
    state, decay = carry
    fin_ref[...] = state.astype(BF16)
    dec_ref[...] = jnp.broadcast_to(decay, (8, WIDTH))


def scan_kernel(
    place_ref, x_ref, g_ref, wst_ref, w_ref, down_ref, vp_ref, gate_ref, u_ref, eloc_ref, ein_ref,
    cum_ref, turned_ref, bs_ref, cs_ref,
    out_ref, o_ref, ent_ref, aux_ref, sg_ref, gup_ref,
    score_scr, gained_scr, side_scr, square_scr,
):
    group = pl.program_id(0)
    row_count, _, part = x_ref.shape
    blocks = eloc_ref.shape[0]

    @pl.when(group == 0)
    def _():
        side_scr[...] = jnp.zeros_like(side_scr)
        square_scr[...] = jnp.zeros_like(square_scr)
        keep = iota((BLOCK, BLOCK), 0) >= iota((BLOCK, BLOCK), 1)

        @pl.loop(0, blocks)
        def _(k):
            score = mm_nt(cs_ref[at_block(k), :], bs_ref[at_block(k), :])
            score_scr[k] = jnp.where(keep, score, 0.0)

    taps = vp_ref[0]

    down_rows = padded_rows(down_ref[0, 0], OUT_LANE)

    def one_block(k, before):
        rows = at_block(k)
        pre = u_ref[rows, :].astype(F32)
        conv = pre * sigmoid(pre)
        cum = to_front(cum_ref[rows, :], group)
        xs = conv.astype(BF16)
        score = score_scr[k]
        entering = (eloc_ref[k].astype(F32) + before * ein_ref[...]).astype(BF16)
        ent_ref[k] = entering
        total = widen(jnp.exp2(cum)) * mm(cs_ref[rows, :], entering)
        for h in range(QUAD):
            spread = cum[:, h : h + 1] + turned_ref[0, QUAD + h : QUAD + h + 1, rows]
            weights = (score * jnp.exp2(jnp.minimum(spread, CAP))).astype(BF16)
            total = total + mm(weights, head_only(xs, h))
        output = total + taps[6:7] * conv
        o_ref[rows, :] = output.astype(BF16)
        gate = gate_ref[rows, :].astype(F32)
        gated = output * gate * sigmoid(gate)
        square = gated * gated
        square_scr[rows, :] += square[:, :LANES] + square[:, LANES:]
        gained = (gated * taps[5:6]).astype(BF16)
        gained_scr[group, rows, :] = gained
        side_scr[rows, :] += mm_nt(gained, down_rows)
        return before * widen(jnp.exp2(cum[BLOCK - 8 :]))[7:8]

    before = jnp.ones((1, WIDTH), F32)
    for k in range(blocks):
        before = one_block(k, before)

    @pl.when(group == pl.num_programs(0) - 1)
    def _():
        gup_ref[...] = jnp.zeros_like(gup_ref)

        @pl.loop(0, blocks)
        def _(k):
            rows = at_block(k)
            mean = jnp.sum(square_scr[rows, :], axis=1, keepdims=True) / DI
            rms = lax.rsqrt(mean + EPS)
            side_raw = side_scr[rows, :]
            side = (side_raw * rms).astype(BF16)
            side_grad = None
            for r in range(row_count):
                term = mm(g_ref[r, rows, :], wst_ref[r, :, 256:384])
                side_grad = term if side_grad is None else side_grad + term
            side_grad = lane_range(side_grad, OUT_LANE).astype(BF16)
            product = jnp.sum(side_grad.astype(F32) * side_raw, axis=1, keepdims=True)
            for r in range(row_count):
                cols = slice(r * part, (r + 1) * part)
                raw = mm(gained_scr[0, rows, :], out_block(w_ref, 0, r, part))
                for c in range(1, GROUPS):
                    raw = raw + mm(gained_scr[c, rows, :], out_block(w_ref, c, r, part))
                cot = g_ref[r, rows, :]
                product = product + jnp.sum(raw * cot.astype(F32), axis=1, keepdims=True)
                total = x_ref[r, at_rows(k), :].astype(F32) + raw * rms + mm_nt(side, wst_ref[r, :, 256:384])
                out_ref[r, rows, :] = total.astype(BF16)
                gup_ref[:, cols] += mm_tn(side, cot)[OUT_LANE : OUT_LANE + RANK]
            coefficient = rms * rms * rms * product / DI
            lane = iota((BLOCK, LANES), 1)
            aux_ref[rows, :] = jnp.where(lane == 0, rms, coefficient)
            sg_ref[rows, :] = side_grad


def gate_kernel(
    place_ref, g_ref, w_ref, sg_ref, down_ref, vp_ref, gate_ref, o_ref, aux_ref, cum_ref, cs_t_ref,
    dgate_ref, dy_ref, gloc_ref, gfin_ref, gdown_ref,
    sg_t_scr,
):
    group = pl.program_id(0)
    row_count, _, part = g_ref.shape
    blocks = gloc_ref.shape[0]

    @pl.when(group == 0)
    def _():
        @pl.loop(0, blocks)
        def _(k):
            sg_t_scr[k] = sg_ref[at_block(k), :].astype(F32).T[OUT_LANE : OUT_LANE + RANK].astype(BF16)

    taps = vp_ref[0]
    gdown_ref[0] = jnp.zeros((RANK, WIDTH), F32)

    down_rows = padded_rows(down_ref[0, 0], OUT_LANE)

    def one_block(i, state):
        k = blocks - 1 - i
        rows = at_block(k)
        dmix = mm(sg_ref[rows, :], down_rows)
        for r in range(row_count):
            dmix = dmix + mm_nt(g_ref[r, rows, :], out_block(w_ref, 0, r, part))
        gate = gate_ref[rows, :].astype(F32)
        output = o_ref[rows, :].astype(F32)
        sig = sigmoid(gate)
        act = gate * sig
        gated = output * act
        rms = aux_ref[rows, 0:1]
        coefficient = aux_ref[rows, 1:2]
        scale = rms * taps[5:6]
        mixed = (gated * scale).astype(BF16)
        gdown_ref[0] += mm(sg_t_scr[k], mixed)
        gated_grad = scale * dmix - gated * coefficient
        dy = gated_grad * act
        dgate = gated_grad * output * (sig + act * (1.0 - sig))
        dgate_ref[rows, :] = dgate.astype(BF16)
        dy_ref[rows, :] = dy.astype(BF16)
        cum = to_front(cum_ref[rows, :], group)
        factor = widen(jnp.exp2(cum))
        gloc_ref[k] = state.astype(BF16)
        return factor[BLOCK - 1 : BLOCK] * state + mm(cs_t_ref[k], (factor * dy).astype(BF16))

    state = jnp.zeros((STATES, WIDTH), F32)
    for i in range(blocks):
        state = one_block(i, state)
    gfin_ref[...] = state.astype(BF16)


def back_kernel(
    place_ref, x_ref, gain_ref, normed_ref, wst_ref, w_ref, up_ref, adv_ref, vp_ref, sp_ref, hp_ref,
    u_ref, o_ref, dy_ref, dgate_ref, ent_ref, gloc_ref, gin_ref,
    cum_ref, lead_ref, turned_ref, ratio_ref, sig_ref, scpre_ref, bs_ref, cs_ref, out_down_ref, out_up_ref,
    corr_ref, wide_ref, thin_ref,
    score_scr, dscore_scr, db_scr, dc_scr, dcum_scr, dstep_scr, dlast_scr, du_scr, ig_scr, ng_scr, adg_scr, adv_t_scr, up_scr, in_scr,
):
    group = pl.program_id(0)
    row_count, _, part = x_ref.shape
    blocks = gloc_ref.shape[0]
    total_rows = normed_ref.shape[0]

    @pl.when(group == 0)
    def _():
        for ref in (dscore_scr, db_scr, dc_scr, dcum_scr, dstep_scr, dlast_scr, ng_scr, adg_scr):
            ref[...] = jnp.zeros_like(ref)
        du_scr[0:HALO, :] = jnp.zeros((HALO, WIDTH), F32)
        du_scr[total_rows : total_rows + HALO, :] = jnp.zeros((HALO, WIDTH), F32)

        @pl.loop(0, blocks)
        def _(k):
            score_scr[k] = mm_nt(bs_ref[at_block(k), :], cs_ref[at_block(k), :])
            adv_t_scr[k] = adv_ref[at_rows(k), :].astype(F32).T[IN_LANE : IN_LANE + RANK].astype(BF16)

    keep = iota((BLOCK, BLOCK), 0) <= iota((BLOCK, BLOCK), 1)
    taps = vp_ref[0]
    pick = (iota((WIDTH, LANES), 1) == QUAD * group + iota((WIDTH, LANES), 0) // P_SIZE).astype(BF16)

    def one_block(i, after):
        k = blocks - 1 - i
        rows = at_block(k)
        pre = u_ref[rows, :].astype(F32)
        sig = sigmoid(pre)
        conv = pre * sig
        xs_low = conv.astype(BF16)
        xs = xs_low.astype(F32)
        cum = to_front(cum_ref[rows, :], group)
        lead = to_front(lead_ref[rows, :], group)
        dy_low = dy_ref[rows, :]
        dy = dy_low.astype(F32)
        b_rows = bs_ref[rows, :]
        c_rows = cs_ref[rows, :]
        score = jnp.where(keep, score_scr[k], 0.0)
        dscore = dscore_scr[k]
        ending = gloc_ref[k].astype(F32) + after * gin_ref[...]
        ending_low = ending.astype(BF16)
        last = cum[BLOCK - 1 : BLOCK]
        to_end = widen(jnp.exp2(last + lead))
        dxs_state = to_end * mm(b_rows, ending_low)
        dxs = dxs_state
        for h in range(QUAD):
            spread = turned_ref[0, h : h + 1, rows] + lead[:, h : h + 1]
            damp = jnp.exp2(jnp.minimum(spread, CAP))
            weights = (score * damp).astype(BF16)
            dy_head = head_only(dy_low, h)
            dxs = dxs + mm(weights, dy_head)
            dscore = dscore + mm_nt(xs_low, dy_head) * damp
        dscore_scr[k] = dscore
        from_start = widen(jnp.exp2(cum))
        fall = from_start[BLOCK - 1 : BLOCK]
        entering_low = ent_ref[k]
        entering = entering_low.astype(F32)
        dc_scr[rows, :] += mm_nt((from_start * dy).astype(BF16), entering_low)
        db_scr[rows, :] += mm_nt((to_end * xs).astype(BF16), ending_low)
        scan_out = o_ref[rows, :].astype(F32) - taps[6:7] * conv
        inward = mm((xs * dxs).astype(BF16), pick)
        dcum_scr[rows, :] += mm((dy * scan_out).astype(BF16), pick) - inward
        dstep_scr[rows, :] += inward
        ends = jnp.sum(xs * dxs_state, axis=0, keepdims=True)
        ends = ends + fall * jnp.sum(entering * ending, axis=0, keepdims=True)
        dlast_scr[k] += split_right(jnp.broadcast_to(ends, (8, WIDTH)), pick)
        dconv = taps[6:7] * dy + dxs
        du_scr[at_rows(k), :] = dconv * (sig + conv * (1.0 - sig))
        return after * fall

    after = jnp.ones((1, WIDTH), F32)
    for i in range(blocks):
        after = one_block(i, after)
    up_rows = padded_rows(up_ref[0, 0], IN_LANE)

    ig_scr[0:HALO, :WIDTH] = jnp.zeros((HALO, WIDTH), BF16)
    for k in range(blocks):
        rows = with_halo(k)
        extra = HALO if k == 0 else 0
        ig_scr[at_rows(k), :WIDTH] = dgate_ref[at_block(k), :]
        window = du_scr[pl.ds(HALO + k * BLOCK - extra, BLOCK + extra + 8), :]
        ig_scr[rows, WIDTH:] = advances(window, taps[0:4], BLOCK + extra).astype(BF16)
        grad = ig_scr[rows, :]
        adg_scr[rows, :] += mm_nt(grad, up_rows)
        for r in range(row_count):
            ng_scr[rows, r * part : (r + 1) * part] += mm_nt(grad, w_ref[0, r, :part, :])
        if k == 0:
            up_scr[...] = mm_tn(adv_ref[0:HALO, :], grad[:HALO])[IN_LANE : IN_LANE + RANK]
        up_scr[...] += mm(adv_t_scr[k], grad[extra:])

    share = RANK // row_count
    for r in range(row_count):
        wide_ref[r, 0, :, : 2 * WIDTH] = up_scr[r * share : (r + 1) * share, :]
        wide_ref[r, 0, :, 2 * WIDTH :] = out_down_ref[0, r * share : (r + 1) * share, :]

    @pl.when(group == pl.num_programs(0) - 1)
    def _():
        upper = (iota((BLOCK, BLOCK), 0) <= iota((BLOCK, BLOCK), 1)).astype(BF16)
        rate = -jnp.exp(hp_ref[1:2])

        @pl.loop(0, blocks)
        def _(k):
            rows = at_block(k)
            dscore = jnp.where(keep, dscore_scr[k], 0.0).astype(BF16)
            db = db_scr[rows, :] + mm(dscore, cs_ref[rows, :])
            dc = dc_scr[rows, :] + mm_tn(dscore, bs_ref[rows, :])
            pre = scpre_ref[rows, :]
            sig = sigmoid(pre)
            slope = sig + pre * sig * (1.0 - sig)
            du_scr[at_rows(k), :] = jnp.concatenate([db, dc], axis=1) * slope
            is_last = iota((BLOCK, LANES), 0) == BLOCK - 1
            dcum = dcum_scr[rows, :] + jnp.where(is_last, dlast_scr[k, 0:1, :], 0.0)
            slower = split_left(upper, dcum) * (rate * sig_ref[rows, :])
            dstep_scr[rows, :] = dstep_scr[rows, :] * ratio_ref[rows, :] + slower

        def finish(rows, window, count, draw):
            dstate = advances(window, sp_ref[...], count).astype(BF16)
            adapt = adg_scr[rows, :].astype(BF16)
            mixed = adapt + draw
            total = jnp.zeros((count, 1), F32)
            square = jnp.zeros((count, 1), F32)
            grads = []
            for r in range(row_count):
                cols = slice(r * part, (r + 1) * part)
                grad = ng_scr[rows, cols] + mm_nt(dstate, wst_ref[r, :, 0:256])
                grad = grad + mm_nt(mixed, wst_ref[r, :, 256:384])
                grad = grad * gain_ref[r]
                piece = x_ref[r, rows, :].astype(F32)
                total = total + jnp.sum(piece * grad, axis=1, keepdims=True)
                square = square + jnp.sum(piece * piece, axis=1, keepdims=True)
                grads.append(grad)
                in_scr[:, cols] += mm_tn(adapt, normed_ref[rows, cols])[IN_LANE : IN_LANE + RANK]
            inv = lax.rsqrt(square / D + EPS)
            factor = inv * inv * inv * total / D
            for r in range(row_count):
                piece = x_ref[r, rows, :].astype(F32)
                corr_ref[r, rows, :] = (inv * grads[r] - factor * piece).astype(BF16)

        in_scr[...] = jnp.zeros_like(in_scr)
        for k in range(blocks):
            extra = HALO if k == 0 else 0
            window = du_scr[pl.ds(HALO + k * BLOCK - extra, BLOCK + extra + 8), :]
            draw = dstep_scr[at_block(k), :].astype(BF16)
            if k == 0:
                draw = jnp.concatenate([jnp.zeros((HALO, LANES), BF16), draw], axis=0)
            finish(with_halo(k), window, BLOCK + extra, draw)

        for r in range(row_count):
            thin_ref[r, 0:RANK, :] = in_scr[:, r * part : (r + 1) * part]
            thin_ref[r, RANK:, :] = out_up_ref[:, r * part : (r + 1) * part]


def on_row(row):
    return {"row": row}


def on_col(col):
    return {"col": col}


def tail_kernel(
    corr_ref, wide_ref, thin_ref, owner_ref,
    corr_out, wide_out, thin_out, up_out, down_out, mine_out,
    wide_pair, thin_pair, wide_both, thin_both, wide_scr, thin_scr, wide_sum, thin_sum, wide_col,
    own_sem, corr_send, corr_recv, pair_send, pair_recv, row_send, row_recv, col_send, col_recv, last_send, last_recv,
    core_send, core_recv,
):
    row_count = corr_ref.shape[0]
    col_count = thin_out.shape[0]
    row = lax.axis_index("row")
    col = lax.axis_index("col")
    barrier = pltpu.get_barrier_semaphore()
    for d in range(1, row_count):
        pl.semaphore_signal(barrier, inc=1, device_id=on_row(lax.rem(row + d, row_count)), device_id_type=MESH)
    for d in range(1, col_count):
        pl.semaphore_signal(barrier, inc=1, device_id=on_col(lax.rem(col + d, col_count)), device_id_type=MESH)
    pl.semaphore_wait(barrier, row_count + col_count - 2)

    def send(source, target, sends, recvs, index, device):
        copy = pltpu.make_async_remote_copy(
            src_ref=source, dst_ref=target, send_sem=sends.at[index], recv_sem=recvs.at[index],
            device_id=device, device_id_type=MESH,
        )
        copy.start()
        return copy

    chips = row_count // 2
    parity = lax.rem(row, 2)
    chip = row // 2
    core = row + 1 - 2 * parity
    first = []
    for j in range(chips):
        theirs = 2 * j + 1 - parity
        first.append(send(wide_ref.at[theirs], wide_pair.at[j], pair_send, pair_recv, j, on_row(core)))
        first.append(send(thin_ref.at[theirs], thin_pair.at[j], pair_send, pair_recv, chips + j, on_row(core)))
    moved = []
    cuts = (0, 8 * corr_ref.shape[1] // 1040 * 16, 45 * corr_ref.shape[1] // 1040 * 16, corr_ref.shape[1])

    def move(step):
        for d in range(1, row_count):
            peer = lax.rem(row + d, row_count)
            part = pl.ds(cuts[step], cuts[step + 1] - cuts[step])
            index = step * row_count + d
            source = corr_ref.at[peer, part]
            moved.append(send(source, corr_out.at[row, part], corr_send, corr_recv, index, on_row(peer)))

    move(0)
    own = pltpu.make_async_copy(corr_ref.at[row], corr_out.at[row], own_sem.at[0])
    own.start()
    for copy in first:
        copy.wait()
    for j in range(chips):
        wide_both[j] = wide_ref[2 * j + parity] + wide_pair[j]
        thin_both[j] = thin_ref[2 * j + parity] + thin_pair[j]
    across = []
    for d in range(1, chips):
        there = lax.rem(chip + d, chips)
        peer = on_row(2 * there + parity)
        across.append(send(wide_both.at[there], wide_scr.at[chip], row_send, row_recv, d, peer))
        across.append(send(thin_both.at[there], thin_scr.at[chip], row_send, row_recv, chips + d, peer))
    move(1)
    for copy in across:
        copy.wait()
    wide = wide_both[chip]
    thin = thin_both[chip]
    for d in range(1, chips):
        there = lax.rem(chip + d, chips)
        wide = wide + wide_scr[there]
        thin = thin + thin_scr[there]
    wide_sum[...] = wide
    thin_sum[...] = thin
    second = []
    for d in range(1, col_count):
        peer = lax.rem(col + d, col_count)
        second.append(send(wide_sum.at[peer], wide_col.at[col], col_send, col_recv, d, on_col(peer)))
        second.append(send(thin_sum, thin_out.at[col], col_send, col_recv, col_count + d, on_col(peer)))
    wide_col[col] = wide_sum[col]
    thin_out[col] = thin
    for copy in second:
        copy.wait()
    third = []
    for d in range(1, chips):
        there = lax.rem(chip + d, chips)
        third.append(send(wide_col, wide_out.at[row], last_send, last_recv, d, on_row(2 * there + parity)))
    fourth = [send(wide_col, wide_out.at[row], core_send, core_recv, 0, on_row(core))]
    move(2)
    wide_out[row] = wide_col[...]
    for d in range(1, chips):
        third[d - 1].wait_recv()
        source = 2 * lax.rem(chip + chips - d, chips) + parity
        fourth.append(send(wide_out.at[source], wide_out.at[source], core_send, core_recv, d, on_row(core)))
    for copy in third:
        copy.wait_send()
    for copy in fourth:
        copy.wait()
    if up_out.shape[0] > RANK:
        lane = iota((wide_out.shape[2], LANES), 1) < P_SIZE
        share = wide_out.shape[2]
        mine = jnp.zeros(mine_out.shape, F32)
        for c in range(col_count):
            mine = mine + jnp.where(owner_ref[c] == col, thin_out[c], 0.0)
        mine_out[...] = mine
        for a in range(up_out.shape[0] // RANK):
            for r in range(row_count):
                total = jnp.zeros(wide_out.shape[2:], F32)
                for c in range(col_count):
                    total = total + jnp.where(owner_ref[c] == a, wide_out[r, c], 0.0)
                rows = slice(a * RANK + r * share, a * RANK + (r + 1) * share)
                tiles = [total[:, i * LANES : (i + 1) * LANES] for i in range(QUAD)]
                turned = [pltpu.roll(tile, P_SIZE, 1) for tile in tiles]
                for h in range(QUAD):
                    gate, value = h // 2, 2 + h // 2
                    if h % 2 == 0:
                        up_out[rows, h, :] = jnp.where(lane, tiles[gate], turned[value])
                    else:
                        up_out[rows, h, :] = jnp.where(lane, turned[gate], tiles[value])
                down_out[rows, :] = total[:, 2 * WIDTH :]
    for copy in moved:
        copy.wait()
    own.wait()


def start_kernel(
    x_ref, w_ref, up_ref, p_ref, down_ref, state_ref, in_ref, out_ref, gain_ref, conv_ref, bias_ref, gate_ref, step_ref, rate_ref,
    skip_ref, adapter_ref,
    x_out, w_out, shared_out, gain_out, vec_out, head_out, place_out,
    block_scr, zero_scr, shared_ref,
    own_sem, send_sem, recv_sem, row_send, row_recv, col_send, col_recv,
):
    col_count, row_count = w_out.shape[:2]
    high_count = col_count // 2
    part = x_ref.shape[1]
    chunk = x_ref.shape[0] // row_count
    rank_part = up_ref.shape[0] // row_count
    row = lax.axis_index("row")
    col = lax.axis_index("col")
    low = lax.rem(col, 2)
    high = col // 2
    core = row + 1 - 2 * lax.rem(row, 2)
    across = lax.rem(row + 2, row_count)
    side = col + 1 - 2 * low
    barrier = pltpu.get_barrier_semaphore()
    for d in range(1, row_count):
        pl.semaphore_signal(barrier, inc=1, device_id=on_row(lax.rem(row + d, row_count)), device_id_type=MESH)
    for d in range(1, col_count):
        pl.semaphore_signal(barrier, inc=1, device_id=on_col(lax.rem(col + d, col_count)), device_id_type=MESH)

    def paired(value):
        lane = iota((value.shape[0], LANES), 1) < P_SIZE
        tiles = [value[:, h * LANES : (h + 1) * LANES].astype(F32) for h in range(QUAD)]
        turned = [pltpu.roll(tile, P_SIZE, 1) for tile in tiles]
        gates = [jnp.where(lane, tiles[h], turned[h + 1]) for h in (0, 2)]
        values = [jnp.where(lane, turned[h], tiles[h + 1]) for h in (0, 2)]
        return jnp.concatenate(gates + values, axis=1).astype(BF16)

    block_scr[0:part, :] = paired(w_ref[...])
    ranks = pl.ds(pl.multiple_of(row * rank_part, rank_part), rank_part)
    block_scr[part : part + rank_part, :] = paired(up_ref[ranks, :])
    first = part + rank_part
    half = WIDTH // 2
    block_scr[first : first + half, :WIDTH] = p_ref[:half, :]
    block_scr[first : first + half, WIDTH:] = p_ref[half:, :]
    first = first + half
    downs = down_ref[ranks, :]
    block_scr[first : first + rank_part // 2, :WIDTH] = downs[: rank_part // 2]
    block_scr[first : first + rank_part // 2, WIDTH:] = downs[rank_part // 2 :]
    zero_scr[...] = jnp.zeros_like(zero_scr)
    adapter = adapter_ref[col]
    shift = adapter * RANK
    per_part = rank_part // RANK
    place_out[0] = adapter // per_part
    place_out[1] = adapter - adapter // per_part * per_part
    source = iota((LANES, LANES), 0) - shift
    target = iota((LANES, LANES), 1)
    chosen = (source >= 0) & (source < RANK)
    ins = (chosen & (source == target - IN_LANE)).astype(F32).astype(BF16)
    outs = (chosen & (source == target - OUT_LANE)).astype(F32).astype(BF16)
    states = 2 * STATES
    shared_ref[:, :states] = state_ref[:states, :].astype(F32).T.astype(BF16)
    steps = jnp.concatenate(
        [state_ref[states:, :].astype(F32), jnp.zeros((LANES - HEADS, part), F32)], axis=0
    ).T
    shared_ref[:, states:] = (steps + mm(in_ref[...], ins) + mm(out_ref[...], outs)).astype(BF16)
    vec_out[col, 0:4, :] = conv_ref[...]
    vec_out[col, 4:5, :] = bias_ref[...]
    vec_out[col, 5:6, :] = gate_ref[...]
    vec_out[col, 6:7, :] = widen(skip_ref[...])
    lane = iota((1, WIDTH), 1)
    scalars = jnp.zeros((1, WIDTH), F32)
    for h in range(QUAD):
        scalars = jnp.where(lane == h, step_ref[:, h : h + 1], scalars)
        scalars = jnp.where(lane == QUAD + h, rate_ref[:, h : h + 1], scalars)
    vec_out[col, 7:8, :] = scalars
    gain_out[row] = gain_ref[...]
    pl.semaphore_wait(barrier, row_count + col_count - 2)

    def remote(source, target, sends, recvs, index, device):
        return pltpu.make_async_remote_copy(
            src_ref=source, dst_ref=target, send_sem=sends.at[index], recv_sem=recvs.at[index],
            device_id=device, device_id_type=MESH,
        )

    own_block = pltpu.make_async_copy(block_scr, w_out.at[col, row], own_sem.at[0])
    own_block.start()

    def whole_window(target, slot, index, peer):
        source = x_ref.at[pl.ds(pl.multiple_of(target * chunk - HALO, HALO), chunk + HALO)]
        return remote(source, x_out.at[slot], row_send, row_recv, index, on_row(peer))

    def first_window(slot, index, peer):
        source = x_ref.at[pl.ds(0, chunk)]
        return remote(source, x_out.at[slot, pl.ds(HALO, chunk)], row_send, row_recv, index, on_row(peer))

    def each_window(sending, act):
        for d in range(1, row_count):
            peer = lax.rem(row + d, row_count)
            chosen = peer if sending else row
            slot = row if sending else lax.rem(row + row_count - d, row_count)

            @pl.when(chosen > 0)
            def _():
                act(whole_window(jnp.maximum(chosen, 1), slot, d, peer))

            @pl.when(chosen == 0)
            def _():
                act(first_window(slot, d, peer))

    @pl.when(row > 0)
    def _():
        source = x_ref.at[pl.ds(pl.multiple_of(jnp.maximum(row, 1) * chunk - HALO, HALO), chunk + HALO)]
        pltpu.make_async_copy(source, x_out.at[row], own_sem.at[1]).start()

    @pl.when(row == 0)
    def _():
        pltpu.make_async_copy(x_ref.at[pl.ds(0, chunk)], x_out.at[row, pl.ds(HALO, chunk)], own_sem.at[1]).start()
        for r in range(row_count):
            pltpu.make_async_copy(zero_scr, x_out.at[r, pl.ds(0, HALO)], own_sem.at[3 + r]).start()

    own_shared = pltpu.make_async_copy(shared_ref, shared_out.at[row], own_sem.at[2])
    own_shared.start()
    small = []
    for d in range(1, col_count):
        peer = lax.rem(col + d, col_count)
        small.append(remote(vec_out.at[col], vec_out.at[col], col_send, col_recv, d, on_col(peer)))
    for d in range(1, row_count):
        peer = lax.rem(row + d, row_count)
        small.append(remote(shared_ref, shared_out.at[row], row_send, row_recv, row_count + d, on_row(peer)))
        small.append(
            remote(gain_out.at[row], gain_out.at[row], row_send, row_recv, 2 * row_count + d, on_row(peer))
        )
    for copy in small:
        copy.start()

    cut = (w_out.shape[2] * 65 // 100 + 8) // 16 * 16
    spans = (pl.ds(0, cut), pl.ds(cut, w_out.shape[2] - cut))
    has_up = high < high_count - 1
    has_down = high > 0
    routes = {
        "up": (0, has_up, on_col(lax.rem(col + 2, col_count))),
        "down": (1, has_down, on_col(lax.rem(col + col_count - 2, col_count))),
        "x": (2, None, on_col(side)),
        "y": (3, None, on_row(across)),
        "core": (4, None, on_row(core)),
    }

    def piece(section, c, r, kind, device):
        ref = w_out.at[c, r, spans[section]]
        return pltpu.make_async_remote_copy(
            src_ref=ref, dst_ref=ref, send_sem=send_sem.at[section, c, r, kind],
            recv_sem=recv_sem.at[section, c, r], device_id=device, device_id_type=MESH,
        )

    def event(starting, section, c, r, names, arrives=True, valid=None):
        def act():
            if starting and arrives:
                piece(section, c, r, 4, on_row(core)).wait_recv()
            for name in names:
                kind, allowed, device = routes[name]
                copy = piece(section, c, r, kind, device)
                if allowed is None:
                    copy.start() if starting else copy.wait_send()
                else:

                    @pl.when(allowed)
                    def _():
                        copy.start() if starting else copy.wait_send()

        if valid is None:
            act()
        else:
            pl.when(valid)(act)

    def far(column, step, distance):
        return lax.rem(column + step * distance + 4 * col_count, col_count)

    def within(step, distance):
        return high >= distance if step < 0 else high + distance < high_count

    onward = {-2: "up", 2: "down"}

    def along(starting, section, distance):
        for step in (-2, 2):
            valid = within(step, distance)
            if section == 0:
                names = (onward[step], "y", "x", "core")
                event(starting, 0, far(col, step, distance), row, names, valid=valid)
            else:
                for column, r in ((col, row), (side, row), (col, across), (side, across)):
                    event(starting, 1, far(column, step, distance), r, (onward[step], "core"), valid=valid)

    def over(starting, distance):
        for step in (-2, 2):
            valid = within(step, distance)
            event(starting, 0, far(side, step, distance), row, ("core",), valid=valid)
            event(starting, 0, far(col, step, distance), across, ("x", "core"), valid=valid)

    def last(starting, distance):
        for step in (-2, 2):
            event(starting, 0, far(side, step, distance), across, ("core",), valid=within(step, distance))

    def relay(starting):
        def windows():
            if starting:
                each_window(True, lambda copy: copy.start())

        event(starting, 0, col, row, ("up", "down"), arrives=False)
        event(starting, 1, col, row, ("x", "y"), arrives=False)
        event(starting, 0, col, row, ("y", "x", "core"), arrives=False)
        event(starting, 1, col, row, ("core",), arrives=False)
        event(starting, 1, side, row, ("y", "core"))
        along(starting, 0, 1)
        event(starting, 1, col, row, ("up", "down"), arrives=False)
        event(starting, 0, col, across, ("x", "core"))
        event(starting, 1, side, row, ("up", "down"), arrives=False)
        event(starting, 1, col, across, ("up", "down", "core"))
        for d in range(2, high_count - 1):
            along(starting, 0, d)
        event(starting, 1, side, across, ("up", "down", "core"))
        over(starting, 1)
        along(starting, 0, high_count - 1)
        windows()
        along(starting, 1, 1)
        over(starting, 2)
        event(starting, 0, side, row, ("core",))
        event(starting, 0, side, across, ("core",))
        last(starting, 1)
        for d in range(2, high_count):
            if d > 2:
                over(starting, d)
            along(starting, 1, d)
            if d > 2:
                last(starting, d - 1)
        last(starting, high_count - 1)

    own_block.wait()
    relay(True)
    for copy in small:
        copy.wait()
    lane = iota((1, LANES), 1) < QUAD
    steps = jnp.zeros((1, LANES), F32)
    rates = jnp.zeros((1, LANES), F32)
    for c in range(col_count):
        values = vec_out[c, 7:8, :LANES]
        steps = steps + pltpu.roll(jnp.where(lane, values, 0.0), (QUAD * c) % LANES, 1)
        values = pltpu.roll(values, LANES - QUAD, 1)
        rates = rates + pltpu.roll(jnp.where(lane, values, 0.0), (QUAD * c) % LANES, 1)
    head_out[...] = jnp.concatenate([steps, rates, jnp.zeros((6, LANES), F32)], axis=0)
    own_shared.wait()
    each_window(True, lambda copy: copy.wait_send())
    each_window(False, lambda copy: copy.wait_recv())

    @pl.when(row > 0)
    def _():
        source = x_ref.at[pl.ds(0, chunk + HALO)]
        pltpu.make_async_copy(source, x_out.at[row], own_sem.at[1]).wait()

    @pl.when(row == 0)
    def _():
        pltpu.make_async_copy(x_ref.at[pl.ds(0, chunk)], x_out.at[row, pl.ds(HALO, chunk)], own_sem.at[1]).wait()
        for r in range(row_count):
            pltpu.make_async_copy(zero_scr, x_out.at[r, pl.ds(0, HALO)], own_sem.at[3 + r]).wait()

    core_across = lax.rem(core + 2, row_count)
    for c in range(col_count):
        for r in (core, core_across):
            for section in range(2):
                piece(section, c, r, 4, on_row(core)).wait_recv()
    relay(False)


def start_exchange(x, w, up, p, down, shared, vectors, adapter_id, row_count, col_count):
    part = x.shape[1]
    rank_part = up.shape[0] // row_count
    block_rows = part + rank_part + WIDTH // 2 + rank_part // 2
    chunk = x.shape[0] // row_count
    vmem = pl.BlockSpec(memory_space=pltpu.VMEM)
    anywhere = pl.BlockSpec(memory_space=pl.ANY)
    dma = pltpu.SemaphoreType.DMA
    return pl.pallas_call(
        start_kernel,
        in_specs=[anywhere] + [vmem] * (7 + len(vectors)) + [pl.BlockSpec(memory_space=pltpu.SMEM)],
        out_specs=[anywhere] * 3 + [vmem] * 3 + [pl.BlockSpec(memory_space=pltpu.SMEM)],
        out_shape=[
            jax.ShapeDtypeStruct((row_count, chunk + HALO, part), BF16),
            jax.ShapeDtypeStruct((col_count, row_count, block_rows, 2 * WIDTH), BF16),
            jax.ShapeDtypeStruct((row_count, part, 384), BF16),
            jax.ShapeDtypeStruct((row_count, 1, part), F32),
            jax.ShapeDtypeStruct((col_count, 8, WIDTH), F32),
            jax.ShapeDtypeStruct((8, LANES), F32),
            jax.ShapeDtypeStruct((2,), jnp.int32),
        ],
        scratch_shapes=[
            pltpu.VMEM((block_rows, 2 * WIDTH), BF16), pltpu.VMEM((HALO, part), BF16),
            pltpu.VMEM((part, 384), BF16), dma((3 + row_count,)), dma((2, col_count, row_count, 5)), dma((2, col_count, row_count)),
            dma((3 * row_count,)), dma((3 * row_count,)), dma((col_count,)), dma((col_count,)),
        ],
        compiler_params=pltpu.CompilerParams(
            collective_id=1, has_side_effects=True, vmem_limit_bytes=VMEM_BYTES
        ),
    )(x, w, up, p, down, *shared, *vectors, adapter_id)


def carry_kernel(
    forward, state_ref, decay_ref,
    out_ref,
    other_scr, other_decay, total_scr, total_in,
    core_send, core_recv, across_send, across_recv, share_send, share_recv,
):
    row = lax.axis_index("row")
    parity = lax.rem(row, 2)
    chip = row // 2
    core = row + 1 - 2 * parity
    across = lax.rem(row + 2, 4)
    barrier = pltpu.get_barrier_semaphore()
    for peer in (core, across):
        pl.semaphore_signal(barrier, inc=1, device_id=on_row(peer), device_id_type=MESH)
    pl.semaphore_wait(barrier, 2)

    def remote(source, target, sends, recvs, index, peer):
        return pltpu.make_async_remote_copy(
            src_ref=source, dst_ref=target, send_sem=sends.at[index], recv_sem=recvs.at[index],
            device_id=on_row(peer), device_id_type=MESH,
        )

    swaps = [
        remote(state_ref, other_scr, core_send, core_recv, 0, core),
        remote(decay_ref, other_decay, core_send, core_recv, 1, core),
    ]
    for copy in swaps:
        copy.start()
    for copy in swaps:
        copy.wait()
    half = state_ref.shape[1] // 2
    rows = state_ref.shape[0] // 2
    second = parity == (1 if forward else 0)
    sends = chip == (0 if forward else 1)

    @pl.when(sends)
    def _():
        for p in range(2):

            @pl.when(parity == p)
            def _():
                cols = slice(p * half, (p + 1) * half)
                for q in range(2):
                    part = slice(q * rows, (q + 1) * rows)
                    mine = state_ref[part, cols].astype(F32)
                    other = other_scr[part, cols].astype(F32)
                    late = mine + other * decay_ref[0:1, cols]
                    early = other + mine * other_decay[0:1, cols]
                    total_scr[q] = jnp.where(second, late, early).astype(BF16)
                    remote(total_scr.at[q], total_in.at[p, q], across_send, across_recv, q, across).start()
        out_ref[...] = jnp.where(second, other_scr[...].astype(F32), 0.0)
        for q in range(2):
            remote(total_scr.at[q], total_in.at[parity, q], across_send, across_recv, q, across).wait_send()

    @pl.when(jnp.logical_not(sends))
    def _():
        for q in range(2):
            remote(total_scr.at[q], total_in.at[parity, q], across_send, across_recv, q, across).wait_recv()
            remote(
                total_in.at[parity, q], total_in.at[parity, q], share_send, share_recv, q, core
            ).start()
        for q in range(2):
            remote(
                total_in.at[parity, q], total_in.at[1 - parity, q], share_send, share_recv, q, core
            ).wait()
        for p in range(2):
            for q in range(2):
                cols = slice(p * half, (p + 1) * half)
                part = slice(q * rows, (q + 1) * rows)
                total = total_in[p, q].astype(F32)
                later = other_scr[part, cols].astype(F32) + total * other_decay[0:1, cols]
                out_ref[part, cols] = jnp.where(second, later, total)


def carry_over(state, decay, forward):
    vmem = pl.BlockSpec(memory_space=pltpu.VMEM)
    dma = pltpu.SemaphoreType.DMA
    rows, cols = state.shape
    return pl.pallas_call(
        functools.partial(carry_kernel, forward),
        in_specs=[vmem, vmem],
        out_specs=vmem,
        out_shape=jax.ShapeDtypeStruct(state.shape, F32),
        scratch_shapes=[
            pltpu.VMEM(state.shape, BF16), pltpu.VMEM(decay.shape, F32),
            pltpu.VMEM((2, rows // 2, cols // 2), BF16), pltpu.VMEM((2, 2, rows // 2, cols // 2), BF16),
            dma((2,)), dma((2,)), dma((2,)), dma((2,)), dma((2,)), dma((2,)),
        ],
        compiler_params=pltpu.CompilerParams(
            collective_id=2 if forward else 3, has_side_effects=True, vmem_limit_bytes=VMEM_BYTES
        ),
    )(state, decay)


def finish_exchange(corr, wide, thin, owner, placed):
    row_count = corr.shape[0]
    col_count = wide.shape[1]
    share, width = wide.shape[2:]
    ranks = RANK * col_count if placed else RANK
    vmem = pl.BlockSpec(memory_space=pltpu.VMEM)
    anywhere = pl.BlockSpec(memory_space=pl.ANY)
    dma = pltpu.SemaphoreType.DMA
    return pl.pallas_call(
        tail_kernel,
        in_specs=[anywhere, vmem, vmem, pl.BlockSpec(memory_space=pltpu.SMEM)],
        out_specs=[anywhere] + [vmem] * 5,
        out_shape=[
            jax.ShapeDtypeStruct(corr.shape, corr.dtype),
            jax.ShapeDtypeStruct((row_count, col_count, share, width), F32),
            jax.ShapeDtypeStruct((col_count,) + thin.shape[1:], F32),
            jax.ShapeDtypeStruct((ranks, QUAD, LANES), F32),
            jax.ShapeDtypeStruct((ranks, WIDTH), F32),
            jax.ShapeDtypeStruct(thin.shape[1:], F32),
        ],
        scratch_shapes=[
            *[pltpu.VMEM((row_count // 2,) + value.shape[1:], F32) for value in (wide, thin) * 3],
            pltpu.VMEM(wide.shape[1:], F32), pltpu.VMEM(thin.shape[1:], F32), pltpu.VMEM(wide.shape[1:], F32),
            dma((1,)), dma((3 * row_count,)), dma((3 * row_count,)), dma((row_count,)), dma((row_count,)),
            dma((row_count,)), dma((row_count,)), dma((2 * col_count,)), dma((2 * col_count,)),
            dma((row_count // 2,)), dma((row_count // 2,)), dma((row_count // 2,)), dma((row_count // 2,)),
        ],
        compiler_params=pltpu.CompilerParams(
            collective_id=0, has_side_effects=True, vmem_limit_bytes=VMEM_BYTES
        ),
    )(corr, wide, thin, owner)


def whole_spec(shape):
    return pl.BlockSpec(shape, lambda c, s: (0,) * len(shape))


def lead_spec(shape):
    return pl.BlockSpec((1,) + tuple(shape[1:]), lambda c, s: (c,) + (0,) * (len(shape) - 1))


def lane_spec(shape):
    block = tuple(shape[:-1]) + (WIDTH,)
    return pl.BlockSpec(block, lambda c, s: (0,) * (len(shape) - 1) + (c,))


def second_spec(shape):
    block = (shape[0], 1) + tuple(shape[2:])
    return pl.BlockSpec(block, lambda c, s: (0, c) + (0,) * (len(shape) - 2))


def front_spec(shape):
    if shape[2] % 3 == 0 and shape[2] // 3 * 2 >= WIDTH and shape[3] == 2 * WIDTH and shape[1] == 4:
        return pl.BlockSpec((1, shape[1], shape[2] // 3 * 2, shape[3]), lambda c, s: (c, 0, 0, 0))
    return lead_spec(shape)


def full_back_spec(shape):
    if shape[2] > WIDTH:
        return pl.BlockSpec((shape[0], shape[1], shape[2] // 3, shape[3]), lambda c, s: (0, 0, 2, 0))
    return whole_spec(shape)


def back_spec(shape):
    if shape[2] > WIDTH:
        return pl.BlockSpec((1, shape[1], shape[2] // 3, shape[3]), lambda c, s: (c, 0, 2, 0))
    return lead_spec(shape)


def up_spec(shape):
    first = WIDTH // RANK if shape[2] > RANK else 0
    return pl.BlockSpec((1, 1, RANK, 2 * WIDTH), lambda c, s: (c, s[0], first + s[1], 0))


def down_spec(shape):
    first = shape[2] // RANK - 1
    return pl.BlockSpec((1, 1, RANK, WIDTH), lambda c, s: (c, s[0], first, s[1]))


KINDS = {
    "a": whole_spec, "c": lead_spec, "l": lane_spec, "s": second_spec, "w": front_spec, "f": full_back_spec,
    "p": back_spec, "u": up_spec, "d": down_spec,
}


def grouped_call(kernel, place, inputs, kinds, outputs, out_kinds, scratch, flops=0):
    return pl.pallas_call(
        kernel,
        grid_spec=pltpu.PrefetchScalarGridSpec(
            num_scalar_prefetch=1,
            grid=(GROUPS,),
            in_specs=[KINDS[kind](value.shape) for kind, value in zip(kinds, inputs)],
            out_specs=[KINDS[kind](shape) for kind, (shape, _) in zip(out_kinds, outputs)],
            scratch_shapes=[pltpu.VMEM(shape, dtype) for shape, dtype in scratch],
        ),
        out_shape=[jax.ShapeDtypeStruct(shape, dtype) for shape, dtype in outputs],
        compiler_params=pltpu.CompilerParams(vmem_limit_bytes=VMEM_BYTES),
        cost_estimate=pl.CostEstimate(flops=flops, bytes_accessed=40_000_000, transcendentals=0),
    )(place, *inputs)


def to_groups(value, heads_here):
    cols = value.shape[0]
    middle = value.shape[1:-1]
    if heads_here == QUAD:
        return value
    if heads_here > QUAD:
        parts = heads_here // QUAD
        value = value.reshape((cols,) + middle + (parts, WIDTH))
        value = jnp.moveaxis(value, -2, 1)
        return value.reshape((GROUPS,) + middle + (WIDTH,))
    parts = QUAD // heads_here
    value = value.reshape((GROUPS, parts) + middle + (heads_here * P_SIZE,))
    value = jnp.moveaxis(value, 1, -2)
    return value.reshape((GROUPS,) + middle + (WIDTH,))


def to_cols(value, heads_here, col_count):
    middle = value.shape[1:-1]
    if heads_here == QUAD:
        return value
    if heads_here > QUAD:
        parts = heads_here // QUAD
        value = value.reshape((col_count, parts) + middle + (WIDTH,))
        value = jnp.moveaxis(value, 1, -2)
        return value.reshape((col_count,) + middle + (heads_here * P_SIZE,))
    parts = QUAD // heads_here
    value = value.reshape((GROUPS,) + middle + (parts, heads_here * P_SIZE))
    value = jnp.moveaxis(value, -2, 1)
    return value.reshape((col_count,) + middle + (heads_here * P_SIZE,))


def pad_lanes(value, width):
    return jnp.pad(value, [(0, 0)] * (value.ndim - 1) + [(0, width - value.shape[-1])])


def carry_in(state, decay, row_count, col_count, seq_cols, forward):
    row = lax.axis_index("row")
    col = lax.axis_index("col")
    total = state
    factor = decay
    before = jnp.zeros(state.shape, F32)
    reach = jnp.ones_like(decay)
    span = 1
    while span < row_count:
        pairs = [(i, i ^ span) for i in range(row_count)]
        other = lax.ppermute(total, "row", pairs).astype(F32)
        other_factor = lax.ppermute(factor, "row", pairs)
        behind = ((row & span) != 0) == forward
        mine = total.astype(F32)
        before = jnp.where(behind, before + reach * other, before)
        reach = jnp.where(behind, reach * other_factor, reach)
        joined = jnp.where(behind, other * factor + mine, mine * other_factor + other)
        total = joined.astype(BF16)
        factor = factor * other_factor
        span *= 2
    place = lax.rem(col, seq_cols)
    for hop in range(1, seq_cols):
        shift = hop if forward else -hop
        pairs = [(i, (i + shift) % col_count) for i in range(col_count)]
        other = lax.ppermute(total, "col", pairs).astype(F32)
        other_factor = lax.ppermute(factor, "col", pairs)
        inside = place >= hop if forward else place < seq_cols - hop
        before = jnp.where(inside, before + reach * other, before)
        reach = jnp.where(inside, reach * other_factor, reach)
    return before


def per_device(
    block_in, norm_gain, proj_inner, proj_state, conv_inner, conv_inner_bias, conv_state, conv_state_bias,
    step_bias, decay_log, skip_gain, gate_gain, proj_out, adapt_in_down, adapt_in_up, adapt_out_down,
    adapt_out_up, adapter_id, cotangent,
):
    row_count = lax.axis_size("row")
    col_count = lax.axis_size("col")
    row = lax.axis_index("row")
    col = lax.axis_index("col")
    col_tokens, part = block_in.shape
    chunk = col_tokens // row_count
    total_rows = chunk + HALO
    blocks = chunk // BLOCK
    seq_cols = SEQ // col_tokens
    heads_here = proj_inner.shape[1]
    local = heads_here * P_SIZE
    rank_total = adapt_in_down.shape[1]
    rank_part = rank_total // row_count
    rank_share = rank_total // col_count
    adapter = lax.dynamic_index_in_dim(adapter_id, col // seq_cols, keepdims=False)

    relayed = row_count == 4 and heads_here == QUAD and seq_cols == 1 and part == WIDTH and rank_share == RANK
    place = jnp.zeros((2,), jnp.int32)
    if relayed:
        x_rows, w_all, w_state, gain_all, vectors, head_rows, place = start_exchange(
            block_in, proj_inner.reshape(part, 2 * local), adapt_in_up.reshape(rank_total, 2 * local), proj_out,
            adapt_out_down, (proj_state.T, adapt_in_down, adapt_out_up),
            (
                norm_gain[None], conv_inner, conv_inner_bias[None], gate_gain[None], step_bias[None],
                decay_log[None], skip_gain[None],
            ),
            adapter_id, row_count, col_count,
        )
        up_all = down_all = p_all = w_all
        x_rows, cot = lax.optimization_barrier((x_rows, cotangent))
        g_rows = lax.all_to_all(cot.reshape(row_count, chunk, part), "row", 0, 0, tiled=True)
    else:
        head = jnp.zeros((HALO, part), BF16)
        if seq_cols > 1:
            pairs = [(i, (i + 1) % col_count) for i in range(col_count)]
            head = lax.ppermute(block_in[-HALO:], "col", pairs)
            head = jnp.where(lax.rem(col, seq_cols) > 0, head, jnp.zeros_like(head))
        padded = jnp.concatenate([head, block_in], axis=0)
        windows = jnp.stack([padded[r * chunk : r * chunk + total_rows] for r in range(row_count)])
        x_rows = lax.all_to_all(windows, "row", 0, 0, tiled=True)
        g_rows = lax.all_to_all(cotangent.reshape(row_count, chunk, part), "row", 0, 0, tiled=True)

        def split_pairs(value):
            value = value.reshape(value.shape[0], heads_here, 2, P_SIZE)
            return jnp.swapaxes(value, 1, 2).reshape(value.shape[0], 2, local)

        up_part = lax.dynamic_slice_in_dim(adapt_in_up, row * rank_part, rank_part, 0)
        w_block = jnp.concatenate([split_pairs(proj_inner), split_pairs(up_part)], axis=0)
        w_all = lax.all_gather(w_block.reshape(part + rank_part, 2 * local), ("col", "row"))
        w_all = w_all.reshape(col_count, row_count, part + rank_part, 2, local)
        w_all = to_groups(w_all, heads_here).reshape(GROUPS, row_count, part + rank_part, 2 * WIDTH)
        up_all = w_all[:, :, part:, :].reshape(GROUPS, rank_total, 2 * WIDTH)
        up_all = lax.dynamic_slice_in_dim(up_all, adapter * RANK, RANK, 1)[:, None]

        down_part = lax.dynamic_slice_in_dim(adapt_out_down, row * rank_part, rank_part, 0)
        p_block = jnp.concatenate([proj_out, down_part.T], axis=1)
        p_all = lax.all_gather(p_block, ("col", "row")).reshape(col_count, row_count, local, part + rank_part)
        if heads_here != QUAD:
            p_all = jnp.moveaxis(p_all, 1, 0).reshape(row_count, GROUPS, WIDTH, part + rank_part)
            p_all = jnp.moveaxis(p_all, 0, 1)
        down_all = jnp.swapaxes(p_all[..., part:], 1, 2).reshape(GROUPS, WIDTH, rank_total)
        down_all = jnp.swapaxes(lax.dynamic_slice_in_dim(down_all, adapter * RANK, RANK, 2), 1, 2)[:, None]

        in_down = lax.dynamic_slice_in_dim(adapt_in_down, adapter * RANK, RANK, 1)
        out_up = lax.dynamic_slice_in_dim(adapt_out_up, adapter * RANK, RANK, 1)
        shared = pad_lanes(jnp.concatenate([proj_state, in_down, out_up], axis=1), 384)
        w_state = lax.all_gather(shared, "row")
        gain_all = lax.all_gather(norm_gain, "row").reshape(row_count, 1, part)

        scalars = jnp.concatenate([step_bias, decay_log, skip_gain])
        vectors = jnp.concatenate(
            [conv_inner, conv_inner_bias[None], gate_gain[None], pad_lanes(scalars, local)[None]], axis=0
        )
        vectors = lax.all_gather(vectors, "col")
        scalars = vectors[:, 6, : 3 * heads_here].reshape(col_count, 3, heads_here)
        scalars = jnp.swapaxes(scalars, 0, 1).reshape(3, HEADS)
        head_rows = jnp.pad(scalars[:2], ((0, 6), (0, LANES - HEADS)))
        skip_wide = jnp.repeat(scalars[2], P_SIZE).reshape(GROUPS, 1, WIDTH)
        vectors = jnp.concatenate(
            [to_groups(vectors[:, :6], heads_here), skip_wide, jnp.zeros_like(skip_wide)], axis=1
        )
    state_taps = conv_state

    token_f32 = ((chunk, LANES), F32)
    token_low = ((chunk, LANES), BF16)
    inner_low = ((chunk, DI), BF16)
    states = ((blocks, STATES, DI), BF16)
    score_box = ((blocks, BLOCK, BLOCK), F32)
    flipped = ((blocks, STATES, BLOCK), BF16)
    (
        normed, scpre, ratio, sig, cum, lead, turned, bs, cs, cs_t, adv, gate, u, eloc, fin, dec,
    ) = grouped_call(
        front_kernel,
        place,
        (x_rows, gain_all, w_state, state_taps, conv_state_bias[None], head_rows, w_all, up_all, vectors),
        "aaaaaawuc",
        [
            ((total_rows, D), BF16), ((chunk, 256), F32), token_f32, token_f32, token_f32, token_f32,
            ((GROUPS, 2 * QUAD, chunk), F32), token_low, token_low, flipped, ((total_rows, LANES), BF16),
            inner_low, inner_low, states, ((STATES, DI), BF16), ((8, DI), F32),
        ],
        "aaaaaaaaaaalllll",
        [((total_rows, 384), F32), flipped, ((total_rows, WIDTH), F32)],
        flops=int(45e9),
    )
    decay = dec[0:1]
    fin, g_rows = lax.optimization_barrier((fin, g_rows))
    if relayed:
        entry = carry_over(fin, dec, True)
    else:
        entry = carry_in(fin, decay, row_count, col_count, seq_cols, True)
    out_rows, o, ent, aux, side_grad, out_up_grad = grouped_call(
        scan_kernel,
        place,
        (x_rows, g_rows, w_state, p_all, down_all, vectors, gate, u, eloc, entry, cum, turned, bs, cs),
        "aaafdcllllacaa",
        [
            ((row_count, chunk, part), BF16), inner_low, ((blocks, STATES, DI), BF16), token_f32, token_low,
            ((RANK, D), F32),
        ],
        "allaaa",
        [score_box, ((GROUPS, chunk, WIDTH), BF16), token_f32, token_f32],
        flops=int(45e9),
    )
    block_out = lax.all_to_all(out_rows, "row", 0, 0, tiled=True).reshape(col_tokens, part)
    dgate, dy, gloc, gfin, out_down_grad = grouped_call(
        gate_kernel,
        place,
        (g_rows, p_all, side_grad, down_all, vectors, gate, o, aux, cum, cs_t),
        "apadcllaaa",
        [inner_low, inner_low, states, ((STATES, DI), BF16), ((GROUPS, RANK, WIDTH), F32)],
        "llllc",
        [((blocks, RANK, BLOCK), BF16)],
        flops=int(25e9),
    )
    gfin, block_out = lax.optimization_barrier((gfin, block_out))
    if relayed:
        exit_grad = carry_over(gfin, dec, False)
    else:
        exit_grad = carry_in(gfin, decay, row_count, col_count, seq_cols, False)
    corr, wide, thin = grouped_call(
        back_kernel,
        place,
        (
            x_rows, gain_all, normed, w_state, w_all, up_all, adv, vectors, state_taps, head_rows,
            u, o, dy, dgate, ent, gloc, exit_grad, cum, lead, turned, ratio, sig, scpre, bs, cs,
            out_down_grad, out_up_grad,
        ),
        "aaaawuacaalllllllaacaaaaaca",
        [
            ((row_count, total_rows, part), BF16), ((row_count, GROUPS, RANK // row_count, 3 * WIDTH), F32),
            ((row_count, 2 * RANK, part), F32),
        ],
        "asa",
        [
            score_box, score_box, token_f32, token_f32, token_f32, token_f32, ((blocks, 8, LANES), F32),
            ((total_rows + HALO, WIDTH), F32), ((total_rows, 2 * WIDTH), BF16), ((total_rows, D), F32),
            ((total_rows, LANES), F32), ((blocks, RANK, BLOCK), BF16),
            ((RANK, 2 * WIDTH), F32), ((RANK, D), F32),
        ],
        flops=int(75e9),
    )

    if heads_here != QUAD:
        share = RANK // row_count
        wide = jnp.swapaxes(wide.reshape(row_count, GROUPS, share, 3, WIDTH), 0, 1)
        wide = to_cols(wide, heads_here, col_count)
        wide = jnp.swapaxes(wide, 0, 1).reshape(row_count, col_count, share, 3 * local)
    corr, wide, thin, in_up, out_down, mine = finish_exchange(corr, wide, thin, adapter_id, relayed)
    late = jnp.zeros((1, HALO, part), BF16)
    if seq_cols > 1:
        pairs = [(i, (i - 1) % col_count) for i in range(col_count)]
        late = lax.ppermute(corr[0:1, :HALO], "col", pairs)
        late = jnp.where(lax.rem(col, seq_cols) < seq_cols - 1, late, jnp.zeros_like(late))
    early = jnp.concatenate([corr[1:, :HALO], late], axis=0)
    early = jnp.pad(early, ((0, 0), (chunk - HALO, 0), (0, 0))).astype(F32)
    input_grad = cotangent.reshape(row_count, chunk, part).astype(F32) + corr[:, HALO:].astype(F32) + early
    input_grad = input_grad.reshape(col_tokens, part)
    if relayed:
        mine = jnp.swapaxes(mine.reshape(2, RANK, part), 1, 2)
        return block_out, input_grad, mine[0], in_up, out_down, mine[1]
    wide = jnp.swapaxes(wide, 0, 1).reshape(col_count, RANK, 3 * local)
    owner = jnp.repeat(adapter_id, seq_cols)
    adapters = rank_total // RANK
    chosen = owner[:, None] == jnp.arange(adapters, dtype=jnp.int32)[None, :]
    wide = jnp.sum(jnp.where(chosen[:, :, None, None], wide[:, None], 0.0), axis=0)
    wide = wide.reshape(rank_total, 3 * local)
    in_up = wide[:, : 2 * local].reshape(rank_total, 2, heads_here, P_SIZE)
    in_up = jnp.swapaxes(in_up, 1, 2).reshape(rank_total, heads_here, 2 * P_SIZE)
    out_down = wide[:, 2 * local :]
    if rank_share <= RANK:
        mine = owner == (col * rank_share) // RANK
        thin = jnp.sum(jnp.where(mine[:, None, None], thin, 0.0), axis=0).reshape(2, RANK, part)
        thin = lax.dynamic_slice_in_dim(thin, lax.rem(col * rank_share, RANK), rank_share, 1)
        thin = jnp.swapaxes(thin, 1, 2)
    else:
        thin = jnp.sum(jnp.where(chosen[:, :, None, None], thin[:, None], 0.0), axis=0)
        thin = thin.reshape(adapters, 2, RANK, part)
        thin = jnp.transpose(thin, (1, 3, 0, 2)).reshape(2, part, rank_total)
        thin = lax.dynamic_slice_in_dim(thin, col * rank_share, rank_share, 2)
    return block_out, input_grad, thin[0], in_up, out_down, thin[1]


def solution(mesh):
    placed = (
        P("col", "row"), P("row"), P("row", "col", None), P("row", None), P(None, "col"), P("col"), P(), P(),
        P("col"), P("col"), P("col"), P("col"), P("col", "row"), P("row", None), P(None, "col", None),
        P(None, "col"), P("row", None), P(), P("col", "row"),
    )
    return jax.shard_map(
        per_device,
        mesh=mesh,
        in_specs=placed,
        out_specs=(
            P("col", "row"), P("col", "row"), P("row", "col"), P(None, "col", None), P(None, "col"),
            P("row", "col"),
        ),
        check_vma=False,
    )
```

```python
import functools

import jax
import jax.numpy as jnp
from jax import lax
from jax.experimental import pallas as pl
from jax.experimental.pallas import tpu as pltpu
from jax.sharding import PartitionSpec as P

D = 1024
HEADS = 32
P_SIZE = 64
STATES = 128
BLOCK = 256
RANK = 16
SEQ = 4096
DI = 2048
EPS = 1e-05
LOG2E = 1.4426950408889634

HALO = 16
IN_LANE = 32
OUT_LANE = 48
CAP = 80.0
QUAD = 4
WIDTH = QUAD * P_SIZE
GROUPS = HEADS // QUAD
LANES = 128
VMEM_BYTES = 60 * 1024 * 1024
F32 = jnp.float32
BF16 = jnp.bfloat16
MESH = pl.DeviceIdType.MESH


def mm(left, right):
    return jnp.dot(left, right, preferred_element_type=F32)


def mm_nt(left, right):
    return lax.dot_general(left, right, (((1,), (1,)), ((), ())), preferred_element_type=F32)


def mm_tn(left, right):
    return lax.dot_general(left, right, (((0,), (0,)), ((), ())), preferred_element_type=F32)


def split_left(ones, value):
    high = value.astype(BF16)
    rest = value - high.astype(F32)
    middle = rest.astype(BF16)
    low = (rest - middle.astype(F32)).astype(BF16)
    return mm(ones, high) + mm(ones, middle) + mm(ones, low)


def split_right(value, ones):
    high = value.astype(BF16)
    low = (value - high.astype(F32)).astype(BF16)
    return mm(high, ones) + mm(low, ones)


def sigmoid(value):
    return 0.5 * jnp.tanh(0.5 * value) + 0.5


def iota(shape, axis):
    return lax.broadcasted_iota(jnp.int32, shape, axis)


def widen(cols):
    lane = iota((cols.shape[0], LANES), 1) < P_SIZE
    left = jnp.where(lane, cols[:, 0:1], cols[:, 1:2])
    right = jnp.where(lane, cols[:, 2:3], cols[:, 3:4])
    return jnp.concatenate([left, right], axis=1)


def to_front(cols, group):
    return pltpu.roll(cols, lax.rem(LANES - QUAD * group, LANES), 1)


def lane_range(values, first):
    lane = iota(values.shape, 1)
    return jnp.where((lane >= first) & (lane < first + RANK), values, 0.0)


def out_block(w_ref, group, row, part):
    if w_ref.shape[2] == WIDTH:
        return w_ref[group, row, :, :part]
    rows = WIDTH // 2
    return jnp.concatenate([w_ref[group, row, :rows, :part], w_ref[group, row, :rows, part:]], axis=0)


def head_only(values, head):
    lane = iota(values.shape, 1) // P_SIZE
    return jnp.where(lane == head, values, jnp.zeros_like(values))


def delays(window, taps, bias):
    total = window[8:] * taps[0:1] + bias
    for k in range(1, 4):
        total = total + pltpu.roll(window, k, 0)[8:] * taps[k : k + 1]
    return total


def advances(window, taps, count):
    length = window.shape[0]
    total = window[:count] * taps[0:1]
    for k in range(1, 4):
        total = total + pltpu.roll(window, length - k, 0)[:count] * taps[k : k + 1]
    return total


def at_block(k):
    if isinstance(k, int):
        return pl.ds(k * BLOCK, BLOCK)
    return pl.ds(pl.multiple_of(k * BLOCK, BLOCK), BLOCK)


def at_rows(k):
    if isinstance(k, int):
        return pl.ds(HALO + k * BLOCK, BLOCK)
    return pl.ds(pl.multiple_of(HALO + k * BLOCK, HALO), BLOCK)


def with_halo(k):
    if k == 0:
        return pl.ds(0, HALO + BLOCK)
    return pl.ds(HALO + k * BLOCK, BLOCK)


def padded_rows(value, first):
    before = jnp.zeros((first, value.shape[1]), value.dtype)
    after = jnp.zeros((LANES - first - value.shape[0], value.shape[1]), value.dtype)
    return jnp.concatenate([before, value, after], axis=0)


def front_kernel(
    place_ref, x_ref, gain_ref, wst_ref, sp_ref, sb_ref, hp_ref, w_ref, up_ref, vp_ref,
    normed_ref, scpre_ref, ratio_ref, sig_ref, cum_ref, lead_ref, turned_ref, bs_ref, cs_ref, cs_t_ref, adv_ref,
    gate_ref, u_ref, eloc_ref, fin_ref, dec_ref,
    st_scr, bs_t_scr, val_scr,
):
    group = pl.program_id(0)
    row_count, _, part = x_ref.shape
    blocks = eloc_ref.shape[0]

    @pl.when(group == 0)
    def _():
        def project(rows):
            pieces = [x_ref[r, rows, :].astype(F32) for r in range(row_count)]
            square = sum(jnp.sum(piece * piece, axis=1, keepdims=True) for piece in pieces)
            inv = lax.rsqrt(square / D + EPS)
            total = None
            for r in range(row_count):
                normed = (pieces[r] * inv * gain_ref[r]).astype(BF16)
                normed_ref[rows, r * part : (r + 1) * part] = normed
                term = mm(normed, wst_ref[r])
                total = term if total is None else total + term
            st_scr[rows, :] = total
            adv_ref[rows, :] = lane_range(total[:, 256:384], IN_LANE).astype(BF16)

        project(pl.ds(0, HALO))

        @pl.loop(0, blocks)
        def _(k):
            project(at_rows(k))

        lower = (iota((BLOCK, BLOCK), 0) >= iota((BLOCK, BLOCK), 1)).astype(BF16)
        rate = -jnp.exp(hp_ref[1:2]) * LOG2E

        @pl.loop(0, blocks)
        def _(k):
            window = st_scr[pl.ds(pl.multiple_of(8 + k * BLOCK, 8), BLOCK + 8), :256]
            pre = delays(window, sp_ref[...], sb_ref[...])
            conv = pre * sigmoid(pre)
            b_rows = conv[:, :STATES].astype(BF16)
            c_rows = conv[:, STATES:].astype(BF16)
            scpre_ref[at_block(k), :] = pre
            bs_ref[at_block(k), :] = b_rows
            cs_ref[at_block(k), :] = c_rows
            bs_t_scr[k] = conv[:, :STATES].T.astype(BF16)
            cs_t_ref[k] = conv[:, STATES:].T.astype(BF16)
            raw = st_scr[at_rows(k), 256:384] + hp_ref[0:1]
            small = jnp.exp(-jnp.abs(raw))
            tail = jnp.where(
                small < 0.01, small * (1.0 - small * (0.5 - small * (1.0 / 3.0))), jnp.log(1.0 + small)
            )
            step = jnp.maximum(raw, 0.0) + tail
            cum = split_left(lower, step * rate)
            sig = sigmoid(raw)
            ratio_ref[at_block(k), :] = jnp.where(raw < -20.0, 1.0, sig / jnp.maximum(step, 1e-30))
            sig_ref[at_block(k), :] = sig
            lead = jnp.log(jnp.maximum(step, 1e-37)) * LOG2E - cum
            cum_ref[at_block(k), :] = cum
            lead_ref[at_block(k), :] = lead
            flipped = cum.T
            flipped_lead = lead.T
            for g in range(GROUPS):
                turned_ref[g, :QUAD, at_block(k)] = flipped[g * QUAD : (g + 1) * QUAD]
                turned_ref[g, QUAD:, at_block(k)] = flipped_lead[g * QUAD : (g + 1) * QUAD]

    up_rows = padded_rows(up_ref[0, 0], IN_LANE)

    def inner(rows):
        total = mm(adv_ref[rows, :], up_rows)
        for r in range(row_count):
            total = total + mm(normed_ref[rows, r * part : (r + 1) * part], w_ref[0, r, :part, :])
        return total

    taps = vp_ref[0]

    def one_block(k, carry):
        state, decay = carry
        product = inner(with_halo(k))
        skip = HALO if k == 0 else 0
        gate_ref[at_block(k), :] = product[skip:, :WIDTH].astype(BF16)
        val_scr[with_halo(k), :] = product[:, WIDTH:]
        window = val_scr[pl.ds(8 + k * BLOCK, BLOCK + 8), :]
        pre = delays(window, taps[0:4], taps[4:5])
        u_ref[at_block(k), :] = pre.astype(BF16)
        xs = (pre * sigmoid(pre)).astype(BF16).astype(F32)
        cum = cum_ref[at_block(k), :]
        last = cum[BLOCK - 1 : BLOCK]
        weight = to_front(jnp.exp2(last + lead_ref[at_block(k), :]), group)
        weighted = (xs * widen(weight)).astype(BF16)
        eloc_ref[k] = state.astype(BF16)
        last8 = to_front(jnp.broadcast_to(last, (8, LANES)), group)
        fall = widen(jnp.exp2(last8))[0:1]
        return fall * state + mm(bs_t_scr[k], weighted), decay * fall

    carry = (jnp.zeros((STATES, WIDTH), F32), jnp.ones((1, WIDTH), F32))
    for k in range(blocks):
        carry = one_block(k, carry)
    state, decay = carry
    fin_ref[...] = state.astype(BF16)
    dec_ref[...] = jnp.broadcast_to(decay, (8, WIDTH))


def scan_kernel(
    place_ref, x_ref, g_ref, wst_ref, w_ref, down_ref, vp_ref, gate_ref, u_ref, eloc_ref, ein_ref,
    cum_ref, turned_ref, bs_ref, cs_ref,
    out_ref, o_ref, ent_ref, aux_ref, sg_ref, gup_ref,
    score_scr, gained_scr, side_scr, square_scr,
):
    group = pl.program_id(0)
    row_count, _, part = x_ref.shape
    blocks = eloc_ref.shape[0]

    @pl.when(group == 0)
    def _():
        side_scr[...] = jnp.zeros_like(side_scr)
        square_scr[...] = jnp.zeros_like(square_scr)
        keep = iota((BLOCK, BLOCK), 0) >= iota((BLOCK, BLOCK), 1)

        @pl.loop(0, blocks)
        def _(k):
            score = mm_nt(cs_ref[at_block(k), :], bs_ref[at_block(k), :])
            score_scr[k] = jnp.where(keep, score, 0.0)

    taps = vp_ref[0]

    down_rows = padded_rows(down_ref[0, 0], OUT_LANE)

    def one_block(k, before):
        rows = at_block(k)
        pre = u_ref[rows, :].astype(F32)
        conv = pre * sigmoid(pre)
        cum = to_front(cum_ref[rows, :], group)
        xs = conv.astype(BF16)
        score = score_scr[k]
        entering = (eloc_ref[k].astype(F32) + before * ein_ref[...]).astype(BF16)
        ent_ref[k] = entering
        total = widen(jnp.exp2(cum)) * mm(cs_ref[rows, :], entering)
        for h in range(QUAD):
            spread = cum[:, h : h + 1] + turned_ref[0, QUAD + h : QUAD + h + 1, rows]
            weights = (score * jnp.exp2(jnp.minimum(spread, CAP))).astype(BF16)
            total = total + mm(weights, head_only(xs, h))
        output = total + taps[6:7] * conv
        o_ref[rows, :] = output.astype(BF16)
        gate = gate_ref[rows, :].astype(F32)
        gated = output * gate * sigmoid(gate)
        square = gated * gated
        square_scr[rows, :] += square[:, :LANES] + square[:, LANES:]
        gained = (gated * taps[5:6]).astype(BF16)
        gained_scr[group, rows, :] = gained
        side_scr[rows, :] += mm_nt(gained, down_rows)
        return before * widen(jnp.exp2(cum[BLOCK - 8 :]))[7:8]

    before = jnp.ones((1, WIDTH), F32)
    for k in range(blocks):
        before = one_block(k, before)

    @pl.when(group == pl.num_programs(0) - 1)
    def _():
        gup_ref[...] = jnp.zeros_like(gup_ref)

        @pl.loop(0, blocks)
        def _(k):
            rows = at_block(k)
            mean = jnp.sum(square_scr[rows, :], axis=1, keepdims=True) / DI
            rms = lax.rsqrt(mean + EPS)
            side_raw = side_scr[rows, :]
            side = (side_raw * rms).astype(BF16)
            side_grad = None
            for r in range(row_count):
                term = mm(g_ref[r, rows, :], wst_ref[r, :, 256:384])
                side_grad = term if side_grad is None else side_grad + term
            side_grad = lane_range(side_grad, OUT_LANE).astype(BF16)
            product = jnp.sum(side_grad.astype(F32) * side_raw, axis=1, keepdims=True)
            for r in range(row_count):
                cols = slice(r * part, (r + 1) * part)
                raw = mm(gained_scr[0, rows, :], out_block(w_ref, 0, r, part))
                for c in range(1, GROUPS):
                    raw = raw + mm(gained_scr[c, rows, :], out_block(w_ref, c, r, part))
                cot = g_ref[r, rows, :]
                product = product + jnp.sum(raw * cot.astype(F32), axis=1, keepdims=True)
                total = x_ref[r, at_rows(k), :].astype(F32) + raw * rms + mm_nt(side, wst_ref[r, :, 256:384])
                out_ref[r, rows, :] = total.astype(BF16)
                gup_ref[:, cols] += mm_tn(side, cot)[OUT_LANE : OUT_LANE + RANK]
            coefficient = rms * rms * rms * product / DI
            lane = iota((BLOCK, LANES), 1)
            aux_ref[rows, :] = jnp.where(lane == 0, rms, coefficient)
            sg_ref[rows, :] = side_grad


def gate_kernel(
    place_ref, g_ref, w_ref, sg_ref, down_ref, vp_ref, gate_ref, o_ref, aux_ref, cum_ref, cs_t_ref,
    dgate_ref, dy_ref, gloc_ref, gfin_ref, gdown_ref,
    sg_t_scr,
):
    group = pl.program_id(0)
    row_count, _, part = g_ref.shape
    blocks = gloc_ref.shape[0]

    @pl.when(group == 0)
    def _():
        @pl.loop(0, blocks)
        def _(k):
            sg_t_scr[k] = sg_ref[at_block(k), :].astype(F32).T[OUT_LANE : OUT_LANE + RANK].astype(BF16)

    taps = vp_ref[0]
    gdown_ref[0] = jnp.zeros((RANK, WIDTH), F32)

    down_rows = padded_rows(down_ref[0, 0], OUT_LANE)

    def one_block(i, state):
        k = blocks - 1 - i
        rows = at_block(k)
        dmix = mm(sg_ref[rows, :], down_rows)
        for r in range(row_count):
            dmix = dmix + mm_nt(g_ref[r, rows, :], out_block(w_ref, 0, r, part))
        gate = gate_ref[rows, :].astype(F32)
        output = o_ref[rows, :].astype(F32)
        sig = sigmoid(gate)
        act = gate * sig
        gated = output * act
        rms = aux_ref[rows, 0:1]
        coefficient = aux_ref[rows, 1:2]
        scale = rms * taps[5:6]
        mixed = (gated * scale).astype(BF16)
        gdown_ref[0] += mm(sg_t_scr[k], mixed)
        gated_grad = scale * dmix - gated * coefficient
        dy = gated_grad * act
        dgate = gated_grad * output * (sig + act * (1.0 - sig))
        dgate_ref[rows, :] = dgate.astype(BF16)
        dy_ref[rows, :] = dy.astype(BF16)
        cum = to_front(cum_ref[rows, :], group)
        factor = widen(jnp.exp2(cum))
        gloc_ref[k] = state.astype(BF16)
        return factor[BLOCK - 1 : BLOCK] * state + mm(cs_t_ref[k], (factor * dy).astype(BF16))

    state = jnp.zeros((STATES, WIDTH), F32)
    for i in range(blocks):
        state = one_block(i, state)
    gfin_ref[...] = state.astype(BF16)


def back_kernel(
    place_ref, x_ref, gain_ref, normed_ref, wst_ref, w_ref, up_ref, adv_ref, vp_ref, sp_ref, hp_ref,
    u_ref, o_ref, dy_ref, dgate_ref, ent_ref, gloc_ref, gin_ref,
    cum_ref, lead_ref, turned_ref, ratio_ref, sig_ref, scpre_ref, bs_ref, cs_ref, out_down_ref, out_up_ref,
    corr_ref, wide_ref, thin_ref,
    score_scr, dscore_scr, db_scr, dc_scr, dcum_scr, dstep_scr, dlast_scr, du_scr, ig_scr, ng_scr, adg_scr, adv_t_scr, up_scr, in_scr,
):
    group = pl.program_id(0)
    row_count, _, part = x_ref.shape
    blocks = gloc_ref.shape[0]
    total_rows = normed_ref.shape[0]

    @pl.when(group == 0)
    def _():
        for ref in (dscore_scr, db_scr, dc_scr, dcum_scr, dstep_scr, dlast_scr, ng_scr, adg_scr):
            ref[...] = jnp.zeros_like(ref)
        du_scr[0:HALO, :] = jnp.zeros((HALO, WIDTH), F32)
        du_scr[total_rows : total_rows + HALO, :] = jnp.zeros((HALO, WIDTH), F32)

        @pl.loop(0, blocks)
        def _(k):
            score_scr[k] = mm_nt(bs_ref[at_block(k), :], cs_ref[at_block(k), :])
            adv_t_scr[k] = adv_ref[at_rows(k), :].astype(F32).T[IN_LANE : IN_LANE + RANK].astype(BF16)

    keep = iota((BLOCK, BLOCK), 0) <= iota((BLOCK, BLOCK), 1)
    taps = vp_ref[0]
    pick = (iota((WIDTH, LANES), 1) == QUAD * group + iota((WIDTH, LANES), 0) // P_SIZE).astype(BF16)

    def one_block(i, after):
        k = blocks - 1 - i
        rows = at_block(k)
        pre = u_ref[rows, :].astype(F32)
        sig = sigmoid(pre)
        conv = pre * sig
        xs_low = conv.astype(BF16)
        xs = xs_low.astype(F32)
        cum = to_front(cum_ref[rows, :], group)
        lead = to_front(lead_ref[rows, :], group)
        dy_low = dy_ref[rows, :]
        dy = dy_low.astype(F32)
        b_rows = bs_ref[rows, :]
        c_rows = cs_ref[rows, :]
        score = jnp.where(keep, score_scr[k], 0.0)
        dscore = dscore_scr[k]
        ending = gloc_ref[k].astype(F32) + after * gin_ref[...]
        ending_low = ending.astype(BF16)
        last = cum[BLOCK - 1 : BLOCK]
        to_end = widen(jnp.exp2(last + lead))
        dxs_state = to_end * mm(b_rows, ending_low)
        dxs = dxs_state
        for h in range(QUAD):
            spread = turned_ref[0, h : h + 1, rows] + lead[:, h : h + 1]
            damp = jnp.exp2(jnp.minimum(spread, CAP))
            weights = (score * damp).astype(BF16)
            dy_head = head_only(dy_low, h)
            dxs = dxs + mm(weights, dy_head)
            dscore = dscore + mm_nt(xs_low, dy_head) * damp
        dscore_scr[k] = dscore
        from_start = widen(jnp.exp2(cum))
        fall = from_start[BLOCK - 1 : BLOCK]
        entering_low = ent_ref[k]
        entering = entering_low.astype(F32)
        dc_scr[rows, :] += mm_nt((from_start * dy).astype(BF16), entering_low)
        db_scr[rows, :] += mm_nt((to_end * xs).astype(BF16), ending_low)
        scan_out = o_ref[rows, :].astype(F32) - taps[6:7] * conv
        inward = mm((xs * dxs).astype(BF16), pick)
        dcum_scr[rows, :] += mm((dy * scan_out).astype(BF16), pick) - inward
        dstep_scr[rows, :] += inward
        ends = jnp.sum(xs * dxs_state, axis=0, keepdims=True)
        ends = ends + fall * jnp.sum(entering * ending, axis=0, keepdims=True)
        dlast_scr[k] += split_right(jnp.broadcast_to(ends, (8, WIDTH)), pick)
        dconv = taps[6:7] * dy + dxs
        du_scr[at_rows(k), :] = dconv * (sig + conv * (1.0 - sig))
        return after * fall

    after = jnp.ones((1, WIDTH), F32)
    for i in range(blocks):
        after = one_block(i, after)
    up_rows = padded_rows(up_ref[0, 0], IN_LANE)

    ig_scr[0:HALO, :WIDTH] = jnp.zeros((HALO, WIDTH), BF16)
    for k in range(blocks):
        rows = with_halo(k)
        extra = HALO if k == 0 else 0
        ig_scr[at_rows(k), :WIDTH] = dgate_ref[at_block(k), :]
        window = du_scr[pl.ds(HALO + k * BLOCK - extra, BLOCK + extra + 8), :]
        ig_scr[rows, WIDTH:] = advances(window, taps[0:4], BLOCK + extra).astype(BF16)
        grad = ig_scr[rows, :]
        adg_scr[rows, :] += mm_nt(grad, up_rows)
        for r in range(row_count):
            ng_scr[rows, r * part : (r + 1) * part] += mm_nt(grad, w_ref[0, r, :part, :])
        if k == 0:
            up_scr[...] = mm_tn(adv_ref[0:HALO, :], grad[:HALO])[IN_LANE : IN_LANE + RANK]
        up_scr[...] += mm(adv_t_scr[k], grad[extra:])

    share = RANK // row_count
    for r in range(row_count):
        wide_ref[r, 0, :, : 2 * WIDTH] = up_scr[r * share : (r + 1) * share, :]
        wide_ref[r, 0, :, 2 * WIDTH :] = out_down_ref[0, r * share : (r + 1) * share, :]

    @pl.when(group == pl.num_programs(0) - 1)
    def _():
        upper = (iota((BLOCK, BLOCK), 0) <= iota((BLOCK, BLOCK), 1)).astype(BF16)
        rate = -jnp.exp(hp_ref[1:2])

        @pl.loop(0, blocks)
        def _(k):
            rows = at_block(k)
            dscore = jnp.where(keep, dscore_scr[k], 0.0).astype(BF16)
            db = db_scr[rows, :] + mm(dscore, cs_ref[rows, :])
            dc = dc_scr[rows, :] + mm_tn(dscore, bs_ref[rows, :])
            pre = scpre_ref[rows, :]
            sig = sigmoid(pre)
            slope = sig + pre * sig * (1.0 - sig)
            du_scr[at_rows(k), :] = jnp.concatenate([db, dc], axis=1) * slope
            is_last = iota((BLOCK, LANES), 0) == BLOCK - 1
            dcum = dcum_scr[rows, :] + jnp.where(is_last, dlast_scr[k, 0:1, :], 0.0)
            slower = split_left(upper, dcum) * (rate * sig_ref[rows, :])
            dstep_scr[rows, :] = dstep_scr[rows, :] * ratio_ref[rows, :] + slower

        def finish(rows, window, count, draw):
            dstate = advances(window, sp_ref[...], count).astype(BF16)
            adapt = adg_scr[rows, :].astype(BF16)
            mixed = adapt + draw
            total = jnp.zeros((count, 1), F32)
            square = jnp.zeros((count, 1), F32)
            grads = []
            for r in range(row_count):
                cols = slice(r * part, (r + 1) * part)
                grad = ng_scr[rows, cols] + mm_nt(dstate, wst_ref[r, :, 0:256])
                grad = grad + mm_nt(mixed, wst_ref[r, :, 256:384])
                grad = grad * gain_ref[r]
                piece = x_ref[r, rows, :].astype(F32)
                total = total + jnp.sum(piece * grad, axis=1, keepdims=True)
                square = square + jnp.sum(piece * piece, axis=1, keepdims=True)
                grads.append(grad)
                in_scr[:, cols] += mm_tn(adapt, normed_ref[rows, cols])[IN_LANE : IN_LANE + RANK]
            inv = lax.rsqrt(square / D + EPS)
            factor = inv * inv * inv * total / D
            for r in range(row_count):
                piece = x_ref[r, rows, :].astype(F32)
                corr_ref[r, rows, :] = (inv * grads[r] - factor * piece).astype(BF16)

        in_scr[...] = jnp.zeros_like(in_scr)
        for k in range(blocks):
            extra = HALO if k == 0 else 0
            window = du_scr[pl.ds(HALO + k * BLOCK - extra, BLOCK + extra + 8), :]
            draw = dstep_scr[at_block(k), :].astype(BF16)
            if k == 0:
                draw = jnp.concatenate([jnp.zeros((HALO, LANES), BF16), draw], axis=0)
            finish(with_halo(k), window, BLOCK + extra, draw)

        for r in range(row_count):
            thin_ref[r, 0:RANK, :] = in_scr[:, r * part : (r + 1) * part]
            thin_ref[r, RANK:, :] = out_up_ref[:, r * part : (r + 1) * part]


def on_row(row):
    return {"row": row}


def on_col(col):
    return {"col": col}


def tail_kernel(
    corr_ref, wide_ref, thin_ref, owner_ref,
    corr_out, wide_out, thin_out, up_out, down_out, mine_out,
    wide_pair, thin_pair, wide_both, thin_both, wide_scr, thin_scr, wide_sum, thin_sum, wide_col,
    own_sem, corr_send, corr_recv, pair_send, pair_recv, row_send, row_recv, col_send, col_recv, last_send, last_recv,
    core_send, core_recv,
):
    row_count = corr_ref.shape[0]
    col_count = thin_out.shape[0]
    row = lax.axis_index("row")
    col = lax.axis_index("col")
    barrier = pltpu.get_barrier_semaphore()
    for d in range(1, row_count):
        pl.semaphore_signal(barrier, inc=1, device_id=on_row(lax.rem(row + d, row_count)), device_id_type=MESH)
    for d in range(1, col_count):
        pl.semaphore_signal(barrier, inc=1, device_id=on_col(lax.rem(col + d, col_count)), device_id_type=MESH)
    pl.semaphore_wait(barrier, row_count + col_count - 2)

    def send(source, target, sends, recvs, index, device):
        copy = pltpu.make_async_remote_copy(
            src_ref=source, dst_ref=target, send_sem=sends.at[index], recv_sem=recvs.at[index],
            device_id=device, device_id_type=MESH,
        )
        copy.start()
        return copy

    chips = row_count // 2
    parity = lax.rem(row, 2)
    chip = row // 2
    core = row + 1 - 2 * parity
    first = []
    for j in range(chips):
        theirs = 2 * j + 1 - parity
        first.append(send(wide_ref.at[theirs], wide_pair.at[j], pair_send, pair_recv, j, on_row(core)))
        first.append(send(thin_ref.at[theirs], thin_pair.at[j], pair_send, pair_recv, chips + j, on_row(core)))
    moved = []
    cuts = (0, 8 * corr_ref.shape[1] // 1040 * 16, 45 * corr_ref.shape[1] // 1040 * 16, corr_ref.shape[1])

    def move(step):
        for d in range(1, row_count):
            peer = lax.rem(row + d, row_count)
            part = pl.ds(cuts[step], cuts[step + 1] - cuts[step])
            index = step * row_count + d
            source = corr_ref.at[peer, part]
            moved.append(send(source, corr_out.at[row, part], corr_send, corr_recv, index, on_row(peer)))

    move(0)
    own = pltpu.make_async_copy(corr_ref.at[row], corr_out.at[row], own_sem.at[0])
    own.start()
    for copy in first:
        copy.wait()
    for j in range(chips):
        wide_both[j] = wide_ref[2 * j + parity] + wide_pair[j]
        thin_both[j] = thin_ref[2 * j + parity] + thin_pair[j]
    across = []
    for d in range(1, chips):
        there = lax.rem(chip + d, chips)
        peer = on_row(2 * there + parity)
        across.append(send(wide_both.at[there], wide_scr.at[chip], row_send, row_recv, d, peer))
        across.append(send(thin_both.at[there], thin_scr.at[chip], row_send, row_recv, chips + d, peer))
    move(1)
    for copy in across:
        copy.wait()
    wide = wide_both[chip]
    thin = thin_both[chip]
    for d in range(1, chips):
        there = lax.rem(chip + d, chips)
        wide = wide + wide_scr[there]
        thin = thin + thin_scr[there]
    wide_sum[...] = wide
    thin_sum[...] = thin
    second = []
    for d in range(1, col_count):
        peer = lax.rem(col + d, col_count)
        second.append(send(wide_sum.at[peer], wide_col.at[col], col_send, col_recv, d, on_col(peer)))
        second.append(send(thin_sum, thin_out.at[col], col_send, col_recv, col_count + d, on_col(peer)))
    wide_col[col] = wide_sum[col]
    thin_out[col] = thin
    for copy in second:
        copy.wait()
    third = []
    for d in range(1, chips):
        there = lax.rem(chip + d, chips)
        third.append(send(wide_col, wide_out.at[row], last_send, last_recv, d, on_row(2 * there + parity)))
    fourth = [send(wide_col, wide_out.at[row], core_send, core_recv, 0, on_row(core))]
    move(2)
    wide_out[row] = wide_col[...]
    for d in range(1, chips):
        third[d - 1].wait_recv()
        source = 2 * lax.rem(chip + chips - d, chips) + parity
        fourth.append(send(wide_out.at[source], wide_out.at[source], core_send, core_recv, d, on_row(core)))
    for copy in third:
        copy.wait_send()
    for copy in fourth:
        copy.wait()
    if up_out.shape[0] > RANK:
        lane = iota((wide_out.shape[2], LANES), 1) < P_SIZE
        share = wide_out.shape[2]
        mine = jnp.zeros(mine_out.shape, F32)
        for c in range(col_count):
            mine = mine + jnp.where(owner_ref[c] == col, thin_out[c], 0.0)
        mine_out[...] = mine
        for a in range(up_out.shape[0] // RANK):
            for r in range(row_count):
                total = jnp.zeros(wide_out.shape[2:], F32)
                for c in range(col_count):
                    total = total + jnp.where(owner_ref[c] == a, wide_out[r, c], 0.0)
                rows = slice(a * RANK + r * share, a * RANK + (r + 1) * share)
                tiles = [total[:, i * LANES : (i + 1) * LANES] for i in range(QUAD)]
                turned = [pltpu.roll(tile, P_SIZE, 1) for tile in tiles]
                for h in range(QUAD):
                    gate, value = h // 2, 2 + h // 2
                    if h % 2 == 0:
                        up_out[rows, h, :] = jnp.where(lane, tiles[gate], turned[value])
                    else:
                        up_out[rows, h, :] = jnp.where(lane, turned[gate], tiles[value])
                down_out[rows, :] = total[:, 2 * WIDTH :]
    for copy in moved:
        copy.wait()
    own.wait()


def start_kernel(
    x_ref, w_ref, up_ref, p_ref, down_ref, state_ref, in_ref, out_ref, gain_ref, conv_ref, bias_ref, gate_ref, step_ref, rate_ref,
    skip_ref, adapter_ref,
    x_out, w_out, shared_out, gain_out, vec_out, head_out, place_out,
    block_scr, zero_scr, shared_ref,
    own_sem, send_sem, recv_sem, row_send, row_recv, col_send, col_recv,
):
    col_count, row_count = w_out.shape[:2]
    high_count = col_count // 2
    part = x_ref.shape[1]
    chunk = x_ref.shape[0] // row_count
    rank_part = up_ref.shape[0] // row_count
    row = lax.axis_index("row")
    col = lax.axis_index("col")
    low = lax.rem(col, 2)
    high = col // 2
    core = row + 1 - 2 * lax.rem(row, 2)
    across = lax.rem(row + 2, row_count)
    side = col + 1 - 2 * low
    barrier = pltpu.get_barrier_semaphore()
    for d in range(1, row_count):
        pl.semaphore_signal(barrier, inc=1, device_id=on_row(lax.rem(row + d, row_count)), device_id_type=MESH)
    for d in range(1, col_count):
        pl.semaphore_signal(barrier, inc=1, device_id=on_col(lax.rem(col + d, col_count)), device_id_type=MESH)

    def paired(value):
        lane = iota((value.shape[0], LANES), 1) < P_SIZE
        tiles = [value[:, h, :].astype(F32) for h in range(QUAD)]
        turned = [pltpu.roll(tile, P_SIZE, 1) for tile in tiles]
        gates = [jnp.where(lane, tiles[h], turned[h + 1]) for h in (0, 2)]
        values = [jnp.where(lane, turned[h], tiles[h + 1]) for h in (0, 2)]
        return jnp.concatenate(gates + values, axis=1).astype(BF16)

    block_scr[0:part, :] = paired(w_ref)
    ranks = pl.ds(pl.multiple_of(row * rank_part, rank_part), rank_part)
    block_scr[part : part + rank_part, :] = paired(up_ref.at[ranks])
    first = part + rank_part
    half = WIDTH // 2
    block_scr[first : first + half, :WIDTH] = p_ref[:half, :]
    block_scr[first : first + half, WIDTH:] = p_ref[half:, :]
    first = first + half
    downs = down_ref[ranks, :]
    block_scr[first : first + rank_part // 2, :WIDTH] = downs[: rank_part // 2]
    block_scr[first : first + rank_part // 2, WIDTH:] = downs[rank_part // 2 :]
    zero_scr[...] = jnp.zeros_like(zero_scr)
    adapter = adapter_ref[col]
    shift = adapter * RANK
    per_part = rank_part // RANK
    place_out[0] = adapter // per_part
    place_out[1] = adapter - adapter // per_part * per_part
    source = iota((LANES, LANES), 0) - shift
    target = iota((LANES, LANES), 1)
    chosen = (source >= 0) & (source < RANK)
    ins = (chosen & (source == target - IN_LANE)).astype(F32).astype(BF16)
    outs = (chosen & (source == target - OUT_LANE)).astype(F32).astype(BF16)
    states = 2 * STATES
    shared_ref[:, :states] = state_ref[:states, :].astype(F32).T.astype(BF16)
    steps = jnp.concatenate(
        [state_ref[states:, :].astype(F32), jnp.zeros((LANES - HEADS, part), F32)], axis=0
    ).T
    shared_ref[:, states:] = (steps + mm(in_ref[...], ins) + mm(out_ref[...], outs)).astype(BF16)
    vec_out[col, 0:4, :] = conv_ref[...]
    vec_out[col, 4:5, :] = bias_ref[...]
    vec_out[col, 5:6, :] = gate_ref[...]
    vec_out[col, 6:7, :] = widen(skip_ref[...])
    lane = iota((1, WIDTH), 1)
    scalars = jnp.zeros((1, WIDTH), F32)
    for h in range(QUAD):
        scalars = jnp.where(lane == h, step_ref[:, h : h + 1], scalars)
        scalars = jnp.where(lane == QUAD + h, rate_ref[:, h : h + 1], scalars)
    vec_out[col, 7:8, :] = scalars
    gain_out[row] = gain_ref[...]
    pl.semaphore_wait(barrier, row_count + col_count - 2)

    def remote(source, target, sends, recvs, index, device):
        return pltpu.make_async_remote_copy(
            src_ref=source, dst_ref=target, send_sem=sends.at[index], recv_sem=recvs.at[index],
            device_id=device, device_id_type=MESH,
        )

    own_block = pltpu.make_async_copy(block_scr, w_out.at[col, row], own_sem.at[0])
    own_block.start()

    def whole_window(target, slot, index, peer):
        source = x_ref.at[pl.ds(pl.multiple_of(target * chunk - HALO, HALO), chunk + HALO)]
        return remote(source, x_out.at[slot], row_send, row_recv, index, on_row(peer))

    def first_window(slot, index, peer):
        source = x_ref.at[pl.ds(0, chunk)]
        return remote(source, x_out.at[slot, pl.ds(HALO, chunk)], row_send, row_recv, index, on_row(peer))

    def each_window(sending, act):
        for d in range(1, row_count):
            peer = lax.rem(row + d, row_count)
            chosen = peer if sending else row
            slot = row if sending else lax.rem(row + row_count - d, row_count)

            @pl.when(chosen > 0)
            def _():
                act(whole_window(jnp.maximum(chosen, 1), slot, d, peer))

            @pl.when(chosen == 0)
            def _():
                act(first_window(slot, d, peer))

    @pl.when(row > 0)
    def _():
        source = x_ref.at[pl.ds(pl.multiple_of(jnp.maximum(row, 1) * chunk - HALO, HALO), chunk + HALO)]
        pltpu.make_async_copy(source, x_out.at[row], own_sem.at[1]).start()

    @pl.when(row == 0)
    def _():
        pltpu.make_async_copy(x_ref.at[pl.ds(0, chunk)], x_out.at[row, pl.ds(HALO, chunk)], own_sem.at[1]).start()
        for r in range(row_count):
            pltpu.make_async_copy(zero_scr, x_out.at[r, pl.ds(0, HALO)], own_sem.at[3 + r]).start()

    own_shared = pltpu.make_async_copy(shared_ref, shared_out.at[row], own_sem.at[2])
    own_shared.start()
    small = []
    for d in range(1, col_count):
        peer = lax.rem(col + d, col_count)
        small.append(remote(vec_out.at[col], vec_out.at[col], col_send, col_recv, d, on_col(peer)))
    for d in range(1, row_count):
        peer = lax.rem(row + d, row_count)
        small.append(remote(shared_ref, shared_out.at[row], row_send, row_recv, row_count + d, on_row(peer)))
        small.append(
            remote(gain_out.at[row], gain_out.at[row], row_send, row_recv, 2 * row_count + d, on_row(peer))
        )
    for copy in small:
        copy.start()

    cut = (w_out.shape[2] * 65 // 100 + 8) // 16 * 16
    spans = (pl.ds(0, cut), pl.ds(cut, w_out.shape[2] - cut))
    has_up = high < high_count - 1
    has_down = high > 0
    routes = {
        "up": (0, has_up, on_col(lax.rem(col + 2, col_count))),
        "down": (1, has_down, on_col(lax.rem(col + col_count - 2, col_count))),
        "x": (2, None, on_col(side)),
        "y": (3, None, on_row(across)),
        "core": (4, None, on_row(core)),
    }

    def piece(section, c, r, kind, device):
        ref = w_out.at[c, r, spans[section]]
        return pltpu.make_async_remote_copy(
            src_ref=ref, dst_ref=ref, send_sem=send_sem.at[section, c, r, kind],
            recv_sem=recv_sem.at[section, c, r], device_id=device, device_id_type=MESH,
        )

    def event(starting, section, c, r, names, arrives=True, valid=None):
        def act():
            if starting and arrives:
                piece(section, c, r, 4, on_row(core)).wait_recv()
            for name in names:
                kind, allowed, device = routes[name]
                copy = piece(section, c, r, kind, device)
                if allowed is None:
                    copy.start() if starting else copy.wait_send()
                else:

                    @pl.when(allowed)
                    def _():
                        copy.start() if starting else copy.wait_send()

        if valid is None:
            act()
        else:
            pl.when(valid)(act)

    def far(column, step, distance):
        return lax.rem(column + step * distance + 4 * col_count, col_count)

    def within(step, distance):
        return high >= distance if step < 0 else high + distance < high_count

    onward = {-2: "up", 2: "down"}

    def along(starting, section, distance):
        for step in (-2, 2):
            valid = within(step, distance)
            if section == 0:
                names = (onward[step], "y", "x", "core")
                event(starting, 0, far(col, step, distance), row, names, valid=valid)
            else:
                for column, r in ((col, row), (side, row), (col, across), (side, across)):
                    event(starting, 1, far(column, step, distance), r, (onward[step], "core"), valid=valid)

    def over(starting, distance):
        for step in (-2, 2):
            valid = within(step, distance)
            event(starting, 0, far(side, step, distance), row, ("core",), valid=valid)
            event(starting, 0, far(col, step, distance), across, ("x", "core"), valid=valid)

    def last(starting, distance):
        for step in (-2, 2):
            event(starting, 0, far(side, step, distance), across, ("core",), valid=within(step, distance))

    def relay(starting):
        def windows():
            if starting:
                each_window(True, lambda copy: copy.start())

        event(starting, 0, col, row, ("up", "down"), arrives=False)
        event(starting, 1, col, row, ("x", "y"), arrives=False)
        event(starting, 0, col, row, ("y", "x", "core"), arrives=False)
        event(starting, 1, col, row, ("core",), arrives=False)
        event(starting, 1, side, row, ("y", "core"))
        along(starting, 0, 1)
        event(starting, 1, col, row, ("up", "down"), arrives=False)
        event(starting, 0, col, across, ("x", "core"))
        event(starting, 1, side, row, ("up", "down"), arrives=False)
        event(starting, 1, col, across, ("up", "down", "core"))
        for d in range(2, high_count - 1):
            along(starting, 0, d)
        event(starting, 1, side, across, ("up", "down", "core"))
        over(starting, 1)
        along(starting, 0, high_count - 1)
        windows()
        along(starting, 1, 1)
        over(starting, 2)
        event(starting, 0, side, row, ("core",))
        event(starting, 0, side, across, ("core",))
        last(starting, 1)
        for d in range(2, high_count):
            if d > 2:
                over(starting, d)
            along(starting, 1, d)
            if d > 2:
                last(starting, d - 1)
        last(starting, high_count - 1)

    own_block.wait()
    relay(True)
    for copy in small:
        copy.wait()
    lane = iota((1, LANES), 1) < QUAD
    steps = jnp.zeros((1, LANES), F32)
    rates = jnp.zeros((1, LANES), F32)
    for c in range(col_count):
        values = vec_out[c, 7:8, :LANES]
        steps = steps + pltpu.roll(jnp.where(lane, values, 0.0), (QUAD * c) % LANES, 1)
        values = pltpu.roll(values, LANES - QUAD, 1)
        rates = rates + pltpu.roll(jnp.where(lane, values, 0.0), (QUAD * c) % LANES, 1)
    head_out[...] = jnp.concatenate([steps, rates, jnp.zeros((6, LANES), F32)], axis=0)
    own_shared.wait()
    each_window(True, lambda copy: copy.wait_send())
    each_window(False, lambda copy: copy.wait_recv())

    @pl.when(row > 0)
    def _():
        source = x_ref.at[pl.ds(0, chunk + HALO)]
        pltpu.make_async_copy(source, x_out.at[row], own_sem.at[1]).wait()

    @pl.when(row == 0)
    def _():
        pltpu.make_async_copy(x_ref.at[pl.ds(0, chunk)], x_out.at[row, pl.ds(HALO, chunk)], own_sem.at[1]).wait()
        for r in range(row_count):
            pltpu.make_async_copy(zero_scr, x_out.at[r, pl.ds(0, HALO)], own_sem.at[3 + r]).wait()

    core_across = lax.rem(core + 2, row_count)
    for c in range(col_count):
        for r in (core, core_across):
            for section in range(2):
                piece(section, c, r, 4, on_row(core)).wait_recv()
    relay(False)


def start_exchange(x, w, up, p, down, shared, vectors, adapter_id, row_count, col_count):
    part = x.shape[1]
    rank_part = up.shape[0] // row_count
    block_rows = part + rank_part + WIDTH // 2 + rank_part // 2
    chunk = x.shape[0] // row_count
    vmem = pl.BlockSpec(memory_space=pltpu.VMEM)
    anywhere = pl.BlockSpec(memory_space=pl.ANY)
    dma = pltpu.SemaphoreType.DMA
    return pl.pallas_call(
        start_kernel,
        in_specs=[anywhere] + [vmem] * (7 + len(vectors)) + [pl.BlockSpec(memory_space=pltpu.SMEM)],
        out_specs=[anywhere] * 3 + [vmem] * 3 + [pl.BlockSpec(memory_space=pltpu.SMEM)],
        out_shape=[
            jax.ShapeDtypeStruct((row_count, chunk + HALO, part), BF16),
            jax.ShapeDtypeStruct((col_count, row_count, block_rows, 2 * WIDTH), BF16),
            jax.ShapeDtypeStruct((row_count, part, 384), BF16),
            jax.ShapeDtypeStruct((row_count, 1, part), F32),
            jax.ShapeDtypeStruct((col_count, 8, WIDTH), F32),
            jax.ShapeDtypeStruct((8, LANES), F32),
            jax.ShapeDtypeStruct((2,), jnp.int32),
        ],
        scratch_shapes=[
            pltpu.VMEM((block_rows, 2 * WIDTH), BF16), pltpu.VMEM((HALO, part), BF16),
            pltpu.VMEM((part, 384), BF16), dma((3 + row_count,)), dma((2, col_count, row_count, 5)), dma((2, col_count, row_count)),
            dma((3 * row_count,)), dma((3 * row_count,)), dma((col_count,)), dma((col_count,)),
        ],
        compiler_params=pltpu.CompilerParams(
            collective_id=1, has_side_effects=True, vmem_limit_bytes=VMEM_BYTES
        ),
    )(x, w, up, p, down, *shared, *vectors, adapter_id)


def carry_kernel(
    forward, state_ref, decay_ref,
    out_ref,
    other_scr, other_decay, total_scr, total_in,
    core_send, core_recv, across_send, across_recv, share_send, share_recv,
):
    row = lax.axis_index("row")
    parity = lax.rem(row, 2)
    chip = row // 2
    core = row + 1 - 2 * parity
    across = lax.rem(row + 2, 4)
    barrier = pltpu.get_barrier_semaphore()
    for peer in (core, across):
        pl.semaphore_signal(barrier, inc=1, device_id=on_row(peer), device_id_type=MESH)
    pl.semaphore_wait(barrier, 2)

    def remote(source, target, sends, recvs, index, peer):
        return pltpu.make_async_remote_copy(
            src_ref=source, dst_ref=target, send_sem=sends.at[index], recv_sem=recvs.at[index],
            device_id=on_row(peer), device_id_type=MESH,
        )

    swaps = [
        remote(state_ref, other_scr, core_send, core_recv, 0, core),
        remote(decay_ref, other_decay, core_send, core_recv, 1, core),
    ]
    for copy in swaps:
        copy.start()
    for copy in swaps:
        copy.wait()
    half = state_ref.shape[1] // 2
    rows = state_ref.shape[0] // 2
    second = parity == (1 if forward else 0)
    sends = chip == (0 if forward else 1)

    @pl.when(sends)
    def _():
        for p in range(2):

            @pl.when(parity == p)
            def _():
                cols = slice(p * half, (p + 1) * half)
                for q in range(2):
                    part = slice(q * rows, (q + 1) * rows)
                    mine = state_ref[part, cols].astype(F32)
                    other = other_scr[part, cols].astype(F32)
                    late = mine + other * decay_ref[0:1, cols]
                    early = other + mine * other_decay[0:1, cols]
                    total_scr[q] = jnp.where(second, late, early).astype(BF16)
                    remote(total_scr.at[q], total_in.at[p, q], across_send, across_recv, q, across).start()
        out_ref[...] = jnp.where(second, other_scr[...].astype(F32), 0.0)
        for q in range(2):
            remote(total_scr.at[q], total_in.at[parity, q], across_send, across_recv, q, across).wait_send()

    @pl.when(jnp.logical_not(sends))
    def _():
        for q in range(2):
            remote(total_scr.at[q], total_in.at[parity, q], across_send, across_recv, q, across).wait_recv()
            remote(
                total_in.at[parity, q], total_in.at[parity, q], share_send, share_recv, q, core
            ).start()
        for q in range(2):
            remote(
                total_in.at[parity, q], total_in.at[1 - parity, q], share_send, share_recv, q, core
            ).wait()
        for p in range(2):
            for q in range(2):
                cols = slice(p * half, (p + 1) * half)
                part = slice(q * rows, (q + 1) * rows)
                total = total_in[p, q].astype(F32)
                later = other_scr[part, cols].astype(F32) + total * other_decay[0:1, cols]
                out_ref[part, cols] = jnp.where(second, later, total)


def carry_over(state, decay, forward):
    vmem = pl.BlockSpec(memory_space=pltpu.VMEM)
    dma = pltpu.SemaphoreType.DMA
    rows, cols = state.shape
    return pl.pallas_call(
        functools.partial(carry_kernel, forward),
        in_specs=[vmem, vmem],
        out_specs=vmem,
        out_shape=jax.ShapeDtypeStruct(state.shape, F32),
        scratch_shapes=[
            pltpu.VMEM(state.shape, BF16), pltpu.VMEM(decay.shape, F32),
            pltpu.VMEM((2, rows // 2, cols // 2), BF16), pltpu.VMEM((2, 2, rows // 2, cols // 2), BF16),
            dma((2,)), dma((2,)), dma((2,)), dma((2,)), dma((2,)), dma((2,)),
        ],
        compiler_params=pltpu.CompilerParams(
            collective_id=2 if forward else 3, has_side_effects=True, vmem_limit_bytes=VMEM_BYTES
        ),
    )(state, decay)


def finish_exchange(corr, wide, thin, owner, placed):
    row_count = corr.shape[0]
    col_count = wide.shape[1]
    share, width = wide.shape[2:]
    ranks = RANK * col_count if placed else RANK
    vmem = pl.BlockSpec(memory_space=pltpu.VMEM)
    anywhere = pl.BlockSpec(memory_space=pl.ANY)
    dma = pltpu.SemaphoreType.DMA
    return pl.pallas_call(
        tail_kernel,
        in_specs=[anywhere, vmem, vmem, pl.BlockSpec(memory_space=pltpu.SMEM)],
        out_specs=[anywhere] + [vmem] * 5,
        out_shape=[
            jax.ShapeDtypeStruct(corr.shape, corr.dtype),
            jax.ShapeDtypeStruct((row_count, col_count, share, width), F32),
            jax.ShapeDtypeStruct((col_count,) + thin.shape[1:], F32),
            jax.ShapeDtypeStruct((ranks, QUAD, LANES), F32),
            jax.ShapeDtypeStruct((ranks, WIDTH), F32),
            jax.ShapeDtypeStruct(thin.shape[1:], F32),
        ],
        scratch_shapes=[
            *[pltpu.VMEM((row_count // 2,) + value.shape[1:], F32) for value in (wide, thin) * 3],
            pltpu.VMEM(wide.shape[1:], F32), pltpu.VMEM(thin.shape[1:], F32), pltpu.VMEM(wide.shape[1:], F32),
            dma((1,)), dma((3 * row_count,)), dma((3 * row_count,)), dma((row_count,)), dma((row_count,)),
            dma((row_count,)), dma((row_count,)), dma((2 * col_count,)), dma((2 * col_count,)),
            dma((row_count // 2,)), dma((row_count // 2,)), dma((row_count // 2,)), dma((row_count // 2,)),
        ],
        compiler_params=pltpu.CompilerParams(
            collective_id=0, has_side_effects=True, vmem_limit_bytes=VMEM_BYTES
        ),
    )(corr, wide, thin, owner)


def whole_spec(shape):
    return pl.BlockSpec(shape, lambda c, s: (0,) * len(shape))


def lead_spec(shape):
    return pl.BlockSpec((1,) + tuple(shape[1:]), lambda c, s: (c,) + (0,) * (len(shape) - 1))


def lane_spec(shape):
    block = tuple(shape[:-1]) + (WIDTH,)
    return pl.BlockSpec(block, lambda c, s: (0,) * (len(shape) - 1) + (c,))


def second_spec(shape):
    block = (shape[0], 1) + tuple(shape[2:])
    return pl.BlockSpec(block, lambda c, s: (0, c) + (0,) * (len(shape) - 2))


def front_spec(shape):
    if shape[2] % 3 == 0 and shape[2] // 3 * 2 >= WIDTH and shape[3] == 2 * WIDTH and shape[1] == 4:
        return pl.BlockSpec((1, shape[1], shape[2] // 3 * 2, shape[3]), lambda c, s: (c, 0, 0, 0))
    return lead_spec(shape)


def full_back_spec(shape):
    if shape[2] > WIDTH:
        return pl.BlockSpec((shape[0], shape[1], shape[2] // 3, shape[3]), lambda c, s: (0, 0, 2, 0))
    return whole_spec(shape)


def back_spec(shape):
    if shape[2] > WIDTH:
        return pl.BlockSpec((1, shape[1], shape[2] // 3, shape[3]), lambda c, s: (c, 0, 2, 0))
    return lead_spec(shape)


def up_spec(shape):
    first = WIDTH // RANK if shape[2] > RANK else 0
    return pl.BlockSpec((1, 1, RANK, 2 * WIDTH), lambda c, s: (c, s[0], first + s[1], 0))


def down_spec(shape):
    first = shape[2] // RANK - 1
    return pl.BlockSpec((1, 1, RANK, WIDTH), lambda c, s: (c, s[0], first, s[1]))


KINDS = {
    "a": whole_spec, "c": lead_spec, "l": lane_spec, "s": second_spec, "w": front_spec, "f": full_back_spec,
    "p": back_spec, "u": up_spec, "d": down_spec,
}


def grouped_call(kernel, place, inputs, kinds, outputs, out_kinds, scratch, flops=0):
    return pl.pallas_call(
        kernel,
        grid_spec=pltpu.PrefetchScalarGridSpec(
            num_scalar_prefetch=1,
            grid=(GROUPS,),
            in_specs=[KINDS[kind](value.shape) for kind, value in zip(kinds, inputs)],
            out_specs=[KINDS[kind](shape) for kind, (shape, _) in zip(out_kinds, outputs)],
            scratch_shapes=[pltpu.VMEM(shape, dtype) for shape, dtype in scratch],
        ),
        out_shape=[jax.ShapeDtypeStruct(shape, dtype) for shape, dtype in outputs],
        compiler_params=pltpu.CompilerParams(vmem_limit_bytes=VMEM_BYTES),
        cost_estimate=pl.CostEstimate(flops=flops, bytes_accessed=40_000_000, transcendentals=0),
    )(place, *inputs)


def to_groups(value, heads_here):
    cols = value.shape[0]
    middle = value.shape[1:-1]
    if heads_here == QUAD:
        return value
    if heads_here > QUAD:
        parts = heads_here // QUAD
        value = value.reshape((cols,) + middle + (parts, WIDTH))
        value = jnp.moveaxis(value, -2, 1)
        return value.reshape((GROUPS,) + middle + (WIDTH,))
    parts = QUAD // heads_here
    value = value.reshape((GROUPS, parts) + middle + (heads_here * P_SIZE,))
    value = jnp.moveaxis(value, 1, -2)
    return value.reshape((GROUPS,) + middle + (WIDTH,))


def to_cols(value, heads_here, col_count):
    middle = value.shape[1:-1]
    if heads_here == QUAD:
        return value
    if heads_here > QUAD:
        parts = heads_here // QUAD
        value = value.reshape((col_count, parts) + middle + (WIDTH,))
        value = jnp.moveaxis(value, 1, -2)
        return value.reshape((col_count,) + middle + (heads_here * P_SIZE,))
    parts = QUAD // heads_here
    value = value.reshape((GROUPS,) + middle + (parts, heads_here * P_SIZE))
    value = jnp.moveaxis(value, -2, 1)
    return value.reshape((col_count,) + middle + (heads_here * P_SIZE,))


def pad_lanes(value, width):
    return jnp.pad(value, [(0, 0)] * (value.ndim - 1) + [(0, width - value.shape[-1])])


def carry_in(state, decay, row_count, col_count, seq_cols, forward):
    row = lax.axis_index("row")
    col = lax.axis_index("col")
    total = state
    factor = decay
    before = jnp.zeros(state.shape, F32)
    reach = jnp.ones_like(decay)
    span = 1
    while span < row_count:
        pairs = [(i, i ^ span) for i in range(row_count)]
        other = lax.ppermute(total, "row", pairs).astype(F32)
        other_factor = lax.ppermute(factor, "row", pairs)
        behind = ((row & span) != 0) == forward
        mine = total.astype(F32)
        before = jnp.where(behind, before + reach * other, before)
        reach = jnp.where(behind, reach * other_factor, reach)
        joined = jnp.where(behind, other * factor + mine, mine * other_factor + other)
        total = joined.astype(BF16)
        factor = factor * other_factor
        span *= 2
    place = lax.rem(col, seq_cols)
    for hop in range(1, seq_cols):
        shift = hop if forward else -hop
        pairs = [(i, (i + shift) % col_count) for i in range(col_count)]
        other = lax.ppermute(total, "col", pairs).astype(F32)
        other_factor = lax.ppermute(factor, "col", pairs)
        inside = place >= hop if forward else place < seq_cols - hop
        before = jnp.where(inside, before + reach * other, before)
        reach = jnp.where(inside, reach * other_factor, reach)
    return before


def per_device(
    block_in, norm_gain, proj_inner, proj_state, conv_inner, conv_inner_bias, conv_state, conv_state_bias,
    step_bias, decay_log, skip_gain, gate_gain, proj_out, adapt_in_down, adapt_in_up, adapt_out_down,
    adapt_out_up, adapter_id, cotangent,
):
    row_count = lax.axis_size("row")
    col_count = lax.axis_size("col")
    row = lax.axis_index("row")
    col = lax.axis_index("col")
    col_tokens, part = block_in.shape
    chunk = col_tokens // row_count
    total_rows = chunk + HALO
    blocks = chunk // BLOCK
    seq_cols = SEQ // col_tokens
    heads_here = proj_inner.shape[1]
    local = heads_here * P_SIZE
    rank_total = adapt_in_down.shape[1]
    rank_part = rank_total // row_count
    rank_share = rank_total // col_count
    adapter = lax.dynamic_index_in_dim(adapter_id, col // seq_cols, keepdims=False)

    relayed = row_count == 4 and heads_here == QUAD and seq_cols == 1 and part == WIDTH and rank_share == RANK
    place = jnp.zeros((2,), jnp.int32)
    if relayed:
        x_rows, w_all, w_state, gain_all, vectors, head_rows, place = start_exchange(
            block_in, proj_inner, adapt_in_up, proj_out,
            adapt_out_down, (proj_state.T, adapt_in_down, adapt_out_up),
            (
                norm_gain[None], conv_inner, conv_inner_bias[None], gate_gain[None], step_bias[None],
                decay_log[None], skip_gain[None],
            ),
            adapter_id, row_count, col_count,
        )
        up_all = down_all = p_all = w_all
        x_rows, cot = lax.optimization_barrier((x_rows, cotangent))
        g_rows = lax.all_to_all(cot.reshape(row_count, chunk, part), "row", 0, 0, tiled=True)
    else:
        head = jnp.zeros((HALO, part), BF16)
        if seq_cols > 1:
            pairs = [(i, (i + 1) % col_count) for i in range(col_count)]
            head = lax.ppermute(block_in[-HALO:], "col", pairs)
            head = jnp.where(lax.rem(col, seq_cols) > 0, head, jnp.zeros_like(head))
        padded = jnp.concatenate([head, block_in], axis=0)
        windows = jnp.stack([padded[r * chunk : r * chunk + total_rows] for r in range(row_count)])
        x_rows = lax.all_to_all(windows, "row", 0, 0, tiled=True)
        g_rows = lax.all_to_all(cotangent.reshape(row_count, chunk, part), "row", 0, 0, tiled=True)

        def split_pairs(value):
            value = value.reshape(value.shape[0], heads_here, 2, P_SIZE)
            return jnp.swapaxes(value, 1, 2).reshape(value.shape[0], 2, local)

        up_part = lax.dynamic_slice_in_dim(adapt_in_up, row * rank_part, rank_part, 0)
        w_block = jnp.concatenate([split_pairs(proj_inner), split_pairs(up_part)], axis=0)
        w_all = lax.all_gather(w_block.reshape(part + rank_part, 2 * local), ("col", "row"))
        w_all = w_all.reshape(col_count, row_count, part + rank_part, 2, local)
        w_all = to_groups(w_all, heads_here).reshape(GROUPS, row_count, part + rank_part, 2 * WIDTH)
        up_all = w_all[:, :, part:, :].reshape(GROUPS, rank_total, 2 * WIDTH)
        up_all = lax.dynamic_slice_in_dim(up_all, adapter * RANK, RANK, 1)[:, None]

        down_part = lax.dynamic_slice_in_dim(adapt_out_down, row * rank_part, rank_part, 0)
        p_block = jnp.concatenate([proj_out, down_part.T], axis=1)
        p_all = lax.all_gather(p_block, ("col", "row")).reshape(col_count, row_count, local, part + rank_part)
        if heads_here != QUAD:
            p_all = jnp.moveaxis(p_all, 1, 0).reshape(row_count, GROUPS, WIDTH, part + rank_part)
            p_all = jnp.moveaxis(p_all, 0, 1)
        down_all = jnp.swapaxes(p_all[..., part:], 1, 2).reshape(GROUPS, WIDTH, rank_total)
        down_all = jnp.swapaxes(lax.dynamic_slice_in_dim(down_all, adapter * RANK, RANK, 2), 1, 2)[:, None]

        in_down = lax.dynamic_slice_in_dim(adapt_in_down, adapter * RANK, RANK, 1)
        out_up = lax.dynamic_slice_in_dim(adapt_out_up, adapter * RANK, RANK, 1)
        shared = pad_lanes(jnp.concatenate([proj_state, in_down, out_up], axis=1), 384)
        w_state = lax.all_gather(shared, "row")
        gain_all = lax.all_gather(norm_gain, "row").reshape(row_count, 1, part)

        scalars = jnp.concatenate([step_bias, decay_log, skip_gain])
        vectors = jnp.concatenate(
            [conv_inner, conv_inner_bias[None], gate_gain[None], pad_lanes(scalars, local)[None]], axis=0
        )
        vectors = lax.all_gather(vectors, "col")
        scalars = vectors[:, 6, : 3 * heads_here].reshape(col_count, 3, heads_here)
        scalars = jnp.swapaxes(scalars, 0, 1).reshape(3, HEADS)
        head_rows = jnp.pad(scalars[:2], ((0, 6), (0, LANES - HEADS)))
        skip_wide = jnp.repeat(scalars[2], P_SIZE).reshape(GROUPS, 1, WIDTH)
        vectors = jnp.concatenate(
            [to_groups(vectors[:, :6], heads_here), skip_wide, jnp.zeros_like(skip_wide)], axis=1
        )
    state_taps = conv_state

    token_f32 = ((chunk, LANES), F32)
    token_low = ((chunk, LANES), BF16)
    inner_low = ((chunk, DI), BF16)
    states = ((blocks, STATES, DI), BF16)
    score_box = ((blocks, BLOCK, BLOCK), F32)
    flipped = ((blocks, STATES, BLOCK), BF16)
    (
        normed, scpre, ratio, sig, cum, lead, turned, bs, cs, cs_t, adv, gate, u, eloc, fin, dec,
    ) = grouped_call(
        front_kernel,
        place,
        (x_rows, gain_all, w_state, state_taps, conv_state_bias[None], head_rows, w_all, up_all, vectors),
        "aaaaaawuc",
        [
            ((total_rows, D), BF16), ((chunk, 256), F32), token_f32, token_f32, token_f32, token_f32,
            ((GROUPS, 2 * QUAD, chunk), F32), token_low, token_low, flipped, ((total_rows, LANES), BF16),
            inner_low, inner_low, states, ((STATES, DI), BF16), ((8, DI), F32),
        ],
        "aaaaaaaaaaalllll",
        [((total_rows, 384), F32), flipped, ((total_rows, WIDTH), F32)],
        flops=int(45e9),
    )
    decay = dec[0:1]
    fin, g_rows = lax.optimization_barrier((fin, g_rows))
    if relayed:
        entry = carry_over(fin, dec, True)
    else:
        entry = carry_in(fin, decay, row_count, col_count, seq_cols, True)
    out_rows, o, ent, aux, side_grad, out_up_grad = grouped_call(
        scan_kernel,
        place,
        (x_rows, g_rows, w_state, p_all, down_all, vectors, gate, u, eloc, entry, cum, turned, bs, cs),
        "aaafdcllllacaa",
        [
            ((row_count, chunk, part), BF16), inner_low, ((blocks, STATES, DI), BF16), token_f32, token_low,
            ((RANK, D), F32),
        ],
        "allaaa",
        [score_box, ((GROUPS, chunk, WIDTH), BF16), token_f32, token_f32],
        flops=int(45e9),
    )
    block_out = lax.all_to_all(out_rows, "row", 0, 0, tiled=True).reshape(col_tokens, part)
    dgate, dy, gloc, gfin, out_down_grad = grouped_call(
        gate_kernel,
        place,
        (g_rows, p_all, side_grad, down_all, vectors, gate, o, aux, cum, cs_t),
        "apadcllaaa",
        [inner_low, inner_low, states, ((STATES, DI), BF16), ((GROUPS, RANK, WIDTH), F32)],
        "llllc",
        [((blocks, RANK, BLOCK), BF16)],
        flops=int(25e9),
    )
    gfin, block_out = lax.optimization_barrier((gfin, block_out))
    if relayed:
        exit_grad = carry_over(gfin, dec, False)
    else:
        exit_grad = carry_in(gfin, decay, row_count, col_count, seq_cols, False)
    corr, wide, thin = grouped_call(
        back_kernel,
        place,
        (
            x_rows, gain_all, normed, w_state, w_all, up_all, adv, vectors, state_taps, head_rows,
            u, o, dy, dgate, ent, gloc, exit_grad, cum, lead, turned, ratio, sig, scpre, bs, cs,
            out_down_grad, out_up_grad,
        ),
        "aaaawuacaalllllllaacaaaaaca",
        [
            ((row_count, total_rows, part), BF16), ((row_count, GROUPS, RANK // row_count, 3 * WIDTH), F32),
            ((row_count, 2 * RANK, part), F32),
        ],
        "asa",
        [
            score_box, score_box, token_f32, token_f32, token_f32, token_f32, ((blocks, 8, LANES), F32),
            ((total_rows + HALO, WIDTH), F32), ((total_rows, 2 * WIDTH), BF16), ((total_rows, D), F32),
            ((total_rows, LANES), F32), ((blocks, RANK, BLOCK), BF16),
            ((RANK, 2 * WIDTH), F32), ((RANK, D), F32),
        ],
        flops=int(75e9),
    )

    if heads_here != QUAD:
        share = RANK // row_count
        wide = jnp.swapaxes(wide.reshape(row_count, GROUPS, share, 3, WIDTH), 0, 1)
        wide = to_cols(wide, heads_here, col_count)
        wide = jnp.swapaxes(wide, 0, 1).reshape(row_count, col_count, share, 3 * local)
    corr, wide, thin, in_up, out_down, mine = finish_exchange(corr, wide, thin, adapter_id, relayed)
    late = jnp.zeros((1, HALO, part), BF16)
    if seq_cols > 1:
        pairs = [(i, (i - 1) % col_count) for i in range(col_count)]
        late = lax.ppermute(corr[0:1, :HALO], "col", pairs)
        late = jnp.where(lax.rem(col, seq_cols) < seq_cols - 1, late, jnp.zeros_like(late))
    early = jnp.concatenate([corr[1:, :HALO], late], axis=0)
    early = jnp.pad(early, ((0, 0), (chunk - HALO, 0), (0, 0))).astype(F32)
    input_grad = cotangent.reshape(row_count, chunk, part).astype(F32) + corr[:, HALO:].astype(F32) + early
    input_grad = input_grad.reshape(col_tokens, part)
    if relayed:
        mine = jnp.swapaxes(mine.reshape(2, RANK, part), 1, 2)
        return block_out, input_grad, mine[0], in_up, out_down, mine[1]
    wide = jnp.swapaxes(wide, 0, 1).reshape(col_count, RANK, 3 * local)
    owner = jnp.repeat(adapter_id, seq_cols)
    adapters = rank_total // RANK
    chosen = owner[:, None] == jnp.arange(adapters, dtype=jnp.int32)[None, :]
    wide = jnp.sum(jnp.where(chosen[:, :, None, None], wide[:, None], 0.0), axis=0)
    wide = wide.reshape(rank_total, 3 * local)
    in_up = wide[:, : 2 * local].reshape(rank_total, 2, heads_here, P_SIZE)
    in_up = jnp.swapaxes(in_up, 1, 2).reshape(rank_total, heads_here, 2 * P_SIZE)
    out_down = wide[:, 2 * local :]
    if rank_share <= RANK:
        mine = owner == (col * rank_share) // RANK
        thin = jnp.sum(jnp.where(mine[:, None, None], thin, 0.0), axis=0).reshape(2, RANK, part)
        thin = lax.dynamic_slice_in_dim(thin, lax.rem(col * rank_share, RANK), rank_share, 1)
        thin = jnp.swapaxes(thin, 1, 2)
    else:
        thin = jnp.sum(jnp.where(chosen[:, :, None, None], thin[:, None], 0.0), axis=0)
        thin = thin.reshape(adapters, 2, RANK, part)
        thin = jnp.transpose(thin, (1, 3, 0, 2)).reshape(2, part, rank_total)
        thin = lax.dynamic_slice_in_dim(thin, col * rank_share, rank_share, 2)
    return block_out, input_grad, thin[0], in_up, out_down, thin[1]


def solution(mesh):
    placed = (
        P("col", "row"), P("row"), P("row", "col", None), P("row", None), P(None, "col"), P("col"), P(), P(),
        P("col"), P("col"), P("col"), P("col"), P("col", "row"), P("row", None), P(None, "col", None),
        P(None, "col"), P("row", None), P(), P("col", "row"),
    )
    return jax.shard_map(
        per_device,
        mesh=mesh,
        in_specs=placed,
        out_specs=(
            P("col", "row"), P("col", "row"), P("row", "col"), P(None, "col", None), P(None, "col"),
            P("row", "col"),
        ),
        check_vma=False,
    )
```

```python
import functools

import jax
import jax.numpy as jnp
from jax import lax
from jax.experimental import pallas as pl
from jax.experimental.pallas import tpu as pltpu
from jax.sharding import PartitionSpec as P

D = 1024
HEADS = 32
P_SIZE = 64
STATES = 128
BLOCK = 256
RANK = 16
SEQ = 4096
DI = 2048
EPS = 1e-05
LOG2E = 1.4426950408889634

HALO = 16
IN_LANE = 32
OUT_LANE = 48
CAP = 80.0
SHARE_STEP = 4
QUAD = 4
WIDTH = QUAD * P_SIZE
GROUPS = HEADS // QUAD
LANES = 128
VMEM_BYTES = 60 * 1024 * 1024
F32 = jnp.float32
BF16 = jnp.bfloat16
MESH = pl.DeviceIdType.MESH


def mm(left, right):
    return jnp.dot(left, right, preferred_element_type=F32)


def mm_nt(left, right):
    return lax.dot_general(left, right, (((1,), (1,)), ((), ())), preferred_element_type=F32)


def mm_tn(left, right):
    return lax.dot_general(left, right, (((0,), (0,)), ((), ())), preferred_element_type=F32)


def split_left(ones, value):
    high = value.astype(BF16)
    rest = value - high.astype(F32)
    middle = rest.astype(BF16)
    low = (rest - middle.astype(F32)).astype(BF16)
    return mm(ones, high) + mm(ones, middle) + mm(ones, low)


def split_right(value, ones):
    high = value.astype(BF16)
    low = (value - high.astype(F32)).astype(BF16)
    return mm(high, ones) + mm(low, ones)


def sigmoid(value):
    return 0.5 * jnp.tanh(0.5 * value) + 0.5


def iota(shape, axis):
    return lax.broadcasted_iota(jnp.int32, shape, axis)


def widen(cols):
    lane = iota((cols.shape[0], LANES), 1) < P_SIZE
    left = jnp.where(lane, cols[:, 0:1], cols[:, 1:2])
    right = jnp.where(lane, cols[:, 2:3], cols[:, 3:4])
    return jnp.concatenate([left, right], axis=1)


def to_front(cols, group):
    return pltpu.roll(cols, lax.rem(LANES - QUAD * group, LANES), 1)


def lane_range(values, first):
    lane = iota(values.shape, 1)
    return jnp.where((lane >= first) & (lane < first + RANK), values, 0.0)


def out_block(w_ref, group, row, part):
    if w_ref.shape[2] == WIDTH:
        return w_ref[group, row, :, :part]
    rows = WIDTH // 2
    return jnp.concatenate([w_ref[group, row, :rows, :part], w_ref[group, row, :rows, part:]], axis=0)


def head_only(values, head):
    lane = iota(values.shape, 1) // P_SIZE
    return jnp.where(lane == head, values, jnp.zeros_like(values))


def delays(window, taps, bias):
    total = window[8:] * taps[0:1] + bias
    for k in range(1, 4):
        total = total + pltpu.roll(window, k, 0)[8:] * taps[k : k + 1]
    return total


def advances(window, taps, count):
    length = window.shape[0]
    total = window[:count] * taps[0:1]
    for k in range(1, 4):
        total = total + pltpu.roll(window, length - k, 0)[:count] * taps[k : k + 1]
    return total


def at_block(k):
    if isinstance(k, int):
        return pl.ds(k * BLOCK, BLOCK)
    return pl.ds(pl.multiple_of(k * BLOCK, BLOCK), BLOCK)


def at_rows(k):
    if isinstance(k, int):
        return pl.ds(HALO + k * BLOCK, BLOCK)
    return pl.ds(pl.multiple_of(HALO + k * BLOCK, HALO), BLOCK)


def with_halo(k):
    if k == 0:
        return pl.ds(0, HALO + BLOCK)
    return pl.ds(HALO + k * BLOCK, BLOCK)


def padded_rows(value, first):
    before = jnp.zeros((first, value.shape[1]), value.dtype)
    after = jnp.zeros((LANES - first - value.shape[0], value.shape[1]), value.dtype)
    return jnp.concatenate([before, value, after], axis=0)


def front_kernel(
    place_ref, x_ref, gain_ref, wst_ref, sp_ref, sb_ref, hp_ref, w_ref, up_ref, vp_ref,
    normed_ref, scpre_ref, ratio_ref, sig_ref, cum_ref, lead_ref, turned_ref, bs_ref, cs_ref, cs_t_ref, adv_ref,
    gate_ref, u_ref, eloc_ref, fin_ref, dec_ref,
    st_scr, bs_t_scr, val_scr,
):
    group = pl.program_id(0)
    row_count, _, part = x_ref.shape
    blocks = eloc_ref.shape[0]

    @pl.when(group == 0)
    def _():
        def project(rows):
            pieces = [x_ref[r, rows, :].astype(F32) for r in range(row_count)]
            square = sum(jnp.sum(piece * piece, axis=1, keepdims=True) for piece in pieces)
            inv = lax.rsqrt(square / D + EPS)
            total = None
            for r in range(row_count):
                normed = (pieces[r] * inv * gain_ref[r]).astype(BF16)
                normed_ref[rows, r * part : (r + 1) * part] = normed
                term = mm(normed, wst_ref[r])
                total = term if total is None else total + term
            st_scr[rows, :] = total
            adv_ref[rows, :] = lane_range(total[:, 256:384], IN_LANE).astype(BF16)

        project(pl.ds(0, HALO))

        @pl.loop(0, blocks)
        def _(k):
            project(at_rows(k))

        lower = (iota((BLOCK, BLOCK), 0) >= iota((BLOCK, BLOCK), 1)).astype(BF16)
        rate = -jnp.exp(hp_ref[1:2]) * LOG2E

        @pl.loop(0, blocks)
        def _(k):
            window = st_scr[pl.ds(pl.multiple_of(8 + k * BLOCK, 8), BLOCK + 8), :256]
            pre = delays(window, sp_ref[...], sb_ref[...])
            conv = pre * sigmoid(pre)
            b_rows = conv[:, :STATES].astype(BF16)
            c_rows = conv[:, STATES:].astype(BF16)
            scpre_ref[at_block(k), :] = pre
            bs_ref[at_block(k), :] = b_rows
            cs_ref[at_block(k), :] = c_rows
            bs_t_scr[k] = conv[:, :STATES].T.astype(BF16)
            cs_t_ref[k] = conv[:, STATES:].T.astype(BF16)
            raw = st_scr[at_rows(k), 256:384] + hp_ref[0:1]
            small = jnp.exp(-jnp.abs(raw))
            tail = jnp.where(
                small < 0.01, small * (1.0 - small * (0.5 - small * (1.0 / 3.0))), jnp.log(1.0 + small)
            )
            step = jnp.maximum(raw, 0.0) + tail
            cum = split_left(lower, step * rate)
            sig = sigmoid(raw)
            ratio_ref[at_block(k), :] = jnp.where(raw < -20.0, 1.0, sig / jnp.maximum(step, 1e-30))
            sig_ref[at_block(k), :] = sig
            lead = jnp.log(jnp.maximum(step, 1e-37)) * LOG2E - cum
            cum_ref[at_block(k), :] = cum
            lead_ref[at_block(k), :] = lead
            flipped = cum.T
            flipped_lead = lead.T
            for g in range(GROUPS):
                turned_ref[g, :QUAD, at_block(k)] = flipped[g * QUAD : (g + 1) * QUAD]
                turned_ref[g, QUAD:, at_block(k)] = flipped_lead[g * QUAD : (g + 1) * QUAD]

    up_rows = padded_rows(up_ref[0, 0], IN_LANE)

    def inner(rows):
        total = mm(adv_ref[rows, :], up_rows)
        for r in range(row_count):
            total = total + mm(normed_ref[rows, r * part : (r + 1) * part], w_ref[0, r, :part, :])
        return total

    taps = vp_ref[0]

    def one_block(k, carry):
        state, decay = carry
        product = inner(with_halo(k))
        skip = HALO if k == 0 else 0
        gate_ref[at_block(k), :] = product[skip:, :WIDTH].astype(BF16)
        val_scr[with_halo(k), :] = product[:, WIDTH:]
        window = val_scr[pl.ds(8 + k * BLOCK, BLOCK + 8), :]
        pre = delays(window, taps[0:4], taps[4:5])
        u_ref[at_block(k), :] = pre.astype(BF16)
        xs = (pre * sigmoid(pre)).astype(BF16).astype(F32)
        cum = cum_ref[at_block(k), :]
        last = cum[BLOCK - 1 : BLOCK]
        weight = to_front(jnp.exp2(last + lead_ref[at_block(k), :]), group)
        weighted = (xs * widen(weight)).astype(BF16)
        eloc_ref[k] = state.astype(BF16)
        last8 = to_front(jnp.broadcast_to(last, (8, LANES)), group)
        fall = widen(jnp.exp2(last8))[0:1]
        return fall * state + mm(bs_t_scr[k], weighted), decay * fall

    carry = (jnp.zeros((STATES, WIDTH), F32), jnp.ones((1, WIDTH), F32))
    for k in range(blocks):
        carry = one_block(k, carry)
    state, decay = carry
    fin_ref[...] = state.astype(BF16)
    dec_ref[...] = jnp.broadcast_to(decay, (8, WIDTH))


def inner_products(score, cum, turned_ref, rows, xs):
    total = None
    for h in range(QUAD):
        spread = cum[:, h : h + 1] + turned_ref[0, QUAD + h : QUAD + h + 1, rows]
        weights = (score * jnp.exp2(jnp.minimum(spread, CAP))).astype(BF16)
        term = mm(weights, head_only(xs, h))
        total = term if total is None else total + term
    return total


def scan_kernel(
    ready, place_ref, x_ref, g_ref, wst_ref, w_ref, down_ref, vp_ref, gate_ref, u_ref, eloc_ref, ein_ref,
    cum_ref, turned_ref, bs_ref, cs_ref,
    out_ref, o_ref, ent_ref, aux_ref, sg_ref, gup_ref,
    score_scr, gained_scr, side_scr, square_scr,
):
    group = pl.program_id(0)
    row_count, _, part = x_ref.shape
    blocks = eloc_ref.shape[0]

    @pl.when(group == 0)
    def _():
        side_scr[...] = jnp.zeros_like(side_scr)
        square_scr[...] = jnp.zeros_like(square_scr)
        keep = iota((BLOCK, BLOCK), 0) >= iota((BLOCK, BLOCK), 1)

        if not ready:

            @pl.loop(0, blocks)
            def _(k):
                score = mm_nt(cs_ref[at_block(k), :], bs_ref[at_block(k), :])
                score_scr[k] = jnp.where(keep, score, 0.0)

    taps = vp_ref[0]

    down_rows = padded_rows(down_ref[0, 0], OUT_LANE)

    def one_block(k, before):
        rows = at_block(k)
        pre = u_ref[rows, :].astype(F32)
        conv = pre * sigmoid(pre)
        cum = to_front(cum_ref[rows, :], group)
        entering = (eloc_ref[k].astype(F32) + before * ein_ref[...]).astype(BF16)
        ent_ref[k] = entering
        total = widen(jnp.exp2(cum)) * mm(cs_ref[rows, :], entering)
        if ready:
            total = total + turned_ref[rows, :].astype(F32)
        else:
            score = score_scr[k]
            total = total + inner_products(score, cum, turned_ref, rows, conv.astype(BF16))
        output = total + taps[6:7] * conv
        o_ref[rows, :] = output.astype(BF16)
        gate = gate_ref[rows, :].astype(F32)
        gated = output * gate * sigmoid(gate)
        square = gated * gated
        square_scr[rows, :] += square[:, :LANES] + square[:, LANES:]
        gained = (gated * taps[5:6]).astype(BF16)
        gained_scr[group, rows, :] = gained
        side_scr[rows, :] += mm_nt(gained, down_rows)
        return before * widen(jnp.exp2(cum[BLOCK - 8 :]))[7:8]

    before = jnp.ones((1, WIDTH), F32)
    for k in range(blocks):
        before = one_block(k, before)

    @pl.when(group == pl.num_programs(0) - 1)
    def _():
        gup_ref[...] = jnp.zeros_like(gup_ref)

        @pl.loop(0, blocks)
        def _(k):
            rows = at_block(k)
            mean = jnp.sum(square_scr[rows, :], axis=1, keepdims=True) / DI
            rms = lax.rsqrt(mean + EPS)
            side_raw = side_scr[rows, :]
            side = (side_raw * rms).astype(BF16)
            side_grad = None
            for r in range(row_count):
                term = mm(g_ref[r, rows, :], wst_ref[r, :, 256:384])
                side_grad = term if side_grad is None else side_grad + term
            side_grad = lane_range(side_grad, OUT_LANE).astype(BF16)
            product = jnp.sum(side_grad.astype(F32) * side_raw, axis=1, keepdims=True)
            for r in range(row_count):
                cols = slice(r * part, (r + 1) * part)
                raw = mm(gained_scr[0, rows, :], out_block(w_ref, 0, r, part))
                for c in range(1, GROUPS):
                    raw = raw + mm(gained_scr[c, rows, :], out_block(w_ref, c, r, part))
                cot = g_ref[r, rows, :]
                product = product + jnp.sum(raw * cot.astype(F32), axis=1, keepdims=True)
                total = x_ref[r, at_rows(k), :].astype(F32) + raw * rms + mm_nt(side, wst_ref[r, :, 256:384])
                out_ref[r, rows, :] = total.astype(BF16)
                gup_ref[:, cols] += mm_tn(side, cot)[OUT_LANE : OUT_LANE + RANK]
            coefficient = rms * rms * rms * product / DI
            lane = iota((BLOCK, LANES), 1)
            aux_ref[rows, :] = jnp.where(lane == 0, rms, coefficient)
            sg_ref[rows, :] = side_grad


def gate_kernel(
    place_ref, g_ref, w_ref, sg_ref, down_ref, vp_ref, gate_ref, o_ref, aux_ref, cum_ref, cs_t_ref,
    dgate_ref, dy_ref, gloc_ref, gfin_ref, gdown_ref,
    sg_t_scr,
):
    group = pl.program_id(0)
    row_count, _, part = g_ref.shape
    blocks = gloc_ref.shape[0]

    @pl.when(group == 0)
    def _():
        @pl.loop(0, blocks)
        def _(k):
            sg_t_scr[k] = sg_ref[at_block(k), :].astype(F32).T[OUT_LANE : OUT_LANE + RANK].astype(BF16)

    taps = vp_ref[0]
    gdown_ref[0] = jnp.zeros((RANK, WIDTH), F32)

    down_rows = padded_rows(down_ref[0, 0], OUT_LANE)

    def one_block(i, state):
        k = blocks - 1 - i
        rows = at_block(k)
        dmix = mm(sg_ref[rows, :], down_rows)
        for r in range(row_count):
            dmix = dmix + mm_nt(g_ref[r, rows, :], out_block(w_ref, 0, r, part))
        gate = gate_ref[rows, :].astype(F32)
        output = o_ref[rows, :].astype(F32)
        sig = sigmoid(gate)
        act = gate * sig
        gated = output * act
        rms = aux_ref[rows, 0:1]
        coefficient = aux_ref[rows, 1:2]
        scale = rms * taps[5:6]
        mixed = (gated * scale).astype(BF16)
        gdown_ref[0] += mm(sg_t_scr[k], mixed)
        gated_grad = scale * dmix - gated * coefficient
        dy = gated_grad * act
        dgate = gated_grad * output * (sig + act * (1.0 - sig))
        dgate_ref[rows, :] = dgate.astype(BF16)
        dy_ref[rows, :] = dy.astype(BF16)
        cum = to_front(cum_ref[rows, :], group)
        factor = widen(jnp.exp2(cum))
        gloc_ref[k] = state.astype(BF16)
        return factor[BLOCK - 1 : BLOCK] * state + mm(cs_t_ref[k], (factor * dy).astype(BF16))

    state = jnp.zeros((STATES, WIDTH), F32)
    for i in range(blocks):
        state = one_block(i, state)
    gfin_ref[...] = state.astype(BF16)


def back_kernel(
    place_ref, x_ref, gain_ref, normed_ref, wst_ref, w_ref, up_ref, adv_ref, vp_ref, sp_ref, hp_ref,
    u_ref, o_ref, dy_ref, dgate_ref, ent_ref, gloc_ref, gin_ref,
    cum_ref, lead_ref, turned_ref, ratio_ref, sig_ref, scpre_ref, bs_ref, cs_ref, out_down_ref, out_up_ref,
    corr_ref, wide_ref, thin_ref,
    score_scr, dscore_scr, db_scr, dc_scr, dcum_scr, dstep_scr, dlast_scr, du_scr, ig_scr, ng_scr, adg_scr, adv_t_scr, up_scr, in_scr,
):
    group = pl.program_id(0)
    row_count, _, part = x_ref.shape
    blocks = gloc_ref.shape[0]
    total_rows = normed_ref.shape[0]

    @pl.when(group == 0)
    def _():
        for ref in (dscore_scr, db_scr, dc_scr, dcum_scr, dstep_scr, dlast_scr, ng_scr, adg_scr):
            ref[...] = jnp.zeros_like(ref)
        du_scr[0:HALO, :] = jnp.zeros((HALO, WIDTH), F32)
        du_scr[total_rows : total_rows + HALO, :] = jnp.zeros((HALO, WIDTH), F32)

        @pl.loop(0, blocks)
        def _(k):
            score_scr[k] = mm_nt(bs_ref[at_block(k), :], cs_ref[at_block(k), :])
            adv_t_scr[k] = adv_ref[at_rows(k), :].astype(F32).T[IN_LANE : IN_LANE + RANK].astype(BF16)

    keep = iota((BLOCK, BLOCK), 0) <= iota((BLOCK, BLOCK), 1)
    taps = vp_ref[0]
    pick = (iota((WIDTH, LANES), 1) == QUAD * group + iota((WIDTH, LANES), 0) // P_SIZE).astype(BF16)

    def one_block(i, after):
        k = blocks - 1 - i
        rows = at_block(k)
        pre = u_ref[rows, :].astype(F32)
        sig = sigmoid(pre)
        conv = pre * sig
        xs_low = conv.astype(BF16)
        xs = xs_low.astype(F32)
        cum = to_front(cum_ref[rows, :], group)
        lead = to_front(lead_ref[rows, :], group)
        dy_low = dy_ref[rows, :]
        dy = dy_low.astype(F32)
        b_rows = bs_ref[rows, :]
        c_rows = cs_ref[rows, :]
        score = jnp.where(keep, score_scr[k], 0.0)
        dscore = dscore_scr[k]
        ending = gloc_ref[k].astype(F32) + after * gin_ref[...]
        ending_low = ending.astype(BF16)
        last = cum[BLOCK - 1 : BLOCK]
        to_end = widen(jnp.exp2(last + lead))
        dxs_state = to_end * mm(b_rows, ending_low)
        dxs = dxs_state
        for h in range(QUAD):
            spread = turned_ref[0, h : h + 1, rows] + lead[:, h : h + 1]
            damp = jnp.exp2(jnp.minimum(spread, CAP))
            weights = (score * damp).astype(BF16)
            dy_head = head_only(dy_low, h)
            dxs = dxs + mm(weights, dy_head)
            dscore = dscore + mm_nt(xs_low, dy_head) * damp
        dscore_scr[k] = dscore
        from_start = widen(jnp.exp2(cum))
        fall = from_start[BLOCK - 1 : BLOCK]
        entering_low = ent_ref[k]
        entering = entering_low.astype(F32)
        dc_scr[rows, :] += mm_nt((from_start * dy).astype(BF16), entering_low)
        db_scr[rows, :] += mm_nt((to_end * xs).astype(BF16), ending_low)
        scan_out = o_ref[rows, :].astype(F32) - taps[6:7] * conv
        inward = mm((xs * dxs).astype(BF16), pick)
        dcum_scr[rows, :] += mm((dy * scan_out).astype(BF16), pick) - inward
        dstep_scr[rows, :] += inward
        ends = jnp.sum(xs * dxs_state, axis=0, keepdims=True)
        ends = ends + fall * jnp.sum(entering * ending, axis=0, keepdims=True)
        dlast_scr[k] += split_right(jnp.broadcast_to(ends, (8, WIDTH)), pick)
        dconv = taps[6:7] * dy + dxs
        du_scr[at_rows(k), :] = dconv * (sig + conv * (1.0 - sig))
        return after * fall

    after = jnp.ones((1, WIDTH), F32)
    for i in range(blocks):
        after = one_block(i, after)
    up_rows = padded_rows(up_ref[0, 0], IN_LANE)

    ig_scr[0:HALO, :WIDTH] = jnp.zeros((HALO, WIDTH), BF16)
    for k in range(blocks):
        rows = with_halo(k)
        extra = HALO if k == 0 else 0
        ig_scr[at_rows(k), :WIDTH] = dgate_ref[at_block(k), :]
        window = du_scr[pl.ds(HALO + k * BLOCK - extra, BLOCK + extra + 8), :]
        ig_scr[rows, WIDTH:] = advances(window, taps[0:4], BLOCK + extra).astype(BF16)
        grad = ig_scr[rows, :]
        adg_scr[rows, :] += mm_nt(grad, up_rows)
        for r in range(row_count):
            ng_scr[rows, r * part : (r + 1) * part] += mm_nt(grad, w_ref[0, r, :part, :])
        if k == 0:
            up_scr[...] = mm_tn(adv_ref[0:HALO, :], grad[:HALO])[IN_LANE : IN_LANE + RANK]
        up_scr[...] += mm(adv_t_scr[k], grad[extra:])

    share = RANK // row_count
    for r in range(row_count):
        wide_ref[r, 0, :, : 2 * WIDTH] = up_scr[r * share : (r + 1) * share, :]
        wide_ref[r, 0, :, 2 * WIDTH :] = out_down_ref[0, r * share : (r + 1) * share, :]

    @pl.when(group == pl.num_programs(0) - 1)
    def _():
        upper = (iota((BLOCK, BLOCK), 0) <= iota((BLOCK, BLOCK), 1)).astype(BF16)
        rate = -jnp.exp(hp_ref[1:2])

        @pl.loop(0, blocks)
        def _(k):
            rows = at_block(k)
            dscore = jnp.where(keep, dscore_scr[k], 0.0).astype(BF16)
            db = db_scr[rows, :] + mm(dscore, cs_ref[rows, :])
            dc = dc_scr[rows, :] + mm_tn(dscore, bs_ref[rows, :])
            pre = scpre_ref[rows, :]
            sig = sigmoid(pre)
            slope = sig + pre * sig * (1.0 - sig)
            du_scr[at_rows(k), :] = jnp.concatenate([db, dc], axis=1) * slope
            is_last = iota((BLOCK, LANES), 0) == BLOCK - 1
            dcum = dcum_scr[rows, :] + jnp.where(is_last, dlast_scr[k, 0:1, :], 0.0)
            slower = split_left(upper, dcum) * (rate * sig_ref[rows, :])
            dstep_scr[rows, :] = dstep_scr[rows, :] * ratio_ref[rows, :] + slower

        def finish(rows, window, count, draw):
            dstate = advances(window, sp_ref[...], count).astype(BF16)
            adapt = adg_scr[rows, :].astype(BF16)
            mixed = adapt + draw
            total = jnp.zeros((count, 1), F32)
            square = jnp.zeros((count, 1), F32)
            grads = []
            for r in range(row_count):
                cols = slice(r * part, (r + 1) * part)
                grad = ng_scr[rows, cols] + mm_nt(dstate, wst_ref[r, :, 0:256])
                grad = grad + mm_nt(mixed, wst_ref[r, :, 256:384])
                grad = grad * gain_ref[r]
                piece = x_ref[r, rows, :].astype(F32)
                total = total + jnp.sum(piece * grad, axis=1, keepdims=True)
                square = square + jnp.sum(piece * piece, axis=1, keepdims=True)
                grads.append(grad)
                in_scr[:, cols] += mm_tn(adapt, normed_ref[rows, cols])[IN_LANE : IN_LANE + RANK]
            inv = lax.rsqrt(square / D + EPS)
            factor = inv * inv * inv * total / D
            for r in range(row_count):
                piece = x_ref[r, rows, :].astype(F32)
                corr_ref[r, rows, :] = (inv * grads[r] - factor * piece).astype(BF16)

        in_scr[...] = jnp.zeros_like(in_scr)
        for k in range(blocks):
            extra = HALO if k == 0 else 0
            window = du_scr[pl.ds(HALO + k * BLOCK - extra, BLOCK + extra + 8), :]
            draw = dstep_scr[at_block(k), :].astype(BF16)
            if k == 0:
                draw = jnp.concatenate([jnp.zeros((HALO, LANES), BF16), draw], axis=0)
            finish(with_halo(k), window, BLOCK + extra, draw)

        for r in range(row_count):
            thin_ref[r, 0:RANK, :] = in_scr[:, r * part : (r + 1) * part]
            thin_ref[r, RANK:, :] = out_up_ref[:, r * part : (r + 1) * part]


def on_row(row):
    return {"row": row}


def on_col(col):
    return {"col": col}


def tail_kernel(
    corr_ref, wide_ref, thin_ref, owner_ref,
    corr_out, wide_out, thin_out, up_out, down_out, mine_out,
    wide_pair, thin_pair, wide_both, thin_both, wide_scr, thin_scr, wide_sum, thin_sum, wide_col,
    own_sem, corr_send, corr_recv, pair_send, pair_recv, row_send, row_recv, col_send, col_recv, last_send, last_recv,
    core_send, core_recv,
):
    row_count = corr_ref.shape[0]
    col_count = thin_out.shape[0]
    row = lax.axis_index("row")
    col = lax.axis_index("col")
    barrier = pltpu.get_barrier_semaphore()
    for d in range(1, row_count):
        pl.semaphore_signal(barrier, inc=1, device_id=on_row(lax.rem(row + d, row_count)), device_id_type=MESH)
    for d in range(1, col_count):
        pl.semaphore_signal(barrier, inc=1, device_id=on_col(lax.rem(col + d, col_count)), device_id_type=MESH)
    pl.semaphore_wait(barrier, row_count + col_count - 2)

    def send(source, target, sends, recvs, index, device):
        copy = pltpu.make_async_remote_copy(
            src_ref=source, dst_ref=target, send_sem=sends.at[index], recv_sem=recvs.at[index],
            device_id=device, device_id_type=MESH,
        )
        copy.start()
        return copy

    chips = row_count // 2
    parity = lax.rem(row, 2)
    chip = row // 2
    core = row + 1 - 2 * parity
    first = []
    for j in range(chips):
        theirs = 2 * j + 1 - parity
        first.append(send(wide_ref.at[theirs], wide_pair.at[j], pair_send, pair_recv, j, on_row(core)))
        first.append(send(thin_ref.at[theirs], thin_pair.at[j], pair_send, pair_recv, chips + j, on_row(core)))
    moved = []
    cuts = (0, 8 * corr_ref.shape[1] // 1040 * 16, 45 * corr_ref.shape[1] // 1040 * 16, corr_ref.shape[1])

    def move(step):
        for d in range(1, row_count):
            peer = lax.rem(row + d, row_count)
            part = pl.ds(cuts[step], cuts[step + 1] - cuts[step])
            index = step * row_count + d
            source = corr_ref.at[peer, part]
            moved.append(send(source, corr_out.at[row, part], corr_send, corr_recv, index, on_row(peer)))

    move(0)
    own = pltpu.make_async_copy(corr_ref.at[row], corr_out.at[row], own_sem.at[0])
    own.start()
    for copy in first:
        copy.wait()
    for j in range(chips):
        wide_both[j] = wide_ref[2 * j + parity] + wide_pair[j]
        thin_both[j] = thin_ref[2 * j + parity] + thin_pair[j]
    across = []
    for d in range(1, chips):
        there = lax.rem(chip + d, chips)
        peer = on_row(2 * there + parity)
        across.append(send(wide_both.at[there], wide_scr.at[chip], row_send, row_recv, d, peer))
        across.append(send(thin_both.at[there], thin_scr.at[chip], row_send, row_recv, chips + d, peer))
    move(1)
    for copy in across:
        copy.wait()
    wide = wide_both[chip]
    thin = thin_both[chip]
    for d in range(1, chips):
        there = lax.rem(chip + d, chips)
        wide = wide + wide_scr[there]
        thin = thin + thin_scr[there]
    wide_sum[...] = wide
    thin_sum[...] = thin
    second = []
    for d in range(1, col_count):
        peer = lax.rem(col + d, col_count)
        second.append(send(wide_sum.at[peer], wide_col.at[col], col_send, col_recv, d, on_col(peer)))
        second.append(send(thin_sum, thin_out.at[col], col_send, col_recv, col_count + d, on_col(peer)))
    wide_col[col] = wide_sum[col]
    thin_out[col] = thin
    for copy in second:
        copy.wait()
    third = []
    for d in range(1, chips):
        there = lax.rem(chip + d, chips)
        third.append(send(wide_col, wide_out.at[row], last_send, last_recv, d, on_row(2 * there + parity)))
    fourth = [send(wide_col, wide_out.at[row], core_send, core_recv, 0, on_row(core))]
    move(2)
    wide_out[row] = wide_col[...]
    for d in range(1, chips):
        third[d - 1].wait_recv()
        source = 2 * lax.rem(chip + chips - d, chips) + parity
        fourth.append(send(wide_out.at[source], wide_out.at[source], core_send, core_recv, d, on_row(core)))
    for copy in third:
        copy.wait_send()
    for copy in fourth:
        copy.wait()
    if up_out.shape[0] > RANK:
        lane = iota((wide_out.shape[2], LANES), 1) < P_SIZE
        share = wide_out.shape[2]
        mine = jnp.zeros(mine_out.shape, F32)
        for c in range(col_count):
            mine = mine + jnp.where(owner_ref[c] == col, thin_out[c], 0.0)
        mine_out[...] = mine
        for a in range(up_out.shape[0] // RANK):
            for r in range(row_count):
                total = jnp.zeros(wide_out.shape[2:], F32)
                for c in range(col_count):
                    total = total + jnp.where(owner_ref[c] == a, wide_out[r, c], 0.0)
                rows = slice(a * RANK + r * share, a * RANK + (r + 1) * share)
                tiles = [total[:, i * LANES : (i + 1) * LANES] for i in range(QUAD)]
                turned = [pltpu.roll(tile, P_SIZE, 1) for tile in tiles]
                for h in range(QUAD):
                    gate, value = h // 2, 2 + h // 2
                    if h % 2 == 0:
                        up_out[rows, h, :] = jnp.where(lane, tiles[gate], turned[value])
                    else:
                        up_out[rows, h, :] = jnp.where(lane, turned[gate], tiles[value])
                down_out[rows, :] = total[:, 2 * WIDTH :]
    for copy in moved:
        copy.wait()
    own.wait()


def start_kernel(
    x_ref, w_ref, up_ref, p_ref, down_ref, state_ref, in_ref, out_ref, gain_ref, conv_ref, bias_ref, gate_ref, step_ref, rate_ref,
    skip_ref, adapter_ref,
    x_out, w_out, shared_out, gain_out, vec_out, head_out, place_out,
    block_scr, zero_scr, shared_ref,
    own_sem, send_sem, recv_sem, row_send, row_recv, col_send, col_recv,
):
    col_count, row_count = w_out.shape[:2]
    high_count = col_count // 2
    part = x_ref.shape[1]
    chunk = x_ref.shape[0] // row_count
    rank_part = up_ref.shape[0] // row_count
    row = lax.axis_index("row")
    col = lax.axis_index("col")
    low = lax.rem(col, 2)
    high = col // 2
    core = row + 1 - 2 * lax.rem(row, 2)
    across = lax.rem(row + 2, row_count)
    side = col + 1 - 2 * low
    barrier = pltpu.get_barrier_semaphore()
    for d in range(1, row_count):
        pl.semaphore_signal(barrier, inc=1, device_id=on_row(lax.rem(row + d, row_count)), device_id_type=MESH)
    for d in range(1, col_count):
        pl.semaphore_signal(barrier, inc=1, device_id=on_col(lax.rem(col + d, col_count)), device_id_type=MESH)

    def paired(value):
        lane = iota((value.shape[0], LANES), 1) < P_SIZE
        tiles = [value[:, h, :].astype(F32) for h in range(QUAD)]
        turned = [pltpu.roll(tile, P_SIZE, 1) for tile in tiles]
        gates = [jnp.where(lane, tiles[h], turned[h + 1]) for h in (0, 2)]
        values = [jnp.where(lane, turned[h], tiles[h + 1]) for h in (0, 2)]
        return jnp.concatenate(gates + values, axis=1).astype(BF16)

    block_scr[0:part, :] = paired(w_ref)
    ranks = pl.ds(pl.multiple_of(row * rank_part, rank_part), rank_part)
    block_scr[part : part + rank_part, :] = paired(up_ref.at[ranks])
    first = part + rank_part
    half = WIDTH // 2
    block_scr[first : first + half, :WIDTH] = p_ref[:half, :]
    block_scr[first : first + half, WIDTH:] = p_ref[half:, :]
    first = first + half
    downs = down_ref[ranks, :]
    block_scr[first : first + rank_part // 2, :WIDTH] = downs[: rank_part // 2]
    block_scr[first : first + rank_part // 2, WIDTH:] = downs[rank_part // 2 :]
    zero_scr[...] = jnp.zeros_like(zero_scr)
    adapter = adapter_ref[col]
    shift = adapter * RANK
    per_part = rank_part // RANK
    place_out[0] = adapter // per_part
    place_out[1] = adapter - adapter // per_part * per_part
    source = iota((LANES, LANES), 0) - shift
    target = iota((LANES, LANES), 1)
    chosen = (source >= 0) & (source < RANK)
    ins = (chosen & (source == target - IN_LANE)).astype(F32).astype(BF16)
    outs = (chosen & (source == target - OUT_LANE)).astype(F32).astype(BF16)
    states = 2 * STATES
    shared_ref[:, :states] = state_ref[:states, :].astype(F32).T.astype(BF16)
    steps = jnp.concatenate(
        [state_ref[states:, :].astype(F32), jnp.zeros((LANES - HEADS, part), F32)], axis=0
    ).T
    shared_ref[:, states:] = (steps + mm(in_ref[...], ins) + mm(out_ref[...], outs)).astype(BF16)
    vec_out[col, 0:4, :] = conv_ref[...]
    vec_out[col, 4:5, :] = bias_ref[...]
    vec_out[col, 5:6, :] = gate_ref[...]
    vec_out[col, 6:7, :] = widen(skip_ref[...])
    lane = iota((1, WIDTH), 1)
    scalars = jnp.zeros((1, WIDTH), F32)
    for h in range(QUAD):
        scalars = jnp.where(lane == h, step_ref[:, h : h + 1], scalars)
        scalars = jnp.where(lane == QUAD + h, rate_ref[:, h : h + 1], scalars)
    vec_out[col, 7:8, :] = scalars
    gain_out[row] = gain_ref[...]
    pl.semaphore_wait(barrier, row_count + col_count - 2)

    def remote(source, target, sends, recvs, index, device):
        return pltpu.make_async_remote_copy(
            src_ref=source, dst_ref=target, send_sem=sends.at[index], recv_sem=recvs.at[index],
            device_id=device, device_id_type=MESH,
        )

    own_block = pltpu.make_async_copy(block_scr, w_out.at[col, row], own_sem.at[0])
    own_block.start()

    def whole_window(target, slot, index, peer):
        source = x_ref.at[pl.ds(pl.multiple_of(target * chunk - HALO, HALO), chunk + HALO)]
        return remote(source, x_out.at[slot], row_send, row_recv, index, on_row(peer))

    def first_window(slot, index, peer):
        source = x_ref.at[pl.ds(0, chunk)]
        return remote(source, x_out.at[slot, pl.ds(HALO, chunk)], row_send, row_recv, index, on_row(peer))

    def each_window(sending, act):
        for d in range(1, row_count):
            peer = lax.rem(row + d, row_count)
            chosen = peer if sending else row
            slot = row if sending else lax.rem(row + row_count - d, row_count)

            @pl.when(chosen > 0)
            def _():
                act(whole_window(jnp.maximum(chosen, 1), slot, d, peer))

            @pl.when(chosen == 0)
            def _():
                act(first_window(slot, d, peer))

    @pl.when(row > 0)
    def _():
        source = x_ref.at[pl.ds(pl.multiple_of(jnp.maximum(row, 1) * chunk - HALO, HALO), chunk + HALO)]
        pltpu.make_async_copy(source, x_out.at[row], own_sem.at[1]).start()

    @pl.when(row == 0)
    def _():
        pltpu.make_async_copy(x_ref.at[pl.ds(0, chunk)], x_out.at[row, pl.ds(HALO, chunk)], own_sem.at[1]).start()
        for r in range(row_count):
            pltpu.make_async_copy(zero_scr, x_out.at[r, pl.ds(0, HALO)], own_sem.at[3 + r]).start()

    own_shared = pltpu.make_async_copy(shared_ref, shared_out.at[row], own_sem.at[2])
    own_shared.start()
    small = []
    for d in range(1, col_count):
        peer = lax.rem(col + d, col_count)
        small.append(remote(vec_out.at[col], vec_out.at[col], col_send, col_recv, d, on_col(peer)))
    for d in range(1, row_count):
        peer = lax.rem(row + d, row_count)
        small.append(remote(shared_ref, shared_out.at[row], row_send, row_recv, row_count + d, on_row(peer)))
        small.append(
            remote(gain_out.at[row], gain_out.at[row], row_send, row_recv, 2 * row_count + d, on_row(peer))
        )
    for copy in small:
        copy.start()

    cut = (w_out.shape[2] * 65 // 100 + 8) // 16 * 16
    spans = (pl.ds(0, cut), pl.ds(cut, w_out.shape[2] - cut))
    has_up = high < high_count - 1
    has_down = high > 0
    routes = {
        "up": (0, has_up, on_col(lax.rem(col + 2, col_count))),
        "down": (1, has_down, on_col(lax.rem(col + col_count - 2, col_count))),
        "x": (2, None, on_col(side)),
        "y": (3, None, on_row(across)),
        "core": (4, None, on_row(core)),
    }

    def piece(section, c, r, kind, device):
        ref = w_out.at[c, r, spans[section]]
        return pltpu.make_async_remote_copy(
            src_ref=ref, dst_ref=ref, send_sem=send_sem.at[section, c, r, kind],
            recv_sem=recv_sem.at[section, c, r], device_id=device, device_id_type=MESH,
        )

    def event(starting, section, c, r, names, arrives=True, valid=None):
        def act():
            if starting and arrives:
                piece(section, c, r, 4, on_row(core)).wait_recv()
            for name in names:
                kind, allowed, device = routes[name]
                copy = piece(section, c, r, kind, device)
                if allowed is None:
                    copy.start() if starting else copy.wait_send()
                else:

                    @pl.when(allowed)
                    def _():
                        copy.start() if starting else copy.wait_send()

        if valid is None:
            act()
        else:
            pl.when(valid)(act)

    def far(column, step, distance):
        return lax.rem(column + step * distance + 4 * col_count, col_count)

    def within(step, distance):
        return high >= distance if step < 0 else high + distance < high_count

    onward = {-2: "up", 2: "down"}

    def along(starting, section, distance):
        for step in (-2, 2):
            valid = within(step, distance)
            if section == 0:
                names = (onward[step], "y", "x", "core")
                event(starting, 0, far(col, step, distance), row, names, valid=valid)
            else:
                for column, r in ((col, row), (side, row), (col, across), (side, across)):
                    event(starting, 1, far(column, step, distance), r, (onward[step], "core"), valid=valid)

    def over(starting, distance):
        for step in (-2, 2):
            valid = within(step, distance)
            event(starting, 0, far(side, step, distance), row, ("core",), valid=valid)
            event(starting, 0, far(col, step, distance), across, ("x", "core"), valid=valid)

    def last(starting, distance):
        for step in (-2, 2):
            event(starting, 0, far(side, step, distance), across, ("core",), valid=within(step, distance))

    def relay(starting):
        def windows():
            if starting:
                each_window(True, lambda copy: copy.start())

        event(starting, 0, col, row, ("up", "down"), arrives=False)
        event(starting, 1, col, row, ("x", "y"), arrives=False)
        event(starting, 0, col, row, ("y", "x", "core"), arrives=False)
        event(starting, 1, col, row, ("core",), arrives=False)
        event(starting, 1, side, row, ("y", "core"))
        along(starting, 0, 1)
        event(starting, 1, col, row, ("up", "down"), arrives=False)
        event(starting, 0, col, across, ("x", "core"))
        event(starting, 1, side, row, ("up", "down"), arrives=False)
        event(starting, 1, col, across, ("up", "down", "core"))
        for d in range(2, high_count - 1):
            along(starting, 0, d)
        event(starting, 1, side, across, ("up", "down", "core"))
        over(starting, 1)
        along(starting, 0, high_count - 1)
        windows()
        along(starting, 1, 1)
        over(starting, 2)
        event(starting, 0, side, row, ("core",))
        event(starting, 0, side, across, ("core",))
        last(starting, 1)
        for d in range(2, high_count):
            if d > 2:
                over(starting, d)
            along(starting, 1, d)
            if d > 2:
                last(starting, d - 1)
        last(starting, high_count - 1)

    own_block.wait()
    relay(True)
    for copy in small:
        copy.wait()
    lane = iota((1, LANES), 1) < QUAD
    steps = jnp.zeros((1, LANES), F32)
    rates = jnp.zeros((1, LANES), F32)
    for c in range(col_count):
        values = vec_out[c, 7:8, :LANES]
        steps = steps + pltpu.roll(jnp.where(lane, values, 0.0), (QUAD * c) % LANES, 1)
        values = pltpu.roll(values, LANES - QUAD, 1)
        rates = rates + pltpu.roll(jnp.where(lane, values, 0.0), (QUAD * c) % LANES, 1)
    head_out[...] = jnp.concatenate([steps, rates, jnp.zeros((6, LANES), F32)], axis=0)
    own_shared.wait()
    each_window(True, lambda copy: copy.wait_send())
    each_window(False, lambda copy: copy.wait_recv())

    @pl.when(row > 0)
    def _():
        source = x_ref.at[pl.ds(0, chunk + HALO)]
        pltpu.make_async_copy(source, x_out.at[row], own_sem.at[1]).wait()

    @pl.when(row == 0)
    def _():
        pltpu.make_async_copy(x_ref.at[pl.ds(0, chunk)], x_out.at[row, pl.ds(HALO, chunk)], own_sem.at[1]).wait()
        for r in range(row_count):
            pltpu.make_async_copy(zero_scr, x_out.at[r, pl.ds(0, HALO)], own_sem.at[3 + r]).wait()

    core_across = lax.rem(core + 2, row_count)
    for c in range(col_count):
        for r in (core, core_across):
            for section in range(2):
                piece(section, c, r, 4, on_row(core)).wait_recv()
    relay(False)


def start_exchange(x, w, up, p, down, shared, vectors, adapter_id, row_count, col_count):
    part = x.shape[1]
    rank_part = up.shape[0] // row_count
    block_rows = part + rank_part + WIDTH // 2 + rank_part // 2
    chunk = x.shape[0] // row_count
    vmem = pl.BlockSpec(memory_space=pltpu.VMEM)
    anywhere = pl.BlockSpec(memory_space=pl.ANY)
    dma = pltpu.SemaphoreType.DMA
    return pl.pallas_call(
        start_kernel,
        in_specs=[anywhere] + [vmem] * (7 + len(vectors)) + [pl.BlockSpec(memory_space=pltpu.SMEM)],
        out_specs=[anywhere] * 3 + [vmem] * 3 + [pl.BlockSpec(memory_space=pltpu.SMEM)],
        out_shape=[
            jax.ShapeDtypeStruct((row_count, chunk + HALO, part), BF16),
            jax.ShapeDtypeStruct((col_count, row_count, block_rows, 2 * WIDTH), BF16),
            jax.ShapeDtypeStruct((row_count, part, 384), BF16),
            jax.ShapeDtypeStruct((row_count, 1, part), F32),
            jax.ShapeDtypeStruct((col_count, 8, WIDTH), F32),
            jax.ShapeDtypeStruct((8, LANES), F32),
            jax.ShapeDtypeStruct((2,), jnp.int32),
        ],
        scratch_shapes=[
            pltpu.VMEM((block_rows, 2 * WIDTH), BF16), pltpu.VMEM((HALO, part), BF16),
            pltpu.VMEM((part, 384), BF16), dma((3 + row_count,)), dma((2, col_count, row_count, 5)), dma((2, col_count, row_count)),
            dma((3 * row_count,)), dma((3 * row_count,)), dma((col_count,)), dma((col_count,)),
        ],
        compiler_params=pltpu.CompilerParams(
            collective_id=1, has_side_effects=True, vmem_limit_bytes=VMEM_BYTES
        ),
    )(x, w, up, p, down, *shared, *vectors, adapter_id)


def carry_kernel(
    forward, state_ref, decay_ref,
    out_ref,
    other_scr, other_decay, total_scr, total_in,
    core_send, core_recv, across_send, across_recv, share_send, share_recv,
):
    row = lax.axis_index("row")
    parity = lax.rem(row, 2)
    chip = row // 2
    core = row + 1 - 2 * parity
    across = lax.rem(row + 2, 4)
    barrier = pltpu.get_barrier_semaphore()
    for peer in (core, across):
        pl.semaphore_signal(barrier, inc=1, device_id=on_row(peer), device_id_type=MESH)
    pl.semaphore_wait(barrier, 2)

    def remote(source, target, sends, recvs, index, peer):
        return pltpu.make_async_remote_copy(
            src_ref=source, dst_ref=target, send_sem=sends.at[index], recv_sem=recvs.at[index],
            device_id=on_row(peer), device_id_type=MESH,
        )

    swaps = [
        remote(state_ref, other_scr, core_send, core_recv, 0, core),
        remote(decay_ref, other_decay, core_send, core_recv, 1, core),
    ]
    for copy in swaps:
        copy.start()
    for copy in swaps:
        copy.wait()
    half = state_ref.shape[1] // 2
    rows = state_ref.shape[0] // 2
    second = parity == (1 if forward else 0)
    sends = chip == (0 if forward else 1)

    @pl.when(sends)
    def _():
        for p in range(2):

            @pl.when(parity == p)
            def _():
                cols = slice(p * half, (p + 1) * half)
                for q in range(2):
                    part = slice(q * rows, (q + 1) * rows)
                    mine = state_ref[part, cols].astype(F32)
                    other = other_scr[part, cols].astype(F32)
                    late = mine + other * decay_ref[0:1, cols]
                    early = other + mine * other_decay[0:1, cols]
                    total_scr[q] = jnp.where(second, late, early).astype(BF16)
                    remote(total_scr.at[q], total_in.at[p, q], across_send, across_recv, q, across).start()
        out_ref[...] = jnp.where(second, other_scr[...].astype(F32), 0.0)
        for q in range(2):
            remote(total_scr.at[q], total_in.at[parity, q], across_send, across_recv, q, across).wait_send()

    @pl.when(jnp.logical_not(sends))
    def _():
        for q in range(2):
            remote(total_scr.at[q], total_in.at[parity, q], across_send, across_recv, q, across).wait_recv()
            remote(
                total_in.at[parity, q], total_in.at[parity, q], share_send, share_recv, q, core
            ).start()
        for q in range(2):
            remote(
                total_in.at[parity, q], total_in.at[1 - parity, q], share_send, share_recv, q, core
            ).wait()
        for p in range(2):
            for q in range(2):
                cols = slice(p * half, (p + 1) * half)
                part = slice(q * rows, (q + 1) * rows)
                total = total_in[p, q].astype(F32)
                later = other_scr[part, cols].astype(F32) + total * other_decay[0:1, cols]
                out_ref[part, cols] = jnp.where(second, later, total)


def within_kernel(
    state_ref, decay_ref, u_ref, cum_ref, turned_ref, bs_ref, cs_ref,
    within_ref, out_ref,
    score_scr, other_scr, other_decay, total_scr, total_in,
    core_send, core_recv, across_send, across_recv, share_send, share_recv,
):
    group = pl.program_id(0)
    blocks = score_scr.shape[0]
    row = lax.axis_index("row")
    parity = lax.rem(row, 2)
    sends = row // 2 == 0
    core = row + 1 - 2 * parity
    across = lax.rem(row + 2, 4)
    half = state_ref.shape[1] // 2
    depth = state_ref.shape[0] // 2

    def remote(source, target, sending, receiving, index, peer):
        return pltpu.make_async_remote_copy(
            src_ref=source, dst_ref=target, send_sem=sending.at[index], recv_sem=receiving.at[index],
            device_id=on_row(peer), device_id_type=MESH,
        )

    def swaps():
        return (
            remote(state_ref, other_scr, core_send, core_recv, 0, core),
            remote(decay_ref, other_decay, core_send, core_recv, 1, core),
        )

    def crossing(q):
        return remote(total_scr.at[q], total_in.at[parity, q], across_send, across_recv, q, across)

    @pl.when(group == 0)
    def _():
        barrier = pltpu.get_barrier_semaphore()
        for peer in (core, across):
            pl.semaphore_signal(barrier, inc=1, device_id=on_row(peer), device_id_type=MESH)
        pl.semaphore_wait(barrier, 2)
        for copy in swaps():
            copy.start()
        keep = iota((BLOCK, BLOCK), 0) >= iota((BLOCK, BLOCK), 1)
        for k in range(blocks):
            score = mm_nt(cs_ref[at_block(k), :], bs_ref[at_block(k), :])
            score_scr[k] = jnp.where(keep, score, 0.0)
        for copy in swaps():
            copy.wait()

        @pl.when(sends)
        def _():
            for p in range(2):

                @pl.when(parity == p)
                def _():
                    cols = slice(p * half, (p + 1) * half)
                    for q in range(2):
                        part = slice(q * depth, (q + 1) * depth)
                        mine = state_ref[part, cols].astype(F32)
                        other = other_scr[part, cols].astype(F32)
                        if p == 1:
                            total_scr[q] = (mine + other * decay_ref[0:1, cols]).astype(BF16)
                        else:
                            total_scr[q] = (other + mine * other_decay[0:1, cols]).astype(BF16)
            for q in range(2):
                crossing(q).start()

    for k in range(blocks):
        rows = at_block(k)
        pre = u_ref[rows, :].astype(F32)
        conv = pre * sigmoid(pre)
        cum = to_front(cum_ref[rows, :], group)
        total = inner_products(score_scr[k], cum, turned_ref, rows, conv.astype(BF16))
        within_ref[rows, :] = total.astype(BF16)

    @pl.when((group == SHARE_STEP) & jnp.logical_not(sends))
    def _():
        for q in range(2):
            crossing(q).wait_recv()
            mine = total_in.at[parity, q]
            remote(mine, mine, share_send, share_recv, q, core).start()

    @pl.when((group == SHARE_STEP + 1) & jnp.logical_not(sends))
    def _():
        for q in range(2):
            remote(
                total_in.at[parity, q], total_in.at[1 - parity, q], share_send, share_recv, q, core
            ).wait()
        for p in range(2):
            for q in range(2):
                cols = slice(p * half, (p + 1) * half)
                part = slice(q * depth, (q + 1) * depth)
                total = total_in[p, q].astype(F32)
                later = other_scr[part, cols].astype(F32) + total * other_decay[0:1, cols]
                out_ref[part, cols] = jnp.where(parity == 1, later, total)

    @pl.when((group == SHARE_STEP + 1) & sends)
    def _():
        for q in range(2):
            crossing(q).wait_send()
        out_ref[...] = jnp.where(parity == 1, other_scr[...].astype(F32), 0.0)


def within_and_carry(state, decay, u, cum, turned, bs, cs):
    dma = pltpu.SemaphoreType.DMA
    rows, cols = state.shape
    tokens = u.shape[0]

    def fixed(shape):
        return pl.BlockSpec(shape, lambda c: (0,) * len(shape))

    lanes = pl.BlockSpec((tokens, WIDTH), lambda c: (0, c))
    return pl.pallas_call(
        within_kernel,
        grid=(GROUPS,),
        in_specs=[
            fixed(state.shape), fixed(decay.shape), lanes, fixed(cum.shape),
            pl.BlockSpec((1,) + turned.shape[1:], lambda c: (c, 0, 0)), fixed(bs.shape), fixed(cs.shape),
        ],
        out_specs=[lanes, fixed(state.shape)],
        out_shape=[jax.ShapeDtypeStruct(u.shape, BF16), jax.ShapeDtypeStruct(state.shape, F32)],
        scratch_shapes=[
            pltpu.VMEM((tokens // BLOCK, BLOCK, BLOCK), F32),
            pltpu.VMEM(state.shape, BF16), pltpu.VMEM(decay.shape, F32),
            pltpu.VMEM((2, rows // 2, cols // 2), BF16), pltpu.VMEM((2, 2, rows // 2, cols // 2), BF16),
            dma((2,)), dma((2,)), dma((2,)), dma((2,)), dma((2,)), dma((2,)),
        ],
        compiler_params=pltpu.CompilerParams(
            collective_id=2, has_side_effects=True, vmem_limit_bytes=VMEM_BYTES
        ),
    )(state, decay, u, cum, turned, bs, cs)


def carry_over(state, decay, forward):
    vmem = pl.BlockSpec(memory_space=pltpu.VMEM)
    dma = pltpu.SemaphoreType.DMA
    rows, cols = state.shape
    return pl.pallas_call(
        functools.partial(carry_kernel, forward),
        in_specs=[vmem, vmem],
        out_specs=vmem,
        out_shape=jax.ShapeDtypeStruct(state.shape, F32),
        scratch_shapes=[
            pltpu.VMEM(state.shape, BF16), pltpu.VMEM(decay.shape, F32),
            pltpu.VMEM((2, rows // 2, cols // 2), BF16), pltpu.VMEM((2, 2, rows // 2, cols // 2), BF16),
            dma((2,)), dma((2,)), dma((2,)), dma((2,)), dma((2,)), dma((2,)),
        ],
        compiler_params=pltpu.CompilerParams(
            collective_id=2 if forward else 3, has_side_effects=True, vmem_limit_bytes=VMEM_BYTES
        ),
    )(state, decay)


def finish_exchange(corr, wide, thin, owner, placed):
    row_count = corr.shape[0]
    col_count = wide.shape[1]
    share, width = wide.shape[2:]
    ranks = RANK * col_count if placed else RANK
    vmem = pl.BlockSpec(memory_space=pltpu.VMEM)
    anywhere = pl.BlockSpec(memory_space=pl.ANY)
    dma = pltpu.SemaphoreType.DMA
    return pl.pallas_call(
        tail_kernel,
        in_specs=[anywhere, vmem, vmem, pl.BlockSpec(memory_space=pltpu.SMEM)],
        out_specs=[anywhere] + [vmem] * 5,
        out_shape=[
            jax.ShapeDtypeStruct(corr.shape, corr.dtype),
            jax.ShapeDtypeStruct((row_count, col_count, share, width), F32),
            jax.ShapeDtypeStruct((col_count,) + thin.shape[1:], F32),
            jax.ShapeDtypeStruct((ranks, QUAD, LANES), F32),
            jax.ShapeDtypeStruct((ranks, WIDTH), F32),
            jax.ShapeDtypeStruct(thin.shape[1:], F32),
        ],
        scratch_shapes=[
            *[pltpu.VMEM((row_count // 2,) + value.shape[1:], F32) for value in (wide, thin) * 3],
            pltpu.VMEM(wide.shape[1:], F32), pltpu.VMEM(thin.shape[1:], F32), pltpu.VMEM(wide.shape[1:], F32),
            dma((1,)), dma((3 * row_count,)), dma((3 * row_count,)), dma((row_count,)), dma((row_count,)),
            dma((row_count,)), dma((row_count,)), dma((2 * col_count,)), dma((2 * col_count,)),
            dma((row_count // 2,)), dma((row_count // 2,)), dma((row_count // 2,)), dma((row_count // 2,)),
        ],
        compiler_params=pltpu.CompilerParams(
            collective_id=0, has_side_effects=True, vmem_limit_bytes=VMEM_BYTES
        ),
    )(corr, wide, thin, owner)


def whole_spec(shape):
    return pl.BlockSpec(shape, lambda c, s: (0,) * len(shape))


def lead_spec(shape):
    return pl.BlockSpec((1,) + tuple(shape[1:]), lambda c, s: (c,) + (0,) * (len(shape) - 1))


def lane_spec(shape):
    block = tuple(shape[:-1]) + (WIDTH,)
    return pl.BlockSpec(block, lambda c, s: (0,) * (len(shape) - 1) + (c,))


def second_spec(shape):
    block = (shape[0], 1) + tuple(shape[2:])
    return pl.BlockSpec(block, lambda c, s: (0, c) + (0,) * (len(shape) - 2))


def front_spec(shape):
    if shape[2] % 3 == 0 and shape[2] // 3 * 2 >= WIDTH and shape[3] == 2 * WIDTH and shape[1] == 4:
        return pl.BlockSpec((1, shape[1], shape[2] // 3 * 2, shape[3]), lambda c, s: (c, 0, 0, 0))
    return lead_spec(shape)


def full_back_spec(shape):
    if shape[2] > WIDTH:
        return pl.BlockSpec((shape[0], shape[1], shape[2] // 3, shape[3]), lambda c, s: (0, 0, 2, 0))
    return whole_spec(shape)


def back_spec(shape):
    if shape[2] > WIDTH:
        return pl.BlockSpec((1, shape[1], shape[2] // 3, shape[3]), lambda c, s: (c, 0, 2, 0))
    return lead_spec(shape)


def up_spec(shape):
    first = WIDTH // RANK if shape[2] > RANK else 0
    return pl.BlockSpec((1, 1, RANK, 2 * WIDTH), lambda c, s: (c, s[0], first + s[1], 0))


def down_spec(shape):
    first = shape[2] // RANK - 1
    return pl.BlockSpec((1, 1, RANK, WIDTH), lambda c, s: (c, s[0], first, s[1]))


KINDS = {
    "a": whole_spec, "c": lead_spec, "l": lane_spec, "s": second_spec, "w": front_spec, "f": full_back_spec,
    "p": back_spec, "u": up_spec, "d": down_spec,
}


def grouped_call(kernel, place, inputs, kinds, outputs, out_kinds, scratch, flops=0):
    return pl.pallas_call(
        kernel,
        grid_spec=pltpu.PrefetchScalarGridSpec(
            num_scalar_prefetch=1,
            grid=(GROUPS,),
            in_specs=[KINDS[kind](value.shape) for kind, value in zip(kinds, inputs)],
            out_specs=[KINDS[kind](shape) for kind, (shape, _) in zip(out_kinds, outputs)],
            scratch_shapes=[pltpu.VMEM(shape, dtype) for shape, dtype in scratch],
        ),
        out_shape=[jax.ShapeDtypeStruct(shape, dtype) for shape, dtype in outputs],
        compiler_params=pltpu.CompilerParams(vmem_limit_bytes=VMEM_BYTES),
        cost_estimate=pl.CostEstimate(flops=flops, bytes_accessed=40_000_000, transcendentals=0),
    )(place, *inputs)


def to_groups(value, heads_here):
    cols = value.shape[0]
    middle = value.shape[1:-1]
    if heads_here == QUAD:
        return value
    if heads_here > QUAD:
        parts = heads_here // QUAD
        value = value.reshape((cols,) + middle + (parts, WIDTH))
        value = jnp.moveaxis(value, -2, 1)
        return value.reshape((GROUPS,) + middle + (WIDTH,))
    parts = QUAD // heads_here
    value = value.reshape((GROUPS, parts) + middle + (heads_here * P_SIZE,))
    value = jnp.moveaxis(value, 1, -2)
    return value.reshape((GROUPS,) + middle + (WIDTH,))


def to_cols(value, heads_here, col_count):
    middle = value.shape[1:-1]
    if heads_here == QUAD:
        return value
    if heads_here > QUAD:
        parts = heads_here // QUAD
        value = value.reshape((col_count, parts) + middle + (WIDTH,))
        value = jnp.moveaxis(value, 1, -2)
        return value.reshape((col_count,) + middle + (heads_here * P_SIZE,))
    parts = QUAD // heads_here
    value = value.reshape((GROUPS,) + middle + (parts, heads_here * P_SIZE))
    value = jnp.moveaxis(value, -2, 1)
    return value.reshape((col_count,) + middle + (heads_here * P_SIZE,))


def pad_lanes(value, width):
    return jnp.pad(value, [(0, 0)] * (value.ndim - 1) + [(0, width - value.shape[-1])])


def carry_in(state, decay, row_count, col_count, seq_cols, forward):
    row = lax.axis_index("row")
    col = lax.axis_index("col")
    total = state
    factor = decay
    before = jnp.zeros(state.shape, F32)
    reach = jnp.ones_like(decay)
    span = 1
    while span < row_count:
        pairs = [(i, i ^ span) for i in range(row_count)]
        other = lax.ppermute(total, "row", pairs).astype(F32)
        other_factor = lax.ppermute(factor, "row", pairs)
        behind = ((row & span) != 0) == forward
        mine = total.astype(F32)
        before = jnp.where(behind, before + reach * other, before)
        reach = jnp.where(behind, reach * other_factor, reach)
        joined = jnp.where(behind, other * factor + mine, mine * other_factor + other)
        total = joined.astype(BF16)
        factor = factor * other_factor
        span *= 2
    place = lax.rem(col, seq_cols)
    for hop in range(1, seq_cols):
        shift = hop if forward else -hop
        pairs = [(i, (i + shift) % col_count) for i in range(col_count)]
        other = lax.ppermute(total, "col", pairs).astype(F32)
        other_factor = lax.ppermute(factor, "col", pairs)
        inside = place >= hop if forward else place < seq_cols - hop
        before = jnp.where(inside, before + reach * other, before)
        reach = jnp.where(inside, reach * other_factor, reach)
    return before


def per_device(
    block_in, norm_gain, proj_inner, proj_state, conv_inner, conv_inner_bias, conv_state, conv_state_bias,
    step_bias, decay_log, skip_gain, gate_gain, proj_out, adapt_in_down, adapt_in_up, adapt_out_down,
    adapt_out_up, adapter_id, cotangent,
):
    row_count = lax.axis_size("row")
    col_count = lax.axis_size("col")
    row = lax.axis_index("row")
    col = lax.axis_index("col")
    col_tokens, part = block_in.shape
    chunk = col_tokens // row_count
    total_rows = chunk + HALO
    blocks = chunk // BLOCK
    seq_cols = SEQ // col_tokens
    heads_here = proj_inner.shape[1]
    local = heads_here * P_SIZE
    rank_total = adapt_in_down.shape[1]
    rank_part = rank_total // row_count
    rank_share = rank_total // col_count
    adapter = lax.dynamic_index_in_dim(adapter_id, col // seq_cols, keepdims=False)

    relayed = row_count == 4 and heads_here == QUAD and seq_cols == 1 and part == WIDTH and rank_share == RANK
    place = jnp.zeros((2,), jnp.int32)
    if relayed:
        x_rows, w_all, w_state, gain_all, vectors, head_rows, place = start_exchange(
            block_in, proj_inner, adapt_in_up, proj_out,
            adapt_out_down, (proj_state.T, adapt_in_down, adapt_out_up),
            (
                norm_gain[None], conv_inner, conv_inner_bias[None], gate_gain[None], step_bias[None],
                decay_log[None], skip_gain[None],
            ),
            adapter_id, row_count, col_count,
        )
        up_all = down_all = p_all = w_all
        x_rows, cot = lax.optimization_barrier((x_rows, cotangent))
        g_rows = lax.all_to_all(cot.reshape(row_count, chunk, part), "row", 0, 0, tiled=True)
    else:
        head = jnp.zeros((HALO, part), BF16)
        if seq_cols > 1:
            pairs = [(i, (i + 1) % col_count) for i in range(col_count)]
            head = lax.ppermute(block_in[-HALO:], "col", pairs)
            head = jnp.where(lax.rem(col, seq_cols) > 0, head, jnp.zeros_like(head))
        padded = jnp.concatenate([head, block_in], axis=0)
        windows = jnp.stack([padded[r * chunk : r * chunk + total_rows] for r in range(row_count)])
        x_rows = lax.all_to_all(windows, "row", 0, 0, tiled=True)
        g_rows = lax.all_to_all(cotangent.reshape(row_count, chunk, part), "row", 0, 0, tiled=True)

        def split_pairs(value):
            value = value.reshape(value.shape[0], heads_here, 2, P_SIZE)
            return jnp.swapaxes(value, 1, 2).reshape(value.shape[0], 2, local)

        up_part = lax.dynamic_slice_in_dim(adapt_in_up, row * rank_part, rank_part, 0)
        w_block = jnp.concatenate([split_pairs(proj_inner), split_pairs(up_part)], axis=0)
        w_all = lax.all_gather(w_block.reshape(part + rank_part, 2 * local), ("col", "row"))
        w_all = w_all.reshape(col_count, row_count, part + rank_part, 2, local)
        w_all = to_groups(w_all, heads_here).reshape(GROUPS, row_count, part + rank_part, 2 * WIDTH)
        up_all = w_all[:, :, part:, :].reshape(GROUPS, rank_total, 2 * WIDTH)
        up_all = lax.dynamic_slice_in_dim(up_all, adapter * RANK, RANK, 1)[:, None]

        down_part = lax.dynamic_slice_in_dim(adapt_out_down, row * rank_part, rank_part, 0)
        p_block = jnp.concatenate([proj_out, down_part.T], axis=1)
        p_all = lax.all_gather(p_block, ("col", "row")).reshape(col_count, row_count, local, part + rank_part)
        if heads_here != QUAD:
            p_all = jnp.moveaxis(p_all, 1, 0).reshape(row_count, GROUPS, WIDTH, part + rank_part)
            p_all = jnp.moveaxis(p_all, 0, 1)
        down_all = jnp.swapaxes(p_all[..., part:], 1, 2).reshape(GROUPS, WIDTH, rank_total)
        down_all = jnp.swapaxes(lax.dynamic_slice_in_dim(down_all, adapter * RANK, RANK, 2), 1, 2)[:, None]

        in_down = lax.dynamic_slice_in_dim(adapt_in_down, adapter * RANK, RANK, 1)
        out_up = lax.dynamic_slice_in_dim(adapt_out_up, adapter * RANK, RANK, 1)
        shared = pad_lanes(jnp.concatenate([proj_state, in_down, out_up], axis=1), 384)
        w_state = lax.all_gather(shared, "row")
        gain_all = lax.all_gather(norm_gain, "row").reshape(row_count, 1, part)

        scalars = jnp.concatenate([step_bias, decay_log, skip_gain])
        vectors = jnp.concatenate(
            [conv_inner, conv_inner_bias[None], gate_gain[None], pad_lanes(scalars, local)[None]], axis=0
        )
        vectors = lax.all_gather(vectors, "col")
        scalars = vectors[:, 6, : 3 * heads_here].reshape(col_count, 3, heads_here)
        scalars = jnp.swapaxes(scalars, 0, 1).reshape(3, HEADS)
        head_rows = jnp.pad(scalars[:2], ((0, 6), (0, LANES - HEADS)))
        skip_wide = jnp.repeat(scalars[2], P_SIZE).reshape(GROUPS, 1, WIDTH)
        vectors = jnp.concatenate(
            [to_groups(vectors[:, :6], heads_here), skip_wide, jnp.zeros_like(skip_wide)], axis=1
        )
    state_taps = conv_state

    token_f32 = ((chunk, LANES), F32)
    token_low = ((chunk, LANES), BF16)
    inner_low = ((chunk, DI), BF16)
    states = ((blocks, STATES, DI), BF16)
    score_box = ((blocks, BLOCK, BLOCK), F32)
    flipped = ((blocks, STATES, BLOCK), BF16)
    (
        normed, scpre, ratio, sig, cum, lead, turned, bs, cs, cs_t, adv, gate, u, eloc, fin, dec,
    ) = grouped_call(
        front_kernel,
        place,
        (x_rows, gain_all, w_state, state_taps, conv_state_bias[None], head_rows, w_all, up_all, vectors),
        "aaaaaawuc",
        [
            ((total_rows, D), BF16), ((chunk, 256), F32), token_f32, token_f32, token_f32, token_f32,
            ((GROUPS, 2 * QUAD, chunk), F32), token_low, token_low, flipped, ((total_rows, LANES), BF16),
            inner_low, inner_low, states, ((STATES, DI), BF16), ((8, DI), F32),
        ],
        "aaaaaaaaaaalllll",
        [((total_rows, 384), F32), flipped, ((total_rows, WIDTH), F32)],
        flops=int(45e9),
    )
    decay = dec[0:1]
    fin, g_rows = lax.optimization_barrier((fin, g_rows))
    if relayed:
        within, entry = within_and_carry(fin, dec, u, cum, turned, bs, cs)
    else:
        entry = carry_in(fin, decay, row_count, col_count, seq_cols, True)
    out_rows, o, ent, aux, side_grad, out_up_grad = grouped_call(
        functools.partial(scan_kernel, relayed),
        place,
        (x_rows, g_rows, w_state, p_all, down_all, vectors, gate, u, eloc, entry, cum, within if relayed else turned, bs, cs),
        "aaafdclllla" + ("l" if relayed else "c") + "aa",
        [
            ((row_count, chunk, part), BF16), inner_low, ((blocks, STATES, DI), BF16), token_f32, token_low,
            ((RANK, D), F32),
        ],
        "allaaa",
        [score_box, ((GROUPS, chunk, WIDTH), BF16), token_f32, token_f32],
        flops=int(45e9),
    )
    block_out = lax.all_to_all(out_rows, "row", 0, 0, tiled=True).reshape(col_tokens, part)
    dgate, dy, gloc, gfin, out_down_grad = grouped_call(
        gate_kernel,
        place,
        (g_rows, p_all, side_grad, down_all, vectors, gate, o, aux, cum, cs_t),
        "apadcllaaa",
        [inner_low, inner_low, states, ((STATES, DI), BF16), ((GROUPS, RANK, WIDTH), F32)],
        "llllc",
        [((blocks, RANK, BLOCK), BF16)],
        flops=int(25e9),
    )
    gfin, block_out = lax.optimization_barrier((gfin, block_out))
    if relayed:
        exit_grad = carry_over(gfin, dec, False)
    else:
        exit_grad = carry_in(gfin, decay, row_count, col_count, seq_cols, False)
    corr, wide, thin = grouped_call(
        back_kernel,
        place,
        (
            x_rows, gain_all, normed, w_state, w_all, up_all, adv, vectors, state_taps, head_rows,
            u, o, dy, dgate, ent, gloc, exit_grad, cum, lead, turned, ratio, sig, scpre, bs, cs,
            out_down_grad, out_up_grad,
        ),
        "aaaawuacaalllllllaacaaaaaca",
        [
            ((row_count, total_rows, part), BF16), ((row_count, GROUPS, RANK // row_count, 3 * WIDTH), F32),
            ((row_count, 2 * RANK, part), F32),
        ],
        "asa",
        [
            score_box, score_box, token_f32, token_f32, token_f32, token_f32, ((blocks, 8, LANES), F32),
            ((total_rows + HALO, WIDTH), F32), ((total_rows, 2 * WIDTH), BF16), ((total_rows, D), F32),
            ((total_rows, LANES), F32), ((blocks, RANK, BLOCK), BF16),
            ((RANK, 2 * WIDTH), F32), ((RANK, D), F32),
        ],
        flops=int(75e9),
    )

    if heads_here != QUAD:
        share = RANK // row_count
        wide = jnp.swapaxes(wide.reshape(row_count, GROUPS, share, 3, WIDTH), 0, 1)
        wide = to_cols(wide, heads_here, col_count)
        wide = jnp.swapaxes(wide, 0, 1).reshape(row_count, col_count, share, 3 * local)
    corr, wide, thin, in_up, out_down, mine = finish_exchange(corr, wide, thin, adapter_id, relayed)
    late = jnp.zeros((1, HALO, part), BF16)
    if seq_cols > 1:
        pairs = [(i, (i - 1) % col_count) for i in range(col_count)]
        late = lax.ppermute(corr[0:1, :HALO], "col", pairs)
        late = jnp.where(lax.rem(col, seq_cols) < seq_cols - 1, late, jnp.zeros_like(late))
    early = jnp.concatenate([corr[1:, :HALO], late], axis=0)
    early = jnp.pad(early, ((0, 0), (chunk - HALO, 0), (0, 0))).astype(F32)
    input_grad = cotangent.reshape(row_count, chunk, part).astype(F32) + corr[:, HALO:].astype(F32) + early
    input_grad = input_grad.reshape(col_tokens, part)
    if relayed:
        mine = jnp.swapaxes(mine.reshape(2, RANK, part), 1, 2)
        return block_out, input_grad, mine[0], in_up, out_down, mine[1]
    wide = jnp.swapaxes(wide, 0, 1).reshape(col_count, RANK, 3 * local)
    owner = jnp.repeat(adapter_id, seq_cols)
    adapters = rank_total // RANK
    chosen = owner[:, None] == jnp.arange(adapters, dtype=jnp.int32)[None, :]
    wide = jnp.sum(jnp.where(chosen[:, :, None, None], wide[:, None], 0.0), axis=0)
    wide = wide.reshape(rank_total, 3 * local)
    in_up = wide[:, : 2 * local].reshape(rank_total, 2, heads_here, P_SIZE)
    in_up = jnp.swapaxes(in_up, 1, 2).reshape(rank_total, heads_here, 2 * P_SIZE)
    out_down = wide[:, 2 * local :]
    if rank_share <= RANK:
        mine = owner == (col * rank_share) // RANK
        thin = jnp.sum(jnp.where(mine[:, None, None], thin, 0.0), axis=0).reshape(2, RANK, part)
        thin = lax.dynamic_slice_in_dim(thin, lax.rem(col * rank_share, RANK), rank_share, 1)
        thin = jnp.swapaxes(thin, 1, 2)
    else:
        thin = jnp.sum(jnp.where(chosen[:, :, None, None], thin[:, None], 0.0), axis=0)
        thin = thin.reshape(adapters, 2, RANK, part)
        thin = jnp.transpose(thin, (1, 3, 0, 2)).reshape(2, part, rank_total)
        thin = lax.dynamic_slice_in_dim(thin, col * rank_share, rank_share, 2)
    return block_out, input_grad, thin[0], in_up, out_down, thin[1]


def solution(mesh):
    placed = (
        P("col", "row"), P("row"), P("row", "col", None), P("row", None), P(None, "col"), P("col"), P(), P(),
        P("col"), P("col"), P("col"), P("col"), P("col", "row"), P("row", None), P(None, "col", None),
        P(None, "col"), P("row", None), P(), P("col", "row"),
    )
    return jax.shard_map(
        per_device,
        mesh=mesh,
        in_specs=placed,
        out_specs=(
            P("col", "row"), P("col", "row"), P("row", "col"), P(None, "col", None), P(None, "col"),
            P("row", "col"),
        ),
        check_vma=False,
    )
```
